32 devices in a mesh: dp: 16 (over z, y, core), tensor: 2 (over x).
Axes of the slice: x: 2, y: 2, z: 4, core: 2. Of those that a mesh axis runs over, the one named last changes fastest.
Arguments:
- tokens: bfloat16 [16384, 1024], P(('dp', 'tensor')), may hold values from -6 to 6
- cotangent: bfloat16 [16384, 1024], P(('dp', 'tensor')), may hold values from -6 to 6
- segment_ids: int32 [16384], P('dp'), may hold values from 0 to 4, as said below
- padding: int32 [16384], P('dp'), may hold values from 0 to 1, as said below
- shared_weights: float32 [2, 6297600], P('tensor', 'dp')
- first_moment: float32 [2, 16, 4, 393600], P('tensor', 'dp')
- second_moment: float32 [2, 16, 4, 393600], P('tensor', 'dp'), as said below
- outer_momentum: float32 [2, 6297600], P('tensor', 'dp'), may hold values from -0.04 to 0.04
Outputs:
- block_out: bfloat16 [16384, 1024], P(('dp', 'tensor'))
- input_grad: bfloat16 [16384, 1024], P(('dp', 'tensor'))
- group_grads: float32 [2, 16, 4, 393600], P('tensor', 'dp')
- group_first: float32 [2, 16, 4, 393600], P('tensor', 'dp')
- group_second: float32 [2, 16, 4, 393600], P('tensor', 'dp')
- group_weights: float32 [2, 16, 4, 393600], P('tensor', 'dp')
- mean_diff: float32 [2, 6297600], P('tensor', 'dp')
- new_momentum: float32 [2, 6297600], P('tensor', 'dp')
- new_weights: float32 [2, 6297600], P('tensor', 'dp')
The draws below stay inside these ranges and needn't reach their ends.
Inputs may be any that keep to these rules, and one draw needn't show every extreme that they name: `segment_ids`: within each sequence of 1024 tokens the ids start at 0 and rise by one at each document boundary; a document has 60 to 800 tokens, except that a sequence's last one may be cut and its first one may be shorter, and each sequence holds a document of exactly 800 tokens. In each sequence the real tokens come first and at most 256 are padding; some sequence has no padding. `second_moment`: Positive.
All inputs are finite; a program needn't handle non-finite values.
Results may differ from the reference program's by a relative error of at most 0.018.
Values may be sent and summed in bfloat16 or wider, within the bound.
A program may use at most 256 MiB of HBM per device.

```python
import math
import jax
import jax.numpy as jnp
from jax import lax

D = 1024
HEADS = 16
HD = 64
FF = 4096
SEQ_LEN = 1024
SEQ_DEV = 1
GROUPS = 4
STEP = 10
SEQS = 16
TOKENS = 16384
PT = 6297600
PIECE = 393600
N_DP = 16
N_TENSOR = 2


def segment_lengths(tensor_size):
    local_width = D // tensor_size
    hidden = FF // tensor_size
    return [3 * D * local_width, local_width * D, D * hidden, hidden * D, local_width, local_width, hidden, 6 * local_width]


def per_column(tensor_size, leading, vector_rows):
    local_width = D // tensor_size
    lengths = segment_lengths(tensor_size)
    head_parts = [jnp.full((lengths[number],), leading[number], jnp.float32) for number in range(7)]
    tail_part = jnp.repeat(jnp.array(vector_rows, jnp.float32), local_width)
    return jnp.concatenate(head_parts + [tail_part])


def state_factor():
    flat_rows = per_column(N_TENSOR, [0.3, 0.15, 0.3, 0.5, 0.3, 0.3, 0.3], [1.0, 1.0, 1.0, 1.0, 1.0, 1.0])
    slots = N_DP // GROUPS
    grid_view = flat_rows.reshape(GROUPS, slots, PIECE).transpose(1, 0, 2)
    return jnp.tile(grid_view, (GROUPS, 1, 1))[None]


def gradient_size():
    return math.sqrt(N_DP // GROUPS * SEQ_DEV * SEQ_LEN)


def draw_segment_ids(key, part):
    key = jax.random.fold_in(key, 11)
    longest = SEQ_LEN * 25 // 32
    shortest = max(1, SEQ_LEN * 15 // 256)
    slots = SEQ_LEN // shortest + 2
    short_count = (SEQ_LEN - longest) // shortest
    keys = jax.random.split(key, 4)
    lengths = jax.random.randint(keys[0], (SEQS, slots), shortest, longest + 1)
    leading = jax.random.randint(keys[1], (SEQS, 1), shortest, SEQ_LEN - longest + 1)
    which = jax.random.randint(keys[2], (SEQS, 1), 0, 2)
    packed_one = jax.random.randint(keys[3], (), 0, SEQS)
    column = jnp.arange(slots, dtype=jnp.int32)[None, :]
    lengths = jnp.where(column == which, longest, lengths)
    lengths = jnp.where((which == 1) & (column == 0), leading, lengths)
    packed_row = jnp.where(column < short_count, shortest, jnp.where(column == short_count, longest, lengths))
    row_number = jnp.arange(SEQS, dtype=jnp.int32)[:, None]
    lengths = jnp.where(row_number == packed_one, packed_row, lengths)
    ends = jnp.cumsum(lengths, axis=1)
    positions = jnp.arange(SEQ_LEN, dtype=jnp.int32)
    ids = jnp.sum((positions[None, :, None] >= ends[:, None, :]).astype(jnp.int32), axis=2)
    return ids.reshape(TOKENS).astype(jnp.int32)


def draw_padding(key, part):
    key = jax.random.fold_in(key, 13)
    keys = jax.random.split(key, 2)
    tails = jax.random.randint(keys[0], (SEQS, 1), 0, SEQ_LEN // 4 + 1)
    full_one = jax.random.randint(keys[1], (), 0, SEQS)
    tails = jnp.where(jnp.arange(SEQS, dtype=jnp.int32)[:, None] == full_one, 0, tails)
    positions = jnp.arange(SEQ_LEN, dtype=jnp.int32)
    live = (positions[None, :] < SEQ_LEN - tails).astype(jnp.int32)
    return live.reshape(TOKENS)


def draw_shared_weights(key, part):
    key = jax.random.fold_in(key, 5)
    base = jax.random.truncated_normal(key, -3.0, 3.0, (N_TENSOR, PT), jnp.float32)
    scales = per_column(N_TENSOR, [D ** (-0.5), 4.0 * D ** (-0.5), D ** (-0.5), FF ** (-0.5), 0.5, 0.5, 0.5], [0.2, 0.3, 0.2, 0.3, 0.3, 0.3])
    offsets = per_column(N_TENSOR, [0.0, 0.0, 0.0, 0.0, 0.0, 0.0, 0.0], [1.0, 0.0, 1.0, 0.0, 0.0, 0.0])
    return offsets[None, :] + scales[None, :] * base


def draw_first_moment(key, part):
    key = jax.random.fold_in(key, 7)
    shape = (N_TENSOR, N_DP, GROUPS, PIECE)
    base = jax.random.truncated_normal(key, -3.0, 3.0, shape, jnp.float32)
    return 0.1 / 0.9 * gradient_size() * state_factor() * base


def draw_second_moment(key, part):
    key = jax.random.fold_in(key, 9)
    shape = (N_TENSOR, N_DP, GROUPS, PIECE)
    spread = jnp.exp(jax.random.uniform(key, shape, jnp.float32, math.log(0.5), math.log(8.0)))
    size = gradient_size() * state_factor()
    return 0.001 / 0.999 * size * size * spread


def levels(rng, shape, shards, least, high):
    def one(dim, blocks):
        heights = jax.random.uniform(jax.random.fold_in(jax.random.fold_in(rng, 6), dim), (blocks,), jnp.float32, least / len(shards), high / len(shards))
        return jnp.repeat(jnp.exp(heights), shape[dim] // blocks).reshape((-1,) + (1,) * (len(shape) - dim - 1))

    gain = one(*shards[0])
    for cut in shards[1:]:
        gain = gain * one(*cut)
    return gain


def normal_values(own_key, extent, scale, reach, cuts=(), kind=jnp.bfloat16):
    drawn = scale * jax.random.normal(own_key, extent, jnp.float32)
    if cuts:
        drawn = drawn * levels(own_key, extent, cuts, -0.22, 0.18)
    return jnp.clip(drawn, -reach, reach).astype(kind)


def setup_inputs(seed: int = 0) -> dict:
    streams_of = jax.random.split(jax.random.key(seed), 9)
    return {
        "tokens": normal_values(streams_of[0], (TOKENS, D), 1.0, 6.0, ((0, 32),)),
        "cotangent": normal_values(streams_of[1], (TOKENS, D), 1.0, 6.0, ((0, 32),)),
        "segment_ids": draw_segment_ids(jax.random.fold_in(streams_of[8], 71), 0),
        "padding": draw_padding(jax.random.fold_in(streams_of[8], 71), 0),
        "shared_weights": draw_shared_weights(jax.random.fold_in(streams_of[8], 71), 0),
        "first_moment": draw_first_moment(jax.random.fold_in(streams_of[8], 71), 0),
        "second_moment": draw_second_moment(jax.random.fold_in(streams_of[8], 71), 0),
        "outer_momentum": normal_values(streams_of[7], (N_TENSOR, PT), 0.01, 0.04, ((0, 2), (1, 16)), jnp.float32),
    }


@jax.custom_vjp
def low(v):
    return lax.optimization_barrier(v.astype(jnp.bfloat16)).astype(jnp.float32)

@jax.custom_vjp
def low_back(v):
    return v

def low_keep(v):
    return (low(v), None)

def low_pass(kept, grad):
    return (grad,)

def back_keep(v):
    return (v, None)

def back_low(kept, grad):
    return (low(grad),)
low.defvjp(low_keep, low_pass)
low_back.defvjp(back_keep, back_low)
PRECISE = lax.Precision.HIGHEST
NORM_EPS = 1e-05
MASKED = -1000000000.0
BETA_ONE = 0.9
BETA_TWO = 0.999
ADAM_EPS = 1e-08
INNER_RATE = 0.02
DECAY = 0.01
OUTER_MU = 0.9
OUTER_RATE = 0.7

def boundaries(tensor_size):
    local_width = D // tensor_size
    hidden = FF // tensor_size
    lengths = [3 * D * local_width, local_width * D, D * hidden, hidden * D, local_width, local_width, hidden, 6 * local_width]
    points = [0]
    for amount in lengths:
        points.append(points[-1] + amount)
    return points

def assemble(flat_rows):
    tensor_size = flat_rows.shape[0]
    local_width = D // tensor_size
    hidden = FF // tensor_size
    points = boundaries(tensor_size)
    segments = [flat_rows[:, points[number]:points[number + 1]] for number in range(8)]
    projection = segments[0].reshape(tensor_size, 3, D, local_width).transpose(1, 2, 0, 3).reshape(3, D, D)
    out_weight = segments[1].reshape(D, D)
    in_weight = segments[2].reshape(tensor_size, D, hidden).transpose(1, 0, 2).reshape(D, FF)
    down_weight = segments[3].reshape(FF, D)
    query_bias = segments[4].reshape(D)
    value_bias = segments[5].reshape(D)
    inner_bias = segments[6].reshape(FF)
    vectors = segments[7].reshape(tensor_size, 6, local_width).transpose(1, 0, 2).reshape(6, D)
    return (projection, out_weight, in_weight, down_weight, query_bias, value_bias, inner_bias, vectors)

def layer_norm(values, norm_gain, norm_shift):
    average = lax.optimization_barrier(jnp.mean(values, axis=-1, keepdims=True))
    centred = values - average
    variance = lax.optimization_barrier(jnp.mean(centred * centred, axis=-1, keepdims=True))
    return centred * lax.rsqrt(variance + NORM_EPS) * norm_gain + norm_shift

def attend(query, keys, values, seg_ids, live_ids):
    length = query.shape[0]
    block_rows = min(512, length)
    key_pos = jnp.arange(length, dtype=jnp.int32)
    score_scale = HD ** (-0.5)

    def one_block(block_index):
        offset = block_index * block_rows
        query_block = lax.dynamic_slice_in_dim(query, offset, block_rows, 0)
        seg_block = lax.dynamic_slice_in_dim(seg_ids, offset, block_rows, 0)
        query_pos = offset + jnp.arange(block_rows, dtype=jnp.int32)
        allowed = (seg_block[:, None] == seg_ids[None, :]) & ((live_ids[None, :] == 1) | (query_pos[:, None] == key_pos[None, :]))
        scores = low_back(jnp.einsum('qhd,khd->hqk', query_block, keys, precision=PRECISE) * score_scale)
        scores = jnp.where(allowed[None], scores, MASKED)
        probabilities = low(jax.nn.softmax(scores, axis=-1))
        return jnp.einsum('hqk,khd->qhd', probabilities, values, precision=PRECISE)
    context = lax.map(jax.checkpoint(one_block), jnp.arange(length // block_rows, dtype=jnp.int32))
    return context.reshape(length, HEADS, HD)

def group_forward(flat_rows, inputs, seg_ids, live_ids):
    projection, out_weight, in_weight, down_weight, query_bias, value_bias, inner_bias, vectors = assemble(flat_rows)
    projection = low(projection)
    out_weight = low(out_weight)
    in_weight = low(in_weight)
    down_weight = low(down_weight)

    def one_sequence(item):
        x_seq, seg_seq, live_seq = item
        length = x_seq.shape[0]
        projected = jnp.einsum('td,kde->kte', x_seq, projection, precision=PRECISE)
        query = low(low_back(projected[0] + query_bias))
        keys = low(low_back(projected[1]))
        values = low(low_back(projected[2] + value_bias))
        context = attend(query.reshape(length, HEADS, HD), keys.reshape(length, HEADS, HD), values.reshape(length, HEADS, HD), seg_seq, live_seq)
        context = low(low_back(context.reshape(length, D)))
        resid_one = x_seq + (low_back(jnp.dot(context, out_weight, precision=PRECISE)) + vectors[4])
        middle = layer_norm(resid_one, vectors[0], vectors[1])
        inner = low_back(jnp.dot(low(middle), in_weight, precision=PRECISE) + inner_bias)
        activated = low(jax.nn.gelu(inner, approximate=False))
        resid_two = middle + (low_back(jnp.dot(activated, down_weight, precision=PRECISE)) + vectors[5])
        return layer_norm(resid_two, vectors[2], vectors[3])
    return lax.map(jax.checkpoint(one_sequence), (inputs, seg_ids, live_ids))

def reference(tokens, cotangent, segment_ids, padding, shared_weights, first_moment, second_moment, outer_momentum):
    tensor_size = shared_weights.shape[0]
    per_group = SEQS // GROUPS
    slots = N_DP // GROUPS
    inputs = tokens.astype(jnp.float32).reshape(SEQS, SEQ_LEN, D)
    backs = cotangent.astype(jnp.float32).reshape(SEQS, SEQ_LEN, D)
    seg_all = segment_ids.reshape(SEQS, SEQ_LEN)
    live_all = padding.reshape(SEQS, SEQ_LEN)

    def to_blocks(flat_rows):
        return flat_rows.reshape(tensor_size, GROUPS, slots, PIECE).transpose(0, 2, 1, 3)
    matrix_count = (4 * D * D + 2 * D * FF) // tensor_size
    flat_mask = (jnp.arange(PT, dtype=jnp.int32) < matrix_count).astype(jnp.float32)
    decay_mask = to_blocks(jnp.broadcast_to(flat_mask[None, :], (tensor_size, PT)))
    weight_blocks = to_blocks(shared_weights)
    outputs, grads_in, grads_all, firsts, seconds, weights_all = ([], [], [], [], [], [])
    diff_total = jnp.zeros_like(weight_blocks)
    for group in range(GROUPS):
        group_rows = slice(group * per_group, (group + 1) * per_group)

        def forward_run(flat_rows, group_inputs, seg_ids=seg_all[group_rows], live_ids=live_all[group_rows]):
            return group_forward(flat_rows, group_inputs, seg_ids, live_ids)
        result, pullback = jax.vjp(forward_run, shared_weights, inputs[group_rows])
        grad_flat, grad_inputs = pullback(backs[group_rows])
        outputs.append(result)
        grads_in.append(grad_inputs)
        grad_blocks = to_blocks(grad_flat)
        first_old = first_moment[:, group * slots:(group + 1) * slots]
        second_old = second_moment[:, group * slots:(group + 1) * slots]
        first_new = BETA_ONE * first_old + (1 - BETA_ONE) * grad_blocks
        second_new = BETA_TWO * second_old + (1 - BETA_TWO) * grad_blocks * grad_blocks
        first_hat = first_new / (1 - BETA_ONE ** STEP)
        second_hat = second_new / (1 - BETA_TWO ** STEP)
        stepped = weight_blocks - INNER_RATE * (first_hat / (jnp.sqrt(second_hat) + ADAM_EPS) + DECAY * decay_mask * weight_blocks)
        diff_total = diff_total + (weight_blocks - stepped)
        grads_all.append(grad_blocks)
        firsts.append(first_new)
        seconds.append(second_new)
        weights_all.append(stepped)
    block_out = jnp.concatenate(outputs, axis=0).reshape(TOKENS, D).astype(jnp.bfloat16)
    input_grad = jnp.concatenate(grads_in, axis=0).reshape(TOKENS, D).astype(jnp.bfloat16)
    mean_diff = (diff_total / GROUPS).transpose(0, 2, 1, 3).reshape(tensor_size, PT)
    new_momentum = OUTER_MU * outer_momentum + mean_diff
    new_weights = shared_weights - OUTER_RATE * (mean_diff + OUTER_MU * new_momentum)
    return (block_out, input_grad, jnp.concatenate(grads_all, axis=1), jnp.concatenate(firsts, axis=1), jnp.concatenate(seconds, axis=1), jnp.concatenate(weights_all, axis=1), mean_diff, new_momentum, new_weights)
```

```python
import functools

import jax
import jax.numpy as jnp
import numpy as np
from jax import lax
from jax.experimental import pallas as pl
from jax.experimental.pallas import tpu as pltpu
from jax.sharding import Mesh
from jax.sharding import PartitionSpec as P

D = 1024
HEADS = 16
HD = 64
FF = 4096
SEQ_LEN = 1024
GROUPS = 4
STEP = 10


NORM_EPS = 1e-05
MASKED = -1000000000.0
BETA_ONE = 0.9
BETA_TWO = 0.999
ADAM_EPS = 1e-08
INNER_RATE = 0.02
DECAY = 0.01
OUTER_MU = 0.9
OUTER_RATE = 0.7
ROOT_HALF = 0.7071067811865476
INV_ROOT_TWO_PI = 0.3989422804014327


def from_partner(block, axis, stride):
    count = lax.axis_size(axis)
    route = []
    for low in range(count):
        high = low | 1 << stride
        if high != low and high < count:
            route += [(low, high), (high, low)]
    return lax.ppermute(block, axis, route)


def boundaries(tensor_size):
    local_width = D // tensor_size
    hidden = FF // tensor_size
    lengths = [
        3 * D * local_width,
        local_width * D,
        D * hidden,
        hidden * D,
        local_width,
        local_width,
        hidden,
        6 * local_width,
    ]
    points = [0]
    for amount in lengths:
        points.append(points[-1] + amount)
    return points


def layer_norm(values, norm_gain, norm_shift):
    average = jnp.mean(values, axis=-1, keepdims=True)
    centred = values - average
    variance = jnp.mean(centred * centred, axis=-1, keepdims=True)
    inv_dev = lax.rsqrt(variance + NORM_EPS)
    normed = centred * inv_dev
    return (normed * norm_gain + norm_shift, normed, inv_dev)


def norm_back(grad_normed, normed, inv_dev):
    first_part = jnp.mean(grad_normed, axis=-1, keepdims=True)
    second_part = jnp.mean(grad_normed * normed, axis=-1, keepdims=True)
    return inv_dev * (grad_normed - first_part - normed * second_part)


def gelu_slope(inner):
    return (
        0.5 * (1.0 + jax.scipy.special.erf(inner * ROOT_HALF))
        + inner * jnp.exp(-0.5 * inner * inner) * INV_ROOT_TWO_PI
    )


def row_contract(left_side, right_side):
    return lax.dot_general(
        left_side, right_side, (((0,), (0,)), ((), ())), preferred_element_type=jnp.float32
    )


def col_contract(left_side, right_side):
    return lax.dot_general(
        left_side, right_side, (((1,), (1,)), ((), ())), preferred_element_type=jnp.float32
    )


def halve_rounds(values, bit_list, first_axis, top_bit, dp_index, site_call):
    for bit_number in bit_list:
        axis_number = first_axis + top_bit - bit_number
        my_bit = dp_index >> bit_number & 1
        kept = lax.dynamic_index_in_dim(values, my_bit, axis_number, keepdims=True)
        outgoing = lax.dynamic_index_in_dim(values, 1 - my_bit, axis_number, keepdims=True)
        values = kept + site_call(outgoing, bit_number)
    return values


def local_general(
    tokens,
    cotangent,
    segment_ids,
    padding,
    shared_weights,
    first_moment,
    second_moment,
    outer_momentum,
):
    tensor_size = lax.axis_size("tensor")
    local_width = D // tensor_size
    hidden = FF // tensor_size
    local_heads = HEADS // tensor_size
    seq_rows = segment_ids.shape[0]
    seq_count = seq_rows // SEQ_LEN
    block_rows = min(512, SEQ_LEN)
    per_seq = SEQ_LEN // block_rows
    block_total = seq_count * per_seq
    score_scale = HD ** (-0.5)
    bf16 = jnp.bfloat16
    f32 = jnp.float32
    masters = lax.all_gather(shared_weights, "dp", axis=1, tiled=True)[0]
    points = boundaries(tensor_size)
    segments = [masters[points[number] : points[number + 1]] for number in range(8)]
    proj_weight = segments[0].reshape(3, D, local_width).astype(bf16)
    out_weight = segments[1].reshape(local_width, D).astype(bf16)
    in_weight = segments[2].reshape(D, hidden).astype(bf16)
    down_weight = segments[3].reshape(hidden, D).astype(bf16)
    query_bias = segments[4]
    value_bias = segments[5]
    inner_bias = segments[6]
    vectors = lax.all_gather(segments[7].reshape(6, local_width), "tensor", axis=1, tiled=True)
    inputs_all = lax.all_gather(tokens, "tensor", axis=0, tiled=True)
    projected = jnp.einsum("td,kde->kte", inputs_all, proj_weight, preferred_element_type=f32)
    query = (projected[0] + query_bias).astype(bf16)
    keys = projected[1].astype(bf16)
    values = (projected[2] + value_bias).astype(bf16)
    query_four = query.reshape(seq_count, SEQ_LEN, local_heads, HD)
    keys_four = keys.reshape(seq_count, SEQ_LEN, local_heads, HD)
    values_four = values.reshape(seq_count, SEQ_LEN, local_heads, HD)
    seg_two = segment_ids.reshape(seq_count, SEQ_LEN)
    live_two = padding.reshape(seq_count, SEQ_LEN)
    key_pos = jnp.arange(SEQ_LEN, dtype=jnp.int32)

    def block_scores(block_index):
        sequence = block_index // per_seq
        offset = block_index % per_seq * block_rows
        query_rows = lax.dynamic_index_in_dim(query_four, sequence, 0, keepdims=False)
        query_block = lax.dynamic_slice_in_dim(query_rows, offset, block_rows, 0)
        key_rows = lax.dynamic_index_in_dim(keys_four, sequence, 0, keepdims=False)
        seg_row = lax.dynamic_index_in_dim(seg_two, sequence, 0, keepdims=False)
        live_row = lax.dynamic_index_in_dim(live_two, sequence, 0, keepdims=False)
        seg_block = lax.dynamic_slice_in_dim(seg_row, offset, block_rows, 0)
        query_pos = offset + jnp.arange(block_rows, dtype=jnp.int32)
        allowed = (seg_block[:, None] == seg_row[None, :]) & (
            (live_row[None, :] == 1) | (query_pos[:, None] == key_pos[None, :])
        )
        raw_scores = (
            jnp.einsum("qhd,khd->hqk", query_block, key_rows, preferred_element_type=f32)
            * score_scale
        )
        return (
            jnp.where(allowed[None], raw_scores, MASKED),
            query_block,
            key_rows,
            sequence,
            offset,
        )

    def forward_block(block_index):
        scores, query_block, key_rows, sequence, offset = block_scores(block_index)
        value_rows = lax.dynamic_index_in_dim(values_four, sequence, 0, keepdims=False)
        highest = jnp.max(scores, axis=-1, keepdims=True)
        exponent = jnp.exp(scores - highest)
        summed = jnp.sum(exponent, axis=-1, keepdims=True)
        probabilities = (exponent / summed).astype(bf16)
        context = jnp.einsum("hqk,khd->qhd", probabilities, value_rows, preferred_element_type=f32)
        return (context, (highest + jnp.log(summed))[..., 0])

    context_blocks, log_totals = lax.map(forward_block, jnp.arange(block_total, dtype=jnp.int32))
    context_low = context_blocks.reshape(seq_rows, local_width).astype(bf16)
    attn_sum = lax.psum_scatter(
        jnp.dot(context_low, out_weight, preferred_element_type=f32).astype(jnp.bfloat16),
        "tensor",
        scatter_dimension=0,
        tiled=True,
    ).astype(jnp.float32)
    tokens_f = tokens.astype(f32)
    middle, normed_one, inv_one = layer_norm(
        tokens_f + (attn_sum + vectors[4]), vectors[0], vectors[1]
    )
    middle_all = lax.all_gather(middle.astype(bf16), "tensor", axis=0, tiled=True)
    inner = jnp.dot(middle_all, in_weight, preferred_element_type=f32) + inner_bias
    activated = jax.nn.gelu(inner, approximate=False).astype(bf16)
    ffn_sum = lax.psum_scatter(
        jnp.dot(activated, down_weight, preferred_element_type=f32).astype(jnp.bfloat16),
        "tensor",
        scatter_dimension=0,
        tiled=True,
    ).astype(jnp.float32)
    result, normed_two, inv_two = layer_norm(
        middle + (ffn_sum + vectors[5]), vectors[2], vectors[3]
    )
    block_out = result.astype(bf16)
    grad_out = cotangent.astype(f32)
    grad_gain_two = jnp.sum(grad_out * normed_two, axis=0)
    grad_shift_two = jnp.sum(grad_out, axis=0)
    grad_two = norm_back(grad_out * vectors[2], normed_two, inv_two)
    grad_down_bias = jnp.sum(grad_two, axis=0)
    back_all = lax.all_gather(grad_two.astype(bf16), "tensor", axis=0, tiled=True)
    grad_down_weight = row_contract(activated, back_all)
    grad_act = col_contract(back_all, down_weight)
    grad_inner = (grad_act * gelu_slope(inner)).astype(bf16)
    grad_inner_bias = jnp.sum(grad_inner.astype(f32), axis=0)
    grad_in_weight = row_contract(middle_all, grad_inner)
    grad_middle = grad_two + lax.psum_scatter(
        col_contract(grad_inner, in_weight).astype(jnp.bfloat16),
        "tensor",
        scatter_dimension=0,
        tiled=True,
    ).astype(jnp.float32)
    grad_gain_one = jnp.sum(grad_middle * normed_one, axis=0)
    grad_shift_one = jnp.sum(grad_middle, axis=0)
    grad_one = norm_back(grad_middle * vectors[0], normed_one, inv_one)
    grad_out_bias = jnp.sum(grad_one, axis=0)
    attn_back_all = lax.all_gather(grad_one.astype(bf16), "tensor", axis=0, tiled=True)
    grad_out_weight = row_contract(context_low, attn_back_all)
    grad_context = col_contract(attn_back_all, out_weight).astype(bf16)
    grad_context_four = grad_context.reshape(seq_count, SEQ_LEN, local_heads, HD)

    def backward_block(carry, block_index):
        grad_keys, grad_values = carry
        scores, query_block, key_rows, sequence, offset = block_scores(block_index)
        value_rows = lax.dynamic_index_in_dim(values_four, sequence, 0, keepdims=False)
        log_total = lax.dynamic_index_in_dim(log_totals, block_index, 0, keepdims=False)
        probabilities = jnp.exp(scores - log_total[..., None])
        prob_low = probabilities.astype(bf16)
        grad_rows = lax.dynamic_index_in_dim(grad_context_four, sequence, 0, keepdims=False)
        grad_block = lax.dynamic_slice_in_dim(grad_rows, offset, block_rows, 0)
        grad_probs = jnp.einsum("qhd,khd->hqk", grad_block, value_rows, preferred_element_type=f32)
        grad_scores = probabilities * (
            grad_probs - jnp.sum(grad_probs * probabilities, axis=-1, keepdims=True)
        )
        scores_low = grad_scores.astype(bf16)
        grad_query = (
            jnp.einsum("hqk,khd->qhd", scores_low, key_rows, preferred_element_type=f32)
            * score_scale
        )
        key_term = (
            jnp.einsum("hqk,qhd->khd", scores_low, query_block, preferred_element_type=f32)
            * score_scale
        )
        value_term = jnp.einsum("hqk,qhd->khd", prob_low, grad_block, preferred_element_type=f32)
        grad_keys = lax.dynamic_update_index_in_dim(
            grad_keys,
            lax.dynamic_index_in_dim(grad_keys, sequence, 0, keepdims=False) + key_term,
            sequence,
            0,
        )
        grad_values = lax.dynamic_update_index_in_dim(
            grad_values,
            lax.dynamic_index_in_dim(grad_values, sequence, 0, keepdims=False) + value_term,
            sequence,
            0,
        )
        return ((grad_keys, grad_values), grad_query)

    empty = jnp.zeros((seq_count, SEQ_LEN, local_heads, HD), f32)
    (grad_keys, grad_values), grad_queries = lax.scan(
        backward_block, (empty, empty), jnp.arange(block_total, dtype=jnp.int32)
    )
    grad_proj = jnp.stack(
        [
            grad_queries.reshape(seq_rows, local_width),
            grad_keys.reshape(seq_rows, local_width),
            grad_values.reshape(seq_rows, local_width),
        ]
    ).astype(bf16)
    grad_proj_weight = jnp.einsum("td,kte->kde", inputs_all, grad_proj, preferred_element_type=f32)
    grad_query_bias = jnp.sum(grad_proj[0].astype(f32), axis=0)
    grad_value_bias = jnp.sum(grad_proj[2].astype(f32), axis=0)
    input_part = jnp.einsum("kte,kde->td", grad_proj, proj_weight, preferred_element_type=f32)
    vector_part = jnp.stack(
        [
            grad_gain_one,
            grad_shift_one,
            grad_gain_two,
            grad_shift_two,
            grad_out_bias,
            grad_down_bias,
        ]
    )
    input_share, vector_grad = (
        lax.psum_scatter(
            input_part.astype(jnp.bfloat16), "tensor", scatter_dimension=0, tiled=True
        ).astype(jnp.float32),
        lax.psum_scatter(
            vector_part.astype(jnp.bfloat16), "tensor", scatter_dimension=1, tiled=True
        ).astype(jnp.float32),
    )
    input_grad = (grad_one + input_share).astype(bf16)
    flat_grad = jnp.concatenate(
        [
            grad_proj_weight.reshape(-1),
            grad_out_weight.reshape(-1),
            grad_in_weight.reshape(-1),
            grad_down_weight.reshape(-1),
            grad_query_bias,
            grad_value_bias,
            grad_inner_bias,
            vector_grad.reshape(-1),
        ]
    )
    dp_size = lax.axis_size("dp")
    per_group = dp_size // GROUPS
    inner_bits = per_group.bit_length() - 1
    all_bits = dp_size.bit_length() - 1
    dp_index = lax.axis_index("dp")
    slot_index = dp_index % per_group
    piece_len = shared_weights.shape[1]
    grid_view = flat_grad.reshape(GROUPS, per_group, piece_len)
    inner_list = list(range(inner_bits))
    outer_list = list(range(inner_bits, all_bits))
    inner_list = inner_list[::-1]
    outer_list = outer_list[::-1]
    summed_grid = grid_view
    for bit_number in inner_list:
        summed_grid = summed_grid + from_partner(
            summed_grid.astype(jnp.bfloat16), "dp", bit_number
        ).astype(summed_grid.dtype)
    grad_block = lax.dynamic_index_in_dim(summed_grid, slot_index, 1, keepdims=False)
    weights_block = lax.dynamic_index_in_dim(
        masters.reshape(GROUPS, per_group, piece_len), slot_index, 1, keepdims=False
    )
    matrix_count = (4 * D * D + 2 * D * FF) // tensor_size
    flat_index = (
        jnp.arange(GROUPS, dtype=jnp.int32)[:, None] * per_group + slot_index
    ) * piece_len + jnp.arange(piece_len, dtype=jnp.int32)[None, :]
    decay_mask = (flat_index < matrix_count).astype(f32)
    first_new = BETA_ONE * first_moment[0, 0] + (1 - BETA_ONE) * grad_block
    second_new = BETA_TWO * second_moment[0, 0] + (1 - BETA_TWO) * grad_block * grad_block
    first_hat = first_new / (1 - BETA_ONE**STEP)
    second_hat = second_new / (1 - BETA_TWO**STEP)
    group_weights = weights_block - INNER_RATE * (
        first_hat / (jnp.sqrt(second_hat) + ADAM_EPS) + DECAY * decay_mask * weights_block
    )
    difference = weights_block - group_weights

    def outer_swap(outgoing, bit_number):
        return from_partner(outgoing.astype(jnp.bfloat16), "dp", bit_number).astype(outgoing.dtype)

    outer_bits = all_bits - inner_bits
    diff_view = difference.reshape((2,) * outer_bits + (piece_len,))
    diff_sum = halve_rounds(diff_view, outer_list, 0, all_bits - 1, dp_index, outer_swap).reshape(
        piece_len
    )
    mean_diff = diff_sum / GROUPS
    new_momentum = OUTER_MU * outer_momentum[0] + mean_diff
    new_weights = shared_weights[0] - OUTER_RATE * (mean_diff + OUTER_MU * new_momentum)
    return (
        block_out,
        input_grad,
        grad_block[None, None],
        first_new[None, None],
        second_new[None, None],
        group_weights[None, None],
        mean_diff[None],
        new_momentum[None],
        new_weights[None],
    )


LANES = 128
NT = (((1,), (1,)), ((), ()))
NN = (((1,), (0,)), ((), ()))
TN = (((0,), (0,)), ((), ()))
VMEM_BYTES = 58 << 20
f32 = jnp.float32
bf16 = jnp.bfloat16


def dot(left, right, dims):
    return lax.dot_general(left, right, dims, preferred_element_type=f32)


def params(**more):
    return pltpu.CompilerParams(vmem_limit_bytes=VMEM_BYTES, **more)


def round_up(number, step):
    return -(-number // step) * step


def attn_bwd_kernel(
    q_ref, k_ref, v_ref, ctx_ref, dctx_ref, code_ref, seg_ref, lse_ref, dq_ref, dk_ref, dv_ref, *, rows_q
):
    n = q_ref.shape[0]
    low = lax.broadcasted_iota(jnp.int32, (1, LANES), 1) < HD
    zero = jnp.zeros((), bf16)
    k = k_ref[...]
    v = v_ref[...]
    k_t = k.T
    code = code_ref[...]
    pick = (
        lax.broadcasted_iota(jnp.int32, (8, LANES), 1) // HD
        == lax.broadcasted_iota(jnp.int32, (8, LANES), 0)
    ).astype(f32)
    dks = [jnp.zeros((n, LANES), f32)] * 2
    dvs = [jnp.zeros((n, LANES), f32)] * 2
    scale = jnp.asarray(HD**-0.5, bf16)
    for i in range(n // rows_q):
        r = pl.ds(i * rows_q, rows_q)
        q = q_ref[r, :] * scale
        do = dctx_ref[r, :]
        prod = do.astype(f32) * ctx_ref[r, :].astype(f32)
        delta = lax.dot_general(
            pick, prod, NT, precision=lax.Precision.HIGHEST, preferred_element_type=f32
        )
        keys = lax.broadcasted_iota(jnp.int32, (n, rows_q), 0)
        qs = lax.broadcasted_iota(jnp.int32, (n, rows_q), 1) + i * rows_q
        allowed = (code == seg_ref[:, r]) | (keys == qs)
        dqs = []
        for h in range(2):
            qh = jnp.where(low, q, zero) if h == 0 else jnp.where(low, zero, q)
            doh = jnp.where(low, do, zero) if h == 0 else jnp.where(low, zero, do)
            s = jnp.where(allowed, dot(k, qh, NT), MASKED)
            p = jnp.exp(s - lse_ref[0, h : h + 1, r])
            dp = dot(v, doh, NT)
            ds = (p * (dp - delta[h : h + 1])).astype(bf16)
            dvs[h] = dvs[h] + dot(p.astype(bf16), do, NN)
            dks[h] = dks[h] + dot(ds, q, NN)
            dqs.append(dot(k_t[h * HD : (h + 1) * HD], ds, NN))
        dq_ref[r, :] = (jnp.concatenate(dqs, axis=0).T * (HD**-0.5)).astype(bf16)
    dk_ref[...] = jnp.where(low, dks[0], dks[1]).astype(bf16)
    dv_ref[...] = jnp.where(low, dvs[0], dvs[1]).astype(bf16)


def attn_bwd(q, k, v, ctx, dctx, code_col, seg_row, lse, rows_q=256):
    n, w = q.shape
    pairs = w // LANES
    blk = pl.BlockSpec((n, LANES), lambda h: (0, h))
    out = jax.ShapeDtypeStruct((n, w), bf16)
    return pl.pallas_call(
        functools.partial(attn_bwd_kernel, rows_q=rows_q),
        grid=(pairs,),
        in_specs=[blk] * 5
        + [
            pl.BlockSpec((n, 1), lambda h: (0, 0)),
            pl.BlockSpec((1, n), lambda h: (0, 0)),
            pl.BlockSpec((1, 2, n), lambda h: (h, 0, 0)),
        ],
        out_specs=[blk] * 3,
        out_shape=[out] * 3,
        cost_estimate=pl.CostEstimate(
            flops=20 * n * n * w, bytes_accessed=16 * n * w, transcendentals=n * n * w // HD
        ),
        compiler_params=params(),
        name="attn_bwd",
    )(q, k, v, ctx, dctx, code_col, seg_row, lse)


def matrix_table(tensor_size):
    local_width = D // tensor_size
    hidden = FF // tensor_size
    table = []
    offset = 0
    for rows, columns in ((3 * D, local_width), (local_width, D), (D, hidden), (hidden, D)):
        blocks = columns // LANES
        table.append((offset, rows, blocks))
        offset += rows * blocks
    return table, offset


def chunk_plan(table, first, end, tail_at, tail_rows):
    segments = []
    base = None
    for number, (offset, rows, blocks) in enumerate(table):
        low = max(first, offset)
        high = min(end, offset + rows * blocks)
        if low >= high:
            continue
        row_low = (low - offset) // blocks // 16 * 16
        row_high = min(rows, round_up(-(-(high - offset) // blocks), 16))
        if base is None:
            base = offset + row_low * blocks
        segments.append((number, row_low, row_high, blocks, offset + row_low * blocks - base))
    size = max(at + (high - low) * blocks for _, low, high, blocks, at in segments)
    if end > tail_at:
        size = max(size, tail_at + tail_rows - base)
    return segments, base, size


def flatten_kernel(slot_ref, *refs, segments, skip, tail_at, tail_rows, per, piece_rows, padded):
    count = len(segments)
    keep, send, flat = refs[-3:]
    for ref, (_, low, high, blocks, at) in zip(refs[:count], segments):
        chunk = 16 if (high - low) % 64 else 64

        @pl.loop(0, (high - low) // chunk)
        def _(c, ref=ref, low=low, blocks=blocks, at=at, chunk=chunk):
            rows = pl.ds(pl.multiple_of(low + c * chunk, 16), chunk)
            for j in range(blocks):
                to_rows = pl.ds(at + c * (chunk * blocks) + j, chunk, stride=blocks)
                flat[to_rows, :] = ref[rows, j * LANES : (j + 1) * LANES].astype(f32)

    if tail_at is not None:
        flat[pl.ds(tail_at, tail_rows), :] = jnp.zeros((tail_rows, LANES), f32)
    step = 128
    full = piece_rows // step
    rest = piece_rows - full * step
    slot = slot_ref[0]
    for j in range(per):
        out = send if j % 2 else keep
        start = skip + (slot ^ j) * piece_rows

        @pl.loop(0, full)
        def _(i, out=out, j=j, start=start):
            rows = flat[pl.ds(start + i * step, step), :]
            out[j // 2, pl.ds(pl.multiple_of(i * step, step), step), :] = rows.astype(bf16)

        parts = [jnp.zeros((padded - piece_rows, LANES), f32)]
        if rest:
            parts = [flat[pl.ds(start + full * step, rest), :]] + parts
        out[j // 2, full * step : padded, :] = jnp.concatenate(parts, axis=0).astype(bf16)


def flatten(b, slot, matrices, table, tail_at, tail_rows, per, piece_rows, padded):
    first = b * per * piece_rows
    end = first + per * piece_rows
    segments, base, size = chunk_plan(table, first, end, tail_at, tail_rows)
    operands = [matrices[segment[0]] for segment in segments]
    whole = pl.BlockSpec(memory_space=pltpu.VMEM)
    shape = jax.ShapeDtypeStruct((per // 2, padded, LANES), bf16)
    return pl.pallas_call(
        functools.partial(
            flatten_kernel,
            segments=segments,
            skip=first - base,
            tail_at=tail_at - base if end > tail_at else None,
            tail_rows=tail_rows,
            per=per,
            piece_rows=piece_rows,
            padded=padded,
        ),
        in_specs=[pl.BlockSpec(memory_space=pltpu.SMEM)] + [whole] * len(operands),
        out_specs=[whole, whole],
        out_shape=[shape, shape],
        scratch_shapes=[pltpu.VMEM((size + 8, LANES), f32)],
        cost_estimate=pl.CostEstimate(
            flops=per * piece_rows * LANES,
            bytes_accessed=6 * per * piece_rows * LANES,
            transcendentals=0,
        ),
        compiler_params=params(),
        name=f"flatten_{b}",
    )(slot, *operands)


def row_parts(rows, count):
    size = rows // count // 16 * 16
    starts = [size * i for i in range(count)] + [rows]
    return [(low, high - low) for low, high in zip(starts[:-1], starts[1:])]


def in_steps(start, rows, step, body):
    @pl.loop(0, rows // step)
    def _(i):
        body(pl.multiple_of(start + i * step, 16), step)

    if rows % step:
        body(start + rows // step * step, rows % step)


def adamw_kernel(slot_ref, keep, near, far, w_ref, m_hbm, v_hbm, *refs, b, piece_rows, matrix_row, parts):
    go, mo, vo, wo, d_ref, m_in, v_in, g_out, m_out, v_out, w_out, sems = refs[-12:]
    loads = []
    for n, (at, rows) in enumerate(parts):
        r = pl.ds(at, rows)
        pair = (
            pltpu.make_async_copy(m_hbm.at[r, b, :], m_in.at[r], sems.at[0, n]),
            pltpu.make_async_copy(v_hbm.at[r, b, :], v_in.at[r], sems.at[1, n]),
        )
        for copy in pair:
            copy.start()
        loads.append(pair)
    stores = []

    def update(at, rows):
        r = pl.ds(at, rows)
        g = keep[0, r, :].astype(f32) + near[0, r, :].astype(f32) + far[r, :].astype(f32)
        w = w_ref[0, r, :].astype(f32)
        m_new = BETA_ONE * m_in[r, :] + (1 - BETA_ONE) * g
        v_new = BETA_TWO * v_in[r, :] + (1 - BETA_TWO) * g * g
        root = jnp.sqrt(v_new * (1 / (1 - BETA_TWO**STEP))) + ADAM_EPS
        decay = INNER_RATE * DECAY
        if matrix_row is not None:
            here = lax.broadcasted_iota(jnp.int32, (rows, LANES), 0) + at
            decay = jnp.where(here < matrix_row[0] - slot_ref[0] * piece_rows, decay, 0.0)
        d = (INNER_RATE / (1 - BETA_ONE**STEP)) * m_new / root + decay * w
        g_out[r, :] = g
        m_out[r, :] = m_new
        v_out[r, :] = v_new
        w_out[r, :] = w - d
        d_ref[r, :] = d.astype(bf16)

    for n, (at, rows) in enumerate(parts):
        for copy in loads[n]:
            copy.wait()
        in_steps(at, rows, 64, update)
        r = pl.ds(at, rows)
        for k, (src, dst) in enumerate(((g_out, go), (m_out, mo), (v_out, vo), (w_out, wo))):
            copy = pltpu.make_async_copy(src.at[r], dst.at[r, b, :], sems.at[2 + k, n])
            copy.start()
            stores.append(copy)
    for copy in stores:
        copy.wait()


def adamw(b, slot, keep, near, far, pieces, first, second, held, per, matrix_rows):
    piece_rows = first.shape[0]
    padded = far.shape[0]
    hbm = pl.BlockSpec(memory_space=pl.ANY)
    shape = jax.ShapeDtypeStruct(first.shape, f32)
    state = pltpu.VMEM((piece_rows, LANES), f32)
    parts = row_parts(piece_rows, 3)
    matrix_row = None
    if (b + 1) * per * piece_rows > matrix_rows:
        matrix_row = (matrix_rows - b * per * piece_rows,)
    return pl.pallas_call(
        functools.partial(
            adamw_kernel, b=b, piece_rows=piece_rows, matrix_row=matrix_row, parts=parts
        ),
        grid_spec=pltpu.PrefetchScalarGridSpec(
            num_scalar_prefetch=1,
            grid=(1,),
            in_specs=[
                pl.BlockSpec((1, padded, LANES), lambda i, s: (0, 0, 0)),
                pl.BlockSpec((1, padded, LANES), lambda i, s: (0, 0, 0)),
                pl.BlockSpec((padded, LANES), lambda i, s: (0, 0)),
                pl.BlockSpec((1, padded, LANES), lambda i, s: (b, 0, 0)),
                hbm,
                hbm,
            ]
            + [hbm] * len(held),
            out_specs=[hbm] * 4 + [pl.BlockSpec((padded, LANES), lambda i, s: (0, 0))],
            scratch_shapes=[state] * 6 + [pltpu.SemaphoreType.DMA((6, len(parts)))],
        ),
        out_shape=[shape] * 4 + [jax.ShapeDtypeStruct((padded, LANES), bf16)],
        input_output_aliases={7 + k: k for k in range(len(held))},
        cost_estimate=pl.CostEstimate(
            flops=30 * piece_rows * LANES,
            bytes_accessed=30 * piece_rows * LANES,
            transcendentals=2 * piece_rows * LANES,
        ),
        compiler_params=params(),
        name=f"adamw_{b}",
    )(slot, keep, near, far, pieces, first, second, *held)


def outer_kernel(d0, d1, d2, d3, w_hbm, o_hbm, mean_out, mom_out, new_out, w_in, o_in, mean, mom, new, sems, *, parts):
    loads = []
    for n, (at, rows) in enumerate(parts):
        r = pl.ds(at, rows)
        pair = (
            pltpu.make_async_copy(w_hbm.at[r, 0, :], w_in.at[r], sems.at[0, n]),
            pltpu.make_async_copy(o_hbm.at[r, 0, :], o_in.at[r], sems.at[1, n]),
        )
        for copy in pair:
            copy.start()
        loads.append(pair)
    stores = []

    def update(at, rows):
        r = pl.ds(at, rows)
        total = (d0[r, :].astype(f32) + d1[r, :].astype(f32)) + (
            d2[r, :].astype(f32) + d3[r, :].astype(f32)
        )
        average = total / GROUPS
        momentum = OUTER_MU * o_in[r, :] + average
        mean[r, :] = average
        mom[r, :] = momentum
        new[r, :] = w_in[r, :] - OUTER_RATE * (average + OUTER_MU * momentum)

    for n, (at, rows) in enumerate(parts):
        for copy in loads[n]:
            copy.wait()
        in_steps(at, rows, 64, update)
        r = pl.ds(at, rows)
        for k, (src, dst) in enumerate(((mean, mean_out), (mom, mom_out), (new, new_out))):
            copy = pltpu.make_async_copy(src.at[r], dst.at[r, 0, :], sems.at[2 + k, n])
            copy.start()
            stores.append(copy)
    for copy in stores:
        copy.wait()


def outer(diffs, own_rows, momentum_rows):
    piece_rows = own_rows.shape[0]
    hbm = pl.BlockSpec(memory_space=pl.ANY)
    whole = pl.BlockSpec(memory_space=pltpu.VMEM)
    parts = row_parts(piece_rows, 3)
    return pl.pallas_call(
        functools.partial(outer_kernel, parts=parts),
        in_specs=[whole] * 4 + [hbm] * 2,
        out_specs=[hbm] * 3,
        out_shape=[jax.ShapeDtypeStruct(own_rows.shape, f32)] * 3,
        scratch_shapes=[pltpu.VMEM((piece_rows, LANES), f32)] * 5
        + [pltpu.SemaphoreType.DMA((5, len(parts)))],
        compiler_params=params(),
        name="outer_step",
    )(*diffs, own_rows, momentum_rows)


def attend_block(q, k, v_ones, code, seg_col, offset):
    rows_q, n = q.shape[0], k.shape[0]
    low = lax.broadcasted_iota(jnp.int32, (1, LANES), 1) < HD
    zero = jnp.zeros((), bf16)
    q = q * jnp.asarray(HD**-0.5, bf16)
    rows = lax.broadcasted_iota(jnp.int32, (rows_q, n), 0) + offset
    cols = lax.broadcasted_iota(jnp.int32, (rows_q, n), 1)
    allowed = (seg_col == code) | (rows == cols)
    outs = []
    tops = []
    for h in range(2):
        qh = jnp.where(low, q, zero) if h == 0 else jnp.where(low, zero, q)
        s = jnp.where(allowed, dot(qh, k, NT), MASKED)
        top = jnp.max(s, axis=1, keepdims=True)
        p = jnp.exp(s - top).astype(bf16)
        outs.append(dot(p, v_ones[h], NN))
        tops.append(top)
    num = jnp.where(low, outs[0], outs[1])
    den = pltpu.roll(jnp.where(low, outs[1], outs[0]), HD, 1)
    lse = (jnp.where(low, tops[0], tops[1]) + jnp.log(den)).T
    return (num / den).astype(bf16), lse[0:1], lse[HD : HD + 1]


def bring_rows(buf, flat, margin, offset, count, piece_rows):
    for p in range(offset // piece_rows, -(-(offset + count) // piece_rows)):
        low = max(offset - p * piece_rows, 0) // 16 * 16
        high = min(round_up(min(offset + count - p * piece_rows, piece_rows), 16), buf.shape[1])
        to = margin + p * piece_rows + low - offset
        step = 128
        full = (high - low) // step

        @pl.loop(0, full)
        def _(i, p=p, low=low, to=to):
            rows = buf[p, pl.ds(pl.multiple_of(low + i * step, 16), step), :]
            flat[pl.ds(to + i * step, step), :] = rows.astype(f32)

        rest = (high - low) % step
        if rest:
            flat[pl.ds(to + full * step, rest), :] = buf[p, low + full * step : high, :].astype(f32)


def emit_matrix(flat, out, margin, rows, blocks):
    chunk = 64

    @pl.loop(0, rows // chunk)
    def _(c):
        at = pl.ds(pl.multiple_of(c * chunk, chunk), chunk)
        for j in range(blocks):
            from_rows = pl.ds(margin + c * (chunk * blocks) + j, chunk, stride=blocks)
            out[at, j * LANES : (j + 1) * LANES] = flat[from_rows, :].astype(bf16)


def start_kernel(
    own_hbm, tokens_hbm, code_ref, seg_ref,
    proj_out, outw_out, inw_out, down_out, pieces_out, tail_out, x_out, q_ref, k_ref, v_ref, ctx_ref, lse_ref,
    rows32, buf, xbuf, flat, proj_s, outw_s, inw_s, down_s,
    zdown, zup, zrecv, ysend, yrecv, csend, crecv, xsem, local_sems,
    *, piece_rows, tail_rows, table, cuts, rows_q
):
    z = lax.axis_index("group")
    slot = lax.axis_index("slot")
    me = lax.axis_index("tensor")
    depth = GROUPS
    padded = buf.shape[1]
    half = tokens_hbm.shape[0]
    n = 2 * half
    mesh_id = pl.DeviceIdType.MESH

    load = pltpu.make_async_copy(own_hbm.at[:, 0, :], rows32, local_sems.at[0])
    load.start()
    x_load = pltpu.make_async_copy(tokens_hbm, xbuf.at[pl.ds(0, half)], local_sems.at[1])
    x_load.start()

    barrier = pltpu.get_barrier_semaphore()
    for where in ({"slot": slot ^ 1}, {"slot": slot ^ 2}, {"tensor": 1 - me}):
        pl.semaphore_signal(barrier, inc=1, device_id=where, device_id_type=mesh_id)

    @pl.when(z > 0)
    def _():
        pl.semaphore_signal(barrier, inc=1, device_id={"group": z - 1}, device_id_type=mesh_id)

    @pl.when(z < depth - 1)
    def _():
        pl.semaphore_signal(barrier, inc=1, device_id={"group": z + 1}, device_id_type=mesh_id)

    pl.semaphore_wait(barrier, 3 + jnp.where(z > 0, 1, 0) + jnp.where(z < depth - 1, 1, 0))

    load.wait()
    own = z * 4 + slot
    step = 128
    full = piece_rows // step

    @pl.loop(0, full)
    def _(i):
        r = pl.ds(pl.multiple_of(i * step, step), step)
        buf[own, r, :] = rows32[r, :].astype(bf16)

    tail = rows32[piece_rows - tail_rows :, :]
    left = tail - tail.astype(bf16).astype(f32)
    zeros = jnp.zeros((padded - piece_rows - tail_rows, LANES), f32)
    buf[own, full * step :, :] = jnp.concatenate([rows32[full * step :, :], left, zeros], axis=0).astype(bf16)

    def copy_of(piece, h, send, recv, where):
        part = buf.at[piece, pl.ds(*cuts[h])]
        return pltpu.make_async_remote_copy(
            src_ref=part, dst_ref=part, send_sem=send, recv_sem=recv, device_id=where, device_id_type=mesh_id
        )

    def down(b, h):
        return copy_of(b * 4 + slot, h, zdown.at[b, h], zrecv.at[b, h], {"group": z + 1})

    def up(b, h):
        return copy_of(b * 4 + slot, h, zup.at[b, h], zrecv.at[b, h], {"group": z - 1})

    def side(b, h):
        return copy_of(b * 4 + slot, h, ysend.at[b, h], yrecv.at[b, h], {"slot": slot ^ 2})

    def side_in(b, h):
        return copy_of(b * 4 + (slot ^ 2), h, ysend.at[b, h], yrecv.at[b, h], {"slot": slot ^ 2})

    def twin(b, h, k):
        return copy_of(
            b * 4 + (slot ^ (2 * k)), h, csend.at[2 * b + k, h], crecv.at[2 * b + k, h], {"slot": slot ^ 1}
        )

    def twin_in(b, h, k):
        return copy_of(
            b * 4 + (slot ^ 1 ^ (2 * k)), h, csend.at[2 * b + k, h], crecv.at[2 * b + k, h], {"slot": slot ^ 1}
        )

    parts = range(len(cuts))
    tail_part = len(cuts) - 1
    order = [tail_part] + list(range(tail_part))
    last = depth - 1
    ranked = (
        z,
        jnp.where(z == 0, 1, 0),
        jnp.where(z == 2, 3, 2),
        jnp.where(z < 2, 3, 1),
    )
    middle = (z == 1) | (z == 2)

    def pass_on(b, h):
        up(b, h).wait_recv()

        @pl.when((b < z) & (z < last))
        def _():
            down(b, h).start()

        @pl.when((b > z) & (z > 0))
        def _():
            up(b, h).start()

        side(b, h).start()
        twin(b, h, 0).start()

    def serve_z(b, h, when=None):
        if h == tail_part:
            when = (b != last) if when is None else when & (b != last)
        if when is None:
            pass_on(b, h)
        else:
            pl.when(when)(functools.partial(pass_on, b, h))

    def serve_y(rank, h):
        b = ranked[rank]

        def go():
            side_in(b, h).wait_recv()
            twin(b, h, 1).start()

        if h == tail_part:
            pl.when(b != last)(go)
        else:
            go()

    early = order[:3]
    for h in order:

        @pl.when(z > 0)
        def _(h=h):
            up(z, h).start()

        @pl.when(z == 0)
        def _(h=h):
            down(z, h).start()

        if h in early:
            side(z, h).start()
        twin(z, h, 0).start()

    x_load.wait()
    x_copy = pltpu.make_async_remote_copy(
        src_ref=xbuf.at[pl.ds(0, half)],
        dst_ref=xbuf.at[pl.ds(half, half)],
        send_sem=xsem.at[0],
        recv_sem=xsem.at[1],
        device_id={"tensor": 1 - me},
        device_id_type=mesh_id,
    )
    x_copy.start()

    pl.when(z != last)(functools.partial(pass_on, last, tail_part))
    for h in order:
        serve_z(ranked[1], h)
    for h in order:

        @pl.when((z > 0) & (z < last))
        def _(h=h):
            down(z, h).start()

        if h not in early:
            side(z, h).start()
    for h in order:
        serve_z(ranked[2], h, middle)
    side_in(last, tail_part).wait_recv()
    twin(last, tail_part, 1).start()
    for h in early:
        serve_y(0, h)
    for h in order:
        serve_y(1, h)
    for h in order:
        if h not in early:
            serve_y(0, h)
    for k in range(2):
        twin_in(last, tail_part, k).wait_recv()
        for rank in range(2):
            b = ranked[rank]
            for h in parts:
                if h == tail_part:
                    pl.when(b != last)(lambda b=b, h=h, k=k: twin_in(b, h, k).wait_recv())
                else:
                    twin_in(b, h, k).wait_recv()

    at = (piece_rows - tail_rows) // 16 * 16
    shift = piece_rows - tail_rows - at
    ends = buf[4 * depth - 1, at:, :].astype(f32)
    vectors = ends[shift : shift + tail_rows] + ends[shift + tail_rows : shift + 2 * tail_rows]
    tail_out[...] = vectors

    margin = 16
    (offset, rows, blocks) = table[0]
    bring_rows(buf, flat, margin, offset, rows * blocks, piece_rows)
    emit_matrix(flat, proj_s, margin, rows, blocks)
    out_copies = [pltpu.make_async_copy(proj_s, proj_out, local_sems.at[2])]
    out_copies[0].start()
    x_copy.wait()
    out_copies.append(pltpu.make_async_copy(xbuf, x_out, local_sems.at[3]))
    out_copies[1].start()
    query_bias = jnp.concatenate([vectors[j : j + 1] for j in range(blocks)], axis=1)
    value_bias = jnp.concatenate([vectors[blocks + j : blocks + j + 1] for j in range(blocks)], axis=1)
    depth_in = rows // 3
    for m, (ref, bias) in enumerate(((q_ref, query_bias), (k_ref, None), (v_ref, value_bias))):

        @pl.loop(0, n // 256)
        def _(i, m=m, ref=ref, bias=bias):
            r = pl.ds(pl.multiple_of(i * 256, 256), 256)
            acc = dot(xbuf[r, :], proj_s[m * depth_in : (m + 1) * depth_in, :], NN)
            if bias is not None:
                acc = acc + bias
            ref[r, :] = acc.astype(bf16)

        for h in order[2 * m : 2 * m + 2]:
            serve_z(jnp.where(middle, ranked[3], ranked[2]), h)

    edge = jnp.logical_not(middle)
    todo = [functools.partial(serve_z, ranked[3], h, edge) for h in order]
    late = [functools.partial(serve_y, 2, h) for h in order]
    todo = [act for both_acts in zip(late, todo) for act in both_acts]
    todo += [functools.partial(serve_y, 3, h) for h in order]
    low = lax.broadcasted_iota(jnp.int32, (1, LANES), 1) < HD
    one = jnp.ones((), bf16)
    code = code_ref[...]
    for pair in range(blocks):
        c = slice(pair * LANES, (pair + 1) * LANES)
        k = k_ref[:, c]
        v = v_ref[:, c]
        v_ones = (jnp.where(low, v, one), jnp.where(low, one, v))
        for i in range(n // rows_q):
            r = slice(i * rows_q, (i + 1) * rows_q)
            ctx, lse_0, lse_1 = attend_block(q_ref[r, c], k, v_ones, code, seg_ref[r, :], i * rows_q)
            ctx_ref[r, c] = ctx
            lse_ref[pair, 0:1, r] = lse_0
            lse_ref[pair, 1:2, r] = lse_1
            for _ in range(1):
                if todo:
                    todo.pop(0)()
    for act in todo:
        act()
    for rank in range(2, 4):
        b = ranked[rank]
        for h in parts:
            for k in range(2):
                if h == tail_part:
                    pl.when(b != last)(lambda b=b, h=h, k=k: twin_in(b, h, k).wait_recv())
                else:
                    twin_in(b, h, k).wait_recv()

    for b in range(depth):
        copy = pltpu.make_async_copy(buf.at[b * 4 + slot], pieces_out.at[b], local_sems.at[7 + b])
        copy.start()
        out_copies.append(copy)
    for m, (scr, out) in enumerate(((outw_s, outw_out), (inw_s, inw_out), (down_s, down_out))):
        (offset, rows, blocks) = table[1 + m]
        bring_rows(buf, flat, margin, offset, rows * blocks, piece_rows)
        emit_matrix(flat, scr, margin, rows, blocks)
        copy = pltpu.make_async_copy(scr, out, local_sems.at[4 + m])
        copy.start()
        out_copies.append(copy)

    for b in range(depth):
        for h in parts:

            @pl.when((b <= z) & (z < depth - 1))
            def _(b=b, h=h):
                down(b, h).wait_send()

            @pl.when((b >= z) & (z > 0))
            def _(b=b, h=h):
                up(b, h).wait_send()

            side(b, h).wait_send()
            for k in range(2):
                twin(b, h, k).wait_send()
    for copy in out_copies:
        copy.wait()


def start(own_rows, tokens, code_row, seg_col, table, tail_rows, padded, cuts, rows_q=256):
    piece_rows = own_rows.shape[0]
    half, width = tokens.shape
    n = 2 * half
    pairs = table[0][2]
    local_width = pairs * LANES
    hbm = pl.BlockSpec(memory_space=pl.ANY)
    whole = pl.BlockSpec(memory_space=pltpu.VMEM)
    mats = [jax.ShapeDtypeStruct((rows, blocks * LANES), bf16) for _, rows, blocks in table]
    acts = [jax.ShapeDtypeStruct((n, local_width), bf16)] * 4
    most = max(rows * blocks for _, rows, blocks in table)
    parts = len(cuts)
    dma = pltpu.SemaphoreType.DMA
    return pl.pallas_call(
        functools.partial(
            start_kernel, piece_rows=piece_rows, tail_rows=tail_rows, table=table, cuts=cuts, rows_q=rows_q
        ),
        in_specs=[hbm, hbm, whole, whole],
        out_specs=[hbm] * 5 + [whole] + [hbm] + [whole] * 5,
        out_shape=mats
        + [
            jax.ShapeDtypeStruct((GROUPS, padded, LANES), bf16),
            jax.ShapeDtypeStruct((tail_rows, LANES), f32),
            jax.ShapeDtypeStruct((n, width), bf16),
        ]
        + acts
        + [jax.ShapeDtypeStruct((pairs, 2, n), f32)],
        scratch_shapes=[
            pltpu.VMEM((piece_rows, LANES), f32),
            pltpu.VMEM((4 * GROUPS, padded, LANES), bf16),
            pltpu.VMEM((n, width), bf16),
            pltpu.VMEM((most + 48, LANES), f32),
        ]
        + [pltpu.VMEM(m.shape, bf16) for m in mats]
        + [
            dma((GROUPS, parts)),
            dma((GROUPS, parts)),
            dma((GROUPS, parts)),
            dma((GROUPS, parts)),
            dma((GROUPS, parts)),
            dma((2 * GROUPS, parts)),
            dma((2 * GROUPS, parts)),
            dma((2,)),
            dma((11,)),
        ],
        cost_estimate=pl.CostEstimate(
            flops=6 * n * width * local_width, bytes_accessed=60 << 20, transcendentals=8 * n * n
        ),
        compiler_params=params(collective_id=1, has_side_effects=True),
        name="start",
    )(own_rows, tokens, code_row, seg_col)


def partner(block):
    return lax.ppermute(block, "tensor", [(0, 1), (1, 0)])


def both(own):
    return jnp.concatenate([own, partner(own)], axis=0)


def own_sum(partial):
    half = partial.shape[0] // 2
    return partial[:half].astype(f32) + partner(partial[half:].astype(bf16)).astype(f32)


def local_fast(
    tokens,
    cotangent,
    segment_ids,
    padding,
    shared_weights,
    first_moment,
    second_moment,
    outer_momentum,
):
    me = lax.axis_index("tensor")
    per = lax.axis_size("slot")
    rows = tokens.shape[0]
    local_width = D // 2
    piece_rows = shared_weights.shape[1] // LANES
    table, tail_at = matrix_table(2)
    tail_rows = GROUPS * per * piece_rows - tail_at
    padded = round_up(piece_rows + tail_rows, 16)

    own_rows = shared_weights.reshape(piece_rows, 1, LANES)
    seg = jnp.where(me == 0, segment_ids, jnp.roll(segment_ids, rows))
    live = jnp.where(me == 0, padding, jnp.roll(padding, rows))
    code = jnp.where(live == 1, seg, -1)
    end = padded - round_up(2 * tail_rows + 16, 16)
    marks = [end * i // 4 // 16 * 16 for i in range(4)] + [end, padded]
    cuts = [(low, high - low) for low, high in zip(marks[:-1], marks[1:])]
    (
        proj_w, out_w, in_w, down_w, pieces, tail_all, x_all, query, keys, values, context, lse
    ) = start(own_rows, tokens, code[None], seg[:, None], table, tail_rows, padded, cuts)
    proj_w = proj_w.reshape(3, D, local_width)
    flat_tail = tail_all.reshape(-1)
    inner_bias = flat_tail[2 * local_width : 2 * local_width + FF // 2]
    vec_own = flat_tail[2 * local_width + FF // 2 :].reshape(6, local_width)
    vec_other = partner(vec_own)
    vectors = jnp.where(
        me == 0,
        jnp.concatenate([vec_own, vec_other], axis=1),
        jnp.concatenate([vec_other, vec_own], axis=1),
    )

    attn_sum = own_sum(jnp.dot(context, out_w, preferred_element_type=f32))
    middle, normed_one, inv_one = layer_norm(
        tokens.astype(f32) + (attn_sum + vectors[4]), vectors[0], vectors[1]
    )
    middle_all = both(middle.astype(bf16))
    inner = jnp.dot(middle_all, in_w, preferred_element_type=f32) + inner_bias
    activated = jax.nn.gelu(inner, approximate=False).astype(bf16)
    ffn_sum = own_sum(jnp.dot(activated, down_w, preferred_element_type=f32))
    result, normed_two, inv_two = layer_norm(
        middle + (ffn_sum + vectors[5]), vectors[2], vectors[3]
    )
    block_out = result.astype(bf16)

    grad_out = cotangent.astype(f32)
    grad_gain_two = jnp.sum(grad_out * normed_two, axis=0)
    grad_shift_two = jnp.sum(grad_out, axis=0)
    grad_two = norm_back(grad_out * vectors[2], normed_two, inv_two)
    grad_down_bias = jnp.sum(grad_two, axis=0)
    back_all = both(grad_two.astype(bf16))
    grad_down_w = row_contract(activated, back_all).astype(bf16)
    grad_act = col_contract(back_all, down_w)
    grad_inner = (grad_act * gelu_slope(inner)).astype(bf16)
    grad_inner_bias = jnp.sum(grad_inner.astype(f32), axis=0)
    grad_in_w = row_contract(middle_all, grad_inner).astype(bf16)
    grad_middle = grad_two + own_sum(col_contract(grad_inner, in_w))
    grad_gain_one = jnp.sum(grad_middle * normed_one, axis=0)
    grad_shift_one = jnp.sum(grad_middle, axis=0)
    grad_one = norm_back(grad_middle * vectors[0], normed_one, inv_one)
    grad_out_bias = jnp.sum(grad_one, axis=0)
    attn_back_all = both(grad_one.astype(bf16))
    grad_out_w = row_contract(context, attn_back_all).astype(bf16)
    grad_context = col_contract(attn_back_all, out_w).astype(bf16)
    dq, dk, dv = attn_bwd(query, keys, values, context, grad_context, code[:, None], seg[None], lse)
    grad_proj = jnp.stack([dq, dk, dv])
    grad_proj_w = jnp.einsum("td,kte->kde", x_all, grad_proj, preferred_element_type=f32)
    grad_query_bias = jnp.sum(dq.astype(f32), axis=0)
    grad_value_bias = jnp.sum(dv.astype(f32), axis=0)
    input_share = own_sum(jnp.einsum("kte,kde->td", grad_proj, proj_w, preferred_element_type=f32))
    input_grad = (grad_one + input_share).astype(bf16)

    vector_part = jnp.stack(
        [
            grad_gain_one,
            grad_shift_one,
            grad_gain_two,
            grad_shift_two,
            grad_out_bias,
            grad_down_bias,
        ]
    )
    halves = vector_part.reshape(6, 2, local_width)
    vec_keep = jnp.where(me == 0, halves[:, 0], halves[:, 1])
    vec_send = jnp.where(me == 0, halves[:, 1], halves[:, 0])
    vector_grad = vec_keep + partner(vec_send)
    tail_grad = jnp.concatenate(
        [grad_query_bias, grad_value_bias, grad_inner_bias, vector_grad.reshape(-1)]
    ).reshape(tail_rows, LANES)

    matrices = [
        grad_proj_w.astype(bf16).reshape(3 * D, local_width),
        grad_out_w,
        grad_in_w,
        grad_down_w,
    ]
    short = round_up(piece_rows, 16)
    slot = lax.axis_index("slot").astype(jnp.int32)
    group = lax.axis_index("group")

    def across(block, axis, bit):
        return lax.ppermute(block, axis, [(i, i ^ bit) for i in range(lax.axis_size(axis))])

    tail_sum = tail_grad + across(tail_grad, "slot", 1)
    tail_sum = tail_sum + across(tail_sum, "slot", 2)

    def blocked(state):
        return state.reshape(GROUPS, piece_rows, LANES).transpose(1, 0, 2)

    def unblocked(state):
        return state.transpose(1, 0, 2).reshape(1, 1, GROUPS, piece_rows * LANES)

    first = blocked(first_moment)
    second = blocked(second_moment)
    held = []
    diffs = [None] * GROUPS
    slot_word = slot.reshape(1)
    for b in reversed(range(GROUPS)):
        keep, send = flatten(b, slot_word, matrices, table, tail_at, tail_rows, per, piece_rows, short)
        near = across(send, "slot", 1)
        far = across((keep[1].astype(f32) + near[1].astype(f32)).astype(bf16), "slot", 2)
        if b == GROUPS - 1:
            there = far[piece_rows - tail_rows : piece_rows]
            there = jnp.where(slot == per - 1, tail_sum.astype(bf16), there)
            far = lax.dynamic_update_slice(far, there, (piece_rows - tail_rows, 0))
        *held, diffs[b] = adamw(b, slot_word, keep, near, far, pieces, first, second, held, per, tail_at)

    def turned(k):
        picked = diffs[(GROUPS - 1) ^ k]
        for z in range(GROUPS - 1):
            picked = jnp.where(group == z, diffs[z ^ k], picked)
        return picked

    gathered = [turned(0)] + [across(turned(k), "group", k) for k in (1, 2, 3)]
    mean_diff, new_momentum, new_weights = [
        rows_out.reshape(1, piece_rows * LANES)
        for rows_out in outer(gathered, own_rows, outer_momentum.reshape(piece_rows, 1, LANES))
    ]
    return (block_out, input_grad, *[unblocked(state) for state in held], mean_diff, new_momentum, new_weights)


def solution(mesh):
    dp = mesh.shape["dp"]
    tensor_size = mesh.shape["tensor"]
    piece = (4 * D * D + 2 * D * FF + 8 * D + FF) // tensor_size // dp
    if tensor_size == 2 and piece % LANES == 0 and dp % GROUPS == 0:
        mesh = Mesh(
            mesh.devices.reshape(GROUPS, dp // GROUPS, tensor_size), ("group", "slot", "tensor")
        )
        data = ("group", "slot")
        body = local_fast
    else:
        data = "dp"
        body = local_general
    every = ("group", "slot", "tensor") if body is local_fast else ("dp", "tensor")
    in_specs = (
        P(every, None),
        P(every, None),
        P(data),
        P(data),
        P("tensor", data),
        P("tensor", data, None, None),
        P("tensor", data, None, None),
        P("tensor", data),
    )
    out_specs = (
        P(every, None),
        P(every, None),
        P("tensor", data, None, None),
        P("tensor", data, None, None),
        P("tensor", data, None, None),
        P("tensor", data, None, None),
        P("tensor", data),
        P("tensor", data),
        P("tensor", data),
    )
    return jax.shard_map(body, mesh=mesh, in_specs=in_specs, out_specs=out_specs, check_vma=False)
```

```python
import functools

import jax
import jax.numpy as jnp
import numpy as np
from jax import lax
from jax.experimental import pallas as pl
from jax.experimental.pallas import tpu as pltpu
from jax.sharding import Mesh
from jax.sharding import PartitionSpec as P

D = 1024
HEADS = 16
HD = 64
FF = 4096
SEQ_LEN = 1024
GROUPS = 4
STEP = 10


NORM_EPS = 1e-05
MASKED = -1000000000.0
BETA_ONE = 0.9
BETA_TWO = 0.999
ADAM_EPS = 1e-08
INNER_RATE = 0.02
DECAY = 0.01
OUTER_MU = 0.9
OUTER_RATE = 0.7
ROOT_HALF = 0.7071067811865476
INV_ROOT_TWO_PI = 0.3989422804014327


def from_partner(block, axis, stride):
    count = lax.axis_size(axis)
    route = []
    for low in range(count):
        high = low | 1 << stride
        if high != low and high < count:
            route += [(low, high), (high, low)]
    return lax.ppermute(block, axis, route)


def boundaries(tensor_size):
    local_width = D // tensor_size
    hidden = FF // tensor_size
    lengths = [
        3 * D * local_width,
        local_width * D,
        D * hidden,
        hidden * D,
        local_width,
        local_width,
        hidden,
        6 * local_width,
    ]
    points = [0]
    for amount in lengths:
        points.append(points[-1] + amount)
    return points


def layer_norm(values, norm_gain, norm_shift):
    average = jnp.mean(values, axis=-1, keepdims=True)
    centred = values - average
    variance = jnp.mean(centred * centred, axis=-1, keepdims=True)
    inv_dev = lax.rsqrt(variance + NORM_EPS)
    normed = centred * inv_dev
    return (normed * norm_gain + norm_shift, normed, inv_dev)


def norm_back(grad_normed, normed, inv_dev):
    first_part = jnp.mean(grad_normed, axis=-1, keepdims=True)
    second_part = jnp.mean(grad_normed * normed, axis=-1, keepdims=True)
    return inv_dev * (grad_normed - first_part - normed * second_part)


def gelu_slope(inner):
    return (
        0.5 * (1.0 + jax.scipy.special.erf(inner * ROOT_HALF))
        + inner * jnp.exp(-0.5 * inner * inner) * INV_ROOT_TWO_PI
    )


def row_contract(left_side, right_side):
    return lax.dot_general(
        left_side, right_side, (((0,), (0,)), ((), ())), preferred_element_type=jnp.float32
    )


def col_contract(left_side, right_side):
    return lax.dot_general(
        left_side, right_side, (((1,), (1,)), ((), ())), preferred_element_type=jnp.float32
    )


def halve_rounds(values, bit_list, first_axis, top_bit, dp_index, site_call):
    for bit_number in bit_list:
        axis_number = first_axis + top_bit - bit_number
        my_bit = dp_index >> bit_number & 1
        kept = lax.dynamic_index_in_dim(values, my_bit, axis_number, keepdims=True)
        outgoing = lax.dynamic_index_in_dim(values, 1 - my_bit, axis_number, keepdims=True)
        values = kept + site_call(outgoing, bit_number)
    return values


def local_general(
    tokens,
    cotangent,
    segment_ids,
    padding,
    shared_weights,
    first_moment,
    second_moment,
    outer_momentum,
):
    tensor_size = lax.axis_size("tensor")
    local_width = D // tensor_size
    hidden = FF // tensor_size
    local_heads = HEADS // tensor_size
    seq_rows = segment_ids.shape[0]
    seq_count = seq_rows // SEQ_LEN
    block_rows = min(512, SEQ_LEN)
    per_seq = SEQ_LEN // block_rows
    block_total = seq_count * per_seq
    score_scale = HD ** (-0.5)
    bf16 = jnp.bfloat16
    f32 = jnp.float32
    masters = lax.all_gather(shared_weights, "dp", axis=1, tiled=True)[0]
    points = boundaries(tensor_size)
    segments = [masters[points[number] : points[number + 1]] for number in range(8)]
    proj_weight = segments[0].reshape(3, D, local_width).astype(bf16)
    out_weight = segments[1].reshape(local_width, D).astype(bf16)
    in_weight = segments[2].reshape(D, hidden).astype(bf16)
    down_weight = segments[3].reshape(hidden, D).astype(bf16)
    query_bias = segments[4]
    value_bias = segments[5]
    inner_bias = segments[6]
    vectors = lax.all_gather(segments[7].reshape(6, local_width), "tensor", axis=1, tiled=True)
    inputs_all = lax.all_gather(tokens, "tensor", axis=0, tiled=True)
    projected = jnp.einsum("td,kde->kte", inputs_all, proj_weight, preferred_element_type=f32)
    query = (projected[0] + query_bias).astype(bf16)
    keys = projected[1].astype(bf16)
    values = (projected[2] + value_bias).astype(bf16)
    query_four = query.reshape(seq_count, SEQ_LEN, local_heads, HD)
    keys_four = keys.reshape(seq_count, SEQ_LEN, local_heads, HD)
    values_four = values.reshape(seq_count, SEQ_LEN, local_heads, HD)
    seg_two = segment_ids.reshape(seq_count, SEQ_LEN)
    live_two = padding.reshape(seq_count, SEQ_LEN)
    key_pos = jnp.arange(SEQ_LEN, dtype=jnp.int32)

    def block_scores(block_index):
        sequence = block_index // per_seq
        offset = block_index % per_seq * block_rows
        query_rows = lax.dynamic_index_in_dim(query_four, sequence, 0, keepdims=False)
        query_block = lax.dynamic_slice_in_dim(query_rows, offset, block_rows, 0)
        key_rows = lax.dynamic_index_in_dim(keys_four, sequence, 0, keepdims=False)
        seg_row = lax.dynamic_index_in_dim(seg_two, sequence, 0, keepdims=False)
        live_row = lax.dynamic_index_in_dim(live_two, sequence, 0, keepdims=False)
        seg_block = lax.dynamic_slice_in_dim(seg_row, offset, block_rows, 0)
        query_pos = offset + jnp.arange(block_rows, dtype=jnp.int32)
        allowed = (seg_block[:, None] == seg_row[None, :]) & (
            (live_row[None, :] == 1) | (query_pos[:, None] == key_pos[None, :])
        )
        raw_scores = (
            jnp.einsum("qhd,khd->hqk", query_block, key_rows, preferred_element_type=f32)
            * score_scale
        )
        return (
            jnp.where(allowed[None], raw_scores, MASKED),
            query_block,
            key_rows,
            sequence,
            offset,
        )

    def forward_block(block_index):
        scores, query_block, key_rows, sequence, offset = block_scores(block_index)
        value_rows = lax.dynamic_index_in_dim(values_four, sequence, 0, keepdims=False)
        highest = jnp.max(scores, axis=-1, keepdims=True)
        exponent = jnp.exp(scores - highest)
        summed = jnp.sum(exponent, axis=-1, keepdims=True)
        probabilities = (exponent / summed).astype(bf16)
        context = jnp.einsum("hqk,khd->qhd", probabilities, value_rows, preferred_element_type=f32)
        return (context, (highest + jnp.log(summed))[..., 0])

    context_blocks, log_totals = lax.map(forward_block, jnp.arange(block_total, dtype=jnp.int32))
    context_low = context_blocks.reshape(seq_rows, local_width).astype(bf16)
    attn_sum = lax.psum_scatter(
        jnp.dot(context_low, out_weight, preferred_element_type=f32).astype(jnp.bfloat16),
        "tensor",
        scatter_dimension=0,
        tiled=True,
    ).astype(jnp.float32)
    tokens_f = tokens.astype(f32)
    middle, normed_one, inv_one = layer_norm(
        tokens_f + (attn_sum + vectors[4]), vectors[0], vectors[1]
    )
    middle_all = lax.all_gather(middle.astype(bf16), "tensor", axis=0, tiled=True)
    inner = jnp.dot(middle_all, in_weight, preferred_element_type=f32) + inner_bias
    activated = jax.nn.gelu(inner, approximate=False).astype(bf16)
    ffn_sum = lax.psum_scatter(
        jnp.dot(activated, down_weight, preferred_element_type=f32).astype(jnp.bfloat16),
        "tensor",
        scatter_dimension=0,
        tiled=True,
    ).astype(jnp.float32)
    result, normed_two, inv_two = layer_norm(
        middle + (ffn_sum + vectors[5]), vectors[2], vectors[3]
    )
    block_out = result.astype(bf16)
    grad_out = cotangent.astype(f32)
    grad_gain_two = jnp.sum(grad_out * normed_two, axis=0)
    grad_shift_two = jnp.sum(grad_out, axis=0)
    grad_two = norm_back(grad_out * vectors[2], normed_two, inv_two)
    grad_down_bias = jnp.sum(grad_two, axis=0)
    back_all = lax.all_gather(grad_two.astype(bf16), "tensor", axis=0, tiled=True)
    grad_down_weight = row_contract(activated, back_all)
    grad_act = col_contract(back_all, down_weight)
    grad_inner = (grad_act * gelu_slope(inner)).astype(bf16)
    grad_inner_bias = jnp.sum(grad_inner.astype(f32), axis=0)
    grad_in_weight = row_contract(middle_all, grad_inner)
    grad_middle = grad_two + lax.psum_scatter(
        col_contract(grad_inner, in_weight).astype(jnp.bfloat16),
        "tensor",
        scatter_dimension=0,
        tiled=True,
    ).astype(jnp.float32)
    grad_gain_one = jnp.sum(grad_middle * normed_one, axis=0)
    grad_shift_one = jnp.sum(grad_middle, axis=0)
    grad_one = norm_back(grad_middle * vectors[0], normed_one, inv_one)
    grad_out_bias = jnp.sum(grad_one, axis=0)
    attn_back_all = lax.all_gather(grad_one.astype(bf16), "tensor", axis=0, tiled=True)
    grad_out_weight = row_contract(context_low, attn_back_all)
    grad_context = col_contract(attn_back_all, out_weight).astype(bf16)
    grad_context_four = grad_context.reshape(seq_count, SEQ_LEN, local_heads, HD)

    def backward_block(carry, block_index):
        grad_keys, grad_values = carry
        scores, query_block, key_rows, sequence, offset = block_scores(block_index)
        value_rows = lax.dynamic_index_in_dim(values_four, sequence, 0, keepdims=False)
        log_total = lax.dynamic_index_in_dim(log_totals, block_index, 0, keepdims=False)
        probabilities = jnp.exp(scores - log_total[..., None])
        prob_low = probabilities.astype(bf16)
        grad_rows = lax.dynamic_index_in_dim(grad_context_four, sequence, 0, keepdims=False)
        grad_block = lax.dynamic_slice_in_dim(grad_rows, offset, block_rows, 0)
        grad_probs = jnp.einsum("qhd,khd->hqk", grad_block, value_rows, preferred_element_type=f32)
        grad_scores = probabilities * (
            grad_probs - jnp.sum(grad_probs * probabilities, axis=-1, keepdims=True)
        )
        scores_low = grad_scores.astype(bf16)
        grad_query = (
            jnp.einsum("hqk,khd->qhd", scores_low, key_rows, preferred_element_type=f32)
            * score_scale
        )
        key_term = (
            jnp.einsum("hqk,qhd->khd", scores_low, query_block, preferred_element_type=f32)
            * score_scale
        )
        value_term = jnp.einsum("hqk,qhd->khd", prob_low, grad_block, preferred_element_type=f32)
        grad_keys = lax.dynamic_update_index_in_dim(
            grad_keys,
            lax.dynamic_index_in_dim(grad_keys, sequence, 0, keepdims=False) + key_term,
            sequence,
            0,
        )
        grad_values = lax.dynamic_update_index_in_dim(
            grad_values,
            lax.dynamic_index_in_dim(grad_values, sequence, 0, keepdims=False) + value_term,
            sequence,
            0,
        )
        return ((grad_keys, grad_values), grad_query)

    empty = jnp.zeros((seq_count, SEQ_LEN, local_heads, HD), f32)
    (grad_keys, grad_values), grad_queries = lax.scan(
        backward_block, (empty, empty), jnp.arange(block_total, dtype=jnp.int32)
    )
    grad_proj = jnp.stack(
        [
            grad_queries.reshape(seq_rows, local_width),
            grad_keys.reshape(seq_rows, local_width),
            grad_values.reshape(seq_rows, local_width),
        ]
    ).astype(bf16)
    grad_proj_weight = jnp.einsum("td,kte->kde", inputs_all, grad_proj, preferred_element_type=f32)
    grad_query_bias = jnp.sum(grad_proj[0].astype(f32), axis=0)
    grad_value_bias = jnp.sum(grad_proj[2].astype(f32), axis=0)
    input_part = jnp.einsum("kte,kde->td", grad_proj, proj_weight, preferred_element_type=f32)
    vector_part = jnp.stack(
        [
            grad_gain_one,
            grad_shift_one,
            grad_gain_two,
            grad_shift_two,
            grad_out_bias,
            grad_down_bias,
        ]
    )
    input_share, vector_grad = (
        lax.psum_scatter(
            input_part.astype(jnp.bfloat16), "tensor", scatter_dimension=0, tiled=True
        ).astype(jnp.float32),
        lax.psum_scatter(
            vector_part.astype(jnp.bfloat16), "tensor", scatter_dimension=1, tiled=True
        ).astype(jnp.float32),
    )
    input_grad = (grad_one + input_share).astype(bf16)
    flat_grad = jnp.concatenate(
        [
            grad_proj_weight.reshape(-1),
            grad_out_weight.reshape(-1),
            grad_in_weight.reshape(-1),
            grad_down_weight.reshape(-1),
            grad_query_bias,
            grad_value_bias,
            grad_inner_bias,
            vector_grad.reshape(-1),
        ]
    )
    dp_size = lax.axis_size("dp")
    per_group = dp_size // GROUPS
    inner_bits = per_group.bit_length() - 1
    all_bits = dp_size.bit_length() - 1
    dp_index = lax.axis_index("dp")
    slot_index = dp_index % per_group
    piece_len = shared_weights.shape[1]
    grid_view = flat_grad.reshape(GROUPS, per_group, piece_len)
    inner_list = list(range(inner_bits))
    outer_list = list(range(inner_bits, all_bits))
    inner_list = inner_list[::-1]
    outer_list = outer_list[::-1]
    summed_grid = grid_view
    for bit_number in inner_list:
        summed_grid = summed_grid + from_partner(
            summed_grid.astype(jnp.bfloat16), "dp", bit_number
        ).astype(summed_grid.dtype)
    grad_block = lax.dynamic_index_in_dim(summed_grid, slot_index, 1, keepdims=False)
    weights_block = lax.dynamic_index_in_dim(
        masters.reshape(GROUPS, per_group, piece_len), slot_index, 1, keepdims=False
    )
    matrix_count = (4 * D * D + 2 * D * FF) // tensor_size
    flat_index = (
        jnp.arange(GROUPS, dtype=jnp.int32)[:, None] * per_group + slot_index
    ) * piece_len + jnp.arange(piece_len, dtype=jnp.int32)[None, :]
    decay_mask = (flat_index < matrix_count).astype(f32)
    first_new = BETA_ONE * first_moment[0, 0] + (1 - BETA_ONE) * grad_block
    second_new = BETA_TWO * second_moment[0, 0] + (1 - BETA_TWO) * grad_block * grad_block
    first_hat = first_new / (1 - BETA_ONE**STEP)
    second_hat = second_new / (1 - BETA_TWO**STEP)
    group_weights = weights_block - INNER_RATE * (
        first_hat / (jnp.sqrt(second_hat) + ADAM_EPS) + DECAY * decay_mask * weights_block
    )
    difference = weights_block - group_weights

    def outer_swap(outgoing, bit_number):
        return from_partner(outgoing.astype(jnp.bfloat16), "dp", bit_number).astype(outgoing.dtype)

    outer_bits = all_bits - inner_bits
    diff_view = difference.reshape((2,) * outer_bits + (piece_len,))
    diff_sum = halve_rounds(diff_view, outer_list, 0, all_bits - 1, dp_index, outer_swap).reshape(
        piece_len
    )
    mean_diff = diff_sum / GROUPS
    new_momentum = OUTER_MU * outer_momentum[0] + mean_diff
    new_weights = shared_weights[0] - OUTER_RATE * (mean_diff + OUTER_MU * new_momentum)
    return (
        block_out,
        input_grad,
        grad_block[None, None],
        first_new[None, None],
        second_new[None, None],
        group_weights[None, None],
        mean_diff[None],
        new_momentum[None],
        new_weights[None],
    )


LANES = 128
NT = (((1,), (1,)), ((), ()))
NN = (((1,), (0,)), ((), ()))
TN = (((0,), (0,)), ((), ()))
VMEM_BYTES = 58 << 20
f32 = jnp.float32
bf16 = jnp.bfloat16


def dot(left, right, dims):
    return lax.dot_general(left, right, dims, preferred_element_type=f32)


def params(**more):
    return pltpu.CompilerParams(vmem_limit_bytes=VMEM_BYTES, **more)


def round_up(number, step):
    return -(-number // step) * step


def matrix_table(tensor_size):
    local_width = D // tensor_size
    hidden = FF // tensor_size
    table = []
    offset = 0
    for rows, columns in ((3 * D, local_width), (local_width, D), (D, hidden), (hidden, D)):
        blocks = columns // LANES
        table.append((offset, rows, blocks))
        offset += rows * blocks
    return table, offset


def chunk_plan(table, first, end, tail_at, tail_rows):
    segments = []
    base = None
    for number, (offset, rows, blocks) in enumerate(table):
        low = max(first, offset)
        high = min(end, offset + rows * blocks)
        if low >= high:
            continue
        row_low = (low - offset) // blocks // 16 * 16
        row_high = min(rows, round_up(-(-(high - offset) // blocks), 16))
        if base is None:
            base = offset + row_low * blocks
        segments.append((number, row_low, row_high, blocks, offset + row_low * blocks - base))
    size = max(at + (high - low) * blocks for _, low, high, blocks, at in segments)
    if end > tail_at:
        size = max(size, tail_at + tail_rows - base)
    return segments, base, size


def row_parts(rows, count):
    size = rows // count // 16 * 16
    starts = [size * i for i in range(count)] + [rows]
    return [(low, high - low) for low, high in zip(starts[:-1], starts[1:])]


def in_steps(start, rows, step, body):
    @pl.loop(0, rows // step)
    def _(i):
        body(pl.multiple_of(start + i * step, 16), step)

    if rows % step:
        body(start + rows // step * step, rows % step)


def adamw_kernel(slot_ref, g_ref, w_ref, m_hbm, v_hbm, *refs, b, piece_rows, matrix_row, parts):
    go, mo, vo, wo, d_ref, m_in, v_in, g_out, m_out, v_out, w_out, sems = refs[-12:]
    loads = []
    for n, (at, rows) in enumerate(parts):
        r = pl.ds(at, rows)
        pair = (
            pltpu.make_async_copy(m_hbm.at[r, b, :], m_in.at[r], sems.at[0, n]),
            pltpu.make_async_copy(v_hbm.at[r, b, :], v_in.at[r], sems.at[1, n]),
        )
        for copy in pair:
            copy.start()
        loads.append(pair)
    stores = []

    def update(at, rows):
        r = pl.ds(at, rows)
        g = g_ref[0, r, :]
        w = w_ref[0, r, :].astype(f32)
        m_new = BETA_ONE * m_in[r, :] + (1 - BETA_ONE) * g
        v_new = BETA_TWO * v_in[r, :] + (1 - BETA_TWO) * g * g
        root = jnp.sqrt(v_new * (1 / (1 - BETA_TWO**STEP))) + ADAM_EPS
        decay = INNER_RATE * DECAY
        if matrix_row is not None:
            here = lax.broadcasted_iota(jnp.int32, (rows, LANES), 0) + at
            decay = jnp.where(here < matrix_row[0] - slot_ref[0] * piece_rows, decay, 0.0)
        d = (INNER_RATE / (1 - BETA_ONE**STEP)) * m_new / root + decay * w
        g_out[r, :] = g
        m_out[r, :] = m_new
        v_out[r, :] = v_new
        w_out[r, :] = w - d
        d_ref[r, :] = d.astype(bf16)

    for n, (at, rows) in enumerate(parts):
        for copy in loads[n]:
            copy.wait()
        in_steps(at, rows, 64, update)
        r = pl.ds(at, rows)
        for k, (src, dst) in enumerate(((g_out, go), (m_out, mo), (v_out, vo), (w_out, wo))):
            copy = pltpu.make_async_copy(src.at[r], dst.at[r, b, :], sems.at[2 + k, n])
            copy.start()
            stores.append(copy)
    for copy in stores:
        copy.wait()


def adamw(b, slot, grads, pieces, first, second, held, per, matrix_rows):
    piece_rows = first.shape[0]
    padded = grads.shape[1]
    hbm = pl.BlockSpec(memory_space=pl.ANY)
    shape = jax.ShapeDtypeStruct(first.shape, f32)
    state = pltpu.VMEM((piece_rows, LANES), f32)
    parts = row_parts(piece_rows, 3)
    matrix_row = None
    if (b + 1) * per * piece_rows > matrix_rows:
        matrix_row = (matrix_rows - b * per * piece_rows,)
    return pl.pallas_call(
        functools.partial(
            adamw_kernel, b=b, piece_rows=piece_rows, matrix_row=matrix_row, parts=parts
        ),
        grid_spec=pltpu.PrefetchScalarGridSpec(
            num_scalar_prefetch=1,
            grid=(1,),
            in_specs=[
                pl.BlockSpec((1, padded, LANES), lambda i, s: (b, 0, 0)),
                pl.BlockSpec((1, padded, LANES), lambda i, s: (b, 0, 0)),
                hbm,
                hbm,
            ]
            + [hbm] * len(held),
            out_specs=[hbm] * 4 + [pl.BlockSpec((padded, LANES), lambda i, s: (0, 0))],
            scratch_shapes=[state] * 6 + [pltpu.SemaphoreType.DMA((6, len(parts)))],
        ),
        out_shape=[shape] * 4 + [jax.ShapeDtypeStruct((padded, LANES), bf16)],
        input_output_aliases={5 + k: k for k in range(len(held))},
        cost_estimate=pl.CostEstimate(
            flops=30 * piece_rows * LANES,
            bytes_accessed=30 * piece_rows * LANES,
            transcendentals=2 * piece_rows * LANES,
        ),
        compiler_params=params(),
        name=f"adamw_{b}",
    )(slot, grads, pieces, first, second, *held)


def outer_kernel(d0, d1, d2, d3, w_hbm, o_hbm, mean_out, mom_out, new_out, w_in, o_in, mean, mom, new, sems, *, parts):
    loads = []
    for n, (at, rows) in enumerate(parts):
        r = pl.ds(at, rows)
        pair = (
            pltpu.make_async_copy(w_hbm.at[r, 0, :], w_in.at[r], sems.at[0, n]),
            pltpu.make_async_copy(o_hbm.at[r, 0, :], o_in.at[r], sems.at[1, n]),
        )
        for copy in pair:
            copy.start()
        loads.append(pair)
    stores = []

    def update(at, rows):
        r = pl.ds(at, rows)
        total = (d0[r, :].astype(f32) + d1[r, :].astype(f32)) + (
            d2[r, :].astype(f32) + d3[r, :].astype(f32)
        )
        average = total / GROUPS
        momentum = OUTER_MU * o_in[r, :] + average
        mean[r, :] = average
        mom[r, :] = momentum
        new[r, :] = w_in[r, :] - OUTER_RATE * (average + OUTER_MU * momentum)

    for n, (at, rows) in enumerate(parts):
        for copy in loads[n]:
            copy.wait()
        in_steps(at, rows, 64, update)
        r = pl.ds(at, rows)
        for k, (src, dst) in enumerate(((mean, mean_out), (mom, mom_out), (new, new_out))):
            copy = pltpu.make_async_copy(src.at[r], dst.at[r, 0, :], sems.at[2 + k, n])
            copy.start()
            stores.append(copy)
    for copy in stores:
        copy.wait()


def outer(diffs, own_rows, momentum_rows):
    piece_rows = own_rows.shape[0]
    hbm = pl.BlockSpec(memory_space=pl.ANY)
    whole = pl.BlockSpec(memory_space=pltpu.VMEM)
    parts = row_parts(piece_rows, 3)
    return pl.pallas_call(
        functools.partial(outer_kernel, parts=parts),
        in_specs=[whole] * 4 + [hbm] * 2,
        out_specs=[hbm] * 3,
        out_shape=[jax.ShapeDtypeStruct(own_rows.shape, f32)] * 3,
        scratch_shapes=[pltpu.VMEM((piece_rows, LANES), f32)] * 5
        + [pltpu.SemaphoreType.DMA((5, len(parts)))],
        compiler_params=params(),
        name="outer_step",
    )(*diffs, own_rows, momentum_rows)


def attend_block(q, k, v_ones, code, seg_col, offset):
    rows_q, n = q.shape[0], k.shape[0]
    low = lax.broadcasted_iota(jnp.int32, (1, LANES), 1) < HD
    zero = jnp.zeros((), bf16)
    q = q * jnp.asarray(HD**-0.5, bf16)
    rows = lax.broadcasted_iota(jnp.int32, (rows_q, n), 0) + offset
    cols = lax.broadcasted_iota(jnp.int32, (rows_q, n), 1)
    allowed = (seg_col == code) | (rows == cols)
    outs = []
    tops = []
    for h in range(2):
        qh = jnp.where(low, q, zero) if h == 0 else jnp.where(low, zero, q)
        s = jnp.where(allowed, dot(qh, k, NT), MASKED)
        top = jnp.max(s, axis=1, keepdims=True)
        p = jnp.exp(s - top).astype(bf16)
        outs.append(dot(p, v_ones[h], NN))
        tops.append(top)
    num = jnp.where(low, outs[0], outs[1])
    den = pltpu.roll(jnp.where(low, outs[1], outs[0]), HD, 1)
    lse = (jnp.where(low, tops[0], tops[1]) + jnp.log(den)).T
    return (num / den).astype(bf16), lse[0:1], lse[HD : HD + 1]


def bring_rows(buf, flat, margin, offset, count, piece_rows):
    for p in range(offset // piece_rows, -(-(offset + count) // piece_rows)):
        low = max(offset - p * piece_rows, 0) // 16 * 16
        high = min(round_up(min(offset + count - p * piece_rows, piece_rows), 16), buf.shape[1])
        to = margin + p * piece_rows + low - offset
        step = 128
        full = (high - low) // step

        @pl.loop(0, full)
        def _(i, p=p, low=low, to=to):
            rows = buf[p, pl.ds(pl.multiple_of(low + i * step, 16), step), :]
            flat[pl.ds(to + i * step, step), :] = rows.astype(f32)

        rest = (high - low) % step
        if rest:
            flat[pl.ds(to + full * step, rest), :] = buf[p, low + full * step : high, :].astype(f32)


def emit_matrix(flat, out, margin, rows, blocks):
    chunk = 64

    @pl.loop(0, rows // chunk)
    def _(c):
        at = pl.ds(pl.multiple_of(c * chunk, chunk), chunk)
        for j in range(blocks):
            from_rows = pl.ds(margin + c * (chunk * blocks) + j, chunk, stride=blocks)
            out[at, j * LANES : (j + 1) * LANES] = flat[from_rows, :].astype(bf16)


def start_kernel(
    own_hbm, tokens_hbm, code_ref, seg_ref,
    proj_out, outw_out, inw_out, down_out, pieces_out, tail_out, x_out, q_ref, k_ref, v_ref, ctx_ref, lse_ref,
    rows32, buf, xbuf, flat, proj_s, outw_s, inw_s, down_s,
    zdown, zup, zrecv, ysend, yrecv, csend, crecv, xsem, local_sems,
    *, piece_rows, tail_rows, table, cuts, rows_q
):
    z = lax.axis_index("group")
    slot = lax.axis_index("slot")
    me = lax.axis_index("tensor")
    depth = GROUPS
    padded = buf.shape[1]
    half = tokens_hbm.shape[0]
    n = 2 * half
    mesh_id = pl.DeviceIdType.MESH

    load = pltpu.make_async_copy(own_hbm.at[:, 0, :], rows32, local_sems.at[0])
    load.start()
    x_load = pltpu.make_async_copy(tokens_hbm, xbuf.at[pl.ds(0, half)], local_sems.at[1])
    x_load.start()

    barrier = pltpu.get_barrier_semaphore()
    for where in ({"slot": slot ^ 1}, {"slot": slot ^ 2}, {"tensor": 1 - me}):
        pl.semaphore_signal(barrier, inc=1, device_id=where, device_id_type=mesh_id)

    @pl.when(z > 0)
    def _():
        pl.semaphore_signal(barrier, inc=1, device_id={"group": z - 1}, device_id_type=mesh_id)

    @pl.when(z < depth - 1)
    def _():
        pl.semaphore_signal(barrier, inc=1, device_id={"group": z + 1}, device_id_type=mesh_id)

    pl.semaphore_wait(barrier, 3 + jnp.where(z > 0, 1, 0) + jnp.where(z < depth - 1, 1, 0))

    load.wait()
    own = z * 4 + slot
    step = 128
    full = piece_rows // step

    @pl.loop(0, full)
    def _(i):
        r = pl.ds(pl.multiple_of(i * step, step), step)
        buf[own, r, :] = rows32[r, :].astype(bf16)

    tail = rows32[piece_rows - tail_rows :, :]
    left = tail - tail.astype(bf16).astype(f32)
    zeros = jnp.zeros((padded - piece_rows - tail_rows, LANES), f32)
    buf[own, full * step :, :] = jnp.concatenate([rows32[full * step :, :], left, zeros], axis=0).astype(bf16)

    def copy_of(piece, h, send, recv, where):
        part = buf.at[piece, pl.ds(*cuts[h])]
        return pltpu.make_async_remote_copy(
            src_ref=part, dst_ref=part, send_sem=send, recv_sem=recv, device_id=where, device_id_type=mesh_id
        )

    def down(b, h):
        return copy_of(b * 4 + slot, h, zdown.at[b, h], zrecv.at[b, h], {"group": z + 1})

    def up(b, h):
        return copy_of(b * 4 + slot, h, zup.at[b, h], zrecv.at[b, h], {"group": z - 1})

    def side(b, h):
        return copy_of(b * 4 + slot, h, ysend.at[b, h], yrecv.at[b, h], {"slot": slot ^ 2})

    def side_in(b, h):
        return copy_of(b * 4 + (slot ^ 2), h, ysend.at[b, h], yrecv.at[b, h], {"slot": slot ^ 2})

    def twin(b, h, k):
        return copy_of(
            b * 4 + (slot ^ (2 * k)), h, csend.at[2 * b + k, h], crecv.at[2 * b + k, h], {"slot": slot ^ 1}
        )

    def twin_in(b, h, k):
        return copy_of(
            b * 4 + (slot ^ 1 ^ (2 * k)), h, csend.at[2 * b + k, h], crecv.at[2 * b + k, h], {"slot": slot ^ 1}
        )

    parts = range(len(cuts))
    tail_part = len(cuts) - 1
    order = [tail_part] + list(range(tail_part))
    last = depth - 1
    ranked = (
        z,
        jnp.where(z == 0, 1, 0),
        jnp.where(z == 2, 3, 2),
        jnp.where(z < 2, 3, 1),
    )
    middle = (z == 1) | (z == 2)

    def pass_on(b, h):
        up(b, h).wait_recv()

        @pl.when((b < z) & (z < last))
        def _():
            down(b, h).start()

        @pl.when((b > z) & (z > 0))
        def _():
            up(b, h).start()

        side(b, h).start()
        twin(b, h, 0).start()

    def serve_z(b, h, when=None):
        if h == tail_part:
            when = (b != last) if when is None else when & (b != last)
        if when is None:
            pass_on(b, h)
        else:
            pl.when(when)(functools.partial(pass_on, b, h))

    def serve_y(rank, h):
        b = ranked[rank]

        def go():
            side_in(b, h).wait_recv()
            twin(b, h, 1).start()

        if h == tail_part:
            pl.when(b != last)(go)
        else:
            go()

    early = order[:3]
    for h in order:

        @pl.when(z > 0)
        def _(h=h):
            up(z, h).start()

        @pl.when(z == 0)
        def _(h=h):
            down(z, h).start()

        if h in early:
            side(z, h).start()
        twin(z, h, 0).start()

    x_load.wait()
    x_copy = pltpu.make_async_remote_copy(
        src_ref=xbuf.at[pl.ds(0, half)],
        dst_ref=xbuf.at[pl.ds(half, half)],
        send_sem=xsem.at[0],
        recv_sem=xsem.at[1],
        device_id={"tensor": 1 - me},
        device_id_type=mesh_id,
    )
    x_copy.start()

    pl.when(z != last)(functools.partial(pass_on, last, tail_part))
    for h in order:
        serve_z(ranked[1], h)
    for h in order:

        @pl.when((z > 0) & (z < last))
        def _(h=h):
            down(z, h).start()

        if h not in early:
            side(z, h).start()
    for h in order:
        serve_z(ranked[2], h, middle)
    side_in(last, tail_part).wait_recv()
    twin(last, tail_part, 1).start()
    for h in early:
        serve_y(0, h)
    for h in order:
        serve_y(1, h)
    for h in order:
        if h not in early:
            serve_y(0, h)
    for k in range(2):
        twin_in(last, tail_part, k).wait_recv()
        for rank in range(2):
            b = ranked[rank]
            for h in parts:
                if h == tail_part:
                    pl.when(b != last)(lambda b=b, h=h, k=k: twin_in(b, h, k).wait_recv())
                else:
                    twin_in(b, h, k).wait_recv()

    at = (piece_rows - tail_rows) // 16 * 16
    shift = piece_rows - tail_rows - at
    ends = buf[4 * depth - 1, at:, :].astype(f32)
    vectors = ends[shift : shift + tail_rows] + ends[shift + tail_rows : shift + 2 * tail_rows]
    tail_out[...] = vectors

    margin = 16
    (offset, rows, blocks) = table[0]
    bring_rows(buf, flat, margin, offset, rows * blocks, piece_rows)
    emit_matrix(flat, proj_s, margin, rows, blocks)
    out_copies = [pltpu.make_async_copy(proj_s, proj_out, local_sems.at[2])]
    out_copies[0].start()
    x_copy.wait()
    out_copies.append(pltpu.make_async_copy(xbuf, x_out, local_sems.at[3]))
    out_copies[1].start()
    query_bias = jnp.concatenate([vectors[j : j + 1] for j in range(blocks)], axis=1)
    value_bias = jnp.concatenate([vectors[blocks + j : blocks + j + 1] for j in range(blocks)], axis=1)
    depth_in = rows // 3
    for m, (ref, bias) in enumerate(((q_ref, query_bias), (k_ref, None), (v_ref, value_bias))):

        @pl.loop(0, n // 256)
        def _(i, m=m, ref=ref, bias=bias):
            r = pl.ds(pl.multiple_of(i * 256, 256), 256)
            acc = dot(xbuf[r, :], proj_s[m * depth_in : (m + 1) * depth_in, :], NN)
            if bias is not None:
                acc = acc + bias
            ref[r, :] = acc.astype(bf16)

        for h in order[2 * m : 2 * m + 2]:
            serve_z(jnp.where(middle, ranked[3], ranked[2]), h)

    edge = jnp.logical_not(middle)
    todo = [functools.partial(serve_z, ranked[3], h, edge) for h in order]
    late = [functools.partial(serve_y, 2, h) for h in order]
    todo = [act for both_acts in zip(late, todo) for act in both_acts]
    todo += [functools.partial(serve_y, 3, h) for h in order]
    low = lax.broadcasted_iota(jnp.int32, (1, LANES), 1) < HD
    one = jnp.ones((), bf16)
    code = code_ref[...]
    for pair in range(blocks):
        c = slice(pair * LANES, (pair + 1) * LANES)
        k = k_ref[:, c]
        v = v_ref[:, c]
        v_ones = (jnp.where(low, v, one), jnp.where(low, one, v))
        for i in range(n // rows_q):
            r = slice(i * rows_q, (i + 1) * rows_q)
            ctx, lse_0, lse_1 = attend_block(q_ref[r, c], k, v_ones, code, seg_ref[r, :], i * rows_q)
            ctx_ref[r, c] = ctx
            lse_ref[pair, 0:1, r] = lse_0
            lse_ref[pair, 1:2, r] = lse_1
            for _ in range(1):
                if todo:
                    todo.pop(0)()
    for act in todo:
        act()
    for rank in range(2, 4):
        b = ranked[rank]
        for h in parts:
            for k in range(2):
                if h == tail_part:
                    pl.when(b != last)(lambda b=b, h=h, k=k: twin_in(b, h, k).wait_recv())
                else:
                    twin_in(b, h, k).wait_recv()

    for b in range(depth):
        copy = pltpu.make_async_copy(buf.at[b * 4 + slot], pieces_out.at[b], local_sems.at[7 + b])
        copy.start()
        out_copies.append(copy)
    for m, (scr, out) in enumerate(((outw_s, outw_out), (inw_s, inw_out), (down_s, down_out))):
        (offset, rows, blocks) = table[1 + m]
        bring_rows(buf, flat, margin, offset, rows * blocks, piece_rows)
        emit_matrix(flat, scr, margin, rows, blocks)
        copy = pltpu.make_async_copy(scr, out, local_sems.at[4 + m])
        copy.start()
        out_copies.append(copy)

    for b in range(depth):
        for h in parts:

            @pl.when((b <= z) & (z < depth - 1))
            def _(b=b, h=h):
                down(b, h).wait_send()

            @pl.when((b >= z) & (z > 0))
            def _(b=b, h=h):
                up(b, h).wait_send()

            side(b, h).wait_send()
            for k in range(2):
                twin(b, h, k).wait_send()
    for copy in out_copies:
        copy.wait()


def start(own_rows, tokens, code_row, seg_col, table, tail_rows, padded, cuts, rows_q=256):
    piece_rows = own_rows.shape[0]
    half, width = tokens.shape
    n = 2 * half
    pairs = table[0][2]
    local_width = pairs * LANES
    hbm = pl.BlockSpec(memory_space=pl.ANY)
    whole = pl.BlockSpec(memory_space=pltpu.VMEM)
    mats = [jax.ShapeDtypeStruct((rows, blocks * LANES), bf16) for _, rows, blocks in table]
    acts = [jax.ShapeDtypeStruct((n, local_width), bf16)] * 4
    most = max(rows * blocks for _, rows, blocks in table)
    parts = len(cuts)
    dma = pltpu.SemaphoreType.DMA
    return pl.pallas_call(
        functools.partial(
            start_kernel, piece_rows=piece_rows, tail_rows=tail_rows, table=table, cuts=cuts, rows_q=rows_q
        ),
        in_specs=[hbm, hbm, whole, whole],
        out_specs=[hbm] * 5 + [whole] + [hbm] + [whole] * 5,
        out_shape=mats
        + [
            jax.ShapeDtypeStruct((GROUPS, padded, LANES), bf16),
            jax.ShapeDtypeStruct((tail_rows, LANES), f32),
            jax.ShapeDtypeStruct((n, width), bf16),
        ]
        + acts
        + [jax.ShapeDtypeStruct((pairs, 2, n), f32)],
        scratch_shapes=[
            pltpu.VMEM((piece_rows, LANES), f32),
            pltpu.VMEM((4 * GROUPS, padded, LANES), bf16),
            pltpu.VMEM((n, width), bf16),
            pltpu.VMEM((most + 48, LANES), f32),
        ]
        + [pltpu.VMEM(m.shape, bf16) for m in mats]
        + [
            dma((GROUPS, parts)),
            dma((GROUPS, parts)),
            dma((GROUPS, parts)),
            dma((GROUPS, parts)),
            dma((GROUPS, parts)),
            dma((2 * GROUPS, parts)),
            dma((2 * GROUPS, parts)),
            dma((2,)),
            dma((11,)),
        ],
        cost_estimate=pl.CostEstimate(
            flops=6 * n * width * local_width, bytes_accessed=60 << 20, transcendentals=8 * n * n
        ),
        compiler_params=params(collective_id=1, has_side_effects=True),
        name="start",
    )(own_rows, tokens, code_row, seg_col)


ERF = (0.254829592, -0.284496736, 1.421413741, -1.453152027, 1.061405429)
ERF_P = 0.3275911


def gelu_pair(u):
    bell = jnp.exp(-0.5 * u * u)
    t = 1.0 / (1.0 + (ERF_P * ROOT_HALF) * jnp.abs(u))
    poly = ERF[4]
    for number in ERF[3::-1]:
        poly = poly * t + number
    tail = (0.5 * poly * t) * bell
    phi = jnp.where(u >= 0, 1.0 - tail, tail)
    return u * phi, phi + u * bell * INV_ROOT_TWO_PI


def fold(values):
    return values.reshape(values.shape[0] // 8, 8, values.shape[1]).sum(axis=0)


def middle_kernel(
    ctx_ref, tokens_ref, cot_ref, vec_ref, c1_ref, outw_ref, inw_ref, down_ref,
    block_out, dh1_out, dctx_out, d_outw, d_inw, d_down, tail_out,
    x1, norm1, inv1, x1_all, act, slope, dh2_all, dh1_all, part, dh2, box_send, box_recv, sums, c1_sum, vec_box, send_sems, recv_sems, vec_sems,
    *, chunk
):
    me = lax.axis_index("tensor")
    half, width = tokens_ref.shape
    count = half // chunk
    mesh_id = pl.DeviceIdType.MESH
    other = {"tensor": 1 - me}
    barrier = pltpu.get_barrier_semaphore()
    pl.semaphore_signal(barrier, inc=1, device_id=other, device_id_type=mesh_id)
    pl.semaphore_wait(barrier, 1)

    def rows_of(i):
        return pl.ds(pl.multiple_of(i * chunk, chunk), chunk)

    def far_rows(i):
        return pl.ds(pl.multiple_of(half + i * chunk, chunk), chunk)

    def summed(stage, i):
        return pltpu.make_async_remote_copy(
            src_ref=box_send.at[stage, rows_of(i)],
            dst_ref=box_recv.at[stage, rows_of(i)],
            send_sem=send_sems.at[stage, i],
            recv_sem=recv_sems.at[stage, i],
            device_id=other,
            device_id_type=mesh_id,
        )

    def gathered(stage, ref, i):
        return pltpu.make_async_remote_copy(
            src_ref=ref.at[rows_of(i)],
            dst_ref=ref.at[far_rows(i)],
            send_sem=send_sems.at[3 + stage, i],
            recv_sem=recv_sems.at[3 + stage, i],
            device_id=other,
            device_id_type=mesh_id,
        )

    gain_1, shift_1 = vec_ref[0:1, :], vec_ref[1:2, :]
    gain_2, shift_2 = vec_ref[2:3, :], vec_ref[3:4, :]
    bias_o, bias_2 = vec_ref[4:5, :], vec_ref[5:6, :]
    sums[...] = jnp.zeros_like(sums)
    c1_sum[...] = jnp.zeros_like(c1_sum)

    def normed(h):
        centred = h - jnp.mean(h, axis=-1, keepdims=True)
        inv = lax.rsqrt(jnp.mean(centred * centred, axis=-1, keepdims=True) + NORM_EPS)
        return centred * inv, inv

    def normed_back(dn, n, inv):
        return inv * (
            dn - jnp.mean(dn, axis=-1, keepdims=True) - n * jnp.mean(dn * n, axis=-1, keepdims=True)
        )

    def forward(r):
        u = dot(x1_all[r, :], inw_ref[...], NN) + c1_ref[...]
        a, s = gelu_pair(u)
        act[r, :] = a.astype(bf16)
        slope[r, :] = s.astype(bf16)
        return dot(act[r, :], down_ref[...], NN)

    def backward(r):
        da = dot(dh2_all[r, :], down_ref[...], NT)
        du = da * slope[r, :].astype(f32)
        low = du.astype(bf16)
        slope[r, :] = low
        c1_sum[...] += fold(low.astype(f32))
        return dot(low, inw_ref[...], NT)

    @pl.loop(0, count)
    def _(i):
        box_send[0, rows_of(i), :] = dot(ctx_ref[far_rows(i), :], outw_ref[...], NN).astype(bf16)
        summed(0, i).start()

    @pl.loop(0, count)
    def _(i):
        r = rows_of(i)
        mine = dot(ctx_ref[r, :], outw_ref[...], NN)
        summed(0, i).wait_recv()
        h = tokens_ref[r, :].astype(f32) + (mine + box_recv[0, r, :].astype(f32) + bias_o)
        n, inv = normed(h)
        norm1[r, :] = n
        inv1[r, :] = jnp.broadcast_to(inv, (chunk, LANES))
        middle = n * gain_1 + shift_1
        x1[r, :] = middle
        x1_all[r, :] = middle.astype(bf16)
        gathered(0, x1_all, i).start()
        part[r, :] = forward(r)

    @pl.loop(0, count)
    def _(i):
        gathered(0, x1_all, i).wait_recv()
        box_send[1, rows_of(i), :] = forward(far_rows(i)).astype(bf16)
        summed(1, i).start()

    @pl.loop(0, count)
    def _(i):
        r = rows_of(i)
        summed(1, i).wait_recv()
        h = x1[r, :] + (part[r, :] + box_recv[1, r, :].astype(f32) + bias_2)
        n, inv = normed(h)
        block_out[r, :] = (n * gain_2 + shift_2).astype(bf16)
        dy = cot_ref[r, :].astype(f32)
        dh = normed_back(dy * gain_2, n, inv)
        sums[2] += fold(dy * n)
        sums[3] += fold(dy)
        sums[5] += fold(dh)
        dh2[r, :] = dh
        dh2_all[r, :] = dh.astype(bf16)
        gathered(1, dh2_all, i).start()
        part[r, :] = backward(r)

    @pl.loop(0, count)
    def _(i):
        gathered(1, dh2_all, i).wait_recv()
        box_send[2, rows_of(i), :] = backward(far_rows(i)).astype(bf16)
        summed(2, i).start()

    hidden = act.shape[1]
    block = hidden // 8

    def down_grad(j):
        c = pl.ds(pl.multiple_of(j * block, block), block)
        d_down[c, :] = dot(act[:, c].T, dh2_all[...], NN).astype(bf16)

    def in_grad(j):
        c = pl.ds(pl.multiple_of(j * block, block), block)
        d_inw[:, c] = dot(x1_all[...].T, slope[:, c], NN).astype(bf16)

    per_chunk = 8 // count

    @pl.loop(0, count)
    def _(i):
        for j in range(per_chunk):
            down_grad(i * per_chunk + j)
        r = rows_of(i)
        summed(2, i).wait_recv()
        dx = dh2[r, :] + part[r, :] + box_recv[2, r, :].astype(f32)
        n = norm1[r, :]
        dh = normed_back(dx * gain_1, n, inv1[r, 0:1])
        sums[0] += fold(dx * n)
        sums[1] += fold(dx)
        sums[4] += fold(dh)
        dh1_out[r, :] = dh
        dh1_all[r, :] = dh.astype(bf16)
        gathered(2, dh1_all, i).start()
        dctx_out[r, :] = dot(dh1_all[r, :], outw_ref[...], NT).astype(bf16)

    for row in range(6):
        total = jnp.sum(sums[row], axis=0, keepdims=True)
        low, high = total[:, : width // 2], total[:, width // 2 :]
        mine, theirs = jnp.where(me == 0, low, high), jnp.where(me == 0, high, low)
        spread = width // 2 // LANES
        for j in range(spread):
            at = row * spread + j
            vec_box[0, at : at + 1, :] = mine[:, j * LANES : (j + 1) * LANES]
            vec_box[1, at : at + 1, :] = theirs[:, j * LANES : (j + 1) * LANES]
    vec_copy = pltpu.make_async_remote_copy(
        src_ref=vec_box.at[1],
        dst_ref=vec_box.at[2],
        send_sem=vec_sems.at[0],
        recv_sem=vec_sems.at[1],
        device_id=other,
        device_id_type=mesh_id,
    )
    vec_copy.start()

    @pl.loop(0, count)
    def _(i):
        for j in range(per_chunk):
            in_grad(i * per_chunk + j)
        r = far_rows(i)
        gathered(2, dh1_all, i).wait_recv()
        dctx_out[r, :] = dot(dh1_all[r, :], outw_ref[...], NT).astype(bf16)

    d_outw[...] = dot(ctx_ref[...].T, dh1_all[...], NN).astype(bf16)

    blocks = ctx_ref.shape[1] // LANES
    tail_out[0 : 2 * blocks, :] = jnp.zeros((2 * blocks, LANES), f32)
    c1_total = jnp.sum(c1_sum[...], axis=0, keepdims=True)
    for j in range(hidden // LANES):
        tail_out[2 * blocks + j : 2 * blocks + j + 1, :] = c1_total[:, j * LANES : (j + 1) * LANES]
    vec_copy.wait()
    tail_out[2 * blocks + hidden // LANES :, :] = vec_box[0] + vec_box[2]

    @pl.loop(0, count)
    def _(i):
        for stage in range(3):
            summed(stage, i).wait_send()
        gathered(0, x1_all, i).wait_send()
        gathered(1, dh2_all, i).wait_send()
        gathered(2, dh1_all, i).wait_send()


def middle(context, tokens, cotangent, vectors, inner_bias, out_w, in_w, down_w, chunk=128):
    half, width = tokens.shape
    n = 2 * half
    hidden = in_w.shape[1]
    local_width = context.shape[1]
    whole = pl.BlockSpec(memory_space=pltpu.VMEM)
    wide = pltpu.VMEM((half, width), f32)
    every = pltpu.VMEM((n, width), bf16)
    box = pltpu.VMEM((3, half, width), bf16)
    count = half // chunk
    return pl.pallas_call(
        functools.partial(middle_kernel, chunk=chunk),
        in_specs=[whole] * 8,
        out_specs=[whole] * 7,
        out_shape=[
            jax.ShapeDtypeStruct((half, width), bf16),
            jax.ShapeDtypeStruct((half, width), f32),
            jax.ShapeDtypeStruct((n, local_width), bf16),
            jax.ShapeDtypeStruct(out_w.shape, bf16),
            jax.ShapeDtypeStruct(in_w.shape, bf16),
            jax.ShapeDtypeStruct(down_w.shape, bf16),
            jax.ShapeDtypeStruct(((2 * local_width + hidden + 3 * width) // LANES, LANES), f32),
        ],
        scratch_shapes=[
            wide,
            wide,
            pltpu.VMEM((half, LANES), f32),
            every,
            pltpu.VMEM((n, hidden), bf16),
            pltpu.VMEM((n, hidden), bf16),
            every,
            every,
            wide,
            wide,
            box,
            box,
            pltpu.VMEM((6, 8, width), f32),
            pltpu.VMEM((8, hidden), f32),
            pltpu.VMEM((3, 3 * width // LANES, LANES), f32),
            pltpu.SemaphoreType.DMA((6, count)),
            pltpu.SemaphoreType.DMA((6, count)),
            pltpu.SemaphoreType.DMA((2,)),
        ],
        cost_estimate=pl.CostEstimate(
            flops=14 * n * width * hidden, bytes_accessed=40 << 20, transcendentals=2 * n * hidden
        ),
        compiler_params=params(collective_id=2, has_side_effects=True),
        name="middle",
    )(context, tokens, cotangent, vectors, inner_bias, out_w, in_w, down_w)


def attend_back(q_ref, k_ref, v_ref, ctx_ref, dctx_ref, code, seg_ref, lse_ref, dq_ref, dk_ref, dv_ref, pair, rows_q):
    n = q_ref.shape[0]
    c = slice(pair * LANES, (pair + 1) * LANES)
    low = lax.broadcasted_iota(jnp.int32, (1, LANES), 1) < HD
    zero = jnp.zeros((), bf16)
    k = k_ref[:, c]
    v = v_ref[:, c]
    k_t = k.T
    pick = (
        lax.broadcasted_iota(jnp.int32, (8, LANES), 1) // HD
        == lax.broadcasted_iota(jnp.int32, (8, LANES), 0)
    ).astype(f32)
    dks = [jnp.zeros((n, LANES), f32)] * 2
    dvs = [jnp.zeros((n, LANES), f32)] * 2
    scale = jnp.asarray(HD**-0.5, bf16)
    for i in range(n // rows_q):
        r = slice(i * rows_q, (i + 1) * rows_q)
        q = q_ref[r, c] * scale
        do = dctx_ref[r, c]
        prod = do.astype(f32) * ctx_ref[r, c].astype(f32)
        delta = lax.dot_general(
            pick, prod, NT, precision=lax.Precision.HIGHEST, preferred_element_type=f32
        )
        keys = lax.broadcasted_iota(jnp.int32, (n, rows_q), 0)
        qs = lax.broadcasted_iota(jnp.int32, (n, rows_q), 1) + i * rows_q
        allowed = (code == seg_ref[:, r]) | (keys == qs)
        dqs = []
        for h in range(2):
            qh = jnp.where(low, q, zero) if h == 0 else jnp.where(low, zero, q)
            doh = jnp.where(low, do, zero) if h == 0 else jnp.where(low, zero, do)
            s = jnp.where(allowed, dot(k, qh, NT), MASKED)
            p = jnp.exp(s - lse_ref[pair, h : h + 1, r])
            dp = dot(v, doh, NT)
            ds = (p * (dp - delta[h : h + 1])).astype(bf16)
            dvs[h] = dvs[h] + dot(p.astype(bf16), do, NN)
            dks[h] = dks[h] + dot(ds, q, NN)
            dqs.append(dot(k_t[h * HD : (h + 1) * HD], ds, NN))
        dq_ref[r, c] = (jnp.concatenate(dqs, axis=0).T * (HD**-0.5)).astype(bf16)
    dk_ref[:, c] = jnp.where(low, dks[0], dks[1]).astype(bf16)
    dv_ref[:, c] = jnp.where(low, dvs[0], dvs[1]).astype(bf16)


def lay_flat(ref, low, high, blocks, flat, at):
    chunk = 16 if (high - low) % 64 else 64

    @pl.loop(0, (high - low) // chunk)
    def _(c):
        rows = pl.ds(pl.multiple_of(low + c * chunk, 16), chunk)
        for j in range(blocks):
            to_rows = pl.ds(at + c * (chunk * blocks) + j, chunk, stride=blocks)
            flat[to_rows, :] = ref[rows, j * LANES : (j + 1) * LANES].astype(f32)


def emit_pieces(flat, keep, send, slot, skip, piece_rows):
    padded = send.shape[1]
    step = 128
    full = piece_rows // step
    rest = piece_rows - full * step
    for j in (3, 1, 2, 0):
        out = send if j % 2 else keep
        start = skip + (slot ^ j) * piece_rows

        @pl.loop(0, full)
        def _(i, out=out, j=j, start=start):
            rows = flat[pl.ds(start + i * step, step), :]
            out[j // 2, pl.ds(pl.multiple_of(i * step, step), step), :] = rows.astype(bf16)

        parts = [jnp.zeros((padded - piece_rows, LANES), f32)]
        if rest:
            parts = [flat[pl.ds(start + full * step, rest), :]] + parts
        out[j // 2, full * step : padded, :] = jnp.concatenate(parts, axis=0).astype(bf16)


def back_kernel(
    q_ref, k_ref, v_ref, ctx_ref, dctx_ref, code_ref, seg_ref, lse_ref, x_ref, outw_ref, inw_ref, down_ref, tail_ref,
    dq_ref, dk_ref, dv_ref, g_out,
    flat, keep, send, near, far, tails, g_stage, near_send, near_recv, far_send, far_recv, tail_send, tail_recv, out_sems,
    *, plans, tail_at, piece_rows, rows_q
):
    slot = lax.axis_index("slot")
    mesh_id = pl.DeviceIdType.MESH
    core = {"slot": slot ^ 1}
    side = {"slot": slot ^ 2}
    tail_rows = tail_ref.shape[0]
    padded = send.shape[1]
    barrier = pltpu.get_barrier_semaphore()
    for where in (core, side):
        pl.semaphore_signal(barrier, inc=1, device_id=where, device_id_type=mesh_id)
    pl.semaphore_wait(barrier, 2)

    def to_core(b, j):
        return pltpu.make_async_remote_copy(
            src_ref=send.at[j],
            dst_ref=near.at[b, j],
            send_sem=near_send.at[b, j],
            recv_sem=near_recv.at[b, j],
            device_id=core,
            device_id_type=mesh_id,
        )

    def to_side(b):
        return pltpu.make_async_remote_copy(
            src_ref=keep.at[b, 1],
            dst_ref=far.at[b],
            send_sem=far_send.at[b],
            recv_sem=far_recv.at[b],
            device_id=side,
            device_id_type=mesh_id,
        )

    def tail_copy(k, where):
        return pltpu.make_async_remote_copy(
            src_ref=tails.at[2 * k],
            dst_ref=tails.at[2 * k + 1],
            send_sem=tail_send.at[k],
            recv_sem=tail_recv.at[k],
            device_id=where,
            device_id_type=mesh_id,
        )

    def hand_over(b):
        for j in (1, 0):
            to_core(b, j).start()

    def pass_aside(b):
        to_core(b, 1).wait_recv()

        @pl.loop(0, padded // 16)
        def _(i):
            r = pl.ds(pl.multiple_of(i * 16, 16), 16)
            keep[b, 1, r, :] = (keep[b, 1, r, :].astype(f32) + near[b, 1, r, :].astype(f32)).astype(bf16)

        to_side(b).start()

    def sent(b):
        for j in (1, 0):
            to_core(b, j).wait_send()

    refs = {1: outw_ref, 2: inw_ref, 3: down_ref}
    order = (3, 2, 1)
    for b in order:
        segments, skip, has_tail = plans[b]
        for number, low, high, blocks, at in segments:
            lay_flat(refs[number], low, high, blocks, flat, at)
        if has_tail:
            at = skip + 4 * piece_rows - tail_rows
            flat[pl.ds(at, tail_rows), :] = jnp.zeros((tail_rows, LANES), f32)
        if b != order[0]:
            sent(b + 1)
        emit_pieces(flat, keep.at[b], send, slot, skip, piece_rows)
        hand_over(b)
        if b != order[0]:
            pass_aside(b + 1)

    blocks = q_ref.shape[1] // LANES
    code = code_ref[...]
    for pair in range(blocks):
        attend_back(
            q_ref, k_ref, v_ref, ctx_ref, dctx_ref, code, seg_ref, lse_ref, dq_ref, dk_ref, dv_ref, pair, rows_q
        )
        if pair == 0:
            pass_aside(1)

    width = x_ref.shape[1]
    chunk = 256
    segments, skip, _ = plans[0]
    for m, ref in enumerate((dq_ref, dk_ref, dv_ref)):

        @pl.loop(0, width // chunk)
        def _(c, m=m, ref=ref):
            columns = pl.ds(pl.multiple_of(c * chunk, chunk), chunk)
            acc = dot(x_ref[:, columns].T, ref[...], NN)
            for j in range(blocks):
                to_rows = pl.ds((m * width + c * chunk) * blocks + j, chunk, stride=blocks)
                flat[to_rows, :] = acc[:, j * LANES : (j + 1) * LANES]

    for number, low, high, wide, at in segments:
        if number:
            lay_flat(refs[number], low, high, wide, flat, at)
    sent(1)
    emit_pieces(flat, keep.at[0], send, slot, skip, piece_rows)
    hand_over(0)

    tails[0] = tail_ref[...]
    for m, ref in enumerate((dq_ref, dv_ref)):
        total = jnp.sum(ref[...].astype(f32), axis=0, keepdims=True)
        for j in range(blocks):
            row = m * blocks + j
            tails[0, row : row + 1, :] = total[:, j * LANES : (j + 1) * LANES]
    tail_copy(0, core).start()
    pass_aside(0)
    tail_copy(0, core).wait()
    tails[2] = tails[0] + tails[1]
    tail_copy(1, side).start()

    def total(b):
        to_core(b, 0).wait_recv()
        to_side(b).wait_recv()
        half = (b % 2) if b else 0

        def add(at, rows):
            r = pl.ds(at, rows)
            g_stage[half, r, :] = (
                keep[b, 0, r, :].astype(f32) + near[b, 0, r, :].astype(f32) + far[b, r, :].astype(f32)
            )

        in_steps(0, padded, 64, add)
        return pltpu.make_async_copy(g_stage.at[half], g_out.at[b], out_sems.at[b])

    copies = {}
    for b in (3, 2, 1, 0):
        if b in (1, 0):
            copies[b + 2].wait()
        copies[b] = total(b)
        if b == 3:
            tail_copy(1, side).wait()
            ends = slice(piece_rows - tail_rows, piece_rows)
            extra = tails[2] + tails[3]
            g_stage[1, ends, :] += jnp.where(slot == 3, extra, 0.0)
        copies[b].start()
    for b in (1, 0):
        copies[b].wait()
    sent(0)
    for b in range(GROUPS):
        to_side(b).wait_send()


def back(q, k, v, ctx, dctx, code_col, seg_row, lse, x_all, d_outw, d_inw, d_down, tail, table, tail_at, piece_rows, rows_q=256):
    per = 4
    padded = round_up(piece_rows, 16)
    tail_rows = tail.shape[0]
    plans = []
    most = 0
    for b in range(GROUPS):
        first = b * per * piece_rows
        segments, base, size = chunk_plan(table, first, first + per * piece_rows, tail_at, tail_rows)
        plans.append((segments, first - base, first + per * piece_rows > tail_at))
        most = max(most, size)
    whole = pl.BlockSpec(memory_space=pltpu.VMEM)
    dma = pltpu.SemaphoreType.DMA
    n, local_width = q.shape
    grad = jax.ShapeDtypeStruct((n, local_width), bf16)
    return pl.pallas_call(
        functools.partial(back_kernel, plans=plans, tail_at=tail_at, piece_rows=piece_rows, rows_q=rows_q),
        in_specs=[whole] * 13,
        out_specs=[whole] * 3 + [pl.BlockSpec(memory_space=pl.ANY)],
        out_shape=[grad, grad, grad, jax.ShapeDtypeStruct((GROUPS, padded, LANES), f32)],
        scratch_shapes=[
            pltpu.VMEM((round_up(most, 8) + 8, LANES), f32),
            pltpu.VMEM((GROUPS, 2, padded, LANES), bf16),
            pltpu.VMEM((2, padded, LANES), bf16),
            pltpu.VMEM((GROUPS, 2, padded, LANES), bf16),
            pltpu.VMEM((GROUPS, padded, LANES), bf16),
            pltpu.VMEM((4, tail_rows, LANES), f32),
            pltpu.VMEM((2, padded, LANES), f32),
            dma((GROUPS, 2)),
            dma((GROUPS, 2)),
            dma((GROUPS,)),
            dma((GROUPS,)),
            dma((2,)),
            dma((2,)),
            dma((GROUPS,)),
        ],
        cost_estimate=pl.CostEstimate(
            flops=30 * n * n * local_width, bytes_accessed=40 << 20, transcendentals=n * n * 8
        ),
        compiler_params=params(collective_id=4, has_side_effects=True),
        name="back",
    )(q, k, v, ctx, dctx, code_col, seg_row, lse, x_all, d_outw, d_inw, d_down, tail)


def partner(block):
    return lax.ppermute(block, "tensor", [(0, 1), (1, 0)])


def both(own):
    return jnp.concatenate([own, partner(own)], axis=0)


def own_sum(partial):
    half = partial.shape[0] // 2
    return partial[:half].astype(f32) + partner(partial[half:].astype(bf16)).astype(f32)


def local_fast(
    tokens,
    cotangent,
    segment_ids,
    padding,
    shared_weights,
    first_moment,
    second_moment,
    outer_momentum,
):
    me = lax.axis_index("tensor")
    per = lax.axis_size("slot")
    rows = tokens.shape[0]
    local_width = D // 2
    piece_rows = shared_weights.shape[1] // LANES
    table, tail_at = matrix_table(2)
    tail_rows = GROUPS * per * piece_rows - tail_at
    padded = round_up(piece_rows + tail_rows, 16)

    own_rows = shared_weights.reshape(piece_rows, 1, LANES)
    seg = jnp.where(me == 0, segment_ids, jnp.roll(segment_ids, rows))
    live = jnp.where(me == 0, padding, jnp.roll(padding, rows))
    code = jnp.where(live == 1, seg, -1)
    end = padded - round_up(2 * tail_rows + 16, 16)
    marks = [end * i // 4 // 16 * 16 for i in range(4)] + [end, padded]
    cuts = [(low, high - low) for low, high in zip(marks[:-1], marks[1:])]
    (
        proj_w, out_w, in_w, down_w, pieces, tail_all, x_all, query, keys, values, context, lse
    ) = start(own_rows, tokens, code[None], seg[:, None], table, tail_rows, padded, cuts)
    proj_w = proj_w.reshape(3, D, local_width)
    flat_tail = tail_all.reshape(-1)
    inner_bias = flat_tail[2 * local_width : 2 * local_width + FF // 2]
    vec_own = flat_tail[2 * local_width + FF // 2 :].reshape(6, local_width)
    vec_other = partner(vec_own)
    vectors = jnp.where(
        me == 0,
        jnp.concatenate([vec_own, vec_other], axis=1),
        jnp.concatenate([vec_other, vec_own], axis=1),
    )

    (
        block_out, grad_one, grad_context, grad_out_w, grad_in_w, grad_down_w, tail_grad
    ) = middle(context, tokens, cotangent, vectors, inner_bias.reshape(1, -1), out_w, in_w, down_w)
    slot = lax.axis_index("slot").astype(jnp.int32)
    slot_word = slot.reshape(1)
    group = lax.axis_index("group")

    def across(block, axis, bit):
        return lax.ppermute(block, axis, [(i, i ^ bit) for i in range(lax.axis_size(axis))])

    dq, dk, dv, grads = back(
        query, keys, values, context, grad_context, code[:, None], seg[None], lse, x_all,
        grad_out_w, grad_in_w, grad_down_w, tail_grad, table, tail_at, piece_rows
    )
    grad_proj = jnp.stack([dq, dk, dv])
    input_share = own_sum(jnp.einsum("kte,kde->td", grad_proj, proj_w, preferred_element_type=f32))
    input_grad = (grad_one + input_share).astype(bf16)

    def blocked(state):
        return state.reshape(GROUPS, piece_rows, LANES).transpose(1, 0, 2)

    def unblocked(state):
        return state.transpose(1, 0, 2).reshape(1, 1, GROUPS, piece_rows * LANES)

    first = blocked(first_moment)
    second = blocked(second_moment)
    held = []
    diffs = [None] * GROUPS
    for b in (3, 2, 1, 0):
        *held, diffs[b] = adamw(b, slot_word, grads, pieces, first, second, held, per, tail_at)

    def turned(k):
        picked = diffs[(GROUPS - 1) ^ k]
        for z in range(GROUPS - 1):
            picked = jnp.where(group == z, diffs[z ^ k], picked)
        return picked

    gathered = [turned(0)] + [across(turned(k), "group", k) for k in (1, 2, 3)]
    mean_diff, new_momentum, new_weights = [
        rows_out.reshape(1, piece_rows * LANES)
        for rows_out in outer(gathered, own_rows, outer_momentum.reshape(piece_rows, 1, LANES))
    ]
    return (block_out, input_grad, *[unblocked(state) for state in held], mean_diff, new_momentum, new_weights)


def solution(mesh):
    dp = mesh.shape["dp"]
    tensor_size = mesh.shape["tensor"]
    piece = (4 * D * D + 2 * D * FF + 8 * D + FF) // tensor_size // dp
    if tensor_size == 2 and piece % LANES == 0 and dp % GROUPS == 0:
        mesh = Mesh(
            mesh.devices.reshape(GROUPS, dp // GROUPS, tensor_size), ("group", "slot", "tensor")
        )
        data = ("group", "slot")
        body = local_fast
    else:
        data = "dp"
        body = local_general
    every = ("group", "slot", "tensor") if body is local_fast else ("dp", "tensor")
    in_specs = (
        P(every, None),
        P(every, None),
        P(data),
        P(data),
        P("tensor", data),
        P("tensor", data, None, None),
        P("tensor", data, None, None),
        P("tensor", data),
    )
    out_specs = (
        P(every, None),
        P(every, None),
        P("tensor", data, None, None),
        P("tensor", data, None, None),
        P("tensor", data, None, None),
        P("tensor", data, None, None),
        P("tensor", data),
        P("tensor", data),
        P("tensor", data),
    )
    return jax.shard_map(body, mesh=mesh, in_specs=in_specs, out_specs=out_specs, check_vma=False)
```

```python
import functools

import jax
import jax.numpy as jnp
import numpy as np
from jax import lax
from jax.experimental import pallas as pl
from jax.experimental.pallas import tpu as pltpu
from jax.sharding import Mesh
from jax.sharding import PartitionSpec as P

D = 1024
HEADS = 16
HD = 64
FF = 4096
SEQ_LEN = 1024
GROUPS = 4
STEP = 10


NORM_EPS = 1e-05
MASKED = -1000000000.0
BETA_ONE = 0.9
BETA_TWO = 0.999
ADAM_EPS = 1e-08
INNER_RATE = 0.02
DECAY = 0.01
OUTER_MU = 0.9
OUTER_RATE = 0.7
ROOT_HALF = 0.7071067811865476
INV_ROOT_TWO_PI = 0.3989422804014327


def from_partner(block, axis, stride):
    count = lax.axis_size(axis)
    route = []
    for low in range(count):
        high = low | 1 << stride
        if high != low and high < count:
            route += [(low, high), (high, low)]
    return lax.ppermute(block, axis, route)


def boundaries(tensor_size):
    local_width = D // tensor_size
    hidden = FF // tensor_size
    lengths = [
        3 * D * local_width,
        local_width * D,
        D * hidden,
        hidden * D,
        local_width,
        local_width,
        hidden,
        6 * local_width,
    ]
    points = [0]
    for amount in lengths:
        points.append(points[-1] + amount)
    return points


def layer_norm(values, norm_gain, norm_shift):
    average = jnp.mean(values, axis=-1, keepdims=True)
    centred = values - average
    variance = jnp.mean(centred * centred, axis=-1, keepdims=True)
    inv_dev = lax.rsqrt(variance + NORM_EPS)
    normed = centred * inv_dev
    return (normed * norm_gain + norm_shift, normed, inv_dev)


def norm_back(grad_normed, normed, inv_dev):
    first_part = jnp.mean(grad_normed, axis=-1, keepdims=True)
    second_part = jnp.mean(grad_normed * normed, axis=-1, keepdims=True)
    return inv_dev * (grad_normed - first_part - normed * second_part)


def gelu_slope(inner):
    return (
        0.5 * (1.0 + jax.scipy.special.erf(inner * ROOT_HALF))
        + inner * jnp.exp(-0.5 * inner * inner) * INV_ROOT_TWO_PI
    )


def row_contract(left_side, right_side):
    return lax.dot_general(
        left_side, right_side, (((0,), (0,)), ((), ())), preferred_element_type=jnp.float32
    )


def col_contract(left_side, right_side):
    return lax.dot_general(
        left_side, right_side, (((1,), (1,)), ((), ())), preferred_element_type=jnp.float32
    )


def halve_rounds(values, bit_list, first_axis, top_bit, dp_index, site_call):
    for bit_number in bit_list:
        axis_number = first_axis + top_bit - bit_number
        my_bit = dp_index >> bit_number & 1
        kept = lax.dynamic_index_in_dim(values, my_bit, axis_number, keepdims=True)
        outgoing = lax.dynamic_index_in_dim(values, 1 - my_bit, axis_number, keepdims=True)
        values = kept + site_call(outgoing, bit_number)
    return values


def local_general(
    tokens,
    cotangent,
    segment_ids,
    padding,
    shared_weights,
    first_moment,
    second_moment,
    outer_momentum,
):
    tensor_size = lax.axis_size("tensor")
    local_width = D // tensor_size
    hidden = FF // tensor_size
    local_heads = HEADS // tensor_size
    seq_rows = segment_ids.shape[0]
    seq_count = seq_rows // SEQ_LEN
    block_rows = min(512, SEQ_LEN)
    per_seq = SEQ_LEN // block_rows
    block_total = seq_count * per_seq
    score_scale = HD ** (-0.5)
    bf16 = jnp.bfloat16
    f32 = jnp.float32
    masters = lax.all_gather(shared_weights, "dp", axis=1, tiled=True)[0]
    points = boundaries(tensor_size)
    segments = [masters[points[number] : points[number + 1]] for number in range(8)]
    proj_weight = segments[0].reshape(3, D, local_width).astype(bf16)
    out_weight = segments[1].reshape(local_width, D).astype(bf16)
    in_weight = segments[2].reshape(D, hidden).astype(bf16)
    down_weight = segments[3].reshape(hidden, D).astype(bf16)
    query_bias = segments[4]
    value_bias = segments[5]
    inner_bias = segments[6]
    vectors = lax.all_gather(segments[7].reshape(6, local_width), "tensor", axis=1, tiled=True)
    inputs_all = lax.all_gather(tokens, "tensor", axis=0, tiled=True)
    projected = jnp.einsum("td,kde->kte", inputs_all, proj_weight, preferred_element_type=f32)
    query = (projected[0] + query_bias).astype(bf16)
    keys = projected[1].astype(bf16)
    values = (projected[2] + value_bias).astype(bf16)
    query_four = query.reshape(seq_count, SEQ_LEN, local_heads, HD)
    keys_four = keys.reshape(seq_count, SEQ_LEN, local_heads, HD)
    values_four = values.reshape(seq_count, SEQ_LEN, local_heads, HD)
    seg_two = segment_ids.reshape(seq_count, SEQ_LEN)
    live_two = padding.reshape(seq_count, SEQ_LEN)
    key_pos = jnp.arange(SEQ_LEN, dtype=jnp.int32)

    def block_scores(block_index):
        sequence = block_index // per_seq
        offset = block_index % per_seq * block_rows
        query_rows = lax.dynamic_index_in_dim(query_four, sequence, 0, keepdims=False)
        query_block = lax.dynamic_slice_in_dim(query_rows, offset, block_rows, 0)
        key_rows = lax.dynamic_index_in_dim(keys_four, sequence, 0, keepdims=False)
        seg_row = lax.dynamic_index_in_dim(seg_two, sequence, 0, keepdims=False)
        live_row = lax.dynamic_index_in_dim(live_two, sequence, 0, keepdims=False)
        seg_block = lax.dynamic_slice_in_dim(seg_row, offset, block_rows, 0)
        query_pos = offset + jnp.arange(block_rows, dtype=jnp.int32)
        allowed = (seg_block[:, None] == seg_row[None, :]) & (
            (live_row[None, :] == 1) | (query_pos[:, None] == key_pos[None, :])
        )
        raw_scores = (
            jnp.einsum("qhd,khd->hqk", query_block, key_rows, preferred_element_type=f32)
            * score_scale
        )
        return (
            jnp.where(allowed[None], raw_scores, MASKED),
            query_block,
            key_rows,
            sequence,
            offset,
        )

    def forward_block(block_index):
        scores, query_block, key_rows, sequence, offset = block_scores(block_index)
        value_rows = lax.dynamic_index_in_dim(values_four, sequence, 0, keepdims=False)
        highest = jnp.max(scores, axis=-1, keepdims=True)
        exponent = jnp.exp(scores - highest)
        summed = jnp.sum(exponent, axis=-1, keepdims=True)
        probabilities = (exponent / summed).astype(bf16)
        context = jnp.einsum("hqk,khd->qhd", probabilities, value_rows, preferred_element_type=f32)
        return (context, (highest + jnp.log(summed))[..., 0])

    context_blocks, log_totals = lax.map(forward_block, jnp.arange(block_total, dtype=jnp.int32))
    context_low = context_blocks.reshape(seq_rows, local_width).astype(bf16)
    attn_sum = lax.psum_scatter(
        jnp.dot(context_low, out_weight, preferred_element_type=f32).astype(jnp.bfloat16),
        "tensor",
        scatter_dimension=0,
        tiled=True,
    ).astype(jnp.float32)
    tokens_f = tokens.astype(f32)
    middle, normed_one, inv_one = layer_norm(
        tokens_f + (attn_sum + vectors[4]), vectors[0], vectors[1]
    )
    middle_all = lax.all_gather(middle.astype(bf16), "tensor", axis=0, tiled=True)
    inner = jnp.dot(middle_all, in_weight, preferred_element_type=f32) + inner_bias
    activated = jax.nn.gelu(inner, approximate=False).astype(bf16)
    ffn_sum = lax.psum_scatter(
        jnp.dot(activated, down_weight, preferred_element_type=f32).astype(jnp.bfloat16),
        "tensor",
        scatter_dimension=0,
        tiled=True,
    ).astype(jnp.float32)
    result, normed_two, inv_two = layer_norm(
        middle + (ffn_sum + vectors[5]), vectors[2], vectors[3]
    )
    block_out = result.astype(bf16)
    grad_out = cotangent.astype(f32)
    grad_gain_two = jnp.sum(grad_out * normed_two, axis=0)
    grad_shift_two = jnp.sum(grad_out, axis=0)
    grad_two = norm_back(grad_out * vectors[2], normed_two, inv_two)
    grad_down_bias = jnp.sum(grad_two, axis=0)
    back_all = lax.all_gather(grad_two.astype(bf16), "tensor", axis=0, tiled=True)
    grad_down_weight = row_contract(activated, back_all)
    grad_act = col_contract(back_all, down_weight)
    grad_inner = (grad_act * gelu_slope(inner)).astype(bf16)
    grad_inner_bias = jnp.sum(grad_inner.astype(f32), axis=0)
    grad_in_weight = row_contract(middle_all, grad_inner)
    grad_middle = grad_two + lax.psum_scatter(
        col_contract(grad_inner, in_weight).astype(jnp.bfloat16),
        "tensor",
        scatter_dimension=0,
        tiled=True,
    ).astype(jnp.float32)
    grad_gain_one = jnp.sum(grad_middle * normed_one, axis=0)
    grad_shift_one = jnp.sum(grad_middle, axis=0)
    grad_one = norm_back(grad_middle * vectors[0], normed_one, inv_one)
    grad_out_bias = jnp.sum(grad_one, axis=0)
    attn_back_all = lax.all_gather(grad_one.astype(bf16), "tensor", axis=0, tiled=True)
    grad_out_weight = row_contract(context_low, attn_back_all)
    grad_context = col_contract(attn_back_all, out_weight).astype(bf16)
    grad_context_four = grad_context.reshape(seq_count, SEQ_LEN, local_heads, HD)

    def backward_block(carry, block_index):
        grad_keys, grad_values = carry
        scores, query_block, key_rows, sequence, offset = block_scores(block_index)
        value_rows = lax.dynamic_index_in_dim(values_four, sequence, 0, keepdims=False)
        log_total = lax.dynamic_index_in_dim(log_totals, block_index, 0, keepdims=False)
        probabilities = jnp.exp(scores - log_total[..., None])
        prob_low = probabilities.astype(bf16)
        grad_rows = lax.dynamic_index_in_dim(grad_context_four, sequence, 0, keepdims=False)
        grad_block = lax.dynamic_slice_in_dim(grad_rows, offset, block_rows, 0)
        grad_probs = jnp.einsum("qhd,khd->hqk", grad_block, value_rows, preferred_element_type=f32)
        grad_scores = probabilities * (
            grad_probs - jnp.sum(grad_probs * probabilities, axis=-1, keepdims=True)
        )
        scores_low = grad_scores.astype(bf16)
        grad_query = (
            jnp.einsum("hqk,khd->qhd", scores_low, key_rows, preferred_element_type=f32)
            * score_scale
        )
        key_term = (
            jnp.einsum("hqk,qhd->khd", scores_low, query_block, preferred_element_type=f32)
            * score_scale
        )
        value_term = jnp.einsum("hqk,qhd->khd", prob_low, grad_block, preferred_element_type=f32)
        grad_keys = lax.dynamic_update_index_in_dim(
            grad_keys,
            lax.dynamic_index_in_dim(grad_keys, sequence, 0, keepdims=False) + key_term,
            sequence,
            0,
        )
        grad_values = lax.dynamic_update_index_in_dim(
            grad_values,
            lax.dynamic_index_in_dim(grad_values, sequence, 0, keepdims=False) + value_term,
            sequence,
            0,
        )
        return ((grad_keys, grad_values), grad_query)

    empty = jnp.zeros((seq_count, SEQ_LEN, local_heads, HD), f32)
    (grad_keys, grad_values), grad_queries = lax.scan(
        backward_block, (empty, empty), jnp.arange(block_total, dtype=jnp.int32)
    )
    grad_proj = jnp.stack(
        [
            grad_queries.reshape(seq_rows, local_width),
            grad_keys.reshape(seq_rows, local_width),
            grad_values.reshape(seq_rows, local_width),
        ]
    ).astype(bf16)
    grad_proj_weight = jnp.einsum("td,kte->kde", inputs_all, grad_proj, preferred_element_type=f32)
    grad_query_bias = jnp.sum(grad_proj[0].astype(f32), axis=0)
    grad_value_bias = jnp.sum(grad_proj[2].astype(f32), axis=0)
    input_part = jnp.einsum("kte,kde->td", grad_proj, proj_weight, preferred_element_type=f32)
    vector_part = jnp.stack(
        [
            grad_gain_one,
            grad_shift_one,
            grad_gain_two,
            grad_shift_two,
            grad_out_bias,
            grad_down_bias,
        ]
    )
    input_share, vector_grad = (
        lax.psum_scatter(
            input_part.astype(jnp.bfloat16), "tensor", scatter_dimension=0, tiled=True
        ).astype(jnp.float32),
        lax.psum_scatter(
            vector_part.astype(jnp.bfloat16), "tensor", scatter_dimension=1, tiled=True
        ).astype(jnp.float32),
    )
    input_grad = (grad_one + input_share).astype(bf16)
    flat_grad = jnp.concatenate(
        [
            grad_proj_weight.reshape(-1),
            grad_out_weight.reshape(-1),
            grad_in_weight.reshape(-1),
            grad_down_weight.reshape(-1),
            grad_query_bias,
            grad_value_bias,
            grad_inner_bias,
            vector_grad.reshape(-1),
        ]
    )
    dp_size = lax.axis_size("dp")
    per_group = dp_size // GROUPS
    inner_bits = per_group.bit_length() - 1
    all_bits = dp_size.bit_length() - 1
    dp_index = lax.axis_index("dp")
    slot_index = dp_index % per_group
    piece_len = shared_weights.shape[1]
    grid_view = flat_grad.reshape(GROUPS, per_group, piece_len)
    inner_list = list(range(inner_bits))
    outer_list = list(range(inner_bits, all_bits))
    inner_list = inner_list[::-1]
    outer_list = outer_list[::-1]
    summed_grid = grid_view
    for bit_number in inner_list:
        summed_grid = summed_grid + from_partner(
            summed_grid.astype(jnp.bfloat16), "dp", bit_number
        ).astype(summed_grid.dtype)
    grad_block = lax.dynamic_index_in_dim(summed_grid, slot_index, 1, keepdims=False)
    weights_block = lax.dynamic_index_in_dim(
        masters.reshape(GROUPS, per_group, piece_len), slot_index, 1, keepdims=False
    )
    matrix_count = (4 * D * D + 2 * D * FF) // tensor_size
    flat_index = (
        jnp.arange(GROUPS, dtype=jnp.int32)[:, None] * per_group + slot_index
    ) * piece_len + jnp.arange(piece_len, dtype=jnp.int32)[None, :]
    decay_mask = (flat_index < matrix_count).astype(f32)
    first_new = BETA_ONE * first_moment[0, 0] + (1 - BETA_ONE) * grad_block
    second_new = BETA_TWO * second_moment[0, 0] + (1 - BETA_TWO) * grad_block * grad_block
    first_hat = first_new / (1 - BETA_ONE**STEP)
    second_hat = second_new / (1 - BETA_TWO**STEP)
    group_weights = weights_block - INNER_RATE * (
        first_hat / (jnp.sqrt(second_hat) + ADAM_EPS) + DECAY * decay_mask * weights_block
    )
    difference = weights_block - group_weights

    def outer_swap(outgoing, bit_number):
        return from_partner(outgoing.astype(jnp.bfloat16), "dp", bit_number).astype(outgoing.dtype)

    outer_bits = all_bits - inner_bits
    diff_view = difference.reshape((2,) * outer_bits + (piece_len,))
    diff_sum = halve_rounds(diff_view, outer_list, 0, all_bits - 1, dp_index, outer_swap).reshape(
        piece_len
    )
    mean_diff = diff_sum / GROUPS
    new_momentum = OUTER_MU * outer_momentum[0] + mean_diff
    new_weights = shared_weights[0] - OUTER_RATE * (mean_diff + OUTER_MU * new_momentum)
    return (
        block_out,
        input_grad,
        grad_block[None, None],
        first_new[None, None],
        second_new[None, None],
        group_weights[None, None],
        mean_diff[None],
        new_momentum[None],
        new_weights[None],
    )


LANES = 128
NT = (((1,), (1,)), ((), ()))
NN = (((1,), (0,)), ((), ()))
TN = (((0,), (0,)), ((), ()))
VMEM_BYTES = 58 << 20
f32 = jnp.float32
bf16 = jnp.bfloat16


def dot(left, right, dims):
    return lax.dot_general(left, right, dims, preferred_element_type=f32)


def params(**more):
    return pltpu.CompilerParams(vmem_limit_bytes=VMEM_BYTES, **more)


def round_up(number, step):
    return -(-number // step) * step


def matrix_table(tensor_size):
    local_width = D // tensor_size
    hidden = FF // tensor_size
    table = []
    offset = 0
    for rows, columns in ((3 * D, local_width), (local_width, D), (D, hidden), (hidden, D)):
        blocks = columns // LANES
        table.append((offset, rows, blocks))
        offset += rows * blocks
    return table, offset


def chunk_plan(table, first, end, tail_at, tail_rows):
    segments = []
    base = None
    for number, (offset, rows, blocks) in enumerate(table):
        low = max(first, offset)
        high = min(end, offset + rows * blocks)
        if low >= high:
            continue
        row_low = (low - offset) // blocks // 16 * 16
        row_high = min(rows, round_up(-(-(high - offset) // blocks), 16))
        if base is None:
            base = offset + row_low * blocks
        segments.append((number, row_low, row_high, blocks, offset + row_low * blocks - base))
    size = max(at + (high - low) * blocks for _, low, high, blocks, at in segments)
    if end > tail_at:
        size = max(size, tail_at + tail_rows - base)
    return segments, base, size


def row_parts(rows, count):
    size = rows // count // 16 * 16
    starts = [size * i for i in range(count)] + [rows]
    return [(low, high - low) for low, high in zip(starts[:-1], starts[1:])]


def in_steps(start, rows, step, body):
    @pl.loop(0, rows // step)
    def _(i):
        body(pl.multiple_of(start + i * step, 16), step)

    if rows % step:
        body(start + rows // step * step, rows % step)


def update_kernel(
    slot_ref, g_hbm, w_hbm, m_hbm, v_hbm, d_hbm, own_hbm, mom_hbm,
    go, mo, vo, wo, mean_out, mom_out, new_out,
    g_s, w_s, m_s, v_s, m_new, v_new, w_new, sems,
    *, piece_rows, tail_rows, parts
):
    slot = slot_ref[0]
    units = [(b, part) for b in range(GROUPS) for part in parts] + [(None, part) for part in parts]

    def loads(u):
        b, (at, rows) = units[u]
        k = u % 3
        r = pl.ds(at, rows)
        wide = pl.ds(at, round_up(rows, 16))
        there, padded = pl.ds(0, rows), pl.ds(0, round_up(rows, 16))
        if b is None:
            pairs = (
                (d_hbm.at[wide], g_s.at[k, padded]),
                (own_hbm.at[r, 0, :], m_s.at[k, there]),
                (mom_hbm.at[r, 0, :], v_s.at[k, there]),
            )
        else:
            pairs = (
                (g_hbm.at[b, wide], g_s.at[k, padded]),
                (m_hbm.at[r, b, :], m_s.at[k, there]),
                (v_hbm.at[r, b, :], v_s.at[k, there]),
                (w_hbm.at[b, wide], w_s.at[k, padded]),
            )
        return [pltpu.make_async_copy(src, dst, sems.at[n, k]) for n, (src, dst) in enumerate(pairs)]

    def stores(u):
        b, (at, rows) = units[u]
        k = u % 3
        r = pl.ds(at, rows)
        there = pl.ds(0, rows)
        if b is None:
            pairs = (
                (m_new.at[k, there], mean_out.at[r, 0, :]),
                (v_new.at[k, there], mom_out.at[r, 0, :]),
                (w_new.at[k, there], new_out.at[r, 0, :]),
            )
        else:
            pairs = (
                (m_new.at[k, there], mo.at[r, b, :]),
                (v_new.at[k, there], vo.at[r, b, :]),
                (w_new.at[k, there], wo.at[r, b, :]),
                (g_s.at[k, there], go.at[r, b, :]),
            )
        return [pltpu.make_async_copy(src, dst, sems.at[4 + n, k]) for n, (src, dst) in enumerate(pairs)]

    for copy in loads(0):
        copy.start()
    for u, (b, (at, rows)) in enumerate(units):
        k = u % 3
        if u > 1:
            for copy in stores(u - 2):
                copy.wait()
        if u + 1 < len(units):
            for copy in loads(u + 1):
                copy.start()
        for copy in loads(u):
            copy.wait()

        def inner(start, count, b=b, at=at, k=k):
            r = pl.ds(start, count)
            g = g_s[k, r, :]
            if b is None:
                average = g / GROUPS
                momentum = OUTER_MU * v_s[k, r, :] + average
                m_new[k, r, :] = average
                v_new[k, r, :] = momentum
                w_new[k, r, :] = m_s[k, r, :] - OUTER_RATE * (average + OUTER_MU * momentum)
                return
            w = w_s[k, r, :].astype(f32)
            first = BETA_ONE * m_s[k, r, :] + (1 - BETA_ONE) * g
            second = BETA_TWO * v_s[k, r, :] + (1 - BETA_TWO) * g * g
            root = jnp.sqrt(second * (1 / (1 - BETA_TWO**STEP))) + ADAM_EPS
            decay = INNER_RATE * DECAY
            if b == GROUPS - 1:
                here = lax.broadcasted_iota(jnp.int32, (count, LANES), 0) + (at + start)
                decay = jnp.where((slot < 3) | (here < piece_rows - tail_rows), decay, 0.0)
            m_new[k, r, :] = first
            v_new[k, r, :] = second
            w_new[k, r, :] = w - ((INNER_RATE / (1 - BETA_ONE**STEP)) * first / root + decay * w)

        in_steps(0, round_up(rows, 16), 128, inner)
        for copy in stores(u):
            copy.start()
    for u in (len(units) - 2, len(units) - 1):
        for copy in stores(u):
            copy.wait()


def update(slot, grads, pieces, first, second, d_sum, own_rows, momentum_rows, tail_rows):
    piece_rows = first.shape[0]
    hbm = pl.BlockSpec(memory_space=pl.ANY)
    parts = row_parts(piece_rows, 3)
    most = round_up(max(rows for _, rows in parts), 16)
    wide = pltpu.VMEM((3, most, LANES), f32)
    state = jax.ShapeDtypeStruct(first.shape, f32)
    piece = jax.ShapeDtypeStruct(own_rows.shape, f32)
    return pl.pallas_call(
        functools.partial(update_kernel, piece_rows=piece_rows, tail_rows=tail_rows, parts=parts),
        in_specs=[pl.BlockSpec(memory_space=pltpu.SMEM)] + [hbm] * 7,
        out_specs=[hbm] * 7,
        out_shape=[state] * 4 + [piece] * 3,
        scratch_shapes=[wide, pltpu.VMEM((3, most, LANES), bf16)]
        + [wide] * 5
        + [pltpu.SemaphoreType.DMA((8, 3))],
        cost_estimate=pl.CostEstimate(
            flops=120 * piece_rows * LANES,
            bytes_accessed=120 * piece_rows * LANES,
            transcendentals=8 * piece_rows * LANES,
        ),
        compiler_params=params(),
        name="update",
    )(slot, grads, pieces, first, second, d_sum, own_rows, momentum_rows)


def attend_block(q, k, v_ones, code, seg_col, offset):
    rows_q, n = q.shape[0], k.shape[0]
    low = lax.broadcasted_iota(jnp.int32, (1, LANES), 1) < HD
    zero = jnp.zeros((), bf16)
    q = q * jnp.asarray(HD**-0.5, bf16)
    rows = lax.broadcasted_iota(jnp.int32, (rows_q, n), 0) + offset
    cols = lax.broadcasted_iota(jnp.int32, (rows_q, n), 1)
    allowed = (seg_col == code) | (rows == cols)
    outs = []
    tops = []
    for h in range(2):
        qh = jnp.where(low, q, zero) if h == 0 else jnp.where(low, zero, q)
        s = jnp.where(allowed, dot(qh, k, NT), MASKED)
        top = jnp.max(s, axis=1, keepdims=True)
        p = jnp.exp(s - top).astype(bf16)
        outs.append(dot(p, v_ones[h], NN))
        tops.append(top)
    num = jnp.where(low, outs[0], outs[1])
    den = pltpu.roll(jnp.where(low, outs[1], outs[0]), HD, 1)
    lse = (jnp.where(low, tops[0], tops[1]) + jnp.log(den)).T
    return (num / den).astype(bf16), lse[0:1], lse[HD : HD + 1]


def bring_rows(buf, flat, margin, offset, count, piece_rows):
    for p in range(offset // piece_rows, -(-(offset + count) // piece_rows)):
        low = max(offset - p * piece_rows, 0) // 16 * 16
        high = min(round_up(min(offset + count - p * piece_rows, piece_rows), 16), buf.shape[1])
        to = margin + p * piece_rows + low - offset
        step = 128
        full = (high - low) // step

        @pl.loop(0, full)
        def _(i, p=p, low=low, to=to):
            rows = buf[p, pl.ds(pl.multiple_of(low + i * step, 16), step), :]
            flat[pl.ds(to + i * step, step), :] = rows.astype(f32)

        rest = (high - low) % step
        if rest:
            flat[pl.ds(to + full * step, rest), :] = buf[p, low + full * step : high, :].astype(f32)


def emit_matrix(flat, out, margin, rows, blocks):
    chunk = 64

    @pl.loop(0, rows // chunk)
    def _(c):
        at = pl.ds(pl.multiple_of(c * chunk, chunk), chunk)
        for j in range(blocks):
            from_rows = pl.ds(margin + c * (chunk * blocks) + j, chunk, stride=blocks)
            out[at, j * LANES : (j + 1) * LANES] = flat[from_rows, :].astype(bf16)


def start_kernel(
    own_hbm, tokens_hbm, code_ref, seg_ref,
    proj_out, outw_out, inw_out, down_out, pieces_out, tail_out, x_out, q_ref, k_ref, v_ref, ctx_ref, lse_ref,
    rows32, buf, xbuf, flat, proj_s, outw_s, inw_s, down_s,
    zdown, zup, zrecv, ysend, yrecv, csend, crecv, xsem, local_sems,
    *, piece_rows, tail_rows, table, cuts, rows_q
):
    z = lax.axis_index("group")
    slot = lax.axis_index("slot")
    me = lax.axis_index("tensor")
    depth = GROUPS
    padded = buf.shape[1]
    half = tokens_hbm.shape[0]
    n = 2 * half
    mesh_id = pl.DeviceIdType.MESH

    load = pltpu.make_async_copy(own_hbm.at[:, 0, :], rows32, local_sems.at[0])
    load.start()
    x_load = pltpu.make_async_copy(tokens_hbm, xbuf.at[pl.ds(0, half)], local_sems.at[1])
    x_load.start()

    barrier = pltpu.get_barrier_semaphore()
    for where in ({"slot": slot ^ 1}, {"slot": slot ^ 2}, {"tensor": 1 - me}):
        pl.semaphore_signal(barrier, inc=1, device_id=where, device_id_type=mesh_id)

    @pl.when(z > 0)
    def _():
        pl.semaphore_signal(barrier, inc=1, device_id={"group": z - 1}, device_id_type=mesh_id)

    @pl.when(z < depth - 1)
    def _():
        pl.semaphore_signal(barrier, inc=1, device_id={"group": z + 1}, device_id_type=mesh_id)

    pl.semaphore_wait(barrier, 3 + jnp.where(z > 0, 1, 0) + jnp.where(z < depth - 1, 1, 0))

    load.wait()
    own = z * 4 + slot
    step = 128
    full = piece_rows // step

    @pl.loop(0, full)
    def _(i):
        r = pl.ds(pl.multiple_of(i * step, step), step)
        buf[own, r, :] = rows32[r, :].astype(bf16)

    tail = rows32[piece_rows - tail_rows :, :]
    left = tail - tail.astype(bf16).astype(f32)
    zeros = jnp.zeros((padded - piece_rows - tail_rows, LANES), f32)
    buf[own, full * step :, :] = jnp.concatenate([rows32[full * step :, :], left, zeros], axis=0).astype(bf16)

    def copy_of(piece, h, send, recv, where):
        part = buf.at[piece, pl.ds(*cuts[h])]
        return pltpu.make_async_remote_copy(
            src_ref=part, dst_ref=part, send_sem=send, recv_sem=recv, device_id=where, device_id_type=mesh_id
        )

    def down(b, h):
        return copy_of(b * 4 + slot, h, zdown.at[b, h], zrecv.at[b, h], {"group": z + 1})

    def up(b, h):
        return copy_of(b * 4 + slot, h, zup.at[b, h], zrecv.at[b, h], {"group": z - 1})

    def side(b, h):
        return copy_of(b * 4 + slot, h, ysend.at[b, h], yrecv.at[b, h], {"slot": slot ^ 2})

    def side_in(b, h):
        return copy_of(b * 4 + (slot ^ 2), h, ysend.at[b, h], yrecv.at[b, h], {"slot": slot ^ 2})

    def twin(b, h, k):
        return copy_of(
            b * 4 + (slot ^ (2 * k)), h, csend.at[2 * b + k, h], crecv.at[2 * b + k, h], {"slot": slot ^ 1}
        )

    def twin_in(b, h, k):
        return copy_of(
            b * 4 + (slot ^ 1 ^ (2 * k)), h, csend.at[2 * b + k, h], crecv.at[2 * b + k, h], {"slot": slot ^ 1}
        )

    parts = range(len(cuts))
    tail_part = len(cuts) - 1
    order = [tail_part] + list(range(tail_part))
    last = depth - 1
    ranked = (
        z,
        jnp.where(z == 0, 1, 0),
        jnp.where(z == 2, 3, 2),
        jnp.where(z < 2, 3, 1),
    )
    middle = (z == 1) | (z == 2)
    edge = jnp.logical_not(middle)

    def pass_on(b, h, aside=True):
        up(b, h).wait_recv()

        @pl.when((b < z) & (z < last))
        def _():
            down(b, h).start()

        @pl.when((b > z) & (z > 0))
        def _():
            up(b, h).start()

        if aside:
            side(b, h).start()
        twin(b, h, 0).start()

    def serve_z(b, h, when=None, aside=True):
        if h == tail_part:
            when = (b != last) if when is None else when & (b != last)
        if when is None:
            pass_on(b, h, aside)
        else:
            pl.when(when)(functools.partial(pass_on, b, h, aside))

    def serve_y(rank, h):
        b = ranked[rank]

        def go():
            side_in(b, h).wait_recv()
            twin(b, h, 1).start()

        if h == tail_part:
            pl.when(b != last)(go)
        else:
            go()

    for number, h in enumerate(order):
        pl.when(z > 0)(lambda h=h: up(z, h).start())
        at_once = (z == 0) | ((z == 1) & (number < 2)) | ((z == 2) & (number < 3))
        pl.when(at_once)(lambda h=h: down(z, h).start())
        side(z, h).start()
        twin(z, h, 0).start()

    x_load.wait()
    x_copy = pltpu.make_async_remote_copy(
        src_ref=xbuf.at[pl.ds(0, half)],
        dst_ref=xbuf.at[pl.ds(half, half)],
        send_sem=xsem.at[0],
        recv_sem=xsem.at[1],
        device_id={"tensor": 1 - me},
        device_id_type=mesh_id,
    )
    x_copy.start()

    pl.when(z != last)(functools.partial(pass_on, last, tail_part))
    for h in order:
        serve_z(ranked[2], h, middle, False)
        serve_z(ranked[1], h)
    for number, h in enumerate(order):
        later = ((z == 1) & (number >= 2)) | ((z == 2) & (number >= 3))
        pl.when(later)(lambda h=h: down(z, h).start())
        aside = middle & (ranked[2] != last) if h == tail_part else middle
        pl.when(aside)(lambda h=h: side(ranked[2], h).start())
    for h in order:
        serve_z(ranked[2], h, edge)
    side_in(last, tail_part).wait_recv()
    twin(last, tail_part, 1).start()
    for rank in range(2):
        for h in order:
            serve_y(rank, h)
    for k in range(2):
        twin_in(last, tail_part, k).wait_recv()
        for rank in range(2):
            b = ranked[rank]
            for h in parts:
                if h == tail_part:
                    pl.when(b != last)(lambda b=b, h=h, k=k: twin_in(b, h, k).wait_recv())
                else:
                    twin_in(b, h, k).wait_recv()

    for h in order:
        serve_z(ranked[3], h, middle)

    at = (piece_rows - tail_rows) // 16 * 16
    shift = piece_rows - tail_rows - at
    ends = buf[4 * depth - 1, at:, :].astype(f32)
    vectors = ends[shift : shift + tail_rows] + ends[shift + tail_rows : shift + 2 * tail_rows]
    tail_out[...] = vectors

    margin = 16
    (offset, rows, blocks) = table[0]
    bring_rows(buf, flat, margin, offset, rows * blocks, piece_rows)
    emit_matrix(flat, proj_s, margin, rows, blocks)
    out_copies = [pltpu.make_async_copy(proj_s, proj_out, local_sems.at[2])]
    out_copies[0].start()
    x_copy.wait()
    out_copies.append(pltpu.make_async_copy(xbuf, x_out, local_sems.at[3]))
    out_copies[1].start()
    query_bias = jnp.concatenate([vectors[j : j + 1] for j in range(blocks)], axis=1)
    value_bias = jnp.concatenate([vectors[blocks + j : blocks + j + 1] for j in range(blocks)], axis=1)
    depth_in = rows // 3
    for m, (ref, bias) in enumerate(((q_ref, query_bias), (k_ref, None), (v_ref, value_bias))):

        @pl.loop(0, n // 256)
        def _(i, m=m, ref=ref, bias=bias):
            r = pl.ds(pl.multiple_of(i * 256, 256), 256)
            acc = dot(xbuf[r, :], proj_s[m * depth_in : (m + 1) * depth_in, :], NN)
            if bias is not None:
                acc = acc + bias
            ref[r, :] = acc.astype(bf16)

    todo = [functools.partial(serve_z, ranked[3], h, edge) for h in order]
    late = [functools.partial(serve_y, 2, h) for h in order]
    todo = todo + late
    low = lax.broadcasted_iota(jnp.int32, (1, LANES), 1) < HD
    one = jnp.ones((), bf16)
    code = code_ref[...]
    for pair in range(blocks):
        c = slice(pair * LANES, (pair + 1) * LANES)
        k = k_ref[:, c]
        v = v_ref[:, c]
        v_ones = (jnp.where(low, v, one), jnp.where(low, one, v))
        for i in range(n // rows_q):
            r = slice(i * rows_q, (i + 1) * rows_q)
            ctx, lse_0, lse_1 = attend_block(q_ref[r, c], k, v_ones, code, seg_ref[r, :], i * rows_q)
            ctx_ref[r, c] = ctx
            lse_ref[pair, 0:1, r] = lse_0
            lse_ref[pair, 1:2, r] = lse_1
            for _ in range(1):
                if todo:
                    todo.pop(0)()
    for act in todo:
        act()

    def landed(rank):
        b = ranked[rank]
        for h in parts:
            for k in range(2):
                if h == tail_part:
                    pl.when(b != last)(lambda b=b, h=h, k=k: twin_in(b, h, k).wait_recv())
                else:
                    twin_in(b, h, k).wait_recv()

    scratches = (None, outw_s, inw_s, down_s)
    mat_copies = [
        None,
        pltpu.make_async_copy(outw_s, outw_out, local_sems.at[4]),
        pltpu.make_async_copy(inw_s, inw_out, local_sems.at[5]),
        pltpu.make_async_copy(down_s, down_out, local_sems.at[6]),
    ]

    def matrix(m):
        (offset, rows, blocks) = table[m]
        bring_rows(buf, flat, margin, offset, rows * blocks, piece_rows)
        emit_matrix(flat, scratches[m], margin, rows, blocks)
        mat_copies[m].start()

    def front():
        matrix(1)
        matrix(2)

    landed(2)
    pl.when(z < 2)(front)
    pl.when(z >= 2)(lambda: matrix(3))
    for h in order:
        serve_y(3, h)
    landed(3)
    pl.when(z < 2)(lambda: matrix(3))
    pl.when(z >= 2)(front)
    for b in range(depth):
        copy = pltpu.make_async_copy(buf.at[b * 4 + slot], pieces_out.at[b], local_sems.at[7 + b])
        copy.start()
        out_copies.append(copy)
    out_copies += mat_copies[1:]

    for b in range(depth):
        for h in parts:

            @pl.when((b <= z) & (z < depth - 1))
            def _(b=b, h=h):
                down(b, h).wait_send()

            @pl.when((b >= z) & (z > 0))
            def _(b=b, h=h):
                up(b, h).wait_send()

            side(b, h).wait_send()
            for k in range(2):
                twin(b, h, k).wait_send()
    for copy in out_copies:
        copy.wait()


def start(own_rows, tokens, code_row, seg_col, table, tail_rows, padded, cuts, rows_q=256):
    piece_rows = own_rows.shape[0]
    half, width = tokens.shape
    n = 2 * half
    pairs = table[0][2]
    local_width = pairs * LANES
    hbm = pl.BlockSpec(memory_space=pl.ANY)
    whole = pl.BlockSpec(memory_space=pltpu.VMEM)
    mats = [jax.ShapeDtypeStruct((rows, blocks * LANES), bf16) for _, rows, blocks in table]
    acts = [jax.ShapeDtypeStruct((n, local_width), bf16)] * 4
    most = max(rows * blocks for _, rows, blocks in table)
    parts = len(cuts)
    dma = pltpu.SemaphoreType.DMA
    return pl.pallas_call(
        functools.partial(
            start_kernel, piece_rows=piece_rows, tail_rows=tail_rows, table=table, cuts=cuts, rows_q=rows_q
        ),
        in_specs=[hbm, hbm, whole, whole],
        out_specs=[hbm] * 5 + [whole] + [hbm] + [whole] * 5,
        out_shape=mats
        + [
            jax.ShapeDtypeStruct((GROUPS, padded, LANES), bf16),
            jax.ShapeDtypeStruct((tail_rows, LANES), f32),
            jax.ShapeDtypeStruct((n, width), bf16),
        ]
        + acts
        + [jax.ShapeDtypeStruct((pairs, 2, n), f32)],
        scratch_shapes=[
            pltpu.VMEM((piece_rows, LANES), f32),
            pltpu.VMEM((4 * GROUPS, padded, LANES), bf16),
            pltpu.VMEM((n, width), bf16),
            pltpu.VMEM((most + 48, LANES), f32),
        ]
        + [pltpu.VMEM(m.shape, bf16) for m in mats]
        + [
            dma((GROUPS, parts)),
            dma((GROUPS, parts)),
            dma((GROUPS, parts)),
            dma((GROUPS, parts)),
            dma((GROUPS, parts)),
            dma((2 * GROUPS, parts)),
            dma((2 * GROUPS, parts)),
            dma((2,)),
            dma((11,)),
        ],
        cost_estimate=pl.CostEstimate(
            flops=6 * n * width * local_width, bytes_accessed=60 << 20, transcendentals=8 * n * n
        ),
        compiler_params=params(collective_id=1, has_side_effects=True),
        name="start",
    )(own_rows, tokens, code_row, seg_col)


ERF = (0.254829592, -0.284496736, 1.421413741, -1.453152027, 1.061405429)
ERF_P = 0.3275911


def gelu_pair(u):
    bell = jnp.exp(-0.5 * u * u)
    t = 1.0 / (1.0 + (ERF_P * ROOT_HALF) * jnp.abs(u))
    poly = ERF[4]
    for number in ERF[3::-1]:
        poly = poly * t + number
    tail = (0.5 * poly * t) * bell
    phi = jnp.where(u >= 0, 1.0 - tail, tail)
    return u * phi, phi + u * bell * INV_ROOT_TWO_PI


def fold(values):
    return values.reshape(values.shape[0] // 8, 8, values.shape[1]).sum(axis=0)


def middle_kernel(
    ctx_ref, tokens_ref, cot_ref, vec_ref, c1_ref, outw_ref, inw_ref, down_ref,
    block_out, dh1_out, dctx_out, d_outw, d_inw, d_down, tail_out,
    x1, norm1, inv1, x1_all, act, slope, dh2_all, dh1_all, part, dh2, box_send, box_recv, sums, c1_sum, vec_box, send_sems, recv_sems, vec_sems,
    *, chunk
):
    me = lax.axis_index("tensor")
    half, width = tokens_ref.shape
    count = half // chunk
    mesh_id = pl.DeviceIdType.MESH
    other = {"tensor": 1 - me}
    barrier = pltpu.get_barrier_semaphore()
    pl.semaphore_signal(barrier, inc=1, device_id=other, device_id_type=mesh_id)
    pl.semaphore_wait(barrier, 1)

    def rows_of(i):
        return pl.ds(pl.multiple_of(i * chunk, chunk), chunk)

    def far_rows(i):
        return pl.ds(pl.multiple_of(half + i * chunk, chunk), chunk)

    def summed(stage, i):
        return pltpu.make_async_remote_copy(
            src_ref=box_send.at[stage, rows_of(i)],
            dst_ref=box_recv.at[stage, rows_of(i)],
            send_sem=send_sems.at[stage, i],
            recv_sem=recv_sems.at[stage, i],
            device_id=other,
            device_id_type=mesh_id,
        )

    def gathered(stage, ref, i):
        return pltpu.make_async_remote_copy(
            src_ref=ref.at[rows_of(i)],
            dst_ref=ref.at[far_rows(i)],
            send_sem=send_sems.at[3 + stage, i],
            recv_sem=recv_sems.at[3 + stage, i],
            device_id=other,
            device_id_type=mesh_id,
        )

    gain_1, shift_1 = vec_ref[0:1, :], vec_ref[1:2, :]
    gain_2, shift_2 = vec_ref[2:3, :], vec_ref[3:4, :]
    bias_o, bias_2 = vec_ref[4:5, :], vec_ref[5:6, :]
    sums[...] = jnp.zeros_like(sums)
    c1_sum[...] = jnp.zeros_like(c1_sum)

    def normed(h):
        centred = h - jnp.mean(h, axis=-1, keepdims=True)
        inv = lax.rsqrt(jnp.mean(centred * centred, axis=-1, keepdims=True) + NORM_EPS)
        return centred * inv, inv

    def normed_back(dn, n, inv):
        return inv * (
            dn - jnp.mean(dn, axis=-1, keepdims=True) - n * jnp.mean(dn * n, axis=-1, keepdims=True)
        )

    def forward(r):
        u = dot(x1_all[r, :], inw_ref[...], NN) + c1_ref[...]
        a, s = gelu_pair(u)
        act[r, :] = a.astype(bf16)
        slope[r, :] = s.astype(bf16)
        return dot(act[r, :], down_ref[...], NN)

    def backward(r):
        da = dot(dh2_all[r, :], down_ref[...], NT)
        du = da * slope[r, :].astype(f32)
        low = du.astype(bf16)
        slope[r, :] = low
        c1_sum[...] += fold(low.astype(f32))
        return dot(low, inw_ref[...], NT)

    @pl.loop(0, count)
    def _(i):
        box_send[0, rows_of(i), :] = dot(ctx_ref[far_rows(i), :], outw_ref[...], NN).astype(bf16)
        summed(0, i).start()

    @pl.loop(0, count)
    def _(i):
        r = rows_of(i)
        mine = dot(ctx_ref[r, :], outw_ref[...], NN)
        summed(0, i).wait_recv()
        h = tokens_ref[r, :].astype(f32) + (mine + box_recv[0, r, :].astype(f32) + bias_o)
        n, inv = normed(h)
        norm1[r, :] = n
        inv1[r, :] = jnp.broadcast_to(inv, (chunk, LANES))
        middle = n * gain_1 + shift_1
        x1[r, :] = middle
        x1_all[r, :] = middle.astype(bf16)
        gathered(0, x1_all, i).start()
        part[r, :] = forward(r)

    @pl.loop(0, count)
    def _(i):
        gathered(0, x1_all, i).wait_recv()
        box_send[1, rows_of(i), :] = forward(far_rows(i)).astype(bf16)
        summed(1, i).start()

    @pl.loop(0, count)
    def _(i):
        r = rows_of(i)
        summed(1, i).wait_recv()
        h = x1[r, :] + (part[r, :] + box_recv[1, r, :].astype(f32) + bias_2)
        n, inv = normed(h)
        block_out[r, :] = (n * gain_2 + shift_2).astype(bf16)
        dy = cot_ref[r, :].astype(f32)
        dh = normed_back(dy * gain_2, n, inv)
        sums[2] += fold(dy * n)
        sums[3] += fold(dy)
        sums[5] += fold(dh)
        dh2[r, :] = dh
        dh2_all[r, :] = dh.astype(bf16)
        gathered(1, dh2_all, i).start()
        part[r, :] = backward(r)

    @pl.loop(0, count)
    def _(i):
        gathered(1, dh2_all, i).wait_recv()
        box_send[2, rows_of(i), :] = backward(far_rows(i)).astype(bf16)
        summed(2, i).start()

    hidden = act.shape[1]
    block = hidden // 8

    def down_grad(j):
        c = pl.ds(pl.multiple_of(j * block, block), block)
        d_down[c, :] = dot(act[:, c].T, dh2_all[...], NN).astype(bf16)

    def in_grad(j):
        c = pl.ds(pl.multiple_of(j * block, block), block)
        d_inw[:, c] = dot(x1_all[...].T, slope[:, c], NN).astype(bf16)

    per_chunk = 8 // count

    @pl.loop(0, count)
    def _(i):
        for j in range(per_chunk):
            down_grad(i * per_chunk + j)
        r = rows_of(i)
        summed(2, i).wait_recv()
        dx = dh2[r, :] + part[r, :] + box_recv[2, r, :].astype(f32)
        n = norm1[r, :]
        dh = normed_back(dx * gain_1, n, inv1[r, 0:1])
        sums[0] += fold(dx * n)
        sums[1] += fold(dx)
        sums[4] += fold(dh)
        dh1_out[r, :] = dh
        dh1_all[r, :] = dh.astype(bf16)
        gathered(2, dh1_all, i).start()
        dctx_out[r, :] = dot(dh1_all[r, :], outw_ref[...], NT).astype(bf16)

    for row in range(6):
        total = jnp.sum(sums[row], axis=0, keepdims=True)
        low, high = total[:, : width // 2], total[:, width // 2 :]
        mine, theirs = jnp.where(me == 0, low, high), jnp.where(me == 0, high, low)
        spread = width // 2 // LANES
        for j in range(spread):
            at = row * spread + j
            vec_box[0, at : at + 1, :] = mine[:, j * LANES : (j + 1) * LANES]
            vec_box[1, at : at + 1, :] = theirs[:, j * LANES : (j + 1) * LANES]
    vec_copy = pltpu.make_async_remote_copy(
        src_ref=vec_box.at[1],
        dst_ref=vec_box.at[2],
        send_sem=vec_sems.at[0],
        recv_sem=vec_sems.at[1],
        device_id=other,
        device_id_type=mesh_id,
    )
    vec_copy.start()

    @pl.loop(0, count)
    def _(i):
        for j in range(per_chunk):
            in_grad(i * per_chunk + j)
        r = far_rows(i)
        gathered(2, dh1_all, i).wait_recv()
        dctx_out[r, :] = dot(dh1_all[r, :], outw_ref[...], NT).astype(bf16)

    d_outw[...] = dot(ctx_ref[...].T, dh1_all[...], NN).astype(bf16)

    blocks = ctx_ref.shape[1] // LANES
    tail_out[0 : 2 * blocks, :] = jnp.zeros((2 * blocks, LANES), f32)
    c1_total = jnp.sum(c1_sum[...], axis=0, keepdims=True)
    for j in range(hidden // LANES):
        tail_out[2 * blocks + j : 2 * blocks + j + 1, :] = c1_total[:, j * LANES : (j + 1) * LANES]
    vec_copy.wait()
    tail_out[2 * blocks + hidden // LANES :, :] = vec_box[0] + vec_box[2]

    @pl.loop(0, count)
    def _(i):
        for stage in range(3):
            summed(stage, i).wait_send()
        gathered(0, x1_all, i).wait_send()
        gathered(1, dh2_all, i).wait_send()
        gathered(2, dh1_all, i).wait_send()


def middle(context, tokens, cotangent, vectors, inner_bias, out_w, in_w, down_w, chunk=128):
    half, width = tokens.shape
    n = 2 * half
    hidden = in_w.shape[1]
    local_width = context.shape[1]
    whole = pl.BlockSpec(memory_space=pltpu.VMEM)
    wide = pltpu.VMEM((half, width), f32)
    every = pltpu.VMEM((n, width), bf16)
    box = pltpu.VMEM((3, half, width), bf16)
    count = half // chunk
    return pl.pallas_call(
        functools.partial(middle_kernel, chunk=chunk),
        in_specs=[whole] * 8,
        out_specs=[whole] * 7,
        out_shape=[
            jax.ShapeDtypeStruct((half, width), bf16),
            jax.ShapeDtypeStruct((half, width), f32),
            jax.ShapeDtypeStruct((n, local_width), bf16),
            jax.ShapeDtypeStruct(out_w.shape, bf16),
            jax.ShapeDtypeStruct(in_w.shape, bf16),
            jax.ShapeDtypeStruct(down_w.shape, bf16),
            jax.ShapeDtypeStruct(((2 * local_width + hidden + 3 * width) // LANES, LANES), f32),
        ],
        scratch_shapes=[
            wide,
            wide,
            pltpu.VMEM((half, LANES), f32),
            every,
            pltpu.VMEM((n, hidden), bf16),
            pltpu.VMEM((n, hidden), bf16),
            every,
            every,
            wide,
            wide,
            box,
            box,
            pltpu.VMEM((6, 8, width), f32),
            pltpu.VMEM((8, hidden), f32),
            pltpu.VMEM((3, 3 * width // LANES, LANES), f32),
            pltpu.SemaphoreType.DMA((6, count)),
            pltpu.SemaphoreType.DMA((6, count)),
            pltpu.SemaphoreType.DMA((2,)),
        ],
        cost_estimate=pl.CostEstimate(
            flops=14 * n * width * hidden, bytes_accessed=40 << 20, transcendentals=2 * n * hidden
        ),
        compiler_params=params(collective_id=2, has_side_effects=True),
        name="middle",
    )(context, tokens, cotangent, vectors, inner_bias, out_w, in_w, down_w)


def attend_back(q_ref, k_ref, v_ref, ctx_ref, dctx_ref, code, seg_ref, lse_ref, dq_ref, dk_ref, dv_ref, pair, rows_q, after_step):
    n = q_ref.shape[0]
    c = slice(pair * LANES, (pair + 1) * LANES)
    low = lax.broadcasted_iota(jnp.int32, (1, LANES), 1) < HD
    zero = jnp.zeros((), bf16)
    k = k_ref[:, c]
    v = v_ref[:, c]
    k_t = k.T
    pick = (
        lax.broadcasted_iota(jnp.int32, (8, LANES), 1) // HD
        == lax.broadcasted_iota(jnp.int32, (8, LANES), 0)
    ).astype(f32)
    dks = [jnp.zeros((n, LANES), f32)] * 2
    dvs = [jnp.zeros((n, LANES), f32)] * 2
    scale = jnp.asarray(HD**-0.5, bf16)
    for i in range(n // rows_q):
        r = slice(i * rows_q, (i + 1) * rows_q)
        q = q_ref[r, c] * scale
        do = dctx_ref[r, c]
        prod = do.astype(f32) * ctx_ref[r, c].astype(f32)
        delta = lax.dot_general(
            pick, prod, NT, precision=lax.Precision.HIGHEST, preferred_element_type=f32
        )
        keys = lax.broadcasted_iota(jnp.int32, (n, rows_q), 0)
        qs = lax.broadcasted_iota(jnp.int32, (n, rows_q), 1) + i * rows_q
        allowed = (code == seg_ref[:, r]) | (keys == qs)
        dqs = []
        for h in range(2):
            qh = jnp.where(low, q, zero) if h == 0 else jnp.where(low, zero, q)
            doh = jnp.where(low, do, zero) if h == 0 else jnp.where(low, zero, do)
            s = jnp.where(allowed, dot(k, qh, NT), MASKED)
            p = jnp.exp(s - lse_ref[pair, h : h + 1, r])
            dp = dot(v, doh, NT)
            ds = (p * (dp - delta[h : h + 1])).astype(bf16)
            dvs[h] = dvs[h] + dot(p.astype(bf16), do, NN)
            dks[h] = dks[h] + dot(ds, q, NN)
            dqs.append(dot(k_t[h * HD : (h + 1) * HD], ds, NN))
        dq_ref[r, c] = (jnp.concatenate(dqs, axis=0).T * (HD**-0.5)).astype(bf16)
        after_step(i)
    dk_ref[:, c] = jnp.where(low, dks[0], dks[1]).astype(bf16)
    dv_ref[:, c] = jnp.where(low, dvs[0], dvs[1]).astype(bf16)


def lay_flat(ref, low, high, blocks, flat, at):
    chunk = 16 if (high - low) % 64 else 64

    @pl.loop(0, (high - low) // chunk)
    def _(c):
        rows = pl.ds(pl.multiple_of(low + c * chunk, 16), chunk)
        for j in range(blocks):
            to_rows = pl.ds(at + c * (chunk * blocks) + j, chunk, stride=blocks)
            flat[to_rows, :] = ref[rows, j * LANES : (j + 1) * LANES].astype(f32)


def emit_pieces(flat, keep, send, slot, skip, piece_rows):
    padded = send.shape[1]
    step = 128
    full = piece_rows // step
    rest = piece_rows - full * step
    for j in (3, 1, 2, 0):
        out = send if j % 2 else keep
        start = skip + (slot ^ j) * piece_rows

        @pl.loop(0, full)
        def _(i, out=out, j=j, start=start):
            rows = flat[pl.ds(start + i * step, step), :]
            out[j // 2, pl.ds(pl.multiple_of(i * step, step), step), :] = rows.astype(bf16)

        parts = [jnp.zeros((padded - piece_rows, LANES), f32)]
        if rest:
            parts = [flat[pl.ds(start + full * step, rest), :]] + parts
        out[j // 2, full * step : padded, :] = jnp.concatenate(parts, axis=0).astype(bf16)


def back_kernel(
    q_ref, k_ref, v_ref, ctx_ref, dctx_ref, code_ref, seg_ref, lse_ref, x_ref, outw_ref, tail_ref,
    inw_hbm, down_hbm, m_hbm, v_hbm, w_hbm, proj_hbm,
    g_out, d_out, dx_out,
    dq_ref, dk_ref, dv_ref,
    flat, down_s, inw_s, keep, send, near, far, tails, zin, g_stage, m_in, v_in, w_in,
    near_send, near_recv, far_send, far_recv, tail_send, tail_recv, z_send, z_recv, load_sems, out_sems,
    x_sems, x_free,
    *, plans, piece_rows, cuts, rows_q
):
    me = lax.axis_index("tensor")
    z = lax.axis_index("group")
    slot = lax.axis_index("slot")
    last = GROUPS - 1
    mesh_id = pl.DeviceIdType.MESH
    core = {"slot": slot ^ 1}
    side = {"slot": slot ^ 2}
    tail_rows = tail_ref.shape[0]
    padded = send.shape[1]
    stage_loads = [
        pltpu.make_async_copy(down_hbm, down_s, load_sems.at[0]),
        pltpu.make_async_copy(inw_hbm, inw_s, load_sems.at[1]),
    ]
    for copy in stage_loads:
        copy.start()
    barrier = pltpu.get_barrier_semaphore()
    for where in (core, side, {"tensor": 1 - me}):
        pl.semaphore_signal(barrier, inc=1, device_id=where, device_id_type=mesh_id)

    @pl.when(z > 0)
    def _():
        pl.semaphore_signal(barrier, inc=1, device_id={"group": z - 1}, device_id_type=mesh_id)

    @pl.when(z < last)
    def _():
        pl.semaphore_signal(barrier, inc=1, device_id={"group": z + 1}, device_id_type=mesh_id)

    pl.semaphore_wait(barrier, 3 + jnp.where(z > 0, 1, 0) + jnp.where(z < last, 1, 0))

    def to_core(b, j):
        return pltpu.make_async_remote_copy(
            src_ref=send.at[j],
            dst_ref=near.at[b, j],
            send_sem=near_send.at[b, j],
            recv_sem=near_recv.at[b, j],
            device_id=core,
            device_id_type=mesh_id,
        )

    def to_side(b, h):
        rows = pl.ds(*cuts[h])
        return pltpu.make_async_remote_copy(
            src_ref=keep.at[b, 1, rows],
            dst_ref=far.at[b, rows],
            send_sem=far_send.at[b, h],
            recv_sem=far_recv.at[b, h],
            device_id=side,
            device_id_type=mesh_id,
        )

    def tail_copy(k, where):
        return pltpu.make_async_remote_copy(
            src_ref=tails.at[2 * k],
            dst_ref=tails.at[2 * k + 1],
            send_sem=tail_send.at[k],
            recv_sem=tail_recv.at[k],
            device_id=where,
            device_id_type=mesh_id,
        )

    def along(b, h, landing, where):
        return pltpu.make_async_remote_copy(
            src_ref=keep.at[b, 0, pl.ds(*cuts[h])],
            dst_ref=zin.at[landing, pl.ds(*cuts[h])],
            send_sem=z_send.at[b, h],
            recv_sem=z_recv.at[landing, h],
            device_id=where,
            device_id_type=mesh_id,
        )

    def upward(b, h):
        return along(b, h, b, {"group": z + 1})

    def downward(b, h):
        return along(b, h, jnp.where(z - 1 == b, GROUPS, b), {"group": z - 1})

    def hand_over(b):
        for j in (1, 0):
            to_core(b, j).start()

    def pass_aside(b):
        to_core(b, 1).wait_recv()
        for h, (start, rows) in enumerate(cuts):

            def add(at, count):
                r = pl.ds(at, count)
                keep[b, 1, r, :] = (keep[b, 1, r, :].astype(f32) + near[b, 1, r, :].astype(f32)).astype(bf16)

            in_steps(start, rows, 128, add)
            to_side(b, h).start()

    def sent(b):
        for j in (1, 0):
            to_core(b, j).wait_send()

    def loads(b):
        rows = pl.ds(0, piece_rows)
        return (
            pltpu.make_async_copy(m_hbm.at[rows, b, :], m_in.at[rows], load_sems.at[2]),
            pltpu.make_async_copy(v_hbm.at[rows, b, :], v_in.at[rows], load_sems.at[3]),
            pltpu.make_async_copy(w_hbm.at[b, pl.ds(0, padded)], w_in, load_sems.at[4]),
        )

    def store(b, h):
        rows = pl.ds(*cuts[h])
        return pltpu.make_async_copy(g_stage.at[rows], g_out.at[b, rows], out_sems.at[b, h])

    turn = (1, 2, 3, 0)

    def differ(b, h):
        k = turn.index(b)
        start, count = cuts[h]
        if h == 0:
            to_core(b, 0).wait_recv()
            for copy in loads(b):
                copy.wait()
        to_side(b, h).wait_recv()
        if b == last and h == len(cuts) - 1:
            at = piece_rows - tail_rows
            low = at // 16 * 16
            extra = jnp.where(slot == last, tails[2] + tails[3], 0.0)
            around = [extra]
            if at > low:
                around = [jnp.zeros((at - low, LANES), f32)] + around
            if padded > piece_rows:
                around = around + [jnp.zeros((padded - piece_rows, LANES), f32)]
            ends = slice(low, padded)
            far[b, ends, :] = (far[b, ends, :].astype(f32) + jnp.concatenate(around, axis=0)).astype(bf16)
        if k:
            store(turn[k - 1], h).wait()

        def step(at, rows):
            r = pl.ds(at, rows)
            g = keep[b, 0, r, :].astype(f32) + near[b, 0, r, :].astype(f32) + far[b, r, :].astype(f32)
            g_stage[r, :] = g
            first = BETA_ONE * m_in[r, :] + (1 - BETA_ONE) * g
            second = BETA_TWO * v_in[r, :] + (1 - BETA_TWO) * g * g
            root = jnp.sqrt(second * (1 / (1 - BETA_TWO**STEP))) + ADAM_EPS
            decay = INNER_RATE * DECAY
            if b == last:
                here = lax.broadcasted_iota(jnp.int32, (rows, LANES), 0) + at
                decay = jnp.where((slot < last) | (here < piece_rows - tail_rows), decay, 0.0)
            d = (INNER_RATE / (1 - BETA_ONE**STEP)) * first / root + decay * w_in[r, :].astype(f32)
            keep[b, 0, r, :] = d.astype(bf16)

        in_steps(start, count, 128, step)
        store(b, h).start()
        if b > 0:
            pl.when(z == 0)(lambda: upward(b, h).start())
        if b < last:
            pl.when(z == last)(lambda: downward(b, h).start())
        if h == len(cuts) - 1 and k + 1 < GROUPS:
            for copy in loads(turn[k + 1]):
                copy.start()

    def hop(b, at, h):
        def go():
            along(b, h, b, {"group": z}).wait_recv()

            def add(at, count):
                r = pl.ds(at, count)
                keep[b, 0, r, :] = (keep[b, 0, r, :].astype(f32) + zin[b, r, :].astype(f32)).astype(bf16)

            in_steps(*cuts[h], 128, add)
            (upward if at < b else downward)(b, h).start()

        pl.when(z == at)(go)

    blank = slice(piece_rows, padded)
    m_in[blank, :] = jnp.zeros((padded - piece_rows, LANES), f32)
    v_in[blank, :] = jnp.zeros((padded - piece_rows, LANES), f32)
    for copy in loads(turn[0]):
        copy.start()
    for copy in stage_loads:
        copy.wait()

    refs = {1: outw_ref, 2: inw_s, 3: down_s}
    for number_of, b in enumerate(turn[:3]):
        segments, skip, has_tail = plans[b]
        for number, low, high, blocks, at in segments:
            lay_flat(refs[number], low, high, blocks, flat, at)
        if has_tail:
            at = skip + 4 * piece_rows - tail_rows
            flat[pl.ds(at, tail_rows), :] = jnp.zeros((tail_rows, LANES), f32)
        if number_of:
            pass_aside(turn[number_of - 1])
            sent(turn[number_of - 1])
        emit_pieces(flat, keep.at[b], send, slot, skip, piece_rows)
        hand_over(b)

    half = q_ref.shape[0] // 2
    local_width = q_ref.shape[1]
    depth_in = x_ref.shape[1]
    pl.semaphore_signal(x_free, inc=1, device_id={"tensor": 1 - me}, device_id_type=mesh_id)
    proj_loads = [
        pltpu.make_async_copy(
            proj_hbm.at[pl.ds(m * depth_in, depth_in)],
            inw_s.at[:, pl.ds(m * local_width, local_width)],
            x_sems.at[2 + m],
        )
        for m in range(3)
    ]
    for copy in proj_loads:
        copy.start()

    parts = range(len(cuts))
    act = functools.partial
    events = {
        0: [act(pass_aside, 3)],
        1: [act(differ, 1, 0)],
        2: [act(differ, 1, 1)],
        3: [act(differ, 1, 2)],
        4: [act(differ, 1, 3)],
        5: [act(hop, 1, 2, 0)],
        6: [act(differ, 2, 0)],
        7: [act(hop, 1, 2, 1)],
        8: [act(differ, 2, 1)],
        9: [act(hop, 1, 2, 2)],
        10: [act(differ, 2, 2)],
        11: [act(hop, 1, 2, 3)],
        13: [act(differ, 2, 3)],
        14: [act(hop, 2, 1, 0)],
        15: [act(hop, 2, 1, 1)],
    }
    blocks = q_ref.shape[1] // LANES
    code = code_ref[...]
    per_pair = q_ref.shape[0] // rows_q

    def after_step(number):
        for act in events.get(number, ()):
            act()

    for pair in range(blocks):
        attend_back(
            q_ref, k_ref, v_ref, ctx_ref, dctx_ref, code, seg_ref, lse_ref, dq_ref, dk_ref, dv_ref, pair, rows_q,
            lambda i, pair=pair: after_step(pair * per_pair + i),
        )

    tails[0] = tail_ref[...]
    for m, ref in enumerate((dq_ref, dv_ref)):
        total = jnp.sum(ref[...].astype(f32), axis=0, keepdims=True)
        for j in range(blocks):
            row = m * blocks + j
            tails[0, row : row + 1, :] = total[:, j * LANES : (j + 1) * LANES]
    tail_copy(0, core).start()

    chunk = 256
    segments, skip, _ = plans[0]
    for m, ref in enumerate((dq_ref, dk_ref, dv_ref)):

        @pl.loop(0, depth_in // chunk)
        def _(c, m=m, ref=ref):
            columns = pl.ds(pl.multiple_of(c * chunk, chunk), chunk)
            acc = dot(x_ref[:, columns].T, ref[...], NN)
            for j in range(blocks):
                to_rows = pl.ds((m * depth_in + c * chunk) * blocks + j, chunk, stride=blocks)
                flat[to_rows, :] = acc[:, j * LANES : (j + 1) * LANES]

        if m == 0:
            tail_copy(0, core).wait()
            tails[2] = tails[0] + tails[1]
            tail_copy(1, side).start()
            hop(2, 1, 2)
        if m == 1:
            hop(2, 1, 3)

    for number, low, high, wide, at in segments:
        if number:
            lay_flat(refs[number], low, high, wide, flat, at)
    sent(3)
    emit_pieces(flat, keep.at[0], send, slot, skip, piece_rows)
    hand_over(0)
    pass_aside(0)
    tail_copy(1, side).wait()
    for h in parts:
        differ(3, h)

    for copy in proj_loads:
        copy.wait()

    def through(row):
        r = pl.ds(row, 256)
        acc = dot(dq_ref[r, :], inw_s[:, 0:local_width], NT)
        acc = acc + dot(dk_ref[r, :], inw_s[:, local_width : 2 * local_width], NT)
        return acc + dot(dv_ref[r, :], inw_s[:, 2 * local_width : 3 * local_width], NT)

    @pl.loop(0, half // 256)
    def _(i):
        down_s[pl.ds(pl.multiple_of(i * 256, 256), 256), :] = through(
            pl.multiple_of(half + i * 256, 256)
        ).astype(bf16)

    pl.semaphore_wait(x_free, 1)
    x_copy = pltpu.make_async_remote_copy(
        src_ref=down_s.at[pl.ds(0, half)],
        dst_ref=down_s.at[pl.ds(half, half)],
        send_sem=x_sems.at[0],
        recv_sem=x_sems.at[1],
        device_id={"tensor": 1 - me},
        device_id_type=mesh_id,
    )
    x_copy.start()
    differ(0, 0)

    @pl.loop(0, half // 256)
    def _(i):
        down_s[pl.ds(pl.multiple_of(2 * half + i * 256, 256), 256), :] = through(
            pl.multiple_of(i * 256, 256)
        ).astype(bf16)

    differ(0, 1)
    hop(3, 1, 0)
    hop(0, 2, 0)
    differ(0, 2)
    hop(3, 1, 1)
    hop(3, 2, 0)
    hop(0, 2, 1)
    differ(0, 3)
    for h in parts:
        if h > 1:
            hop(3, 1, h)
            hop(0, 2, h)
        hop(0, 1, h)
        if h:
            hop(3, 2, h)

    for h in parts:
        store(0, h).wait()
    for b in range(GROUPS):

        def finish(b=b):
            for h in parts:
                if b > 0:
                    along(b, h, b, {"group": z}).wait_recv()
                if b < last:
                    along(b, h, GROUPS, {"group": z}).wait_recv()

                def add(at, count):
                    r = pl.ds(at, count)
                    total = keep[b, 0, r, :].astype(f32)
                    if b > 0:
                        total = total + zin[b, r, :].astype(f32)
                    if b < last:
                        total = total + zin[GROUPS, r, :].astype(f32)
                    g_stage[r, :] = total

                in_steps(*cuts[h], 128, add)

        pl.when(z == b)(finish)
    x_copy.wait()
    dx_copy = pltpu.make_async_copy(down_s.at[pl.ds(half, 2 * half)], dx_out, x_sems.at[5])
    dx_copy.start()
    copy = pltpu.make_async_copy(g_stage, d_out, out_sems.at[GROUPS, 0])
    copy.start()
    for b in range(GROUPS):
        for h in parts:
            to_side(b, h).wait_send()

            @pl.when(z != b)
            def _(b=b, h=h):
                along(b, h, b, {"group": z}).wait_send()

    sent(0)
    copy.wait()
    dx_copy.wait()


def back(
    q, k, v, ctx, dctx, code_col, seg_row, lse, x_all, d_outw, tail, d_inw, d_down, first, second, pieces, proj_w,
    table, tail_at, piece_rows, rows_q=256
):
    per = 4
    padded = round_up(piece_rows, 16)
    tail_rows = tail.shape[0]
    plans = []
    most = 0
    for b in range(GROUPS):
        begin = b * per * piece_rows
        segments, base, size = chunk_plan(table, begin, begin + per * piece_rows, tail_at, tail_rows)
        plans.append((segments, begin - base, begin + per * piece_rows > tail_at))
        most = max(most, size)
    marks = [padded * i // 4 // 16 * 16 for i in range(4)] + [padded]
    cuts = [(low, high - low) for low, high in zip(marks[:-1], marks[1:])]
    whole = pl.BlockSpec(memory_space=pltpu.VMEM)
    hbm = pl.BlockSpec(memory_space=pl.ANY)
    dma = pltpu.SemaphoreType.DMA
    n, local_width = q.shape
    grad = pltpu.VMEM((n, local_width), bf16)
    wide = pltpu.VMEM((padded, LANES), f32)
    return pl.pallas_call(
        functools.partial(back_kernel, plans=plans, piece_rows=piece_rows, cuts=cuts, rows_q=rows_q),
        in_specs=[whole] * 11 + [hbm] * 6,
        out_specs=[hbm] * 3,
        out_shape=[
            jax.ShapeDtypeStruct((GROUPS, padded, LANES), f32),
            jax.ShapeDtypeStruct((padded, LANES), f32),
            jax.ShapeDtypeStruct((n, x_all.shape[1]), bf16),
        ],
        scratch_shapes=[
            grad,
            grad,
            grad,
            pltpu.VMEM((round_up(most, 8) + 8, LANES), f32),
            pltpu.VMEM(d_down.shape, bf16),
            pltpu.VMEM(d_inw.shape, bf16),
            pltpu.VMEM((GROUPS, 2, padded, LANES), bf16),
            pltpu.VMEM((2, padded, LANES), bf16),
            pltpu.VMEM((GROUPS, 2, padded, LANES), bf16),
            pltpu.VMEM((GROUPS, padded, LANES), bf16),
            pltpu.VMEM((4, tail_rows, LANES), f32),
            pltpu.VMEM((GROUPS + 1, padded, LANES), bf16),
            wide,
            wide,
            wide,
            pltpu.VMEM((padded, LANES), bf16),
            dma((GROUPS, 2)),
            dma((GROUPS, 2)),
            dma((GROUPS, 4)),
            dma((GROUPS, 4)),
            dma((2,)),
            dma((2,)),
            dma((GROUPS, 4)),
            dma((GROUPS + 1, 4)),
            dma((5,)),
            dma((GROUPS + 1, 4)),
            dma((6,)),
            pltpu.SemaphoreType.REGULAR,
        ],
        cost_estimate=pl.CostEstimate(
            flops=30 * n * n * local_width, bytes_accessed=40 << 20, transcendentals=n * n * 8
        ),
        compiler_params=params(collective_id=4, has_side_effects=True),
        name="back",
    )(
        q, k, v, ctx, dctx, code_col, seg_row, lse, x_all, d_outw, tail, d_inw, d_down, first, second, pieces, proj_w
    )


def partner(block):
    return lax.ppermute(block, "tensor", [(0, 1), (1, 0)])


def both(own):
    return jnp.concatenate([own, partner(own)], axis=0)


def own_sum(partial):
    half = partial.shape[0] // 2
    return partial[:half].astype(f32) + partner(partial[half:].astype(bf16)).astype(f32)


def local_fast(
    tokens,
    cotangent,
    segment_ids,
    padding,
    shared_weights,
    first_moment,
    second_moment,
    outer_momentum,
):
    me = lax.axis_index("tensor")
    per = lax.axis_size("slot")
    rows = tokens.shape[0]
    local_width = D // 2
    piece_rows = shared_weights.shape[1] // LANES
    table, tail_at = matrix_table(2)
    tail_rows = GROUPS * per * piece_rows - tail_at
    padded = round_up(piece_rows + tail_rows, 16)

    own_rows = shared_weights.reshape(piece_rows, 1, LANES)
    seg = jnp.where(me == 0, segment_ids, jnp.roll(segment_ids, rows))
    live = jnp.where(me == 0, padding, jnp.roll(padding, rows))
    code = jnp.where(live == 1, seg, -1)
    end = padded - round_up(2 * tail_rows + 16, 16)
    marks = [end * i // 4 // 16 * 16 for i in range(4)] + [end, padded]
    cuts = [(low, high - low) for low, high in zip(marks[:-1], marks[1:])]
    (
        proj_w, out_w, in_w, down_w, pieces, tail_all, x_all, query, keys, values, context, lse
    ) = start(own_rows, tokens, code[None], seg[:, None], table, tail_rows, padded, cuts)
    flat_tail = tail_all.reshape(-1)
    inner_bias = flat_tail[2 * local_width : 2 * local_width + FF // 2]
    vec_own = flat_tail[2 * local_width + FF // 2 :].reshape(6, local_width)
    vec_other = partner(vec_own)
    vectors = jnp.where(
        me == 0,
        jnp.concatenate([vec_own, vec_other], axis=1),
        jnp.concatenate([vec_other, vec_own], axis=1),
    )

    (
        block_out, grad_one, grad_context, grad_out_w, grad_in_w, grad_down_w, tail_grad
    ) = middle(context, tokens, cotangent, vectors, inner_bias.reshape(1, -1), out_w, in_w, down_w)
    def blocked(state):
        return state.reshape(GROUPS, piece_rows, LANES).transpose(1, 0, 2)

    def unblocked(state):
        return state.transpose(1, 0, 2).reshape(1, 1, GROUPS, piece_rows * LANES)

    first = blocked(first_moment)
    second = blocked(second_moment)
    grads, d_sum, dx = back(
        query, keys, values, context, grad_context, code[:, None], seg[None], lse, x_all, grad_out_w,
        tail_grad, grad_in_w, grad_down_w, first, second, pieces, proj_w, table, tail_at, piece_rows
    )
    input_grad = (grad_one + dx[:rows].astype(f32) + dx[rows:].astype(f32)).astype(bf16)
    slot_word = lax.axis_index("slot").astype(jnp.int32).reshape(1)
    *states, mean_diff, new_momentum, new_weights = update(
        slot_word, grads, pieces, first, second, d_sum, own_rows,
        outer_momentum.reshape(piece_rows, 1, LANES), tail_rows
    )
    rows_out = [state.reshape(1, piece_rows * LANES) for state in (mean_diff, new_momentum, new_weights)]
    return (block_out, input_grad, *[unblocked(state) for state in states], *rows_out)


def solution(mesh):
    dp = mesh.shape["dp"]
    tensor_size = mesh.shape["tensor"]
    piece = (4 * D * D + 2 * D * FF + 8 * D + FF) // tensor_size // dp
    if tensor_size == 2 and piece % LANES == 0 and dp % GROUPS == 0:
        mesh = Mesh(
            mesh.devices.reshape(GROUPS, dp // GROUPS, tensor_size), ("group", "slot", "tensor")
        )
        data = ("group", "slot")
        body = local_fast
    else:
        data = "dp"
        body = local_general
    every = ("group", "slot", "tensor") if body is local_fast else ("dp", "tensor")
    in_specs = (
        P(every, None),
        P(every, None),
        P(data),
        P(data),
        P("tensor", data),
        P("tensor", data, None, None),
        P("tensor", data, None, None),
        P("tensor", data),
    )
    out_specs = (
        P(every, None),
        P(every, None),
        P("tensor", data, None, None),
        P("tensor", data, None, None),
        P("tensor", data, None, None),
        P("tensor", data, None, None),
        P("tensor", data),
        P("tensor", data),
        P("tensor", data),
    )
    return jax.shard_map(body, mesh=mesh, in_specs=in_specs, out_specs=out_specs, check_vma=False)
```

```python
import functools

import jax
import jax.numpy as jnp
import numpy as np
from jax import lax
from jax.experimental import pallas as pl
from jax.experimental.pallas import tpu as pltpu
from jax.sharding import Mesh
from jax.sharding import PartitionSpec as P

D = 1024
HEADS = 16
HD = 64
FF = 4096
SEQ_LEN = 1024
GROUPS = 4
STEP = 10


NORM_EPS = 1e-05
MASKED = -1000000000.0
BETA_ONE = 0.9
BETA_TWO = 0.999
ADAM_EPS = 1e-08
INNER_RATE = 0.02
DECAY = 0.01
OUTER_MU = 0.9
OUTER_RATE = 0.7
ROOT_HALF = 0.7071067811865476
INV_ROOT_TWO_PI = 0.3989422804014327


def from_partner(block, axis, stride):
    count = lax.axis_size(axis)
    route = []
    for low in range(count):
        high = low | 1 << stride
        if high != low and high < count:
            route += [(low, high), (high, low)]
    return lax.ppermute(block, axis, route)


def boundaries(tensor_size):
    local_width = D // tensor_size
    hidden = FF // tensor_size
    lengths = [
        3 * D * local_width,
        local_width * D,
        D * hidden,
        hidden * D,
        local_width,
        local_width,
        hidden,
        6 * local_width,
    ]
    points = [0]
    for amount in lengths:
        points.append(points[-1] + amount)
    return points


def layer_norm(values, norm_gain, norm_shift):
    average = jnp.mean(values, axis=-1, keepdims=True)
    centred = values - average
    variance = jnp.mean(centred * centred, axis=-1, keepdims=True)
    inv_dev = lax.rsqrt(variance + NORM_EPS)
    normed = centred * inv_dev
    return (normed * norm_gain + norm_shift, normed, inv_dev)


def norm_back(grad_normed, normed, inv_dev):
    first_part = jnp.mean(grad_normed, axis=-1, keepdims=True)
    second_part = jnp.mean(grad_normed * normed, axis=-1, keepdims=True)
    return inv_dev * (grad_normed - first_part - normed * second_part)


def gelu_slope(inner):
    return (
        0.5 * (1.0 + jax.scipy.special.erf(inner * ROOT_HALF))
        + inner * jnp.exp(-0.5 * inner * inner) * INV_ROOT_TWO_PI
    )


def row_contract(left_side, right_side):
    return lax.dot_general(
        left_side, right_side, (((0,), (0,)), ((), ())), preferred_element_type=jnp.float32
    )


def col_contract(left_side, right_side):
    return lax.dot_general(
        left_side, right_side, (((1,), (1,)), ((), ())), preferred_element_type=jnp.float32
    )


def halve_rounds(values, bit_list, first_axis, top_bit, dp_index, site_call):
    for bit_number in bit_list:
        axis_number = first_axis + top_bit - bit_number
        my_bit = dp_index >> bit_number & 1
        kept = lax.dynamic_index_in_dim(values, my_bit, axis_number, keepdims=True)
        outgoing = lax.dynamic_index_in_dim(values, 1 - my_bit, axis_number, keepdims=True)
        values = kept + site_call(outgoing, bit_number)
    return values


def local_general(
    tokens,
    cotangent,
    segment_ids,
    padding,
    shared_weights,
    first_moment,
    second_moment,
    outer_momentum,
):
    tensor_size = lax.axis_size("tensor")
    local_width = D // tensor_size
    hidden = FF // tensor_size
    local_heads = HEADS // tensor_size
    seq_rows = segment_ids.shape[0]
    seq_count = seq_rows // SEQ_LEN
    block_rows = min(512, SEQ_LEN)
    per_seq = SEQ_LEN // block_rows
    block_total = seq_count * per_seq
    score_scale = HD ** (-0.5)
    bf16 = jnp.bfloat16
    f32 = jnp.float32
    masters = lax.all_gather(shared_weights, "dp", axis=1, tiled=True)[0]
    points = boundaries(tensor_size)
    segments = [masters[points[number] : points[number + 1]] for number in range(8)]
    proj_weight = segments[0].reshape(3, D, local_width).astype(bf16)
    out_weight = segments[1].reshape(local_width, D).astype(bf16)
    in_weight = segments[2].reshape(D, hidden).astype(bf16)
    down_weight = segments[3].reshape(hidden, D).astype(bf16)
    query_bias = segments[4]
    value_bias = segments[5]
    inner_bias = segments[6]
    vectors = lax.all_gather(segments[7].reshape(6, local_width), "tensor", axis=1, tiled=True)
    inputs_all = lax.all_gather(tokens, "tensor", axis=0, tiled=True)
    projected = jnp.einsum("td,kde->kte", inputs_all, proj_weight, preferred_element_type=f32)
    query = (projected[0] + query_bias).astype(bf16)
    keys = projected[1].astype(bf16)
    values = (projected[2] + value_bias).astype(bf16)
    query_four = query.reshape(seq_count, SEQ_LEN, local_heads, HD)
    keys_four = keys.reshape(seq_count, SEQ_LEN, local_heads, HD)
    values_four = values.reshape(seq_count, SEQ_LEN, local_heads, HD)
    seg_two = segment_ids.reshape(seq_count, SEQ_LEN)
    live_two = padding.reshape(seq_count, SEQ_LEN)
    key_pos = jnp.arange(SEQ_LEN, dtype=jnp.int32)

    def block_scores(block_index):
        sequence = block_index // per_seq
        offset = block_index % per_seq * block_rows
        query_rows = lax.dynamic_index_in_dim(query_four, sequence, 0, keepdims=False)
        query_block = lax.dynamic_slice_in_dim(query_rows, offset, block_rows, 0)
        key_rows = lax.dynamic_index_in_dim(keys_four, sequence, 0, keepdims=False)
        seg_row = lax.dynamic_index_in_dim(seg_two, sequence, 0, keepdims=False)
        live_row = lax.dynamic_index_in_dim(live_two, sequence, 0, keepdims=False)
        seg_block = lax.dynamic_slice_in_dim(seg_row, offset, block_rows, 0)
        query_pos = offset + jnp.arange(block_rows, dtype=jnp.int32)
        allowed = (seg_block[:, None] == seg_row[None, :]) & (
            (live_row[None, :] == 1) | (query_pos[:, None] == key_pos[None, :])
        )
        raw_scores = (
            jnp.einsum("qhd,khd->hqk", query_block, key_rows, preferred_element_type=f32)
            * score_scale
        )
        return (
            jnp.where(allowed[None], raw_scores, MASKED),
            query_block,
            key_rows,
            sequence,
            offset,
        )

    def forward_block(block_index):
        scores, query_block, key_rows, sequence, offset = block_scores(block_index)
        value_rows = lax.dynamic_index_in_dim(values_four, sequence, 0, keepdims=False)
        highest = jnp.max(scores, axis=-1, keepdims=True)
        exponent = jnp.exp(scores - highest)
        summed = jnp.sum(exponent, axis=-1, keepdims=True)
        probabilities = (exponent / summed).astype(bf16)
        context = jnp.einsum("hqk,khd->qhd", probabilities, value_rows, preferred_element_type=f32)
        return (context, (highest + jnp.log(summed))[..., 0])

    context_blocks, log_totals = lax.map(forward_block, jnp.arange(block_total, dtype=jnp.int32))
    context_low = context_blocks.reshape(seq_rows, local_width).astype(bf16)
    attn_sum = lax.psum_scatter(
        jnp.dot(context_low, out_weight, preferred_element_type=f32).astype(jnp.bfloat16),
        "tensor",
        scatter_dimension=0,
        tiled=True,
    ).astype(jnp.float32)
    tokens_f = tokens.astype(f32)
    middle, normed_one, inv_one = layer_norm(
        tokens_f + (attn_sum + vectors[4]), vectors[0], vectors[1]
    )
    middle_all = lax.all_gather(middle.astype(bf16), "tensor", axis=0, tiled=True)
    inner = jnp.dot(middle_all, in_weight, preferred_element_type=f32) + inner_bias
    activated = jax.nn.gelu(inner, approximate=False).astype(bf16)
    ffn_sum = lax.psum_scatter(
        jnp.dot(activated, down_weight, preferred_element_type=f32).astype(jnp.bfloat16),
        "tensor",
        scatter_dimension=0,
        tiled=True,
    ).astype(jnp.float32)
    result, normed_two, inv_two = layer_norm(
        middle + (ffn_sum + vectors[5]), vectors[2], vectors[3]
    )
    block_out = result.astype(bf16)
    grad_out = cotangent.astype(f32)
    grad_gain_two = jnp.sum(grad_out * normed_two, axis=0)
    grad_shift_two = jnp.sum(grad_out, axis=0)
    grad_two = norm_back(grad_out * vectors[2], normed_two, inv_two)
    grad_down_bias = jnp.sum(grad_two, axis=0)
    back_all = lax.all_gather(grad_two.astype(bf16), "tensor", axis=0, tiled=True)
    grad_down_weight = row_contract(activated, back_all)
    grad_act = col_contract(back_all, down_weight)
    grad_inner = (grad_act * gelu_slope(inner)).astype(bf16)
    grad_inner_bias = jnp.sum(grad_inner.astype(f32), axis=0)
    grad_in_weight = row_contract(middle_all, grad_inner)
    grad_middle = grad_two + lax.psum_scatter(
        col_contract(grad_inner, in_weight).astype(jnp.bfloat16),
        "tensor",
        scatter_dimension=0,
        tiled=True,
    ).astype(jnp.float32)
    grad_gain_one = jnp.sum(grad_middle * normed_one, axis=0)
    grad_shift_one = jnp.sum(grad_middle, axis=0)
    grad_one = norm_back(grad_middle * vectors[0], normed_one, inv_one)
    grad_out_bias = jnp.sum(grad_one, axis=0)
    attn_back_all = lax.all_gather(grad_one.astype(bf16), "tensor", axis=0, tiled=True)
    grad_out_weight = row_contract(context_low, attn_back_all)
    grad_context = col_contract(attn_back_all, out_weight).astype(bf16)
    grad_context_four = grad_context.reshape(seq_count, SEQ_LEN, local_heads, HD)

    def backward_block(carry, block_index):
        grad_keys, grad_values = carry
        scores, query_block, key_rows, sequence, offset = block_scores(block_index)
        value_rows = lax.dynamic_index_in_dim(values_four, sequence, 0, keepdims=False)
        log_total = lax.dynamic_index_in_dim(log_totals, block_index, 0, keepdims=False)
        probabilities = jnp.exp(scores - log_total[..., None])
        prob_low = probabilities.astype(bf16)
        grad_rows = lax.dynamic_index_in_dim(grad_context_four, sequence, 0, keepdims=False)
        grad_block = lax.dynamic_slice_in_dim(grad_rows, offset, block_rows, 0)
        grad_probs = jnp.einsum("qhd,khd->hqk", grad_block, value_rows, preferred_element_type=f32)
        grad_scores = probabilities * (
            grad_probs - jnp.sum(grad_probs * probabilities, axis=-1, keepdims=True)
        )
        scores_low = grad_scores.astype(bf16)
        grad_query = (
            jnp.einsum("hqk,khd->qhd", scores_low, key_rows, preferred_element_type=f32)
            * score_scale
        )
        key_term = (
            jnp.einsum("hqk,qhd->khd", scores_low, query_block, preferred_element_type=f32)
            * score_scale
        )
        value_term = jnp.einsum("hqk,qhd->khd", prob_low, grad_block, preferred_element_type=f32)
        grad_keys = lax.dynamic_update_index_in_dim(
            grad_keys,
            lax.dynamic_index_in_dim(grad_keys, sequence, 0, keepdims=False) + key_term,
            sequence,
            0,
        )
        grad_values = lax.dynamic_update_index_in_dim(
            grad_values,
            lax.dynamic_index_in_dim(grad_values, sequence, 0, keepdims=False) + value_term,
            sequence,
            0,
        )
        return ((grad_keys, grad_values), grad_query)

    empty = jnp.zeros((seq_count, SEQ_LEN, local_heads, HD), f32)
    (grad_keys, grad_values), grad_queries = lax.scan(
        backward_block, (empty, empty), jnp.arange(block_total, dtype=jnp.int32)
    )
    grad_proj = jnp.stack(
        [
            grad_queries.reshape(seq_rows, local_width),
            grad_keys.reshape(seq_rows, local_width),
            grad_values.reshape(seq_rows, local_width),
        ]
    ).astype(bf16)
    grad_proj_weight = jnp.einsum("td,kte->kde", inputs_all, grad_proj, preferred_element_type=f32)
    grad_query_bias = jnp.sum(grad_proj[0].astype(f32), axis=0)
    grad_value_bias = jnp.sum(grad_proj[2].astype(f32), axis=0)
    input_part = jnp.einsum("kte,kde->td", grad_proj, proj_weight, preferred_element_type=f32)
    vector_part = jnp.stack(
        [
            grad_gain_one,
            grad_shift_one,
            grad_gain_two,
            grad_shift_two,
            grad_out_bias,
            grad_down_bias,
        ]
    )
    input_share, vector_grad = (
        lax.psum_scatter(
            input_part.astype(jnp.bfloat16), "tensor", scatter_dimension=0, tiled=True
        ).astype(jnp.float32),
        lax.psum_scatter(
            vector_part.astype(jnp.bfloat16), "tensor", scatter_dimension=1, tiled=True
        ).astype(jnp.float32),
    )
    input_grad = (grad_one + input_share).astype(bf16)
    flat_grad = jnp.concatenate(
        [
            grad_proj_weight.reshape(-1),
            grad_out_weight.reshape(-1),
            grad_in_weight.reshape(-1),
            grad_down_weight.reshape(-1),
            grad_query_bias,
            grad_value_bias,
            grad_inner_bias,
            vector_grad.reshape(-1),
        ]
    )
    dp_size = lax.axis_size("dp")
    per_group = dp_size // GROUPS
    inner_bits = per_group.bit_length() - 1
    all_bits = dp_size.bit_length() - 1
    dp_index = lax.axis_index("dp")
    slot_index = dp_index % per_group
    piece_len = shared_weights.shape[1]
    grid_view = flat_grad.reshape(GROUPS, per_group, piece_len)
    inner_list = list(range(inner_bits))
    outer_list = list(range(inner_bits, all_bits))
    inner_list = inner_list[::-1]
    outer_list = outer_list[::-1]
    summed_grid = grid_view
    for bit_number in inner_list:
        summed_grid = summed_grid + from_partner(
            summed_grid.astype(jnp.bfloat16), "dp", bit_number
        ).astype(summed_grid.dtype)
    grad_block = lax.dynamic_index_in_dim(summed_grid, slot_index, 1, keepdims=False)
    weights_block = lax.dynamic_index_in_dim(
        masters.reshape(GROUPS, per_group, piece_len), slot_index, 1, keepdims=False
    )
    matrix_count = (4 * D * D + 2 * D * FF) // tensor_size
    flat_index = (
        jnp.arange(GROUPS, dtype=jnp.int32)[:, None] * per_group + slot_index
    ) * piece_len + jnp.arange(piece_len, dtype=jnp.int32)[None, :]
    decay_mask = (flat_index < matrix_count).astype(f32)
    first_new = BETA_ONE * first_moment[0, 0] + (1 - BETA_ONE) * grad_block
    second_new = BETA_TWO * second_moment[0, 0] + (1 - BETA_TWO) * grad_block * grad_block
    first_hat = first_new / (1 - BETA_ONE**STEP)
    second_hat = second_new / (1 - BETA_TWO**STEP)
    group_weights = weights_block - INNER_RATE * (
        first_hat / (jnp.sqrt(second_hat) + ADAM_EPS) + DECAY * decay_mask * weights_block
    )
    difference = weights_block - group_weights

    def outer_swap(outgoing, bit_number):
        return from_partner(outgoing.astype(jnp.bfloat16), "dp", bit_number).astype(outgoing.dtype)

    outer_bits = all_bits - inner_bits
    diff_view = difference.reshape((2,) * outer_bits + (piece_len,))
    diff_sum = halve_rounds(diff_view, outer_list, 0, all_bits - 1, dp_index, outer_swap).reshape(
        piece_len
    )
    mean_diff = diff_sum / GROUPS
    new_momentum = OUTER_MU * outer_momentum[0] + mean_diff
    new_weights = shared_weights[0] - OUTER_RATE * (mean_diff + OUTER_MU * new_momentum)
    return (
        block_out,
        input_grad,
        grad_block[None, None],
        first_new[None, None],
        second_new[None, None],
        group_weights[None, None],
        mean_diff[None],
        new_momentum[None],
        new_weights[None],
    )


LANES = 128
NT = (((1,), (1,)), ((), ()))
NN = (((1,), (0,)), ((), ()))
TN = (((0,), (0,)), ((), ()))
VMEM_BYTES = 58 << 20
f32 = jnp.float32
bf16 = jnp.bfloat16


def dot(left, right, dims):
    return lax.dot_general(left, right, dims, preferred_element_type=f32)


def params(**more):
    return pltpu.CompilerParams(vmem_limit_bytes=VMEM_BYTES, **more)


def round_up(number, step):
    return -(-number // step) * step


def matrix_table(tensor_size):
    local_width = D // tensor_size
    hidden = FF // tensor_size
    table = []
    offset = 0
    for rows, columns in ((3 * D, local_width), (local_width, D), (D, hidden), (hidden, D)):
        blocks = columns // LANES
        table.append((offset, rows, blocks))
        offset += rows * blocks
    return table, offset


def chunk_plan(table, first, end, tail_at, tail_rows):
    segments = []
    base = None
    for number, (offset, rows, blocks) in enumerate(table):
        low = max(first, offset)
        high = min(end, offset + rows * blocks)
        if low >= high:
            continue
        row_low = (low - offset) // blocks // 16 * 16
        row_high = min(rows, round_up(-(-(high - offset) // blocks), 16))
        if base is None:
            base = offset + row_low * blocks
        segments.append((number, row_low, row_high, blocks, offset + row_low * blocks - base))
    size = max(at + (high - low) * blocks for _, low, high, blocks, at in segments)
    if end > tail_at:
        size = max(size, tail_at + tail_rows - base)
    return segments, base, size


def row_parts(rows, count):
    size = rows // count // 16 * 16
    starts = [size * i for i in range(count)] + [rows]
    return [(low, high - low) for low, high in zip(starts[:-1], starts[1:])]


def in_steps(start, rows, step, body):
    @pl.loop(0, rows // step)
    def _(i):
        body(pl.multiple_of(start + i * step, 16), step)

    if rows % step:
        body(start + rows // step * step, rows % step)


def update_kernel(
    slot_ref, g_hbm, w_hbm, m_hbm, v_hbm, d_hbm, own_hbm, mom_hbm,
    go, mo, vo, wo, mean_out, mom_out, new_out,
    g_s, w_s, m_s, v_s, m_new, v_new, w_new, sems,
    *, piece_rows, tail_rows, parts
):
    slot = slot_ref[0]
    units = [(b, part) for b in range(GROUPS) for part in parts] + [(None, part) for part in parts]

    def loads(u):
        b, (at, rows) = units[u]
        k = u % 3
        r = pl.ds(at, rows)
        wide = pl.ds(at, round_up(rows, 16))
        there, padded = pl.ds(0, rows), pl.ds(0, round_up(rows, 16))
        if b is None:
            pairs = (
                (d_hbm.at[wide], g_s.at[k, padded]),
                (own_hbm.at[r, 0, :], m_s.at[k, there]),
                (mom_hbm.at[r, 0, :], v_s.at[k, there]),
            )
        else:
            pairs = (
                (g_hbm.at[b, wide], g_s.at[k, padded]),
                (m_hbm.at[r, b, :], m_s.at[k, there]),
                (v_hbm.at[r, b, :], v_s.at[k, there]),
                (w_hbm.at[b, wide], w_s.at[k, padded]),
            )
        return [pltpu.make_async_copy(src, dst, sems.at[n, k]) for n, (src, dst) in enumerate(pairs)]

    def stores(u):
        b, (at, rows) = units[u]
        k = u % 3
        r = pl.ds(at, rows)
        there = pl.ds(0, rows)
        if b is None:
            pairs = (
                (m_new.at[k, there], mean_out.at[r, 0, :]),
                (v_new.at[k, there], mom_out.at[r, 0, :]),
                (w_new.at[k, there], new_out.at[r, 0, :]),
            )
        else:
            pairs = (
                (m_new.at[k, there], mo.at[r, b, :]),
                (v_new.at[k, there], vo.at[r, b, :]),
                (w_new.at[k, there], wo.at[r, b, :]),
                (g_s.at[k, there], go.at[r, b, :]),
            )
        return [pltpu.make_async_copy(src, dst, sems.at[4 + n, k]) for n, (src, dst) in enumerate(pairs)]

    for copy in loads(0):
        copy.start()
    for u, (b, (at, rows)) in enumerate(units):
        k = u % 3
        if u > 1:
            for copy in stores(u - 2):
                copy.wait()
        if u + 1 < len(units):
            for copy in loads(u + 1):
                copy.start()
        for copy in loads(u):
            copy.wait()

        def inner(start, count, b=b, at=at, k=k):
            r = pl.ds(start, count)
            g = g_s[k, r, :]
            if b is None:
                average = g / GROUPS
                momentum = OUTER_MU * v_s[k, r, :] + average
                m_new[k, r, :] = average
                v_new[k, r, :] = momentum
                w_new[k, r, :] = m_s[k, r, :] - OUTER_RATE * (average + OUTER_MU * momentum)
                return
            w = w_s[k, r, :].astype(f32)
            first = BETA_ONE * m_s[k, r, :] + (1 - BETA_ONE) * g
            second = BETA_TWO * v_s[k, r, :] + (1 - BETA_TWO) * g * g
            root = jnp.sqrt(second * (1 / (1 - BETA_TWO**STEP))) + ADAM_EPS
            decay = INNER_RATE * DECAY
            if b == GROUPS - 1:
                here = lax.broadcasted_iota(jnp.int32, (count, LANES), 0) + (at + start)
                decay = jnp.where((slot < 3) | (here < piece_rows - tail_rows), decay, 0.0)
            m_new[k, r, :] = first
            v_new[k, r, :] = second
            w_new[k, r, :] = w - ((INNER_RATE / (1 - BETA_ONE**STEP)) * first / root + decay * w)

        in_steps(0, round_up(rows, 16), 128, inner)
        for copy in stores(u):
            copy.start()
    for u in (len(units) - 2, len(units) - 1):
        for copy in stores(u):
            copy.wait()


def update(slot, grads, pieces, first, second, d_sum, own_rows, momentum_rows, tail_rows):
    piece_rows = first.shape[0]
    hbm = pl.BlockSpec(memory_space=pl.ANY)
    parts = row_parts(piece_rows, 3)
    most = round_up(max(rows for _, rows in parts), 16)
    wide = pltpu.VMEM((3, most, LANES), f32)
    state = jax.ShapeDtypeStruct(first.shape, f32)
    piece = jax.ShapeDtypeStruct(own_rows.shape, f32)
    return pl.pallas_call(
        functools.partial(update_kernel, piece_rows=piece_rows, tail_rows=tail_rows, parts=parts),
        in_specs=[pl.BlockSpec(memory_space=pltpu.SMEM)] + [hbm] * 7,
        out_specs=[hbm] * 7,
        out_shape=[state] * 4 + [piece] * 3,
        scratch_shapes=[wide, pltpu.VMEM((3, most, LANES), bf16)]
        + [wide] * 5
        + [pltpu.SemaphoreType.DMA((8, 3))],
        cost_estimate=pl.CostEstimate(
            flops=120 * piece_rows * LANES,
            bytes_accessed=120 * piece_rows * LANES,
            transcendentals=8 * piece_rows * LANES,
        ),
        compiler_params=params(),
        name="update",
    )(slot, grads, pieces, first, second, d_sum, own_rows, momentum_rows)


def attend_block(q, k, v_ones, code, seg_col, offset):
    rows_q, n = q.shape[0], k.shape[0]
    low = lax.broadcasted_iota(jnp.int32, (1, LANES), 1) < HD
    zero = jnp.zeros((), bf16)
    q = q * jnp.asarray(HD**-0.5, bf16)
    rows = lax.broadcasted_iota(jnp.int32, (rows_q, n), 0) + offset
    cols = lax.broadcasted_iota(jnp.int32, (rows_q, n), 1)
    allowed = (seg_col == code) | (rows == cols)
    outs = []
    tops = []
    for h in range(2):
        qh = jnp.where(low, q, zero) if h == 0 else jnp.where(low, zero, q)
        s = jnp.where(allowed, dot(qh, k, NT), MASKED)
        top = jnp.max(s, axis=1, keepdims=True)
        p = jnp.exp(s - top).astype(bf16)
        outs.append(dot(p, v_ones[h], NN))
        tops.append(top)
    num = jnp.where(low, outs[0], outs[1])
    den = pltpu.roll(jnp.where(low, outs[1], outs[0]), HD, 1)
    lse = (jnp.where(low, tops[0], tops[1]) + jnp.log(den)).T
    return (num / den).astype(bf16), lse[0:1], lse[HD : HD + 1]


def widen(src, low, high, flat, to):
    step = 128
    full = (high - low) // step

    @pl.loop(0, full)
    def _(i):
        rows = src[pl.ds(pl.multiple_of(low + i * step, 16), step), :]
        flat[pl.ds(to + i * step, step), :] = rows.astype(f32)

    rest = (high - low) % step
    if rest:
        flat[pl.ds(to + full * step, rest), :] = src[low + full * step : high, :].astype(f32)


def bring_rows(buf, flat, margin, offset, count, piece_rows):
    for p, low, high, at in piece_spans(offset, count, piece_rows, buf.shape[1]):
        widen(buf.at[p], low, high, flat, margin + at)


def emit_matrix(flat, out, margin, rows, blocks, first=0):
    chunk = 64

    @pl.loop(0, rows // chunk)
    def _(c):
        at = pl.ds(pl.multiple_of(first + c * chunk, chunk), chunk)
        for j in range(blocks):
            from_rows = pl.ds(margin + c * (chunk * blocks) + j, chunk, stride=blocks)
            out[at, j * LANES : (j + 1) * LANES] = flat[from_rows, :].astype(bf16)


def piece_spans(offset, count, piece_rows, padded):
    spans = []
    for p in range(offset // piece_rows, -(-(offset + count) // piece_rows)):
        low = max(offset - p * piece_rows, 0) // 16 * 16
        high = min(round_up(min(offset + count - p * piece_rows, piece_rows), 16), padded)
        spans.append((p, low, high, p * piece_rows + low - offset))
    return spans


def start_kernel(
    own_hbm, tokens_hbm, code_ref, seg_ref,
    proj_out, outw_out, inw_out, down_out, outw2_out, ctx2_out, pieces_out, x_out,
    vec_ref, c1_ref, q_ref, k_ref, v_ref, ctx_ref, lse_ref,
    rows32, buf, xbuf, flat, proj_s, outw_s, inw_s, down_s, outw2_s, obuf, ctx2_s, vec_s,
    zdown, zup, zrecv, ysend, yrecv, csend, crecv, xsem, local_sems, ctx_sems, wo_sems,
    *, piece_rows, tail_rows, table, cuts, rows_q
):
    z = lax.axis_index("group")
    slot = lax.axis_index("slot")
    me = lax.axis_index("tensor")
    depth = GROUPS
    padded = buf.shape[1]
    half = tokens_hbm.shape[0]
    n = 2 * half
    mesh_id = pl.DeviceIdType.MESH

    load = pltpu.make_async_copy(own_hbm.at[:, 0, :], rows32, local_sems.at[0])
    load.start()
    x_load = pltpu.make_async_copy(tokens_hbm, xbuf.at[pl.ds(0, half)], local_sems.at[1])
    x_load.start()

    barrier = pltpu.get_barrier_semaphore()
    for where in ({"slot": slot ^ 1}, {"slot": slot ^ 2}, {"tensor": 1 - me}):
        pl.semaphore_signal(barrier, inc=1, device_id=where, device_id_type=mesh_id)

    @pl.when(z > 0)
    def _():
        pl.semaphore_signal(barrier, inc=1, device_id={"group": z - 1}, device_id_type=mesh_id)

    @pl.when(z < depth - 1)
    def _():
        pl.semaphore_signal(barrier, inc=1, device_id={"group": z + 1}, device_id_type=mesh_id)

    pl.semaphore_wait(barrier, 3 + jnp.where(z > 0, 1, 0) + jnp.where(z < depth - 1, 1, 0))

    load.wait()
    own = z * 4 + slot
    step = 128
    full = piece_rows // step

    @pl.loop(0, full)
    def _(i):
        r = pl.ds(pl.multiple_of(i * step, step), step)
        buf[own, r, :] = rows32[r, :].astype(bf16)

    tail = rows32[piece_rows - tail_rows :, :]
    left = tail - tail.astype(bf16).astype(f32)
    zeros = jnp.zeros((padded - piece_rows - tail_rows, LANES), f32)
    buf[own, full * step :, :] = jnp.concatenate([rows32[full * step :, :], left, zeros], axis=0).astype(bf16)

    def copy_of(piece, h, send, recv, where):
        part = buf.at[piece, pl.ds(*cuts[h])]
        return pltpu.make_async_remote_copy(
            src_ref=part, dst_ref=part, send_sem=send, recv_sem=recv, device_id=where, device_id_type=mesh_id
        )

    def down(b, h):
        return copy_of(b * 4 + slot, h, zdown.at[b, h], zrecv.at[b, h], {"group": z + 1})

    def up(b, h):
        return copy_of(b * 4 + slot, h, zup.at[b, h], zrecv.at[b, h], {"group": z - 1})

    def side(b, h):
        return copy_of(b * 4 + slot, h, ysend.at[b, h], yrecv.at[b, h], {"slot": slot ^ 2})

    def side_in(b, h):
        return copy_of(b * 4 + (slot ^ 2), h, ysend.at[b, h], yrecv.at[b, h], {"slot": slot ^ 2})

    def twin(b, h, k):
        return copy_of(
            b * 4 + (slot ^ (2 * k)), h, csend.at[2 * b + k, h], crecv.at[2 * b + k, h], {"slot": slot ^ 1}
        )

    def twin_in(b, h, k):
        return copy_of(
            b * 4 + (slot ^ 1 ^ (2 * k)), h, csend.at[2 * b + k, h], crecv.at[2 * b + k, h], {"slot": slot ^ 1}
        )

    parts = range(len(cuts))
    tail_part = len(cuts) - 1
    order = [tail_part] + list(range(tail_part))
    last = depth - 1
    ranked = (
        z,
        jnp.where(z == 0, 1, 0),
        jnp.where(z == 0, 2, jnp.where(z == 1, 3, 1)),
        jnp.where((z == 0) | (z == 2), 3, 2),
    )
    middle = (z == 1) | (z == 2)
    edge = jnp.logical_not(middle)

    def pass_on(b, h, aside=True):
        up(b, h).wait_recv()

        @pl.when((b < z) & (z < last))
        def _():
            down(b, h).start()

        @pl.when((b > z) & (z > 0))
        def _():
            up(b, h).start()

        if aside:
            side(b, h).start()
        twin(b, h, 0).start()

    def serve_z(b, h, when=None, aside=True):
        if h == tail_part:
            when = (b != last) if when is None else when & (b != last)
        if when is None:
            pass_on(b, h, aside)
        else:
            pl.when(when)(functools.partial(pass_on, b, h, aside))

    def serve_y(rank, h):
        b = ranked[rank]

        def go():
            side_in(b, h).wait_recv()
            twin(b, h, 1).start()

        if h == tail_part:
            pl.when(b != last)(go)
        else:
            go()

    for number, h in enumerate(order):
        pl.when(z > 0)(lambda h=h: up(z, h).start())
        at_once = (z == 0) | ((z == 1) & (number < 2)) | ((z == 2) & (number < 3))
        pl.when(at_once)(lambda h=h: down(z, h).start())
        side(z, h).start()
        twin(z, h, 0).start()

    x_load.wait()
    x_copy = pltpu.make_async_remote_copy(
        src_ref=xbuf.at[pl.ds(0, half)],
        dst_ref=xbuf.at[pl.ds(half, half)],
        send_sem=xsem.at[0],
        recv_sem=xsem.at[1],
        device_id={"tensor": 1 - me},
        device_id_type=mesh_id,
    )
    x_copy.start()

    pl.when(z == last - 1)(functools.partial(pass_on, last, tail_part))
    for h in order:
        serve_z(ranked[3], h, middle, False)
        serve_z(ranked[1], h)
    pl.when(z < last - 1)(functools.partial(pass_on, last, tail_part))

    def side_later(h):
        aside = middle & (ranked[3] != last) if h == tail_part else middle
        pl.when(aside)(lambda: side(ranked[3], h).start())

    for number, h in enumerate(order):
        later = ((z == 1) & (number >= 2)) | ((z == 2) & (number >= 3))
        pl.when(later)(lambda h=h: down(z, h).start())
        if number < 2:
            side_later(h)
    for h in order:
        serve_z(ranked[2], h, middle)
    for h in order[2:]:
        side_later(h)
    for h in order:
        serve_z(ranked[2], h, z == 0)
    for h in order[:3]:
        serve_z(ranked[3], h, z == last)
    side_in(last, tail_part).wait_recv()
    twin(last, tail_part, 1).start()
    for rank in range(2):
        for h in order:
            serve_y(rank, h)
    for k in range(2):
        twin_in(last, tail_part, k).wait_recv()
        for rank in range(2):
            b = ranked[rank]
            for h in parts:
                if h == tail_part:
                    pl.when(b != last)(lambda b=b, h=h, k=k: twin_in(b, h, k).wait_recv())
                else:
                    twin_in(b, h, k).wait_recv()

    at = (piece_rows - tail_rows) // 16 * 16
    shift = piece_rows - tail_rows - at
    ends = buf[4 * depth - 1, at:, :].astype(f32)
    vectors = ends[shift : shift + tail_rows] + ends[shift + tail_rows : shift + 2 * tail_rows]
    vec_s[0] = vectors

    def to_partner(src, dst, send, recv):
        return pltpu.make_async_remote_copy(
            src_ref=src, dst_ref=dst, send_sem=send, recv_sem=recv,
            device_id={"tensor": 1 - me}, device_id_type=mesh_id,
        )

    vec_copy = to_partner(vec_s.at[0], vec_s.at[1], xsem.at[2], xsem.at[3])
    vec_copy.start()
    margin = 16
    (offset, rows, blocks) = table[0]
    bring_rows(buf, flat, margin, offset, rows * blocks, piece_rows)
    emit_matrix(flat, proj_s, margin, rows, blocks)
    out_copies = [pltpu.make_async_copy(proj_s, proj_out, local_sems.at[2])]
    out_copies[0].start()
    x_copy.wait()
    out_copies.append(pltpu.make_async_copy(xbuf, x_out, local_sems.at[3]))
    out_copies[1].start()
    query_bias = jnp.concatenate([vectors[j : j + 1] for j in range(blocks)], axis=1)
    value_bias = jnp.concatenate([vectors[blocks + j : blocks + j + 1] for j in range(blocks)], axis=1)
    depth_in = rows // 3
    for m, (ref, bias) in enumerate(((q_ref, query_bias), (k_ref, None), (v_ref, value_bias))):

        @pl.loop(0, n // 256)
        def _(i, m=m, ref=ref, bias=bias):
            r = pl.ds(pl.multiple_of(i * 256, 256), 256)
            acc = dot(xbuf[r, :], proj_s[m * depth_in : (m + 1) * depth_in, :], NN)
            if bias is not None:
                acc = acc + bias
            ref[r, :] = acc.astype(bf16)

    third = jnp.where(z == 0, ranked[3], ranked[2])
    todo = [functools.partial(serve_z, third, h, edge) for h in order]
    todo += [functools.partial(serve_z, ranked[3], h, z == last) for h in order[3:]]
    todo += [functools.partial(serve_y, 2, h) for h in order]

    def landed(rank):
        b = ranked[rank]
        for h in parts:
            for k in range(2):
                if h == tail_part:
                    pl.when(b != last)(lambda b=b, h=h, k=k: twin_in(b, h, k).wait_recv())
                else:
                    twin_in(b, h, k).wait_recv()

    (wo_offset, wo_rows, wo_blocks) = table[1]
    spans = piece_spans(wo_offset, wo_rows * wo_blocks, piece_rows, padded)
    total = sum(high - low for _, low, high, _ in spans)
    halves = (round_up(total // 2, 16), total)
    wo_parts = ([], [])
    at = 0
    for p, low, high, _ in spans:
        split = min(max(low + halves[0] - at, low), high)
        if split > low:
            wo_parts[0].append((p, low, split - low, at))
        if high > split:
            wo_parts[1].append((p, split, high - split, at + split - low))
        at += high - low
    in_core = slot % 2

    def wo_copies(c):
        return [
            to_partner(
                buf.at[p, pl.ds(low, count)], obuf.at[pl.ds(to, count)], wo_sems.at[0, j], wo_sems.at[1, j]
            )
            for j, (p, low, count, to) in enumerate(wo_parts[c])
        ]

    def wo_twin(c):
        first, end = (0, halves[0]) if c == 0 else halves
        part = obuf.at[pl.ds(first, end - first)]
        return pltpu.make_async_remote_copy(
            src_ref=part, dst_ref=part, send_sem=wo_sems.at[0, 3], recv_sem=wo_sems.at[1, 3],
            device_id={"slot": slot ^ 1}, device_id_type=mesh_id,
        )

    def by_core(action):
        for c in range(2):
            pl.when(in_core == c)(functools.partial(action, c))

    def wo_send(c):
        for copy in wo_copies(c):
            copy.start()

    def wo_pass(c):
        for copy in wo_copies(c):
            copy.wait_recv()
        wo_twin(c).start()

    def wo_done(c):
        wo_twin(1 - c).wait_recv()

    def wo_sent(c):
        for copy in wo_copies(c):
            copy.wait_send()
        wo_twin(c).wait_send()

    def ctx_copy(pair):
        columns = pl.ds(pair * LANES, LANES)
        return to_partner(
            ctx_ref.at[pl.ds(half, half), columns], ctx2_s.at[:, columns],
            ctx_sems.at[0, pair], ctx_sems.at[1, pair],
        )

    low = lax.broadcasted_iota(jnp.int32, (1, LANES), 1) < HD
    one = jnp.ones((), bf16)
    code = code_ref[...]
    for pair in range(blocks):
        c = slice(pair * LANES, (pair + 1) * LANES)
        k = k_ref[:, c]
        v = v_ref[:, c]
        v_ones = (jnp.where(low, v, one), jnp.where(low, one, v))
        for i in range(n // rows_q):
            r = slice(i * rows_q, (i + 1) * rows_q)
            ctx, lse_0, lse_1 = attend_block(q_ref[r, c], k, v_ones, code, seg_ref[r, :], i * rows_q)
            ctx_ref[r, c] = ctx
            lse_ref[pair, 0:1, r] = lse_0
            lse_ref[pair, 1:2, r] = lse_1
            if todo:
                todo.pop(0)()
            if (pair, i) == (2, n // rows_q - 1):
                for act in todo:
                    act()
                todo = []
                landed(2)
                by_core(wo_send)
        ctx_copy(pair).start()
    scratches = (None, outw_s, inw_s, down_s)
    mat_copies = [
        None,
        pltpu.make_async_copy(outw_s, outw_out, local_sems.at[4]),
        pltpu.make_async_copy(inw_s, inw_out, local_sems.at[5]),
        pltpu.make_async_copy(down_s, down_out, local_sems.at[6]),
    ]

    def matrix(m, first=0, end=None):
        (offset, rows, blocks) = table[m]
        count = (rows if end is None else end) - first
        bring_rows(buf, flat, margin, offset + first * blocks, count * blocks, piece_rows)
        emit_matrix(flat, scratches[m], margin, count, blocks, first)

    chunk_rows = 4 * piece_rows
    in_cut = (2 * chunk_rows - table[2][0]) // table[2][2] // 64 * 64
    down_cut = round_up(-(-(3 * chunk_rows - table[3][0]) // table[3][2]), 64)
    matrix(1)
    matrix(2, 0, in_cut)
    pl.when(ranked[3] == last)(lambda: matrix(2, in_cut))
    pl.when(ranked[3] != last)(lambda: matrix(3, down_cut))
    mat_copies[1].start()
    for h in order:
        serve_y(3, h)
    by_core(wo_pass)
    landed(3)

    @pl.when(ranked[3] == last)
    def _():
        mat_copies[2].start()
        matrix(3, 0, down_cut)
        matrix(3, down_cut)
        mat_copies[3].start()

    @pl.when(ranked[3] != last)
    def _():
        matrix(3, 0, down_cut)
        mat_copies[3].start()
        matrix(2, in_cut)
        mat_copies[2].start()

    by_core(wo_done)
    at = 0
    for p, low, high, to in spans:
        widen(obuf, at, at + high - low, flat, margin + to)
        at += high - low
    emit_matrix(flat, outw2_s, margin, wo_rows, wo_blocks)
    out_copies.append(pltpu.make_async_copy(outw2_s, outw2_out, local_sems.at[11]))
    out_copies[-1].start()

    vec_copy.wait()
    hidden_rows = table[2][2]
    for j in range(hidden_rows):
        c1_ref[0:1, j * LANES : (j + 1) * LANES] = vec_s[0, 2 * blocks + j : 2 * blocks + j + 1, :]
    for row in range(6):
        for j in range(blocks):
            from_row = 2 * blocks + hidden_rows + row * blocks + j
            mine, theirs = vec_s[0, from_row : from_row + 1, :], vec_s[1, from_row : from_row + 1, :]
            left, right = jnp.where(me == 0, mine, theirs), jnp.where(me == 0, theirs, mine)
            vec_ref[row : row + 1, j * LANES : (j + 1) * LANES] = left
            vec_ref[row : row + 1, (blocks + j) * LANES : (blocks + j + 1) * LANES] = right

    for pair in range(blocks):
        ctx_copy(pair).wait()
    out_copies.append(pltpu.make_async_copy(ctx2_s, ctx2_out, local_sems.at[12]))
    out_copies[-1].start()
    by_core(wo_sent)
    for b in range(depth):
        copy = pltpu.make_async_copy(buf.at[b * 4 + slot], pieces_out.at[b], local_sems.at[7 + b])
        copy.start()
        out_copies.append(copy)
    out_copies += mat_copies[1:]

    for b in range(depth):
        for h in parts:

            @pl.when((b <= z) & (z < depth - 1))
            def _(b=b, h=h):
                down(b, h).wait_send()

            @pl.when((b >= z) & (z > 0))
            def _(b=b, h=h):
                up(b, h).wait_send()

            side(b, h).wait_send()
            for k in range(2):
                twin(b, h, k).wait_send()
    for copy in out_copies:
        copy.wait()


def start(own_rows, tokens, code_row, seg_col, table, tail_rows, padded, cuts, rows_q=256):
    piece_rows = own_rows.shape[0]
    half, width = tokens.shape
    n = 2 * half
    pairs = table[0][2]
    local_width = pairs * LANES
    hbm = pl.BlockSpec(memory_space=pl.ANY)
    whole = pl.BlockSpec(memory_space=pltpu.VMEM)
    mats = [jax.ShapeDtypeStruct((rows, blocks * LANES), bf16) for _, rows, blocks in table]
    acts = [jax.ShapeDtypeStruct((n, local_width), bf16)] * 4
    most = max(rows * blocks for _, rows, blocks in table)
    parts = len(cuts)
    dma = pltpu.SemaphoreType.DMA
    return pl.pallas_call(
        functools.partial(
            start_kernel, piece_rows=piece_rows, tail_rows=tail_rows, table=table, cuts=cuts, rows_q=rows_q
        ),
        in_specs=[hbm, hbm, whole, whole],
        out_specs=[hbm] * 8 + [whole] * 7,
        out_shape=mats
        + [
            mats[1],
            jax.ShapeDtypeStruct((half, local_width), bf16),
            jax.ShapeDtypeStruct((GROUPS, padded, LANES), bf16),
            jax.ShapeDtypeStruct((n, width), bf16),
            jax.ShapeDtypeStruct((6, width), f32),
            jax.ShapeDtypeStruct((1, table[2][2] * LANES), f32),
        ]
        + acts
        + [jax.ShapeDtypeStruct((pairs, 2, n), f32)],
        scratch_shapes=[
            pltpu.VMEM((piece_rows, LANES), f32),
            pltpu.VMEM((4 * GROUPS, padded, LANES), bf16),
            pltpu.VMEM((n, width), bf16),
            pltpu.VMEM((most + 48, LANES), f32),
        ]
        + [pltpu.VMEM(m.shape, bf16) for m in mats]
        + [
            pltpu.VMEM(mats[1].shape, bf16),
            pltpu.VMEM((round_up(table[1][1] * table[1][2] + 64, 16), LANES), bf16),
            pltpu.VMEM((half, local_width), bf16),
            pltpu.VMEM((2, tail_rows, LANES), f32),
            dma((GROUPS, parts)),
            dma((GROUPS, parts)),
            dma((GROUPS, parts)),
            dma((GROUPS, parts)),
            dma((GROUPS, parts)),
            dma((2 * GROUPS, parts)),
            dma((2 * GROUPS, parts)),
            dma((4,)),
            dma((13,)),
            dma((2, pairs)),
            dma((2, 4)),
        ],
        cost_estimate=pl.CostEstimate(
            flops=6 * n * width * local_width, bytes_accessed=60 << 20, transcendentals=8 * n * n
        ),
        compiler_params=params(collective_id=1, has_side_effects=True),
        name="start",
    )(own_rows, tokens, code_row, seg_col)


ERF = (0.254829592, -0.284496736, 1.421413741, -1.453152027, 1.061405429)
ERF_P = 0.3275911


def gelu_pair(u):
    bell = jnp.exp(-0.5 * u * u)
    t = 1.0 / (1.0 + (ERF_P * ROOT_HALF) * jnp.abs(u))
    poly = ERF[4]
    for number in ERF[3::-1]:
        poly = poly * t + number
    tail = (0.5 * poly * t) * bell
    phi = jnp.where(u >= 0, 1.0 - tail, tail)
    return u * phi, phi + u * bell * INV_ROOT_TWO_PI


def fold(values):
    return values.reshape(values.shape[0] // 8, 8, values.shape[1]).sum(axis=0)


def middle_kernel(
    ctx_ref, ctx2_ref, tokens_ref, cot_ref, vec_ref, c1_ref, outw_ref, outw2_ref, inw_ref, down_ref,
    block_out, dh1_out, dctx_out, d_outw, d_inw, d_down, tail_out,
    x1, norm1, inv1, x1_all, act, slope, dh2_all, dh1_all, part, dh2, box_send, box_recv, sums, c1_sum, vec_box, send_sems, recv_sems, vec_sems,
    *, chunk
):
    me = lax.axis_index("tensor")
    half, width = tokens_ref.shape
    count = half // chunk
    mesh_id = pl.DeviceIdType.MESH
    other = {"tensor": 1 - me}
    barrier = pltpu.get_barrier_semaphore()
    pl.semaphore_signal(barrier, inc=1, device_id=other, device_id_type=mesh_id)
    pl.semaphore_wait(barrier, 1)

    def rows_of(i):
        return pl.ds(pl.multiple_of(i * chunk, chunk), chunk)

    def far_rows(i):
        return pl.ds(pl.multiple_of(half + i * chunk, chunk), chunk)

    def summed(stage, i):
        return pltpu.make_async_remote_copy(
            src_ref=box_send.at[stage, rows_of(i)],
            dst_ref=box_recv.at[stage, rows_of(i)],
            send_sem=send_sems.at[stage, i],
            recv_sem=recv_sems.at[stage, i],
            device_id=other,
            device_id_type=mesh_id,
        )

    def gathered(stage, ref, i):
        return pltpu.make_async_remote_copy(
            src_ref=ref.at[rows_of(i)],
            dst_ref=ref.at[far_rows(i)],
            send_sem=send_sems.at[2 + stage, i],
            recv_sem=recv_sems.at[2 + stage, i],
            device_id=other,
            device_id_type=mesh_id,
        )

    gain_1, shift_1 = vec_ref[0:1, :], vec_ref[1:2, :]
    gain_2, shift_2 = vec_ref[2:3, :], vec_ref[3:4, :]
    bias_o, bias_2 = vec_ref[4:5, :], vec_ref[5:6, :]
    sums[...] = jnp.zeros_like(sums)
    c1_sum[...] = jnp.zeros_like(c1_sum)

    def normed(h):
        centred = h - jnp.mean(h, axis=-1, keepdims=True)
        inv = lax.rsqrt(jnp.mean(centred * centred, axis=-1, keepdims=True) + NORM_EPS)
        return centred * inv, inv

    def normed_back(dn, n, inv):
        return inv * (
            dn - jnp.mean(dn, axis=-1, keepdims=True) - n * jnp.mean(dn * n, axis=-1, keepdims=True)
        )

    def forward(r):
        u = dot(x1_all[r, :], inw_ref[...], NN) + c1_ref[...]
        a, s = gelu_pair(u)
        act[r, :] = a.astype(bf16)
        slope[r, :] = s.astype(bf16)
        return dot(act[r, :], down_ref[...], NN)

    def backward(r):
        da = dot(dh2_all[r, :], down_ref[...], NT)
        du = da * slope[r, :].astype(f32)
        low = du.astype(bf16)
        slope[r, :] = low
        c1_sum[...] += fold(low.astype(f32))
        return dot(low, inw_ref[...], NT)

    @pl.loop(0, count)
    def _(i):
        r = rows_of(i)
        branch = dot(ctx_ref[r, :], outw_ref[...], NN) + dot(ctx2_ref[r, :], outw2_ref[...], NN)
        h = tokens_ref[r, :].astype(f32) + (branch + bias_o)
        n, inv = normed(h)
        norm1[r, :] = n
        inv1[r, :] = jnp.broadcast_to(inv, (chunk, LANES))
        middle = n * gain_1 + shift_1
        x1[r, :] = middle
        x1_all[r, :] = middle.astype(bf16)
        gathered(0, x1_all, i).start()
        part[r, :] = forward(r)

    @pl.loop(0, count)
    def _(i):
        gathered(0, x1_all, i).wait_recv()
        box_send[0, rows_of(i), :] = forward(far_rows(i)).astype(bf16)
        summed(0, i).start()

    @pl.loop(0, count)
    def _(i):
        r = rows_of(i)
        summed(0, i).wait_recv()
        h = x1[r, :] + (part[r, :] + box_recv[0, r, :].astype(f32) + bias_2)
        n, inv = normed(h)
        block_out[r, :] = (n * gain_2 + shift_2).astype(bf16)
        dy = cot_ref[r, :].astype(f32)
        dh = normed_back(dy * gain_2, n, inv)
        sums[2] += fold(dy * n)
        sums[3] += fold(dy)
        sums[5] += fold(dh)
        dh2[r, :] = dh
        dh2_all[r, :] = dh.astype(bf16)
        gathered(1, dh2_all, i).start()
        part[r, :] = backward(r)

    @pl.loop(0, count)
    def _(i):
        gathered(1, dh2_all, i).wait_recv()
        box_send[1, rows_of(i), :] = backward(far_rows(i)).astype(bf16)
        summed(1, i).start()

    hidden = act.shape[1]
    block = hidden // 8

    def down_grad(j):
        c = pl.ds(pl.multiple_of(j * block, block), block)
        d_down[c, :] = dot(act[:, c].T, dh2_all[...], NN).astype(bf16)

    def in_grad(j):
        c = pl.ds(pl.multiple_of(j * block, block), block)
        d_inw[:, c] = dot(x1_all[...].T, slope[:, c], NN).astype(bf16)

    per_chunk = 8 // count

    @pl.loop(0, count)
    def _(i):
        for j in range(per_chunk):
            down_grad(i * per_chunk + j)
        r = rows_of(i)
        summed(1, i).wait_recv()
        dx = dh2[r, :] + part[r, :] + box_recv[1, r, :].astype(f32)
        n = norm1[r, :]
        dh = normed_back(dx * gain_1, n, inv1[r, 0:1])
        sums[0] += fold(dx * n)
        sums[1] += fold(dx)
        sums[4] += fold(dh)
        dh1_out[r, :] = dh
        dh1_all[r, :] = dh.astype(bf16)
        gathered(2, dh1_all, i).start()
        dctx_out[r, :] = dot(dh1_all[r, :], outw_ref[...], NT).astype(bf16)

    for row in range(6):
        total = jnp.sum(sums[row], axis=0, keepdims=True)
        low, high = total[:, : width // 2], total[:, width // 2 :]
        mine, theirs = jnp.where(me == 0, low, high), jnp.where(me == 0, high, low)
        spread = width // 2 // LANES
        for j in range(spread):
            at = row * spread + j
            vec_box[0, at : at + 1, :] = mine[:, j * LANES : (j + 1) * LANES]
            vec_box[1, at : at + 1, :] = theirs[:, j * LANES : (j + 1) * LANES]
    vec_copy = pltpu.make_async_remote_copy(
        src_ref=vec_box.at[1],
        dst_ref=vec_box.at[2],
        send_sem=vec_sems.at[0],
        recv_sem=vec_sems.at[1],
        device_id=other,
        device_id_type=mesh_id,
    )
    vec_copy.start()

    @pl.loop(0, count)
    def _(i):
        for j in range(per_chunk):
            in_grad(i * per_chunk + j)
        r = far_rows(i)
        gathered(2, dh1_all, i).wait_recv()
        dctx_out[r, :] = dot(dh1_all[r, :], outw_ref[...], NT).astype(bf16)

    d_outw[...] = dot(ctx_ref[...].T, dh1_all[...], NN).astype(bf16)

    blocks = ctx_ref.shape[1] // LANES
    tail_out[0 : 2 * blocks, :] = jnp.zeros((2 * blocks, LANES), f32)
    c1_total = jnp.sum(c1_sum[...], axis=0, keepdims=True)
    for j in range(hidden // LANES):
        tail_out[2 * blocks + j : 2 * blocks + j + 1, :] = c1_total[:, j * LANES : (j + 1) * LANES]
    vec_copy.wait()
    tail_out[2 * blocks + hidden // LANES :, :] = vec_box[0] + vec_box[2]

    @pl.loop(0, count)
    def _(i):
        for stage in range(2):
            summed(stage, i).wait_send()
        gathered(0, x1_all, i).wait_send()
        gathered(1, dh2_all, i).wait_send()
        gathered(2, dh1_all, i).wait_send()


def middle(context, context_2, tokens, cotangent, vectors, inner_bias, out_w, out_w2, in_w, down_w, chunk=128):
    half, width = tokens.shape
    n = 2 * half
    hidden = in_w.shape[1]
    local_width = context.shape[1]
    whole = pl.BlockSpec(memory_space=pltpu.VMEM)
    wide = pltpu.VMEM((half, width), f32)
    every = pltpu.VMEM((n, width), bf16)
    box = pltpu.VMEM((2, half, width), bf16)
    count = half // chunk
    return pl.pallas_call(
        functools.partial(middle_kernel, chunk=chunk),
        in_specs=[whole] * 10,
        out_specs=[whole] * 7,
        out_shape=[
            jax.ShapeDtypeStruct((half, width), bf16),
            jax.ShapeDtypeStruct((half, width), f32),
            jax.ShapeDtypeStruct((n, local_width), bf16),
            jax.ShapeDtypeStruct(out_w.shape, bf16),
            jax.ShapeDtypeStruct(in_w.shape, bf16),
            jax.ShapeDtypeStruct(down_w.shape, bf16),
            jax.ShapeDtypeStruct(((2 * local_width + hidden + 3 * width) // LANES, LANES), f32),
        ],
        scratch_shapes=[
            wide,
            wide,
            pltpu.VMEM((half, LANES), f32),
            every,
            pltpu.VMEM((n, hidden), bf16),
            pltpu.VMEM((n, hidden), bf16),
            every,
            every,
            wide,
            wide,
            box,
            box,
            pltpu.VMEM((6, 8, width), f32),
            pltpu.VMEM((8, hidden), f32),
            pltpu.VMEM((3, 3 * width // LANES, LANES), f32),
            pltpu.SemaphoreType.DMA((5, count)),
            pltpu.SemaphoreType.DMA((5, count)),
            pltpu.SemaphoreType.DMA((2,)),
        ],
        cost_estimate=pl.CostEstimate(
            flops=14 * n * width * hidden, bytes_accessed=40 << 20, transcendentals=2 * n * hidden
        ),
        compiler_params=params(collective_id=2, has_side_effects=True),
        name="middle",
    )(context, context_2, tokens, cotangent, vectors, inner_bias, out_w, out_w2, in_w, down_w)


def attend_back(q_ref, k_ref, v_ref, ctx_ref, dctx_ref, code, seg_ref, lse_ref, dq_ref, dk_ref, dv_ref, pair, rows_q, after_step):
    n = q_ref.shape[0]
    c = slice(pair * LANES, (pair + 1) * LANES)
    low = lax.broadcasted_iota(jnp.int32, (1, LANES), 1) < HD
    zero = jnp.zeros((), bf16)
    k = k_ref[:, c]
    v = v_ref[:, c]
    k_t = k.T
    pick = (
        lax.broadcasted_iota(jnp.int32, (8, LANES), 1) // HD
        == lax.broadcasted_iota(jnp.int32, (8, LANES), 0)
    ).astype(f32)
    dks = [jnp.zeros((n, LANES), f32)] * 2
    dvs = [jnp.zeros((n, LANES), f32)] * 2
    scale = jnp.asarray(HD**-0.5, bf16)
    for i in range(n // rows_q):
        r = slice(i * rows_q, (i + 1) * rows_q)
        q = q_ref[r, c] * scale
        do = dctx_ref[r, c]
        prod = do.astype(f32) * ctx_ref[r, c].astype(f32)
        delta = lax.dot_general(
            pick, prod, NT, precision=lax.Precision.HIGHEST, preferred_element_type=f32
        )
        keys = lax.broadcasted_iota(jnp.int32, (n, rows_q), 0)
        qs = lax.broadcasted_iota(jnp.int32, (n, rows_q), 1) + i * rows_q
        allowed = (code == seg_ref[:, r]) | (keys == qs)
        dqs = []
        for h in range(2):
            qh = jnp.where(low, q, zero) if h == 0 else jnp.where(low, zero, q)
            doh = jnp.where(low, do, zero) if h == 0 else jnp.where(low, zero, do)
            s = jnp.where(allowed, dot(k, qh, NT), MASKED)
            p = jnp.exp(s - lse_ref[pair, h : h + 1, r])
            dp = dot(v, doh, NT)
            ds = (p * (dp - delta[h : h + 1])).astype(bf16)
            dvs[h] = dvs[h] + dot(p.astype(bf16), do, NN)
            dks[h] = dks[h] + dot(ds, q, NN)
            dqs.append(dot(k_t[h * HD : (h + 1) * HD], ds, NN))
        dq_ref[r, c] = (jnp.concatenate(dqs, axis=0).T * (HD**-0.5)).astype(bf16)
        after_step(i)
    dk_ref[:, c] = jnp.where(low, dks[0], dks[1]).astype(bf16)
    dv_ref[:, c] = jnp.where(low, dvs[0], dvs[1]).astype(bf16)


def lay_flat(ref, low, high, blocks, flat, at):
    chunk = 16 if (high - low) % 64 else 64

    @pl.loop(0, (high - low) // chunk)
    def _(c):
        rows = pl.ds(pl.multiple_of(low + c * chunk, 16), chunk)
        for j in range(blocks):
            to_rows = pl.ds(at + c * (chunk * blocks) + j, chunk, stride=blocks)
            flat[to_rows, :] = ref[rows, j * LANES : (j + 1) * LANES].astype(f32)


def emit_pieces(flat, keep, send, slot, skip, piece_rows):
    padded = send.shape[1]
    step = 128
    full = piece_rows // step
    rest = piece_rows - full * step
    for j in (3, 1, 2, 0):
        out = send if j % 2 else keep
        start = skip + (slot ^ j) * piece_rows

        @pl.loop(0, full)
        def _(i, out=out, j=j, start=start):
            rows = flat[pl.ds(start + i * step, step), :]
            out[j // 2, pl.ds(pl.multiple_of(i * step, step), step), :] = rows.astype(bf16)

        parts = [jnp.zeros((padded - piece_rows, LANES), f32)]
        if rest:
            parts = [flat[pl.ds(start + full * step, rest), :]] + parts
        out[j // 2, full * step : padded, :] = jnp.concatenate(parts, axis=0).astype(bf16)


def back_kernel(
    q_ref, k_ref, v_ref, ctx_ref, dctx_ref, code_ref, seg_ref, lse_ref, x_ref, outw_ref, tail_ref,
    inw_hbm, down_hbm, m_hbm, v_hbm, w_hbm, proj_hbm,
    g_out, d_out, dx_out,
    dq_ref, dk_ref, dv_ref,
    flat, down_s, inw_s, keep, send, near, far, tails, zin, g_stage, m_in, v_in, w_in,
    near_send, near_recv, far_send, far_recv, tail_send, tail_recv, z_send, z_recv, load_sems, out_sems,
    x_sems, x_free,
    *, plans, piece_rows, cuts, rows_q
):
    me = lax.axis_index("tensor")
    z = lax.axis_index("group")
    slot = lax.axis_index("slot")
    last = GROUPS - 1
    mesh_id = pl.DeviceIdType.MESH
    core = {"slot": slot ^ 1}
    side = {"slot": slot ^ 2}
    tail_rows = tail_ref.shape[0]
    padded = send.shape[1]
    stage_loads = [
        pltpu.make_async_copy(down_hbm, down_s, load_sems.at[0]),
        pltpu.make_async_copy(inw_hbm, inw_s, load_sems.at[1]),
    ]
    for copy in stage_loads:
        copy.start()
    barrier = pltpu.get_barrier_semaphore()
    for where in (core, side, {"tensor": 1 - me}):
        pl.semaphore_signal(barrier, inc=1, device_id=where, device_id_type=mesh_id)

    @pl.when(z > 0)
    def _():
        pl.semaphore_signal(barrier, inc=1, device_id={"group": z - 1}, device_id_type=mesh_id)

    @pl.when(z < last)
    def _():
        pl.semaphore_signal(barrier, inc=1, device_id={"group": z + 1}, device_id_type=mesh_id)

    pl.semaphore_wait(barrier, 3 + jnp.where(z > 0, 1, 0) + jnp.where(z < last, 1, 0))

    def to_core(b, j):
        return pltpu.make_async_remote_copy(
            src_ref=send.at[j],
            dst_ref=near.at[b, j],
            send_sem=near_send.at[b, j],
            recv_sem=near_recv.at[b, j],
            device_id=core,
            device_id_type=mesh_id,
        )

    def to_side(b, h):
        rows = pl.ds(*cuts[h])
        return pltpu.make_async_remote_copy(
            src_ref=keep.at[b, 1, rows],
            dst_ref=far.at[b, rows],
            send_sem=far_send.at[b, h],
            recv_sem=far_recv.at[b, h],
            device_id=side,
            device_id_type=mesh_id,
        )

    def tail_copy(k, where):
        return pltpu.make_async_remote_copy(
            src_ref=tails.at[2 * k],
            dst_ref=tails.at[2 * k + 1],
            send_sem=tail_send.at[k],
            recv_sem=tail_recv.at[k],
            device_id=where,
            device_id_type=mesh_id,
        )

    def along(b, h, landing, where):
        return pltpu.make_async_remote_copy(
            src_ref=keep.at[b, 0, pl.ds(*cuts[h])],
            dst_ref=zin.at[landing, pl.ds(*cuts[h])],
            send_sem=z_send.at[b, h],
            recv_sem=z_recv.at[landing, h],
            device_id=where,
            device_id_type=mesh_id,
        )

    def upward(b, h):
        return along(b, h, b, {"group": z + 1})

    def downward(b, h):
        return along(b, h, jnp.where(z - 1 == b, GROUPS, b), {"group": z - 1})

    def hand_over(b):
        for j in (1, 0):
            to_core(b, j).start()

    def pass_aside(b):
        to_core(b, 1).wait_recv()
        for h, (start, rows) in enumerate(cuts):

            def add(at, count):
                r = pl.ds(at, count)
                keep[b, 1, r, :] = (keep[b, 1, r, :].astype(f32) + near[b, 1, r, :].astype(f32)).astype(bf16)

            in_steps(start, rows, 128, add)
            to_side(b, h).start()

    def sent(b):
        for j in (1, 0):
            to_core(b, j).wait_send()

    def loads(b):
        rows = pl.ds(0, piece_rows)
        return (
            pltpu.make_async_copy(m_hbm.at[rows, b, :], m_in.at[rows], load_sems.at[2]),
            pltpu.make_async_copy(v_hbm.at[rows, b, :], v_in.at[rows], load_sems.at[3]),
            pltpu.make_async_copy(w_hbm.at[b, pl.ds(0, padded)], w_in, load_sems.at[4]),
        )

    def store(b, h):
        rows = pl.ds(*cuts[h])
        return pltpu.make_async_copy(g_stage.at[rows], g_out.at[b, rows], out_sems.at[b, h])

    turn = (1, 2, 3, 0)

    def differ(b, h):
        k = turn.index(b)
        start, count = cuts[h]
        if h == 0:
            to_core(b, 0).wait_recv()
            for copy in loads(b):
                copy.wait()
        to_side(b, h).wait_recv()
        if b == last and h == len(cuts) - 1:
            at = piece_rows - tail_rows
            low = at // 16 * 16
            extra = jnp.where(slot == last, tails[2] + tails[3], 0.0)
            around = [extra]
            if at > low:
                around = [jnp.zeros((at - low, LANES), f32)] + around
            if padded > piece_rows:
                around = around + [jnp.zeros((padded - piece_rows, LANES), f32)]
            ends = slice(low, padded)
            far[b, ends, :] = (far[b, ends, :].astype(f32) + jnp.concatenate(around, axis=0)).astype(bf16)
        if k:
            store(turn[k - 1], h).wait()

        def step(at, rows):
            r = pl.ds(at, rows)
            g = keep[b, 0, r, :].astype(f32) + near[b, 0, r, :].astype(f32) + far[b, r, :].astype(f32)
            g_stage[r, :] = g
            first = BETA_ONE * m_in[r, :] + (1 - BETA_ONE) * g
            second = BETA_TWO * v_in[r, :] + (1 - BETA_TWO) * g * g
            root = jnp.sqrt(second * (1 / (1 - BETA_TWO**STEP))) + ADAM_EPS
            decay = INNER_RATE * DECAY
            if b == last:
                here = lax.broadcasted_iota(jnp.int32, (rows, LANES), 0) + at
                decay = jnp.where((slot < last) | (here < piece_rows - tail_rows), decay, 0.0)
            d = (INNER_RATE / (1 - BETA_ONE**STEP)) * first / root + decay * w_in[r, :].astype(f32)
            keep[b, 0, r, :] = d.astype(bf16)

        in_steps(start, count, 128, step)
        store(b, h).start()
        if b > 0:
            pl.when(z == 0)(lambda: upward(b, h).start())
        if b < last:
            pl.when(z == last)(lambda: downward(b, h).start())
        if h == len(cuts) - 1 and k + 1 < GROUPS:
            for copy in loads(turn[k + 1]):
                copy.start()

    def hop(b, at, h):
        def go():
            along(b, h, b, {"group": z}).wait_recv()

            def add(at, count):
                r = pl.ds(at, count)
                keep[b, 0, r, :] = (keep[b, 0, r, :].astype(f32) + zin[b, r, :].astype(f32)).astype(bf16)

            in_steps(*cuts[h], 128, add)
            (upward if at < b else downward)(b, h).start()

        pl.when(z == at)(go)

    blank = slice(piece_rows, padded)
    m_in[blank, :] = jnp.zeros((padded - piece_rows, LANES), f32)
    v_in[blank, :] = jnp.zeros((padded - piece_rows, LANES), f32)
    for copy in loads(turn[0]):
        copy.start()
    for copy in stage_loads:
        copy.wait()

    refs = {1: outw_ref, 2: inw_s, 3: down_s}
    for number_of, b in enumerate(turn[:3]):
        segments, skip, has_tail = plans[b]
        for number, low, high, blocks, at in segments:
            lay_flat(refs[number], low, high, blocks, flat, at)
        if has_tail:
            at = skip + 4 * piece_rows - tail_rows
            flat[pl.ds(at, tail_rows), :] = jnp.zeros((tail_rows, LANES), f32)
        if number_of:
            pass_aside(turn[number_of - 1])
            sent(turn[number_of - 1])
        emit_pieces(flat, keep.at[b], send, slot, skip, piece_rows)
        hand_over(b)

    half = q_ref.shape[0] // 2
    local_width = q_ref.shape[1]
    depth_in = x_ref.shape[1]
    pl.semaphore_signal(x_free, inc=1, device_id={"tensor": 1 - me}, device_id_type=mesh_id)
    proj_loads = [
        pltpu.make_async_copy(
            proj_hbm.at[pl.ds(m * depth_in, depth_in)],
            inw_s.at[:, pl.ds(m * local_width, local_width)],
            x_sems.at[2 + m],
        )
        for m in range(3)
    ]
    for copy in proj_loads:
        copy.start()

    parts = range(len(cuts))
    act = functools.partial
    events = {
        0: [act(pass_aside, 3)],
        1: [act(differ, 1, 0)],
        2: [act(differ, 1, 1)],
        3: [act(differ, 1, 2)],
        4: [act(differ, 1, 3)],
        5: [act(hop, 1, 2, 0)],
        6: [act(differ, 2, 0)],
        7: [act(hop, 1, 2, 1)],
        8: [act(differ, 2, 1)],
        9: [act(hop, 1, 2, 2)],
        10: [act(differ, 2, 2)],
        11: [act(hop, 1, 2, 3)],
        13: [act(differ, 2, 3)],
        14: [act(hop, 2, 1, 0)],
        15: [act(hop, 2, 1, 1)],
    }
    blocks = q_ref.shape[1] // LANES
    code = code_ref[...]
    per_pair = q_ref.shape[0] // rows_q

    def after_step(number):
        for act in events.get(number, ()):
            act()

    for pair in range(blocks):
        attend_back(
            q_ref, k_ref, v_ref, ctx_ref, dctx_ref, code, seg_ref, lse_ref, dq_ref, dk_ref, dv_ref, pair, rows_q,
            lambda i, pair=pair: after_step(pair * per_pair + i),
        )

    tails[0] = tail_ref[...]
    for m, ref in enumerate((dq_ref, dv_ref)):
        total = jnp.sum(ref[...].astype(f32), axis=0, keepdims=True)
        for j in range(blocks):
            row = m * blocks + j
            tails[0, row : row + 1, :] = total[:, j * LANES : (j + 1) * LANES]
    tail_copy(0, core).start()

    chunk = 256
    segments, skip, _ = plans[0]
    for m, ref in enumerate((dq_ref, dk_ref, dv_ref)):

        @pl.loop(0, depth_in // chunk)
        def _(c, m=m, ref=ref):
            columns = pl.ds(pl.multiple_of(c * chunk, chunk), chunk)
            acc = dot(x_ref[:, columns].T, ref[...], NN)
            for j in range(blocks):
                to_rows = pl.ds((m * depth_in + c * chunk) * blocks + j, chunk, stride=blocks)
                flat[to_rows, :] = acc[:, j * LANES : (j + 1) * LANES]

        if m == 0:
            tail_copy(0, core).wait()
            tails[2] = tails[0] + tails[1]
            tail_copy(1, side).start()
            hop(2, 1, 2)
        if m == 1:
            hop(2, 1, 3)

    for number, low, high, wide, at in segments:
        if number:
            lay_flat(refs[number], low, high, wide, flat, at)
    sent(3)
    emit_pieces(flat, keep.at[0], send, slot, skip, piece_rows)
    hand_over(0)
    pass_aside(0)
    tail_copy(1, side).wait()
    for h in parts:
        differ(3, h)

    for copy in proj_loads:
        copy.wait()

    def through(row):
        r = pl.ds(row, 256)
        acc = dot(dq_ref[r, :], inw_s[:, 0:local_width], NT)
        acc = acc + dot(dk_ref[r, :], inw_s[:, local_width : 2 * local_width], NT)
        return acc + dot(dv_ref[r, :], inw_s[:, 2 * local_width : 3 * local_width], NT)

    @pl.loop(0, half // 256)
    def _(i):
        down_s[pl.ds(pl.multiple_of(i * 256, 256), 256), :] = through(
            pl.multiple_of(half + i * 256, 256)
        ).astype(bf16)

    pl.semaphore_wait(x_free, 1)
    x_copy = pltpu.make_async_remote_copy(
        src_ref=down_s.at[pl.ds(0, half)],
        dst_ref=down_s.at[pl.ds(half, half)],
        send_sem=x_sems.at[0],
        recv_sem=x_sems.at[1],
        device_id={"tensor": 1 - me},
        device_id_type=mesh_id,
    )
    x_copy.start()
    differ(0, 0)

    @pl.loop(0, half // 256)
    def _(i):
        down_s[pl.ds(pl.multiple_of(2 * half + i * 256, 256), 256), :] = through(
            pl.multiple_of(i * 256, 256)
        ).astype(bf16)

    differ(0, 1)
    hop(3, 1, 0)
    hop(0, 2, 0)
    differ(0, 2)
    hop(3, 1, 1)
    hop(3, 2, 0)
    hop(0, 2, 1)
    differ(0, 3)
    for h in parts:
        if h > 1:
            hop(3, 1, h)
            hop(0, 2, h)
        hop(0, 1, h)
        if h:
            hop(3, 2, h)

    for h in parts:
        store(0, h).wait()
    for b in range(GROUPS):

        def finish(b=b):
            for h in parts:
                if b > 0:
                    along(b, h, b, {"group": z}).wait_recv()
                if b < last:
                    along(b, h, GROUPS, {"group": z}).wait_recv()

                def add(at, count):
                    r = pl.ds(at, count)
                    total = keep[b, 0, r, :].astype(f32)
                    if b > 0:
                        total = total + zin[b, r, :].astype(f32)
                    if b < last:
                        total = total + zin[GROUPS, r, :].astype(f32)
                    g_stage[r, :] = total

                in_steps(*cuts[h], 128, add)

        pl.when(z == b)(finish)
    x_copy.wait()
    dx_copy = pltpu.make_async_copy(down_s.at[pl.ds(half, 2 * half)], dx_out, x_sems.at[5])
    dx_copy.start()
    copy = pltpu.make_async_copy(g_stage, d_out, out_sems.at[GROUPS, 0])
    copy.start()
    for b in range(GROUPS):
        for h in parts:
            to_side(b, h).wait_send()

            @pl.when(z != b)
            def _(b=b, h=h):
                along(b, h, b, {"group": z}).wait_send()

    sent(0)
    copy.wait()
    dx_copy.wait()


def back(
    q, k, v, ctx, dctx, code_col, seg_row, lse, x_all, d_outw, tail, d_inw, d_down, first, second, pieces, proj_w,
    table, tail_at, piece_rows, rows_q=256
):
    per = 4
    padded = round_up(piece_rows, 16)
    tail_rows = tail.shape[0]
    plans = []
    most = 0
    for b in range(GROUPS):
        begin = b * per * piece_rows
        segments, base, size = chunk_plan(table, begin, begin + per * piece_rows, tail_at, tail_rows)
        plans.append((segments, begin - base, begin + per * piece_rows > tail_at))
        most = max(most, size)
    marks = [padded * i // 4 // 16 * 16 for i in range(4)] + [padded]
    cuts = [(low, high - low) for low, high in zip(marks[:-1], marks[1:])]
    whole = pl.BlockSpec(memory_space=pltpu.VMEM)
    hbm = pl.BlockSpec(memory_space=pl.ANY)
    dma = pltpu.SemaphoreType.DMA
    n, local_width = q.shape
    grad = pltpu.VMEM((n, local_width), bf16)
    wide = pltpu.VMEM((padded, LANES), f32)
    return pl.pallas_call(
        functools.partial(back_kernel, plans=plans, piece_rows=piece_rows, cuts=cuts, rows_q=rows_q),
        in_specs=[whole] * 11 + [hbm] * 6,
        out_specs=[hbm] * 3,
        out_shape=[
            jax.ShapeDtypeStruct((GROUPS, padded, LANES), f32),
            jax.ShapeDtypeStruct((padded, LANES), f32),
            jax.ShapeDtypeStruct((n, x_all.shape[1]), bf16),
        ],
        scratch_shapes=[
            grad,
            grad,
            grad,
            pltpu.VMEM((round_up(most, 8) + 8, LANES), f32),
            pltpu.VMEM(d_down.shape, bf16),
            pltpu.VMEM(d_inw.shape, bf16),
            pltpu.VMEM((GROUPS, 2, padded, LANES), bf16),
            pltpu.VMEM((2, padded, LANES), bf16),
            pltpu.VMEM((GROUPS, 2, padded, LANES), bf16),
            pltpu.VMEM((GROUPS, padded, LANES), bf16),
            pltpu.VMEM((4, tail_rows, LANES), f32),
            pltpu.VMEM((GROUPS + 1, padded, LANES), bf16),
            wide,
            wide,
            wide,
            pltpu.VMEM((padded, LANES), bf16),
            dma((GROUPS, 2)),
            dma((GROUPS, 2)),
            dma((GROUPS, 4)),
            dma((GROUPS, 4)),
            dma((2,)),
            dma((2,)),
            dma((GROUPS, 4)),
            dma((GROUPS + 1, 4)),
            dma((5,)),
            dma((GROUPS + 1, 4)),
            dma((6,)),
            pltpu.SemaphoreType.REGULAR,
        ],
        cost_estimate=pl.CostEstimate(
            flops=30 * n * n * local_width, bytes_accessed=40 << 20, transcendentals=n * n * 8
        ),
        compiler_params=params(collective_id=4, has_side_effects=True),
        name="back",
    )(
        q, k, v, ctx, dctx, code_col, seg_row, lse, x_all, d_outw, tail, d_inw, d_down, first, second, pieces, proj_w
    )


def partner(block):
    return lax.ppermute(block, "tensor", [(0, 1), (1, 0)])


def both(own):
    return jnp.concatenate([own, partner(own)], axis=0)


def own_sum(partial):
    half = partial.shape[0] // 2
    return partial[:half].astype(f32) + partner(partial[half:].astype(bf16)).astype(f32)


def local_fast(
    tokens,
    cotangent,
    segment_ids,
    padding,
    shared_weights,
    first_moment,
    second_moment,
    outer_momentum,
):
    me = lax.axis_index("tensor")
    per = lax.axis_size("slot")
    rows = tokens.shape[0]
    local_width = D // 2
    piece_rows = shared_weights.shape[1] // LANES
    table, tail_at = matrix_table(2)
    tail_rows = GROUPS * per * piece_rows - tail_at
    padded = round_up(piece_rows + tail_rows, 16)

    own_rows = shared_weights.reshape(piece_rows, 1, LANES)
    seg = jnp.where(me == 0, segment_ids, jnp.roll(segment_ids, rows))
    live = jnp.where(me == 0, padding, jnp.roll(padding, rows))
    code = jnp.where(live == 1, seg, -1)
    end = padded - round_up(2 * tail_rows + 16, 16)
    marks = [end * i // 4 // 16 * 16 for i in range(4)] + [end, padded]
    cuts = [(low, high - low) for low, high in zip(marks[:-1], marks[1:])]
    (
        proj_w, out_w, in_w, down_w, out_w2, context_2, pieces, x_all,
        vectors, inner_bias, query, keys, values, context, lse
    ) = start(own_rows, tokens, code[None], seg[:, None], table, tail_rows, padded, cuts)
    (
        block_out, grad_one, grad_context, grad_out_w, grad_in_w, grad_down_w, tail_grad
    ) = middle(context, context_2, tokens, cotangent, vectors, inner_bias, out_w, out_w2, in_w, down_w)

    def blocked(state):
        return state.reshape(GROUPS, piece_rows, LANES).transpose(1, 0, 2)

    def unblocked(state):
        return state.transpose(1, 0, 2).reshape(1, 1, GROUPS, piece_rows * LANES)

    first = blocked(first_moment)
    second = blocked(second_moment)
    grads, d_sum, dx = back(
        query, keys, values, context, grad_context, code[:, None], seg[None], lse, x_all, grad_out_w,
        tail_grad, grad_in_w, grad_down_w, first, second, pieces, proj_w, table, tail_at, piece_rows
    )
    input_grad = (grad_one + dx[:rows].astype(f32) + dx[rows:].astype(f32)).astype(bf16)
    slot_word = lax.axis_index("slot").astype(jnp.int32).reshape(1)
    *states, mean_diff, new_momentum, new_weights = update(
        slot_word, grads, pieces, first, second, d_sum, own_rows,
        outer_momentum.reshape(piece_rows, 1, LANES), tail_rows
    )
    rows_out = [state.reshape(1, piece_rows * LANES) for state in (mean_diff, new_momentum, new_weights)]
    return (block_out, input_grad, *[unblocked(state) for state in states], *rows_out)


def solution(mesh):
    dp = mesh.shape["dp"]
    tensor_size = mesh.shape["tensor"]
    piece = (4 * D * D + 2 * D * FF + 8 * D + FF) // tensor_size // dp
    if tensor_size == 2 and piece % LANES == 0 and dp % GROUPS == 0:
        mesh = Mesh(
            mesh.devices.reshape(GROUPS, dp // GROUPS, tensor_size), ("group", "slot", "tensor")
        )
        data = ("group", "slot")
        body = local_fast
    else:
        data = "dp"
        body = local_general
    every = ("group", "slot", "tensor") if body is local_fast else ("dp", "tensor")
    in_specs = (
        P(every, None),
        P(every, None),
        P(data),
        P(data),
        P("tensor", data),
        P("tensor", data, None, None),
        P("tensor", data, None, None),
        P("tensor", data),
    )
    out_specs = (
        P(every, None),
        P(every, None),
        P("tensor", data, None, None),
        P("tensor", data, None, None),
        P("tensor", data, None, None),
        P("tensor", data, None, None),
        P("tensor", data),
        P("tensor", data),
        P("tensor", data),
    )
    return jax.shard_map(body, mesh=mesh, in_specs=in_specs, out_specs=out_specs, check_vma=False)
```

```python
import functools

import jax
import jax.numpy as jnp
import numpy as np
from jax import lax
from jax.experimental import pallas as pl
from jax.experimental.pallas import tpu as pltpu
from jax.sharding import Mesh
from jax.sharding import PartitionSpec as P

D = 1024
HEADS = 16
HD = 64
FF = 4096
SEQ_LEN = 1024
GROUPS = 4
STEP = 10


NORM_EPS = 1e-05
MASKED = -1000000000.0
BETA_ONE = 0.9
BETA_TWO = 0.999
ADAM_EPS = 1e-08
INNER_RATE = 0.02
DECAY = 0.01
OUTER_MU = 0.9
OUTER_RATE = 0.7
ROOT_HALF = 0.7071067811865476
INV_ROOT_TWO_PI = 0.3989422804014327


def from_partner(block, axis, stride):
    count = lax.axis_size(axis)
    route = []
    for low in range(count):
        high = low | 1 << stride
        if high != low and high < count:
            route += [(low, high), (high, low)]
    return lax.ppermute(block, axis, route)


def boundaries(tensor_size):
    local_width = D // tensor_size
    hidden = FF // tensor_size
    lengths = [
        3 * D * local_width,
        local_width * D,
        D * hidden,
        hidden * D,
        local_width,
        local_width,
        hidden,
        6 * local_width,
    ]
    points = [0]
    for amount in lengths:
        points.append(points[-1] + amount)
    return points


def layer_norm(values, norm_gain, norm_shift):
    average = jnp.mean(values, axis=-1, keepdims=True)
    centred = values - average
    variance = jnp.mean(centred * centred, axis=-1, keepdims=True)
    inv_dev = lax.rsqrt(variance + NORM_EPS)
    normed = centred * inv_dev
    return (normed * norm_gain + norm_shift, normed, inv_dev)


def norm_back(grad_normed, normed, inv_dev):
    first_part = jnp.mean(grad_normed, axis=-1, keepdims=True)
    second_part = jnp.mean(grad_normed * normed, axis=-1, keepdims=True)
    return inv_dev * (grad_normed - first_part - normed * second_part)


def gelu_slope(inner):
    return (
        0.5 * (1.0 + jax.scipy.special.erf(inner * ROOT_HALF))
        + inner * jnp.exp(-0.5 * inner * inner) * INV_ROOT_TWO_PI
    )


def row_contract(left_side, right_side):
    return lax.dot_general(
        left_side, right_side, (((0,), (0,)), ((), ())), preferred_element_type=jnp.float32
    )


def col_contract(left_side, right_side):
    return lax.dot_general(
        left_side, right_side, (((1,), (1,)), ((), ())), preferred_element_type=jnp.float32
    )


def halve_rounds(values, bit_list, first_axis, top_bit, dp_index, site_call):
    for bit_number in bit_list:
        axis_number = first_axis + top_bit - bit_number
        my_bit = dp_index >> bit_number & 1
        kept = lax.dynamic_index_in_dim(values, my_bit, axis_number, keepdims=True)
        outgoing = lax.dynamic_index_in_dim(values, 1 - my_bit, axis_number, keepdims=True)
        values = kept + site_call(outgoing, bit_number)
    return values


def local_general(
    tokens,
    cotangent,
    segment_ids,
    padding,
    shared_weights,
    first_moment,
    second_moment,
    outer_momentum,
):
    tensor_size = lax.axis_size("tensor")
    local_width = D // tensor_size
    hidden = FF // tensor_size
    local_heads = HEADS // tensor_size
    seq_rows = segment_ids.shape[0]
    seq_count = seq_rows // SEQ_LEN
    block_rows = min(512, SEQ_LEN)
    per_seq = SEQ_LEN // block_rows
    block_total = seq_count * per_seq
    score_scale = HD ** (-0.5)
    bf16 = jnp.bfloat16
    f32 = jnp.float32
    masters = lax.all_gather(shared_weights, "dp", axis=1, tiled=True)[0]
    points = boundaries(tensor_size)
    segments = [masters[points[number] : points[number + 1]] for number in range(8)]
    proj_weight = segments[0].reshape(3, D, local_width).astype(bf16)
    out_weight = segments[1].reshape(local_width, D).astype(bf16)
    in_weight = segments[2].reshape(D, hidden).astype(bf16)
    down_weight = segments[3].reshape(hidden, D).astype(bf16)
    query_bias = segments[4]
    value_bias = segments[5]
    inner_bias = segments[6]
    vectors = lax.all_gather(segments[7].reshape(6, local_width), "tensor", axis=1, tiled=True)
    inputs_all = lax.all_gather(tokens, "tensor", axis=0, tiled=True)
    projected = jnp.einsum("td,kde->kte", inputs_all, proj_weight, preferred_element_type=f32)
    query = (projected[0] + query_bias).astype(bf16)
    keys = projected[1].astype(bf16)
    values = (projected[2] + value_bias).astype(bf16)
    query_four = query.reshape(seq_count, SEQ_LEN, local_heads, HD)
    keys_four = keys.reshape(seq_count, SEQ_LEN, local_heads, HD)
    values_four = values.reshape(seq_count, SEQ_LEN, local_heads, HD)
    seg_two = segment_ids.reshape(seq_count, SEQ_LEN)
    live_two = padding.reshape(seq_count, SEQ_LEN)
    key_pos = jnp.arange(SEQ_LEN, dtype=jnp.int32)

    def block_scores(block_index):
        sequence = block_index // per_seq
        offset = block_index % per_seq * block_rows
        query_rows = lax.dynamic_index_in_dim(query_four, sequence, 0, keepdims=False)
        query_block = lax.dynamic_slice_in_dim(query_rows, offset, block_rows, 0)
        key_rows = lax.dynamic_index_in_dim(keys_four, sequence, 0, keepdims=False)
        seg_row = lax.dynamic_index_in_dim(seg_two, sequence, 0, keepdims=False)
        live_row = lax.dynamic_index_in_dim(live_two, sequence, 0, keepdims=False)
        seg_block = lax.dynamic_slice_in_dim(seg_row, offset, block_rows, 0)
        query_pos = offset + jnp.arange(block_rows, dtype=jnp.int32)
        allowed = (seg_block[:, None] == seg_row[None, :]) & (
            (live_row[None, :] == 1) | (query_pos[:, None] == key_pos[None, :])
        )
        raw_scores = (
            jnp.einsum("qhd,khd->hqk", query_block, key_rows, preferred_element_type=f32)
            * score_scale
        )
        return (
            jnp.where(allowed[None], raw_scores, MASKED),
            query_block,
            key_rows,
            sequence,
            offset,
        )

    def forward_block(block_index):
        scores, query_block, key_rows, sequence, offset = block_scores(block_index)
        value_rows = lax.dynamic_index_in_dim(values_four, sequence, 0, keepdims=False)
        highest = jnp.max(scores, axis=-1, keepdims=True)
        exponent = jnp.exp(scores - highest)
        summed = jnp.sum(exponent, axis=-1, keepdims=True)
        probabilities = (exponent / summed).astype(bf16)
        context = jnp.einsum("hqk,khd->qhd", probabilities, value_rows, preferred_element_type=f32)
        return (context, (highest + jnp.log(summed))[..., 0])

    context_blocks, log_totals = lax.map(forward_block, jnp.arange(block_total, dtype=jnp.int32))
    context_low = context_blocks.reshape(seq_rows, local_width).astype(bf16)
    attn_sum = lax.psum_scatter(
        jnp.dot(context_low, out_weight, preferred_element_type=f32).astype(jnp.bfloat16),
        "tensor",
        scatter_dimension=0,
        tiled=True,
    ).astype(jnp.float32)
    tokens_f = tokens.astype(f32)
    middle, normed_one, inv_one = layer_norm(
        tokens_f + (attn_sum + vectors[4]), vectors[0], vectors[1]
    )
    middle_all = lax.all_gather(middle.astype(bf16), "tensor", axis=0, tiled=True)
    inner = jnp.dot(middle_all, in_weight, preferred_element_type=f32) + inner_bias
    activated = jax.nn.gelu(inner, approximate=False).astype(bf16)
    ffn_sum = lax.psum_scatter(
        jnp.dot(activated, down_weight, preferred_element_type=f32).astype(jnp.bfloat16),
        "tensor",
        scatter_dimension=0,
        tiled=True,
    ).astype(jnp.float32)
    result, normed_two, inv_two = layer_norm(
        middle + (ffn_sum + vectors[5]), vectors[2], vectors[3]
    )
    block_out = result.astype(bf16)
    grad_out = cotangent.astype(f32)
    grad_gain_two = jnp.sum(grad_out * normed_two, axis=0)
    grad_shift_two = jnp.sum(grad_out, axis=0)
    grad_two = norm_back(grad_out * vectors[2], normed_two, inv_two)
    grad_down_bias = jnp.sum(grad_two, axis=0)
    back_all = lax.all_gather(grad_two.astype(bf16), "tensor", axis=0, tiled=True)
    grad_down_weight = row_contract(activated, back_all)
    grad_act = col_contract(back_all, down_weight)
    grad_inner = (grad_act * gelu_slope(inner)).astype(bf16)
    grad_inner_bias = jnp.sum(grad_inner.astype(f32), axis=0)
    grad_in_weight = row_contract(middle_all, grad_inner)
    grad_middle = grad_two + lax.psum_scatter(
        col_contract(grad_inner, in_weight).astype(jnp.bfloat16),
        "tensor",
        scatter_dimension=0,
        tiled=True,
    ).astype(jnp.float32)
    grad_gain_one = jnp.sum(grad_middle * normed_one, axis=0)
    grad_shift_one = jnp.sum(grad_middle, axis=0)
    grad_one = norm_back(grad_middle * vectors[0], normed_one, inv_one)
    grad_out_bias = jnp.sum(grad_one, axis=0)
    attn_back_all = lax.all_gather(grad_one.astype(bf16), "tensor", axis=0, tiled=True)
    grad_out_weight = row_contract(context_low, attn_back_all)
    grad_context = col_contract(attn_back_all, out_weight).astype(bf16)
    grad_context_four = grad_context.reshape(seq_count, SEQ_LEN, local_heads, HD)

    def backward_block(carry, block_index):
        grad_keys, grad_values = carry
        scores, query_block, key_rows, sequence, offset = block_scores(block_index)
        value_rows = lax.dynamic_index_in_dim(values_four, sequence, 0, keepdims=False)
        log_total = lax.dynamic_index_in_dim(log_totals, block_index, 0, keepdims=False)
        probabilities = jnp.exp(scores - log_total[..., None])
        prob_low = probabilities.astype(bf16)
        grad_rows = lax.dynamic_index_in_dim(grad_context_four, sequence, 0, keepdims=False)
        grad_block = lax.dynamic_slice_in_dim(grad_rows, offset, block_rows, 0)
        grad_probs = jnp.einsum("qhd,khd->hqk", grad_block, value_rows, preferred_element_type=f32)
        grad_scores = probabilities * (
            grad_probs - jnp.sum(grad_probs * probabilities, axis=-1, keepdims=True)
        )
        scores_low = grad_scores.astype(bf16)
        grad_query = (
            jnp.einsum("hqk,khd->qhd", scores_low, key_rows, preferred_element_type=f32)
            * score_scale
        )
        key_term = (
            jnp.einsum("hqk,qhd->khd", scores_low, query_block, preferred_element_type=f32)
            * score_scale
        )
        value_term = jnp.einsum("hqk,qhd->khd", prob_low, grad_block, preferred_element_type=f32)
        grad_keys = lax.dynamic_update_index_in_dim(
            grad_keys,
            lax.dynamic_index_in_dim(grad_keys, sequence, 0, keepdims=False) + key_term,
            sequence,
            0,
        )
        grad_values = lax.dynamic_update_index_in_dim(
            grad_values,
            lax.dynamic_index_in_dim(grad_values, sequence, 0, keepdims=False) + value_term,
            sequence,
            0,
        )
        return ((grad_keys, grad_values), grad_query)

    empty = jnp.zeros((seq_count, SEQ_LEN, local_heads, HD), f32)
    (grad_keys, grad_values), grad_queries = lax.scan(
        backward_block, (empty, empty), jnp.arange(block_total, dtype=jnp.int32)
    )
    grad_proj = jnp.stack(
        [
            grad_queries.reshape(seq_rows, local_width),
            grad_keys.reshape(seq_rows, local_width),
            grad_values.reshape(seq_rows, local_width),
        ]
    ).astype(bf16)
    grad_proj_weight = jnp.einsum("td,kte->kde", inputs_all, grad_proj, preferred_element_type=f32)
    grad_query_bias = jnp.sum(grad_proj[0].astype(f32), axis=0)
    grad_value_bias = jnp.sum(grad_proj[2].astype(f32), axis=0)
    input_part = jnp.einsum("kte,kde->td", grad_proj, proj_weight, preferred_element_type=f32)
    vector_part = jnp.stack(
        [
            grad_gain_one,
            grad_shift_one,
            grad_gain_two,
            grad_shift_two,
            grad_out_bias,
            grad_down_bias,
        ]
    )
    input_share, vector_grad = (
        lax.psum_scatter(
            input_part.astype(jnp.bfloat16), "tensor", scatter_dimension=0, tiled=True
        ).astype(jnp.float32),
        lax.psum_scatter(
            vector_part.astype(jnp.bfloat16), "tensor", scatter_dimension=1, tiled=True
        ).astype(jnp.float32),
    )
    input_grad = (grad_one + input_share).astype(bf16)
    flat_grad = jnp.concatenate(
        [
            grad_proj_weight.reshape(-1),
            grad_out_weight.reshape(-1),
            grad_in_weight.reshape(-1),
            grad_down_weight.reshape(-1),
            grad_query_bias,
            grad_value_bias,
            grad_inner_bias,
            vector_grad.reshape(-1),
        ]
    )
    dp_size = lax.axis_size("dp")
    per_group = dp_size // GROUPS
    inner_bits = per_group.bit_length() - 1
    all_bits = dp_size.bit_length() - 1
    dp_index = lax.axis_index("dp")
    slot_index = dp_index % per_group
    piece_len = shared_weights.shape[1]
    grid_view = flat_grad.reshape(GROUPS, per_group, piece_len)
    inner_list = list(range(inner_bits))
    outer_list = list(range(inner_bits, all_bits))
    inner_list = inner_list[::-1]
    outer_list = outer_list[::-1]
    summed_grid = grid_view
    for bit_number in inner_list:
        summed_grid = summed_grid + from_partner(
            summed_grid.astype(jnp.bfloat16), "dp", bit_number
        ).astype(summed_grid.dtype)
    grad_block = lax.dynamic_index_in_dim(summed_grid, slot_index, 1, keepdims=False)
    weights_block = lax.dynamic_index_in_dim(
        masters.reshape(GROUPS, per_group, piece_len), slot_index, 1, keepdims=False
    )
    matrix_count = (4 * D * D + 2 * D * FF) // tensor_size
    flat_index = (
        jnp.arange(GROUPS, dtype=jnp.int32)[:, None] * per_group + slot_index
    ) * piece_len + jnp.arange(piece_len, dtype=jnp.int32)[None, :]
    decay_mask = (flat_index < matrix_count).astype(f32)
    first_new = BETA_ONE * first_moment[0, 0] + (1 - BETA_ONE) * grad_block
    second_new = BETA_TWO * second_moment[0, 0] + (1 - BETA_TWO) * grad_block * grad_block
    first_hat = first_new / (1 - BETA_ONE**STEP)
    second_hat = second_new / (1 - BETA_TWO**STEP)
    group_weights = weights_block - INNER_RATE * (
        first_hat / (jnp.sqrt(second_hat) + ADAM_EPS) + DECAY * decay_mask * weights_block
    )
    difference = weights_block - group_weights

    def outer_swap(outgoing, bit_number):
        return from_partner(outgoing.astype(jnp.bfloat16), "dp", bit_number).astype(outgoing.dtype)

    outer_bits = all_bits - inner_bits
    diff_view = difference.reshape((2,) * outer_bits + (piece_len,))
    diff_sum = halve_rounds(diff_view, outer_list, 0, all_bits - 1, dp_index, outer_swap).reshape(
        piece_len
    )
    mean_diff = diff_sum / GROUPS
    new_momentum = OUTER_MU * outer_momentum[0] + mean_diff
    new_weights = shared_weights[0] - OUTER_RATE * (mean_diff + OUTER_MU * new_momentum)
    return (
        block_out,
        input_grad,
        grad_block[None, None],
        first_new[None, None],
        second_new[None, None],
        group_weights[None, None],
        mean_diff[None],
        new_momentum[None],
        new_weights[None],
    )


LANES = 128
NT = (((1,), (1,)), ((), ()))
NN = (((1,), (0,)), ((), ()))
TN = (((0,), (0,)), ((), ()))
VMEM_BYTES = 61 << 20
f32 = jnp.float32
bf16 = jnp.bfloat16


def dot(left, right, dims):
    return lax.dot_general(left, right, dims, preferred_element_type=f32)


def params(**more):
    return pltpu.CompilerParams(vmem_limit_bytes=VMEM_BYTES, **more)


def round_up(number, step):
    return -(-number // step) * step


def matrix_table(tensor_size):
    local_width = D // tensor_size
    hidden = FF // tensor_size
    table = []
    offset = 0
    for rows, columns in ((3 * D, local_width), (local_width, D), (D, hidden), (hidden, D)):
        blocks = columns // LANES
        table.append((offset, rows, blocks))
        offset += rows * blocks
    return table, offset


def chunk_plan(table, first, end, tail_at, tail_rows):
    segments = []
    base = None
    for number, (offset, rows, blocks) in enumerate(table):
        low = max(first, offset)
        high = min(end, offset + rows * blocks)
        if low >= high:
            continue
        row_low = (low - offset) // blocks // 16 * 16
        row_high = min(rows, round_up(-(-(high - offset) // blocks), 16))
        if base is None:
            base = offset + row_low * blocks
        segments.append((number, row_low, row_high, blocks, offset + row_low * blocks - base))
    size = max(at + (high - low) * blocks for _, low, high, blocks, at in segments)
    if end > tail_at:
        size = max(size, tail_at + tail_rows - base)
    return segments, base, size


def row_parts(rows, count):
    size = rows // count // 16 * 16
    starts = [size * i for i in range(count)] + [rows]
    return [(low, high - low) for low, high in zip(starts[:-1], starts[1:])]


def in_steps(start, rows, step, body):
    @pl.loop(0, rows // step)
    def _(i):
        body(pl.multiple_of(start + i * step, 16), step)

    if rows % step:
        body(start + rows // step * step, rows % step)


def update_kernel(
    slot_ref, g_hbm, w_hbm, m_hbm, v_hbm, d_hbm, own_hbm, mom_hbm,
    go, mo, vo, wo, mean_out, mom_out, new_out,
    g_s, w_s, m_s, v_s, m_new, v_new, w_new, sems,
    *, piece_rows, tail_rows, parts
):
    slot = slot_ref[0]
    units = [(b, part) for b in range(GROUPS) for part in parts] + [(None, part) for part in parts]

    def loads(u):
        b, (at, rows) = units[u]
        k = u % 3
        r = pl.ds(at, rows)
        wide = pl.ds(at, round_up(rows, 16))
        there, padded = pl.ds(0, rows), pl.ds(0, round_up(rows, 16))
        if b is None:
            pairs = (
                (d_hbm.at[wide], g_s.at[k, padded]),
                (own_hbm.at[r, 0, :], m_s.at[k, there]),
                (mom_hbm.at[r, 0, :], v_s.at[k, there]),
            )
        else:
            pairs = (
                (g_hbm.at[b, wide], g_s.at[k, padded]),
                (m_hbm.at[r, b, :], m_s.at[k, there]),
                (v_hbm.at[r, b, :], v_s.at[k, there]),
                (w_hbm.at[b, wide], w_s.at[k, padded]),
            )
        return [pltpu.make_async_copy(src, dst, sems.at[n, k]) for n, (src, dst) in enumerate(pairs)]

    def stores(u):
        b, (at, rows) = units[u]
        k = u % 3
        r = pl.ds(at, rows)
        there = pl.ds(0, rows)
        if b is None:
            pairs = (
                (m_new.at[k, there], mean_out.at[r, 0, :]),
                (v_new.at[k, there], mom_out.at[r, 0, :]),
                (w_new.at[k, there], new_out.at[r, 0, :]),
            )
        else:
            pairs = (
                (m_new.at[k, there], mo.at[r, b, :]),
                (v_new.at[k, there], vo.at[r, b, :]),
                (w_new.at[k, there], wo.at[r, b, :]),
                (g_s.at[k, there], go.at[r, b, :]),
            )
        return [pltpu.make_async_copy(src, dst, sems.at[4 + n, k]) for n, (src, dst) in enumerate(pairs)]

    for copy in loads(0):
        copy.start()
    for u, (b, (at, rows)) in enumerate(units):
        k = u % 3
        if u > 1:
            for copy in stores(u - 2):
                copy.wait()
        if u + 1 < len(units):
            for copy in loads(u + 1):
                copy.start()
        for copy in loads(u):
            copy.wait()

        def inner(start, count, b=b, at=at, k=k):
            r = pl.ds(start, count)
            g = g_s[k, r, :]
            if b is None:
                average = g / GROUPS
                momentum = OUTER_MU * v_s[k, r, :] + average
                m_new[k, r, :] = average
                v_new[k, r, :] = momentum
                w_new[k, r, :] = m_s[k, r, :] - OUTER_RATE * (average + OUTER_MU * momentum)
                return
            w = w_s[k, r, :].astype(f32)
            first = BETA_ONE * m_s[k, r, :] + (1 - BETA_ONE) * g
            second = BETA_TWO * v_s[k, r, :] + (1 - BETA_TWO) * g * g
            root = jnp.sqrt(second * (1 / (1 - BETA_TWO**STEP))) + ADAM_EPS
            decay = INNER_RATE * DECAY
            if b == GROUPS - 1:
                here = lax.broadcasted_iota(jnp.int32, (count, LANES), 0) + (at + start)
                decay = jnp.where((slot < 3) | (here < piece_rows - tail_rows), decay, 0.0)
            m_new[k, r, :] = first
            v_new[k, r, :] = second
            w_new[k, r, :] = w - ((INNER_RATE / (1 - BETA_ONE**STEP)) * first / root + decay * w)

        in_steps(0, round_up(rows, 16), 128, inner)
        for copy in stores(u):
            copy.start()
    for u in (len(units) - 2, len(units) - 1):
        for copy in stores(u):
            copy.wait()


def update(slot, grads, pieces, first, second, d_sum, own_rows, momentum_rows, tail_rows):
    piece_rows = first.shape[0]
    hbm = pl.BlockSpec(memory_space=pl.ANY)
    parts = row_parts(piece_rows, 3)
    most = round_up(max(rows for _, rows in parts), 16)
    wide = pltpu.VMEM((3, most, LANES), f32)
    state = jax.ShapeDtypeStruct(first.shape, f32)
    piece = jax.ShapeDtypeStruct(own_rows.shape, f32)
    return pl.pallas_call(
        functools.partial(update_kernel, piece_rows=piece_rows, tail_rows=tail_rows, parts=parts),
        in_specs=[pl.BlockSpec(memory_space=pltpu.SMEM)] + [hbm] * 7,
        out_specs=[hbm] * 7,
        out_shape=[state] * 4 + [piece] * 3,
        scratch_shapes=[wide, pltpu.VMEM((3, most, LANES), bf16)]
        + [wide] * 5
        + [pltpu.SemaphoreType.DMA((8, 3))],
        cost_estimate=pl.CostEstimate(
            flops=120 * piece_rows * LANES,
            bytes_accessed=120 * piece_rows * LANES,
            transcendentals=8 * piece_rows * LANES,
        ),
        compiler_params=params(),
        name="update",
    )(slot, grads, pieces, first, second, d_sum, own_rows, momentum_rows)


def document_rows(seg_ref, live_ref, me):
    half = seg_ref.shape[1] // 2

    def own_first(row):
        left, right = row[:, :half], row[:, half:]
        return jnp.concatenate(
            [jnp.where(me == 0, left, right), jnp.where(me == 0, right, left)], axis=1
        )

    seg = own_first(seg_ref[...])
    return seg.astype(f32), jnp.where(own_first(live_ref[...]) == 1, seg, -1).astype(f32)


def as_column(row):
    return jnp.broadcast_to(row, (LANES, row.shape[1])).T


def attend_block(q, k, v_ones, code, seg_col, offset):
    rows_q, n = q.shape[0], k.shape[0]
    low = lax.broadcasted_iota(jnp.int32, (1, LANES), 1) < HD
    zero = jnp.zeros((), bf16)
    q = q * jnp.asarray(HD**-0.5, bf16)
    rows = lax.broadcasted_iota(jnp.int32, (rows_q, n), 0) + offset
    cols = lax.broadcasted_iota(jnp.int32, (rows_q, n), 1)
    allowed = (seg_col == code) | (rows == cols)
    outs = []
    tops = []
    for h in range(2):
        qh = jnp.where(low, q, zero) if h == 0 else jnp.where(low, zero, q)
        s = jnp.where(allowed, dot(qh, k, NT), MASKED)
        top = jnp.max(s, axis=1, keepdims=True)
        p = jnp.exp(s - top).astype(bf16)
        outs.append(dot(p, v_ones[h], NN))
        tops.append(top)
    num = jnp.where(low, outs[0], outs[1])
    den = pltpu.roll(jnp.where(low, outs[1], outs[0]), HD, 1)
    lse = (jnp.where(low, tops[0], tops[1]) + jnp.log(den)).T
    return (num / den).astype(bf16), lse[0:1], lse[HD : HD + 1]


def widen(src, low, high, flat, to):
    step = 128
    full = (high - low) // step

    @pl.loop(0, full)
    def _(i):
        rows = src[pl.ds(pl.multiple_of(low + i * step, 16), step), :]
        flat[pl.ds(to + i * step, step), :] = rows.astype(f32)

    rest = (high - low) % step
    if rest:
        flat[pl.ds(to + full * step, rest), :] = src[low + full * step : high, :].astype(f32)


def bring_rows(buf, flat, margin, offset, count, piece_rows):
    for p, low, high, at in piece_spans(offset, count, piece_rows, buf.shape[1]):
        widen(buf.at[p], low, high, flat, margin + at)


def emit_matrix(flat, out, margin, rows, blocks, first=0):
    chunk = 64

    @pl.loop(0, rows // chunk)
    def _(c):
        at = pl.ds(pl.multiple_of(first + c * chunk, chunk), chunk)
        for j in range(blocks):
            from_rows = pl.ds(margin + c * (chunk * blocks) + j, chunk, stride=blocks)
            out[at, j * LANES : (j + 1) * LANES] = flat[from_rows, :].astype(bf16)


def piece_spans(offset, count, piece_rows, padded):
    spans = []
    for p in range(offset // piece_rows, -(-(offset + count) // piece_rows)):
        low = max(offset - p * piece_rows, 0) // 16 * 16
        high = min(round_up(min(offset + count - p * piece_rows, piece_rows), 16), padded)
        spans.append((p, low, high, p * piece_rows + low - offset))
    return spans


def start_kernel(
    own_hbm, tokens_hbm, seg_ref, live_ref,
    proj_out, outw_out, inw_out, down_out, outw2_out, ctx2_out, pieces_out, x_out,
    q_out, k_out, v_out, ctx_out, vec_ref, c1_ref, lse_ref,
    rows32, buf, xbuf, flat, proj_s, outw_s, inw_s, down_s, outw2_s, obuf, ctx2_s, vec_s,
    zdown, zup, zrecv, ysend, yrecv, csend, crecv, xsem, local_sems, ctx_sems, wo_sems, q_ref, k_ref, v_ref, ctx_ref, seg_s,
    *, piece_rows, tail_rows, table, cuts, rows_q
):
    z = lax.axis_index("group")
    slot = lax.axis_index("slot")
    me = lax.axis_index("tensor")
    depth = GROUPS
    padded = buf.shape[1]
    half = tokens_hbm.shape[0]
    n = 2 * half
    mesh_id = pl.DeviceIdType.MESH

    load = pltpu.make_async_copy(own_hbm.at[:, 0, :], rows32, local_sems.at[0])
    load.start()
    x_load = pltpu.make_async_copy(tokens_hbm, xbuf.at[pl.ds(0, half)], local_sems.at[1])
    x_load.start()

    barrier = pltpu.get_barrier_semaphore()
    for where in ({"slot": slot ^ 1}, {"slot": slot ^ 2}, {"tensor": 1 - me}):
        pl.semaphore_signal(barrier, inc=1, device_id=where, device_id_type=mesh_id)

    @pl.when(z > 0)
    def _():
        pl.semaphore_signal(barrier, inc=1, device_id={"group": z - 1}, device_id_type=mesh_id)

    @pl.when(z < depth - 1)
    def _():
        pl.semaphore_signal(barrier, inc=1, device_id={"group": z + 1}, device_id_type=mesh_id)

    pl.semaphore_wait(barrier, 3 + jnp.where(z > 0, 1, 0) + jnp.where(z < depth - 1, 1, 0))

    load.wait()
    own = z * 4 + slot
    step = 128
    full = piece_rows // step

    @pl.loop(0, full)
    def _(i):
        r = pl.ds(pl.multiple_of(i * step, step), step)
        buf[own, r, :] = rows32[r, :].astype(bf16)

    tail = rows32[piece_rows - tail_rows :, :]
    left = tail - tail.astype(bf16).astype(f32)
    zeros = jnp.zeros((padded - piece_rows - tail_rows, LANES), f32)
    buf[own, full * step :, :] = jnp.concatenate([rows32[full * step :, :], left, zeros], axis=0).astype(bf16)

    def copy_of(piece, h, send, recv, where):
        part = buf.at[piece, pl.ds(*cuts[h])]
        return pltpu.make_async_remote_copy(
            src_ref=part, dst_ref=part, send_sem=send, recv_sem=recv, device_id=where, device_id_type=mesh_id
        )

    def down(b, h):
        return copy_of(b * 4 + slot, h, zdown.at[b, h], zrecv.at[b, h], {"group": z + 1})

    def up(b, h):
        return copy_of(b * 4 + slot, h, zup.at[b, h], zrecv.at[b, h], {"group": z - 1})

    def side(b, h):
        return copy_of(b * 4 + slot, h, ysend.at[b, h], yrecv.at[b, h], {"slot": slot ^ 2})

    def side_in(b, h):
        return copy_of(b * 4 + (slot ^ 2), h, ysend.at[b, h], yrecv.at[b, h], {"slot": slot ^ 2})

    def twin(b, h, k):
        return copy_of(
            b * 4 + (slot ^ (2 * k)), h, csend.at[2 * b + k, h], crecv.at[2 * b + k, h], {"slot": slot ^ 1}
        )

    def twin_in(b, h, k):
        return copy_of(
            b * 4 + (slot ^ 1 ^ (2 * k)), h, csend.at[2 * b + k, h], crecv.at[2 * b + k, h], {"slot": slot ^ 1}
        )

    parts = range(len(cuts))
    tail_part = len(cuts) - 1
    order = [tail_part] + list(range(tail_part))
    last = depth - 1
    ranked = (
        z,
        jnp.where(z == 0, 1, 0),
        jnp.where(z == 0, 2, jnp.where(z == 1, 3, 1)),
        jnp.where((z == 0) | (z == 2), 3, 2),
    )
    middle = (z == 1) | (z == 2)
    edge = jnp.logical_not(middle)

    def pass_on(b, h, aside=True):
        up(b, h).wait_recv()

        @pl.when((b < z) & (z < last))
        def _():
            down(b, h).start()

        @pl.when((b > z) & (z > 0))
        def _():
            up(b, h).start()

        if aside:
            side(b, h).start()
        twin(b, h, 0).start()

    def serve_z(b, h, when=None, aside=True):
        if h == tail_part:
            when = (b != last) if when is None else when & (b != last)
        if when is None:
            pass_on(b, h, aside)
        else:
            pl.when(when)(functools.partial(pass_on, b, h, aside))

    def serve_y(rank, h):
        b = ranked[rank]

        def go():
            side_in(b, h).wait_recv()
            twin(b, h, 1).start()

        if h == tail_part:
            pl.when(b != last)(go)
        else:
            go()

    for number, h in enumerate(order):
        pl.when(z > 0)(lambda h=h: up(z, h).start())
        at_once = (z == 0) | ((z == 1) & (number < 2)) | ((z == 2) & (number < 3))
        pl.when(at_once)(lambda h=h: down(z, h).start())
        side(z, h).start()
        twin(z, h, 0).start()

    x_load.wait()
    x_copy = pltpu.make_async_remote_copy(
        src_ref=xbuf.at[pl.ds(0, half)],
        dst_ref=xbuf.at[pl.ds(half, half)],
        send_sem=xsem.at[0],
        recv_sem=xsem.at[1],
        device_id={"tensor": 1 - me},
        device_id_type=mesh_id,
    )
    x_copy.start()

    pl.when(z == last - 1)(functools.partial(pass_on, last, tail_part))
    for h in order:
        serve_z(ranked[3], h, middle, False)
        serve_z(ranked[1], h)
    pl.when(z < last - 1)(functools.partial(pass_on, last, tail_part))

    def side_later(h):
        aside = middle & (ranked[3] != last) if h == tail_part else middle
        pl.when(aside)(lambda: side(ranked[3], h).start())

    for number, h in enumerate(order):
        later = ((z == 1) & (number >= 2)) | ((z == 2) & (number >= 3))
        pl.when(later)(lambda h=h: down(z, h).start())
        if number < 2:
            side_later(h)
    for h in order:
        serve_z(ranked[2], h, middle)
    for h in order[2:]:
        side_later(h)
    for h in order:
        serve_z(ranked[2], h, z == 0)
    for h in order[:3]:
        serve_z(ranked[3], h, z == last)
    side_in(last, tail_part).wait_recv()
    twin(last, tail_part, 1).start()
    for rank in range(2):
        for h in order:
            serve_y(rank, h)
    for k in range(2):
        twin_in(last, tail_part, k).wait_recv()
        for rank in range(2):
            b = ranked[rank]
            for h in parts:
                if h == tail_part:
                    pl.when(b != last)(lambda b=b, h=h, k=k: twin_in(b, h, k).wait_recv())
                else:
                    twin_in(b, h, k).wait_recv()

    at = (piece_rows - tail_rows) // 16 * 16
    shift = piece_rows - tail_rows - at
    ends = buf[4 * depth - 1, at:, :].astype(f32)
    vectors = ends[shift : shift + tail_rows] + ends[shift + tail_rows : shift + 2 * tail_rows]
    vec_s[0] = vectors

    def to_partner(src, dst, send, recv):
        return pltpu.make_async_remote_copy(
            src_ref=src, dst_ref=dst, send_sem=send, recv_sem=recv,
            device_id={"tensor": 1 - me}, device_id_type=mesh_id,
        )

    vec_copy = to_partner(vec_s.at[0], vec_s.at[1], xsem.at[2], xsem.at[3])
    vec_copy.start()
    margin = 16
    (offset, rows, blocks) = table[0]
    bring_rows(buf, flat, margin, offset, rows * blocks, piece_rows)
    emit_matrix(flat, proj_s, margin, rows, blocks)
    out_copies = [pltpu.make_async_copy(proj_s, proj_out, local_sems.at[2])]
    out_copies[0].start()
    x_copy.wait()
    out_copies.append(pltpu.make_async_copy(xbuf, x_out, local_sems.at[3]))
    out_copies[1].start()
    query_bias = jnp.concatenate([vectors[j : j + 1] for j in range(blocks)], axis=1)
    value_bias = jnp.concatenate([vectors[blocks + j : blocks + j + 1] for j in range(blocks)], axis=1)
    depth_in = rows // 3
    for m, (ref, bias) in enumerate(((q_ref, query_bias), (k_ref, None), (v_ref, value_bias))):

        @pl.loop(0, n // 256)
        def _(i, m=m, ref=ref, bias=bias):
            r = pl.ds(pl.multiple_of(i * 256, 256), 256)
            acc = dot(xbuf[r, :], proj_s[m * depth_in : (m + 1) * depth_in, :], NN)
            if bias is not None:
                acc = acc + bias
            ref[r, :] = acc.astype(bf16)

    for number, (ref, out) in enumerate(((q_ref, q_out), (k_ref, k_out), (v_ref, v_out))):
        out_copies.append(pltpu.make_async_copy(ref, out, local_sems.at[13 + number]))
        out_copies[-1].start()
    third = jnp.where(z == 0, ranked[3], ranked[2])
    todo = [functools.partial(serve_z, third, h, edge) for h in order]
    todo += [functools.partial(serve_z, ranked[3], h, z == last) for h in order[3:]]
    todo += [functools.partial(serve_y, 2, h) for h in order]

    def landed(rank):
        b = ranked[rank]
        for h in parts:
            for k in range(2):
                if h == tail_part:
                    pl.when(b != last)(lambda b=b, h=h, k=k: twin_in(b, h, k).wait_recv())
                else:
                    twin_in(b, h, k).wait_recv()

    (wo_offset, wo_rows, wo_blocks) = table[1]
    spans = piece_spans(wo_offset, wo_rows * wo_blocks, piece_rows, padded)
    total = sum(high - low for _, low, high, _ in spans)
    halves = (round_up(total // 2, 16), total)
    wo_parts = ([], [])
    at = 0
    for p, low, high, _ in spans:
        split = min(max(low + halves[0] - at, low), high)
        if split > low:
            wo_parts[0].append((p, low, split - low, at))
        if high > split:
            wo_parts[1].append((p, split, high - split, at + split - low))
        at += high - low
    in_core = slot % 2

    def wo_copies(c):
        return [
            to_partner(
                buf.at[p, pl.ds(low, count)], obuf.at[pl.ds(to, count)], wo_sems.at[0, j], wo_sems.at[1, j]
            )
            for j, (p, low, count, to) in enumerate(wo_parts[c])
        ]

    def wo_twin(c):
        first, end = (0, halves[0]) if c == 0 else halves
        part = obuf.at[pl.ds(first, end - first)]
        return pltpu.make_async_remote_copy(
            src_ref=part, dst_ref=part, send_sem=wo_sems.at[0, 3], recv_sem=wo_sems.at[1, 3],
            device_id={"slot": slot ^ 1}, device_id_type=mesh_id,
        )

    def by_core(action):
        for c in range(2):
            pl.when(in_core == c)(functools.partial(action, c))

    def wo_send(c):
        for copy in wo_copies(c):
            copy.start()

    def wo_pass(c):
        for copy in wo_copies(c):
            copy.wait_recv()
        wo_twin(c).start()

    def wo_done(c):
        wo_twin(1 - c).wait_recv()

    def wo_sent(c):
        for copy in wo_copies(c):
            copy.wait_send()
        wo_twin(c).wait_send()

    def ctx_copies(pair):
        columns = pl.ds(pair * LANES, LANES)
        return [
            to_partner(
                ctx_ref.at[pl.ds(half - first, half), columns],
                ctx2_s.at[pl.ds(first, half), columns],
                ctx_sems.at[0, 2 * pair + first // half],
                ctx_sems.at[1, 2 * pair + first // half],
            )
            for first in (0, half)
        ]

    low = lax.broadcasted_iota(jnp.int32, (1, LANES), 1) < HD
    one = jnp.ones((), bf16)
    seg, code = document_rows(seg_ref, live_ref, me)
    seg_s[...] = as_column(seg)
    for pair in range(blocks):
        c = slice(pair * LANES, (pair + 1) * LANES)
        k = k_ref[:, c]
        v = v_ref[:, c]
        v_ones = (jnp.where(low, v, one), jnp.where(low, one, v))
        for i in range(n // rows_q):
            r = slice(i * rows_q, (i + 1) * rows_q)
            ctx, lse_0, lse_1 = attend_block(q_ref[r, c], k, v_ones, code, seg_s[r, 0:1], i * rows_q)
            ctx_ref[r, c] = ctx
            lse_ref[pair, 0:1, r] = lse_0
            lse_ref[pair, 1:2, r] = lse_1
            if todo:
                todo.pop(0)()
            if (pair, i) == (2, n // rows_q - 1):
                for act in todo:
                    act()
                todo = []
                landed(2)
                by_core(wo_send)
        for copy in ctx_copies(pair):
            copy.start()
    out_copies.append(pltpu.make_async_copy(ctx_ref, ctx_out, local_sems.at[16]))
    out_copies[-1].start()
    scratches = (None, outw_s, inw_s, down_s)
    mat_copies = [
        None,
        pltpu.make_async_copy(outw_s, outw_out, local_sems.at[4]),
        pltpu.make_async_copy(inw_s, inw_out, local_sems.at[5]),
        pltpu.make_async_copy(down_s, down_out, local_sems.at[6]),
    ]

    def matrix(m, first=0, end=None):
        (offset, rows, blocks) = table[m]
        count = (rows if end is None else end) - first
        bring_rows(buf, flat, margin, offset + first * blocks, count * blocks, piece_rows)
        emit_matrix(flat, scratches[m], margin, count, blocks, first)

    chunk_rows = 4 * piece_rows
    in_cut = (2 * chunk_rows - table[2][0]) // table[2][2] // 64 * 64
    down_cut = round_up(-(-(3 * chunk_rows - table[3][0]) // table[3][2]), 64)
    matrix(1)
    matrix(2, 0, in_cut)
    pl.when(ranked[3] == last)(lambda: matrix(2, in_cut))
    pl.when(ranked[3] != last)(lambda: matrix(3, down_cut))
    mat_copies[1].start()
    for h in order:
        serve_y(3, h)
    by_core(wo_pass)
    landed(3)

    @pl.when(ranked[3] == last)
    def _():
        mat_copies[2].start()
        matrix(3, 0, down_cut)
        matrix(3, down_cut)
        mat_copies[3].start()

    @pl.when(ranked[3] != last)
    def _():
        matrix(3, 0, down_cut)
        mat_copies[3].start()
        matrix(2, in_cut)
        mat_copies[2].start()

    by_core(wo_done)
    at = 0
    for p, low, high, to in spans:
        widen(obuf, at, at + high - low, flat, margin + to)
        at += high - low
    emit_matrix(flat, outw2_s, margin, wo_rows, wo_blocks)
    out_copies.append(pltpu.make_async_copy(outw2_s, outw2_out, local_sems.at[11]))
    out_copies[-1].start()

    vec_copy.wait()
    hidden_rows = table[2][2]
    for j in range(hidden_rows):
        c1_ref[0:1, j * LANES : (j + 1) * LANES] = vec_s[0, 2 * blocks + j : 2 * blocks + j + 1, :]
    for row in range(6):
        for j in range(blocks):
            from_row = 2 * blocks + hidden_rows + row * blocks + j
            mine, theirs = vec_s[0, from_row : from_row + 1, :], vec_s[1, from_row : from_row + 1, :]
            left, right = jnp.where(me == 0, mine, theirs), jnp.where(me == 0, theirs, mine)
            vec_ref[row : row + 1, j * LANES : (j + 1) * LANES] = left
            vec_ref[row : row + 1, (blocks + j) * LANES : (blocks + j + 1) * LANES] = right

    for pair in range(blocks):
        for copy in ctx_copies(pair):
            copy.wait()
    out_copies.append(pltpu.make_async_copy(ctx2_s, ctx2_out, local_sems.at[12]))
    out_copies[-1].start()
    by_core(wo_sent)
    for b in range(depth):
        copy = pltpu.make_async_copy(buf.at[b * 4 + slot], pieces_out.at[b], local_sems.at[7 + b])
        copy.start()
        out_copies.append(copy)
    out_copies += mat_copies[1:]

    for b in range(depth):
        for h in parts:

            @pl.when((b <= z) & (z < depth - 1))
            def _(b=b, h=h):
                down(b, h).wait_send()

            @pl.when((b >= z) & (z > 0))
            def _(b=b, h=h):
                up(b, h).wait_send()

            side(b, h).wait_send()
            for k in range(2):
                twin(b, h, k).wait_send()
    for copy in out_copies:
        copy.wait()


def start(own_rows, tokens, seg_row, live_row, table, tail_rows, padded, cuts, rows_q=256):
    piece_rows = own_rows.shape[0]
    half, width = tokens.shape
    n = 2 * half
    pairs = table[0][2]
    local_width = pairs * LANES
    hbm = pl.BlockSpec(memory_space=pl.ANY)
    whole = pl.BlockSpec(memory_space=pltpu.VMEM)
    mats = [jax.ShapeDtypeStruct((rows, blocks * LANES), bf16) for _, rows, blocks in table]
    acts = [jax.ShapeDtypeStruct((n, local_width), bf16)] * 4
    most = max(rows * blocks for _, rows, blocks in table)
    parts = len(cuts)
    dma = pltpu.SemaphoreType.DMA
    return pl.pallas_call(
        functools.partial(
            start_kernel, piece_rows=piece_rows, tail_rows=tail_rows, table=table, cuts=cuts, rows_q=rows_q
        ),
        in_specs=[hbm, hbm, whole, whole],
        out_specs=[hbm] * 12 + [whole] * 3,
        out_shape=mats
        + [
            mats[1],
            jax.ShapeDtypeStruct((n, local_width), bf16),
            jax.ShapeDtypeStruct((GROUPS, padded, LANES), bf16),
            jax.ShapeDtypeStruct((n, width), bf16),
        ]
        + acts
        + [
            jax.ShapeDtypeStruct((6, width), f32),
            jax.ShapeDtypeStruct((1, table[2][2] * LANES), f32),
            jax.ShapeDtypeStruct((pairs, 2, n), f32)],
        scratch_shapes=[
            pltpu.VMEM((piece_rows, LANES), f32),
            pltpu.VMEM((4 * GROUPS, padded, LANES), bf16),
            pltpu.VMEM((n, width), bf16),
            pltpu.VMEM((most + 48, LANES), f32),
        ]
        + [pltpu.VMEM(m.shape, bf16) for m in mats]
        + [
            pltpu.VMEM(mats[1].shape, bf16),
            pltpu.VMEM((round_up(table[1][1] * table[1][2] + 64, 16), LANES), bf16),
            pltpu.VMEM((n, local_width), bf16),
            pltpu.VMEM((2, tail_rows, LANES), f32),
            dma((GROUPS, parts)),
            dma((GROUPS, parts)),
            dma((GROUPS, parts)),
            dma((GROUPS, parts)),
            dma((GROUPS, parts)),
            dma((2 * GROUPS, parts)),
            dma((2 * GROUPS, parts)),
            dma((4,)),
            dma((17,)),
            dma((2, 2 * pairs)),
            dma((2, 4)),
        ]
        + [pltpu.VMEM(a.shape, bf16) for a in acts]
        + [pltpu.VMEM((n, LANES), f32)],
        cost_estimate=pl.CostEstimate(
            flops=6 * n * width * local_width, bytes_accessed=60 << 20, transcendentals=8 * n * n
        ),
        compiler_params=params(collective_id=1, has_side_effects=True),
        name="start",
    )(own_rows, tokens, seg_row, live_row)


ERF = (0.254829592, -0.284496736, 1.421413741, -1.453152027, 1.061405429)
ERF_P = 0.3275911


def gelu_pair(u):
    bell = jnp.exp(-0.5 * u * u)
    t = 1.0 / (1.0 + (ERF_P * ROOT_HALF) * jnp.abs(u))
    poly = ERF[4]
    for number in ERF[3::-1]:
        poly = poly * t + number
    tail = (0.5 * poly * t) * bell
    phi = jnp.where(u >= 0, 1.0 - tail, tail)
    return u * phi, phi + u * bell * INV_ROOT_TWO_PI


def fold(values):
    return values.reshape(values.shape[0] // 8, 8, values.shape[1]).sum(axis=0)


def middle_kernel(
    outw_hbm, outw2_hbm, ctx_hbm, ctx2_hbm, x_hbm, inw_hbm, down_hbm, cot_hbm, vec_ref, c1_ref,
    block_hbm, dh1_hbm, dctx_hbm, d_outw_hbm, d_outw2_hbm, d_inw_hbm, d_down_hbm, tail_out,
    outw_ref, outw2_ref, ctx_ref, ctx2_ref, x_ref, inw_ref, down_ref, cot_ref,
    block_out, dh1_out, dctx_out, d_outw, d_outw2, d_inw, d_down,
    x1, norm1, inv1, x1_all, act, slope, dh2_all, dh1_low, dctx_send, part, dh2, box_send, box_recv, sums, c1_sum, vec_box, send_sems, recv_sems, vec_sems,
    load_sems, store_sems, in_sems,
    *, chunk
):
    me = lax.axis_index("tensor")
    loads = [
        pltpu.make_async_copy(src, dst, load_sems.at[number])
        for number, (src, dst) in enumerate(
            (
                (outw_hbm, outw_ref),
                (outw2_hbm, outw2_ref),
                (ctx_hbm, ctx_ref),
                (ctx2_hbm, ctx2_ref),
                (x_hbm, x_ref),
                (inw_hbm, inw_ref),
                (down_hbm, down_ref),
                (cot_hbm, cot_ref),
            )
        )
    ]
    for copy in loads:
        copy.start()
    block_store, dh1_store, dctx_store, outw_store, outw2_store, down_store = stores = [
        pltpu.make_async_copy(src, dst, store_sems.at[number])
        for number, (src, dst) in enumerate(
            (
                (block_out, block_hbm),
                (dh1_out, dh1_hbm),
                (dctx_out, dctx_hbm),
                (d_outw, d_outw_hbm),
                (d_outw2, d_outw2_hbm),
                (d_down, d_down_hbm),
            )
        )
    ]
    half, width = cot_ref.shape
    count = half // chunk
    mesh_id = pl.DeviceIdType.MESH
    other = {"tensor": 1 - me}
    barrier = pltpu.get_barrier_semaphore()
    pl.semaphore_signal(barrier, inc=1, device_id=other, device_id_type=mesh_id)
    pl.semaphore_wait(barrier, 1)

    def rows_of(i):
        return pl.ds(pl.multiple_of(i * chunk, chunk), chunk)

    def far_rows(i):
        return pl.ds(pl.multiple_of(half + i * chunk, chunk), chunk)

    def summed(stage, i):
        return pltpu.make_async_remote_copy(
            src_ref=box_send.at[stage, rows_of(i)],
            dst_ref=box_recv.at[stage, rows_of(i)],
            send_sem=send_sems.at[stage, i],
            recv_sem=recv_sems.at[stage, i],
            device_id=other,
            device_id_type=mesh_id,
        )

    def gathered(i):
        return pltpu.make_async_remote_copy(
            src_ref=dh2_all.at[rows_of(i)],
            dst_ref=dh2_all.at[far_rows(i)],
            send_sem=send_sems.at[2, i],
            recv_sem=recv_sems.at[2, i],
            device_id=other,
            device_id_type=mesh_id,
        )

    def handed(i):
        return pltpu.make_async_remote_copy(
            src_ref=dctx_send.at[rows_of(i)],
            dst_ref=dctx_out.at[far_rows(i)],
            send_sem=send_sems.at[3, i],
            recv_sem=recv_sems.at[3, i],
            device_id=other,
            device_id_type=mesh_id,
        )

    gain_1, shift_1 = vec_ref[0:1, :], vec_ref[1:2, :]
    gain_2, shift_2 = vec_ref[2:3, :], vec_ref[3:4, :]
    bias_o, bias_2 = vec_ref[4:5, :], vec_ref[5:6, :]
    sums[...] = jnp.zeros_like(sums)
    c1_sum[...] = jnp.zeros_like(c1_sum)

    def normed(h):
        centred = h - jnp.mean(h, axis=-1, keepdims=True)
        inv = lax.rsqrt(jnp.mean(centred * centred, axis=-1, keepdims=True) + NORM_EPS)
        return centred * inv, inv

    def normed_back(dn, n, inv):
        return inv * (
            dn - jnp.mean(dn, axis=-1, keepdims=True) - n * jnp.mean(dn * n, axis=-1, keepdims=True)
        )

    def forward(r):
        u = dot(x1_all[r, :], inw_ref[...], NN) + c1_ref[...]
        a, s = gelu_pair(u)
        act[r, :] = a.astype(bf16)
        slope[r, :] = s.astype(bf16)
        return dot(act[r, :], down_ref[...], NN)

    def backward(r):
        da = dot(dh2_all[r, :], down_ref[...], NT)
        du = da * slope[r, :].astype(f32)
        low = du.astype(bf16)
        slope[r, :] = low
        c1_sum[...] += fold(low.astype(f32))
        return dot(low, inw_ref[...], NT)

    def first_norm(r):
        branch = dot(ctx_ref[r, :], outw_ref[...], NN) + dot(ctx2_ref[r, :], outw2_ref[...], NN)
        n, inv = normed(x_ref[r, :].astype(f32) + (branch + bias_o))
        middle = n * gain_1 + shift_1
        x1_all[r, :] = middle.astype(bf16)
        return n, inv, middle

    for copy in loads[:5]:
        copy.wait()

    @pl.loop(0, count)
    def _(i):
        first_norm(far_rows(i))

    for copy in loads[5:7]:
        copy.wait()

    @pl.loop(0, count)
    def _(i):
        box_send[0, rows_of(i), :] = forward(far_rows(i)).astype(bf16)
        summed(0, i).start()

    @pl.loop(0, count)
    def _(i):
        r = rows_of(i)
        n, inv, middle = first_norm(r)
        norm1[r, :] = n
        inv1[r, :] = jnp.broadcast_to(inv, (chunk, LANES))
        x1[r, :] = middle
        part[r, :] = forward(r)

    loads[7].wait()

    @pl.loop(0, count)
    def _(i):
        r = rows_of(i)
        summed(0, i).wait_recv()
        h = x1[r, :] + (part[r, :] + box_recv[0, r, :].astype(f32) + bias_2)
        n, inv = normed(h)
        block_out[r, :] = (n * gain_2 + shift_2).astype(bf16)
        dy = cot_ref[r, :].astype(f32)
        dh = normed_back(dy * gain_2, n, inv)
        sums[2] += fold(dy * n)
        sums[3] += fold(dy)
        sums[5] += fold(dh)
        dh2[r, :] = dh
        dh2_all[r, :] = dh.astype(bf16)
        gathered(i).start()
        part[r, :] = backward(r)

    block_store.start()

    @pl.loop(0, count)
    def _(i):
        gathered(i).wait_recv()
        box_send[1, rows_of(i), :] = backward(far_rows(i)).astype(bf16)
        summed(1, i).start()

    hidden = act.shape[1]
    block = hidden // 8

    def down_grad(j):
        c = pl.ds(pl.multiple_of(j * block, block), block)
        d_down[c, :] = dot(act[:, c].T, dh2_all[...], NN).astype(bf16)

    def in_grad(j):
        c = pl.ds(pl.multiple_of(j * block, block), block)
        d_inw[:, c] = dot(x1_all[...].T, slope[:, c], NN).astype(bf16)
        in_store(j).start()

    def in_store(j):
        c = pl.ds(pl.multiple_of(j * block, block), block)
        return pltpu.make_async_copy(d_inw.at[:, c], d_inw_hbm.at[:, c], in_sems.at[j])

    per_chunk = 8 // count

    @pl.loop(0, count)
    def _(i):
        for j in range(per_chunk):
            down_grad(i * per_chunk + j)
        r = rows_of(i)
        summed(1, i).wait_recv()
        dx = dh2[r, :] + part[r, :] + box_recv[1, r, :].astype(f32)
        n = norm1[r, :]
        dh = normed_back(dx * gain_1, n, inv1[r, 0:1])
        sums[0] += fold(dx * n)
        sums[1] += fold(dx)
        sums[4] += fold(dh)
        dh1_out[r, :] = dh
        dh1_low[r, :] = dh.astype(bf16)
        dctx_send[r, :] = dot(dh1_low[r, :], outw2_ref[...], NT).astype(bf16)
        handed(i).start()
        dctx_out[r, :] = dot(dh1_low[r, :], outw_ref[...], NT).astype(bf16)

    dh1_store.start()
    down_store.start()
    for row in range(6):
        total = jnp.sum(sums[row], axis=0, keepdims=True)
        low, high = total[:, : width // 2], total[:, width // 2 :]
        mine, theirs = jnp.where(me == 0, low, high), jnp.where(me == 0, high, low)
        spread = width // 2 // LANES
        for j in range(spread):
            at = row * spread + j
            vec_box[0, at : at + 1, :] = mine[:, j * LANES : (j + 1) * LANES]
            vec_box[1, at : at + 1, :] = theirs[:, j * LANES : (j + 1) * LANES]
    vec_copy = pltpu.make_async_remote_copy(
        src_ref=vec_box.at[1],
        dst_ref=vec_box.at[2],
        send_sem=vec_sems.at[0],
        recv_sem=vec_sems.at[1],
        device_id=other,
        device_id_type=mesh_id,
    )
    vec_copy.start()

    @pl.loop(0, 8)
    def _(j):
        in_grad(j)

    d_outw2[...] = dot(ctx2_ref[0:half, :].T, dh1_low[...], NN).astype(bf16)
    outw2_store.start()
    d_outw[...] = dot(ctx_ref[0:half, :].T, dh1_low[...], NN).astype(bf16)
    outw_store.start()

    @pl.loop(0, count)
    def _(i):
        handed(i).wait_recv()

    dctx_store.start()

    blocks = ctx_ref.shape[1] // LANES
    tail_out[0 : 2 * blocks, :] = jnp.zeros((2 * blocks, LANES), f32)
    c1_total = jnp.sum(c1_sum[...], axis=0, keepdims=True)
    for j in range(hidden // LANES):
        tail_out[2 * blocks + j : 2 * blocks + j + 1, :] = c1_total[:, j * LANES : (j + 1) * LANES]
    vec_copy.wait()
    tail_out[2 * blocks + hidden // LANES :, :] = vec_box[0] + vec_box[2]

    @pl.loop(0, count)
    def _(i):
        for stage in range(2):
            summed(stage, i).wait_send()
        gathered(i).wait_send()
        handed(i).wait_send()

    @pl.loop(0, 8)
    def _(j):
        in_store(j).wait()

    for copy in stores:
        copy.wait()


def middle(context, context_2, x_all, cotangent, vectors, inner_bias, out_w, out_w2, in_w, down_w, chunk=128):
    half, width = cotangent.shape
    n = 2 * half
    hidden = in_w.shape[1]
    local_width = context.shape[1]
    whole = pl.BlockSpec(memory_space=pltpu.VMEM)
    hbm = pl.BlockSpec(memory_space=pl.ANY)
    operands = (out_w, out_w2, context, context_2, x_all, in_w, down_w, cotangent)
    wide = pltpu.VMEM((half, width), f32)
    every = pltpu.VMEM((n, width), bf16)
    box = pltpu.VMEM((2, half, width), bf16)
    count = half // chunk
    return pl.pallas_call(
        functools.partial(middle_kernel, chunk=chunk),
        in_specs=[hbm] * 8 + [whole] * 2,
        out_specs=[hbm] * 7 + [whole],
        out_shape=[
            jax.ShapeDtypeStruct((half, width), bf16),
            jax.ShapeDtypeStruct((half, width), f32),
            jax.ShapeDtypeStruct((n, local_width), bf16),
            jax.ShapeDtypeStruct(out_w.shape, bf16),
            jax.ShapeDtypeStruct(out_w.shape, bf16),
            jax.ShapeDtypeStruct(in_w.shape, bf16),
            jax.ShapeDtypeStruct(down_w.shape, bf16),
            jax.ShapeDtypeStruct(((2 * local_width + hidden + 3 * width) // LANES, LANES), f32),
        ],
        scratch_shapes=[pltpu.VMEM(operand.shape, operand.dtype) for operand in operands]
        + [
            pltpu.VMEM((half, width), bf16),
            wide,
            pltpu.VMEM((n, local_width), bf16),
            pltpu.VMEM(out_w.shape, bf16),
            pltpu.VMEM(out_w.shape, bf16),
            pltpu.VMEM(in_w.shape, bf16),
            pltpu.VMEM(down_w.shape, bf16),
            wide,
            wide,
            pltpu.VMEM((half, LANES), f32),
            every,
            pltpu.VMEM((n, hidden), bf16),
            pltpu.VMEM((n, hidden), bf16),
            every,
            pltpu.VMEM((half, width), bf16),
            pltpu.VMEM((half, local_width), bf16),
            wide,
            wide,
            box,
            box,
            pltpu.VMEM((6, 8, width), f32),
            pltpu.VMEM((8, hidden), f32),
            pltpu.VMEM((3, 3 * width // LANES, LANES), f32),
            pltpu.SemaphoreType.DMA((4, count)),
            pltpu.SemaphoreType.DMA((4, count)),
            pltpu.SemaphoreType.DMA((2,)),
            pltpu.SemaphoreType.DMA((8,)),
            pltpu.SemaphoreType.DMA((6,)),
            pltpu.SemaphoreType.DMA((8,)),
        ],
        cost_estimate=pl.CostEstimate(
            flops=14 * n * width * hidden, bytes_accessed=40 << 20, transcendentals=2 * n * hidden
        ),
        compiler_params=params(collective_id=2, has_side_effects=True),
        name="middle",
    )(*operands, vectors, inner_bias)


def attend_back(q_ref, k_ref, v_ref, ctx_ref, dctx_ref, code, seg_ref, lse_ref, dq_ref, dk_ref, dv_ref, pair, rows_q, after_step):
    n = q_ref.shape[0]
    c = slice(pair * LANES, (pair + 1) * LANES)
    low = lax.broadcasted_iota(jnp.int32, (1, LANES), 1) < HD
    zero = jnp.zeros((), bf16)
    k = k_ref[:, c]
    v = v_ref[:, c]
    k_t = k.T
    pick = (
        lax.broadcasted_iota(jnp.int32, (8, LANES), 1) // HD
        == lax.broadcasted_iota(jnp.int32, (8, LANES), 0)
    ).astype(f32)
    dks = [jnp.zeros((n, LANES), f32)] * 2
    dvs = [jnp.zeros((n, LANES), f32)] * 2
    scale = jnp.asarray(HD**-0.5, bf16)
    for i in range(n // rows_q):
        r = slice(i * rows_q, (i + 1) * rows_q)
        q = q_ref[r, c] * scale
        do = dctx_ref[r, c]
        prod = do.astype(f32) * ctx_ref[r, c].astype(f32)
        delta = lax.dot_general(
            pick, prod, NT, precision=lax.Precision.HIGHEST, preferred_element_type=f32
        )
        keys = lax.broadcasted_iota(jnp.int32, (n, rows_q), 0)
        qs = lax.broadcasted_iota(jnp.int32, (n, rows_q), 1) + i * rows_q
        allowed = (code == seg_ref[:, r]) | (keys == qs)
        dqs = []
        for h in range(2):
            qh = jnp.where(low, q, zero) if h == 0 else jnp.where(low, zero, q)
            doh = jnp.where(low, do, zero) if h == 0 else jnp.where(low, zero, do)
            s = jnp.where(allowed, dot(k, qh, NT), MASKED)
            p = jnp.exp(s - lse_ref[pair, h : h + 1, r])
            dp = dot(v, doh, NT)
            ds = (p * (dp - delta[h : h + 1])).astype(bf16)
            dvs[h] = dvs[h] + dot(p.astype(bf16), do, NN)
            dks[h] = dks[h] + dot(ds, q, NN)
            dqs.append(dot(k_t[h * HD : (h + 1) * HD], ds, NN))
        dq_ref[r, c] = (jnp.concatenate(dqs, axis=0).T * (HD**-0.5)).astype(bf16)
        after_step(i)
    dk_ref[:, c] = jnp.where(low, dks[0], dks[1]).astype(bf16)
    dv_ref[:, c] = jnp.where(low, dvs[0], dvs[1]).astype(bf16)


def lay_flat(ref, low, high, blocks, flat, at):
    chunk = 16 if (high - low) % 64 else 64

    @pl.loop(0, (high - low) // chunk)
    def _(c):
        rows = pl.ds(pl.multiple_of(low + c * chunk, 16), chunk)
        for j in range(blocks):
            to_rows = pl.ds(at + c * (chunk * blocks) + j, chunk, stride=blocks)
            flat[to_rows, :] = ref[rows, j * LANES : (j + 1) * LANES].astype(f32)


def emit_pieces(flat, keep, send, slot, skip, piece_rows):
    padded = send.shape[1]
    step = 128
    full = piece_rows // step
    rest = piece_rows - full * step
    for j in (3, 1, 2, 0):
        out = send if j % 2 else keep
        start = skip + (slot ^ j) * piece_rows

        @pl.loop(0, full)
        def _(i, out=out, j=j, start=start):
            rows = flat[pl.ds(start + i * step, step), :]
            out[j // 2, pl.ds(pl.multiple_of(i * step, step), step), :] = rows.astype(bf16)

        parts = [jnp.zeros((padded - piece_rows, LANES), f32)]
        if rest:
            parts = [flat[pl.ds(start + full * step, rest), :]] + parts
        out[j // 2, full * step : padded, :] = jnp.concatenate(parts, axis=0).astype(bf16)


def back_kernel(
    seg_ref, live_ref, lse_ref, outw_ref, tail_ref,
    q_hbm, k_hbm, v_hbm, ctx_hbm, dctx_hbm, x_hbm, inw_hbm, down_hbm, m_hbm, s_hbm, w_hbm, proj_hbm, outw2_hbm,
    g_out, d_out, dx_out,
    dq_ref, dk_ref, dv_ref,
    flat, down_s, inw_s, keep, send, near, far, tails, zin, g_stage, m_in, v_in, w_in,
    near_send, near_recv, far_send, far_recv, tail_send, tail_recv, z_send, z_recv, load_sems, out_sems,
    x_sems, x_free, q_ref, k_ref, v_ref, ctx_ref, dctx_ref, x_ref, act_sems, seg_s, wo_in,
    *, plans, piece_rows, cuts, rows_q
):
    me = lax.axis_index("tensor")
    z = lax.axis_index("group")
    slot = lax.axis_index("slot")
    last = GROUPS - 1
    mesh_id = pl.DeviceIdType.MESH
    core = {"slot": slot ^ 1}
    side = {"slot": slot ^ 2}
    tail_rows = tail_ref.shape[0]
    padded = send.shape[1]
    stage_loads = [
        pltpu.make_async_copy(down_hbm, down_s, load_sems.at[0]),
        pltpu.make_async_copy(inw_hbm, inw_s, load_sems.at[1]),
    ]
    act_loads = [
        pltpu.make_async_copy(src, dst, act_sems.at[number])
        for number, (src, dst) in enumerate(
            (
                (q_hbm, q_ref),
                (k_hbm, k_ref),
                (v_hbm, v_ref),
                (ctx_hbm, ctx_ref),
                (dctx_hbm, dctx_ref),
                (x_hbm, x_ref),
            )
        )
    ]
    for copy in stage_loads + act_loads:
        copy.start()
    barrier = pltpu.get_barrier_semaphore()
    for where in (core, side, {"tensor": 1 - me}):
        pl.semaphore_signal(barrier, inc=1, device_id=where, device_id_type=mesh_id)

    @pl.when(z > 0)
    def _():
        pl.semaphore_signal(barrier, inc=1, device_id={"group": z - 1}, device_id_type=mesh_id)

    @pl.when(z < last)
    def _():
        pl.semaphore_signal(barrier, inc=1, device_id={"group": z + 1}, device_id_type=mesh_id)

    pl.semaphore_wait(barrier, 3 + jnp.where(z > 0, 1, 0) + jnp.where(z < last, 1, 0))

    def to_core(b, j):
        return pltpu.make_async_remote_copy(
            src_ref=send.at[j],
            dst_ref=near.at[b, j],
            send_sem=near_send.at[b, j],
            recv_sem=near_recv.at[b, j],
            device_id=core,
            device_id_type=mesh_id,
        )

    def to_side(b, h):
        rows = pl.ds(*cuts[h])
        return pltpu.make_async_remote_copy(
            src_ref=keep.at[b, 1, rows],
            dst_ref=far.at[b, rows],
            send_sem=far_send.at[b, h],
            recv_sem=far_recv.at[b, h],
            device_id=side,
            device_id_type=mesh_id,
        )

    def tail_copy(k, where):
        return pltpu.make_async_remote_copy(
            src_ref=tails.at[2 * k],
            dst_ref=tails.at[2 * k + 1],
            send_sem=tail_send.at[k],
            recv_sem=tail_recv.at[k],
            device_id=where,
            device_id_type=mesh_id,
        )

    def along(b, h, landing, where):
        return pltpu.make_async_remote_copy(
            src_ref=keep.at[b, 0, pl.ds(*cuts[h])],
            dst_ref=zin.at[landing, pl.ds(*cuts[h])],
            send_sem=z_send.at[b, h],
            recv_sem=z_recv.at[landing, h],
            device_id=where,
            device_id_type=mesh_id,
        )

    def upward(b, h):
        return along(b, h, b, {"group": z + 1})

    def downward(b, h):
        return along(b, h, jnp.where(z - 1 == b, GROUPS, b), {"group": z - 1})

    def hand_over(b):
        for j in (1, 0):
            to_core(b, j).start()

    def pass_aside(b, first=0, end=None):
        if first == 0:
            to_core(b, 1).wait_recv()
        for h in range(first, len(cuts) if end is None else end):

            def add(at, count):
                r = pl.ds(at, count)
                keep[b, 1, r, :] = (keep[b, 1, r, :].astype(f32) + near[b, 1, r, :].astype(f32)).astype(bf16)

            in_steps(*cuts[h], 128, add)
            to_side(b, h).start()

    def sent(b):
        for j in (1, 0):
            to_core(b, j).wait_send()

    def loads(b):
        rows = pl.ds(0, piece_rows)
        return (
            pltpu.make_async_copy(m_hbm.at[rows, b, :], m_in.at[rows], load_sems.at[2]),
            pltpu.make_async_copy(s_hbm.at[rows, b, :], v_in.at[rows], load_sems.at[3]),
            pltpu.make_async_copy(w_hbm.at[b, pl.ds(0, padded)], w_in, load_sems.at[4]),
        )

    def store(b, h):
        rows = pl.ds(*cuts[h])
        return pltpu.make_async_copy(g_stage.at[rows], g_out.at[b, rows], out_sems.at[b, h])

    turn = (2, 1, 3, 0)

    def differ(b, h):
        k = turn.index(b)
        start, count = cuts[h]
        if h == 0:
            to_core(b, 0).wait_recv()
            for copy in loads(b):
                copy.wait()
        to_side(b, h).wait_recv()
        if b == last and h == len(cuts) - 1:
            at = piece_rows - tail_rows
            low = at // 16 * 16
            extra = jnp.where(slot == last, tails[2] + tails[3], 0.0)
            around = [extra]
            if at > low:
                around = [jnp.zeros((at - low, LANES), f32)] + around
            if padded > piece_rows:
                around = around + [jnp.zeros((padded - piece_rows, LANES), f32)]
            ends = slice(low, padded)
            far[b, ends, :] = (far[b, ends, :].astype(f32) + jnp.concatenate(around, axis=0)).astype(bf16)
        if k:
            store(turn[k - 1], h).wait()

        def step(at, rows):
            r = pl.ds(at, rows)
            g = keep[b, 0, r, :].astype(f32) + near[b, 0, r, :].astype(f32) + far[b, r, :].astype(f32)
            g_stage[r, :] = g
            first = BETA_ONE * m_in[r, :] + (1 - BETA_ONE) * g
            second = BETA_TWO * v_in[r, :] + (1 - BETA_TWO) * g * g
            root = jnp.sqrt(second * (1 / (1 - BETA_TWO**STEP))) + ADAM_EPS
            decay = INNER_RATE * DECAY
            if b == last:
                here = lax.broadcasted_iota(jnp.int32, (rows, LANES), 0) + at
                decay = jnp.where((slot < last) | (here < piece_rows - tail_rows), decay, 0.0)
            d = (INNER_RATE / (1 - BETA_ONE**STEP)) * first / root + decay * w_in[r, :].astype(f32)
            keep[b, 0, r, :] = d.astype(bf16)

        in_steps(start, count, 128, step)
        store(b, h).start()
        if b > 0:
            pl.when(z == 0)(lambda: upward(b, h).start())
        if b < last:
            pl.when(z == last)(lambda: downward(b, h).start())
        if h == len(cuts) - 1 and k + 1 < GROUPS:
            for copy in loads(turn[k + 1]):
                copy.start()

    def hop(b, at, h):
        def go():
            along(b, h, b, {"group": z}).wait_recv()

            def add(at, count):
                r = pl.ds(at, count)
                keep[b, 0, r, :] = (keep[b, 0, r, :].astype(f32) + zin[b, r, :].astype(f32)).astype(bf16)

            in_steps(*cuts[h], 128, add)
            (upward if at < b else downward)(b, h).start()

        pl.when(z == at)(go)

    blank = slice(piece_rows, padded)
    m_in[blank, :] = jnp.zeros((padded - piece_rows, LANES), f32)
    v_in[blank, :] = jnp.zeros((padded - piece_rows, LANES), f32)
    for copy in loads(turn[0]):
        copy.start()

    wo_copy = pltpu.make_async_remote_copy(
        src_ref=outw2_hbm,
        dst_ref=wo_in,
        send_sem=x_sems.at[6],
        recv_sem=x_sems.at[7],
        device_id={"tensor": 1 - me},
        device_id_type=mesh_id,
    )
    wo_copy.start()
    for copy in stage_loads:
        copy.wait()
    refs = {1: wo_in, 2: inw_s, 3: down_s}

    def lay_chunk(b):
        segments, skip, has_tail = plans[b]
        for number, low, high, blocks, at in segments:
            if number:
                lay_flat(refs[number], low, high, blocks, flat, at)
        if has_tail:
            at = skip + 4 * piece_rows - tail_rows
            flat[pl.ds(at, tail_rows), :] = jnp.zeros((tail_rows, LANES), f32)

    def emit_chunk(b):
        emit_pieces(flat, keep.at[b], send, slot, plans[b][1], piece_rows)
        hand_over(b)

    def output_chunk():
        wo_copy.wait()

        @pl.loop(0, wo_in.shape[0] // 16)
        def _(i):
            r = pl.ds(pl.multiple_of(i * 16, 16), 16)
            wo_in[r, :] = (wo_in[r, :].astype(f32) + outw_ref[r, :].astype(f32)).astype(bf16)

        lay_chunk(1)
        sent(3)
        emit_chunk(1)

    lay_chunk(2)
    emit_chunk(2)
    lay_chunk(3)
    pass_aside(2)
    sent(2)
    emit_chunk(3)

    half = q_ref.shape[0] // 2
    local_width = q_ref.shape[1]
    depth_in = x_ref.shape[1]
    proj_loads = [
        pltpu.make_async_copy(
            proj_hbm.at[pl.ds(m * depth_in, depth_in)],
            inw_s.at[:, pl.ds(m * local_width, local_width)],
            x_sems.at[2 + m],
        )
        for m in range(3)
    ]

    def make_free():
        pl.semaphore_signal(x_free, inc=1, device_id={"tensor": 1 - me}, device_id_type=mesh_id)
        for copy in proj_loads:
            copy.start()

    parts = range(len(cuts))
    act = functools.partial
    fourth = len(cuts) // 4

    def differ_some(b, part):
        for h in range(part * fourth, (part + 1) * fourth):
            differ(b, h)

    def hop_some(b, at, part):
        for h in range(part * fourth, (part + 1) * fourth):
            hop(b, at, h)

    events = {
        0: [act(differ_some, 2, 0)],
        2: [act(differ_some, 2, 1)],
        4: [act(differ_some, 2, 2), act(pass_aside, 3, 0, fourth)],
        5: [act(hop_some, 2, 1, 0)],
        6: [output_chunk, make_free],
        7: [act(pass_aside, 1), act(differ_some, 2, 3)],
        8: [act(pass_aside, 3, fourth), act(hop_some, 2, 1, 1)],
        9: [act(hop_some, 2, 1, 2)],
        10: [act(differ_some, 1, 0)],
        11: [act(hop_some, 2, 1, 3)],
        12: [act(differ_some, 1, 1)],
        13: [act(differ_some, 1, 2)],
        14: [act(hop_some, 1, 2, 0)],
        15: [act(differ_some, 1, 3)],
    }
    blocks = q_ref.shape[1] // LANES
    seg, code = document_rows(seg_ref, live_ref, me)
    seg_s[...] = seg
    code = as_column(code)[:, 0:1]
    per_pair = q_ref.shape[0] // rows_q

    def after_step(number):
        for act in events.get(number, ()):
            act()

    for copy in act_loads:
        copy.wait()
    for pair in range(blocks):
        attend_back(
            q_ref, k_ref, v_ref, ctx_ref, dctx_ref, code, seg_s, lse_ref, dq_ref, dk_ref, dv_ref, pair, rows_q,
            lambda i, pair=pair: after_step(pair * per_pair + i),
        )

    tails[0] = tail_ref[...]
    for m, ref in enumerate((dq_ref, dv_ref)):
        total = jnp.sum(ref[...].astype(f32), axis=0, keepdims=True)
        for j in range(blocks):
            row = m * blocks + j
            tails[0, row : row + 1, :] = total[:, j * LANES : (j + 1) * LANES]
    tail_copy(0, core).start()

    chunk = 256
    segments, skip, _ = plans[0]
    for m, ref in enumerate((dq_ref, dk_ref, dv_ref)):

        @pl.loop(0, depth_in // chunk)
        def _(c, m=m, ref=ref):
            columns = pl.ds(pl.multiple_of(c * chunk, chunk), chunk)
            acc = dot(x_ref[:, columns].T, ref[...], NN)
            for j in range(blocks):
                to_rows = pl.ds((m * depth_in + c * chunk) * blocks + j, chunk, stride=blocks)
                flat[to_rows, :] = acc[:, j * LANES : (j + 1) * LANES]

        if m == 0:
            tail_copy(0, core).wait()
            tails[2] = tails[0] + tails[1]
            tail_copy(1, side).start()
            hop_some(1, 2, 1)
        if m == 1:
            hop_some(1, 2, 2)

    for number, low, high, wide, at in segments:
        if number:
            lay_flat(refs[number], low, high, wide, flat, at)
    sent(1)
    emit_chunk(0)
    pass_aside(0)
    hop_some(1, 2, 3)
    tail_copy(1, side).wait()
    for h in parts:
        differ(3, h)

    for copy in proj_loads:
        copy.wait()

    def through(row):
        r = pl.ds(row, 256)
        acc = dot(dq_ref[r, :], inw_s[:, 0:local_width], NT)
        acc = acc + dot(dk_ref[r, :], inw_s[:, local_width : 2 * local_width], NT)
        return acc + dot(dv_ref[r, :], inw_s[:, 2 * local_width : 3 * local_width], NT)

    @pl.loop(0, half // 256)
    def _(i):
        down_s[pl.ds(pl.multiple_of(i * 256, 256), 256), :] = through(
            pl.multiple_of(half + i * 256, 256)
        ).astype(bf16)

    pl.semaphore_wait(x_free, 1)
    x_copy = pltpu.make_async_remote_copy(
        src_ref=down_s.at[pl.ds(0, half)],
        dst_ref=down_s.at[pl.ds(half, half)],
        send_sem=x_sems.at[0],
        recv_sem=x_sems.at[1],
        device_id={"tensor": 1 - me},
        device_id_type=mesh_id,
    )
    x_copy.start()
    differ(0, 0)

    @pl.loop(0, half // 256)
    def _(i):
        down_s[pl.ds(pl.multiple_of(2 * half + i * 256, 256), 256), :] = through(
            pl.multiple_of(i * 256, 256)
        ).astype(bf16)

    count = len(cuts)
    for t in range(1, count + 4):
        for act_on, lag in (
            (act(differ, 0), 0),
            (act(hop, 3, 1), 1),
            (act(hop, 0, 2), 2),
            (act(hop, 3, 2), 3),
            (act(hop, 0, 1), 4),
        ):
            if 0 <= t - lag < count:
                act_on(t - lag)

    for h in parts:
        store(0, h).wait()
    for b in range(GROUPS):

        def finish(b=b):
            for h in parts:
                if b > 0:
                    along(b, h, b, {"group": z}).wait_recv()
                if b < last:
                    along(b, h, GROUPS, {"group": z}).wait_recv()

                def add(at, count):
                    r = pl.ds(at, count)
                    total = keep[b, 0, r, :].astype(f32)
                    if b > 0:
                        total = total + zin[b, r, :].astype(f32)
                    if b < last:
                        total = total + zin[GROUPS, r, :].astype(f32)
                    g_stage[r, :] = total

                in_steps(*cuts[h], 128, add)

        pl.when(z == b)(finish)
    x_copy.wait()
    dx_copy = pltpu.make_async_copy(down_s.at[pl.ds(half, 2 * half)], dx_out, x_sems.at[5])
    dx_copy.start()
    copy = pltpu.make_async_copy(g_stage, d_out, out_sems.at[GROUPS, 0])
    copy.start()
    for b in range(GROUPS):
        for h in parts:
            to_side(b, h).wait_send()

            @pl.when(z != b)
            def _(b=b, h=h):
                along(b, h, b, {"group": z}).wait_send()

    sent(0)
    copy.wait()
    dx_copy.wait()


def back(
    q, k, v, ctx, dctx, seg_row, live_row, lse, x_all, d_outw, d_outw2, tail, d_inw, d_down, first, second, pieces, proj_w,
    table, tail_at, piece_rows, rows_q=256
):
    per = 4
    padded = round_up(piece_rows, 16)
    tail_rows = tail.shape[0]
    plans = []
    most = 0
    for b in range(GROUPS):
        begin = b * per * piece_rows
        segments, base, size = chunk_plan(table, begin, begin + per * piece_rows, tail_at, tail_rows)
        plans.append((segments, begin - base, begin + per * piece_rows > tail_at))
        most = max(most, size)
    parts = 8
    marks = [padded * i // parts // 16 * 16 for i in range(parts)] + [padded]
    cuts = [(low, high - low) for low, high in zip(marks[:-1], marks[1:])]
    whole = pl.BlockSpec(memory_space=pltpu.VMEM)
    hbm = pl.BlockSpec(memory_space=pl.ANY)
    dma = pltpu.SemaphoreType.DMA
    n, local_width = q.shape
    grad = pltpu.VMEM((n, local_width), bf16)
    wide = pltpu.VMEM((padded, LANES), f32)
    return pl.pallas_call(
        functools.partial(back_kernel, plans=plans, piece_rows=piece_rows, cuts=cuts, rows_q=rows_q),
        in_specs=[whole] * 5 + [hbm] * 13,
        out_specs=[hbm] * 3,
        out_shape=[
            jax.ShapeDtypeStruct((GROUPS, padded, LANES), f32),
            jax.ShapeDtypeStruct((padded, LANES), f32),
            jax.ShapeDtypeStruct((n, x_all.shape[1]), bf16),
        ],
        scratch_shapes=[
            grad,
            grad,
            grad,
            pltpu.VMEM((round_up(most, 8) + 8, LANES), f32),
            pltpu.VMEM(d_down.shape, bf16),
            pltpu.VMEM(d_inw.shape, bf16),
            pltpu.VMEM((GROUPS, 2, padded, LANES), bf16),
            pltpu.VMEM((2, padded, LANES), bf16),
            pltpu.VMEM((GROUPS, 2, padded, LANES), bf16),
            pltpu.VMEM((GROUPS, padded, LANES), bf16),
            pltpu.VMEM((4, tail_rows, LANES), f32),
            pltpu.VMEM((GROUPS + 1, padded, LANES), bf16),
            wide,
            wide,
            wide,
            pltpu.VMEM((padded, LANES), bf16),
            dma((GROUPS, 2)),
            dma((GROUPS, 2)),
            dma((GROUPS, parts)),
            dma((GROUPS, parts)),
            dma((2,)),
            dma((2,)),
            dma((GROUPS, parts)),
            dma((GROUPS + 1, parts)),
            dma((5,)),
            dma((GROUPS + 1, parts)),
            dma((8,)),
            pltpu.SemaphoreType.REGULAR,
            grad,
            grad,
            grad,
            grad,
            grad,
            pltpu.VMEM(x_all.shape, bf16),
            dma((6,)),
            pltpu.VMEM((1, n), f32),
            pltpu.VMEM(d_outw.shape, bf16),
        ],
        cost_estimate=pl.CostEstimate(
            flops=30 * n * n * local_width, bytes_accessed=40 << 20, transcendentals=n * n * 8
        ),
        compiler_params=params(collective_id=4, has_side_effects=True),
        name="back",
    )(
        seg_row, live_row, lse, d_outw, tail, q, k, v, ctx, dctx, x_all, d_inw, d_down, first, second, pieces, proj_w, d_outw2
    )


def partner(block):
    return lax.ppermute(block, "tensor", [(0, 1), (1, 0)])


def both(own):
    return jnp.concatenate([own, partner(own)], axis=0)


def own_sum(partial):
    half = partial.shape[0] // 2
    return partial[:half].astype(f32) + partner(partial[half:].astype(bf16)).astype(f32)


def local_fast(
    tokens,
    cotangent,
    segment_ids,
    padding,
    shared_weights,
    first_moment,
    second_moment,
    outer_momentum,
):
    per = lax.axis_size("slot")
    rows = tokens.shape[0]
    local_width = D // 2
    piece_rows = shared_weights.shape[1] // LANES
    table, tail_at = matrix_table(2)
    tail_rows = GROUPS * per * piece_rows - tail_at
    padded = round_up(piece_rows + tail_rows, 16)

    own_rows = shared_weights.reshape(piece_rows, 1, LANES)
    seg_row, live_row = segment_ids[None], padding[None]
    end = padded - round_up(2 * tail_rows + 16, 16)
    marks = [end * i // 4 // 16 * 16 for i in range(4)] + [end, padded]
    cuts = [(low, high - low) for low, high in zip(marks[:-1], marks[1:])]
    (
        proj_w, out_w, in_w, down_w, out_w2, context_2, pieces, x_all,
        query, keys, values, context, vectors, inner_bias, lse
    ) = start(own_rows, tokens, seg_row, live_row, table, tail_rows, padded, cuts)
    (
        block_out, grad_one, grad_context, grad_out_w, grad_out_w2, grad_in_w, grad_down_w, tail_grad
    ) = middle(context, context_2, x_all, cotangent, vectors, inner_bias, out_w, out_w2, in_w, down_w)

    def blocked(state):
        return state.reshape(GROUPS, piece_rows, LANES).transpose(1, 0, 2)

    def unblocked(state):
        return state.transpose(1, 0, 2).reshape(1, 1, GROUPS, piece_rows * LANES)

    first = blocked(first_moment)
    second = blocked(second_moment)
    grads, d_sum, dx = back(
        query, keys, values, context, grad_context, seg_row, live_row, lse, x_all, grad_out_w, grad_out_w2,
        tail_grad, grad_in_w, grad_down_w, first, second, pieces, proj_w, table, tail_at, piece_rows
    )
    input_grad = (grad_one + dx[:rows].astype(f32) + dx[rows:].astype(f32)).astype(bf16)
    slot_word = lax.axis_index("slot").astype(jnp.int32).reshape(1)
    *states, mean_diff, new_momentum, new_weights = update(
        slot_word, grads, pieces, first, second, d_sum, own_rows,
        outer_momentum.reshape(piece_rows, 1, LANES), tail_rows
    )
    rows_out = [state.reshape(1, piece_rows * LANES) for state in (mean_diff, new_momentum, new_weights)]
    return (block_out, input_grad, *[unblocked(state) for state in states], *rows_out)


def solution(mesh):
    dp = mesh.shape["dp"]
    tensor_size = mesh.shape["tensor"]
    piece = (4 * D * D + 2 * D * FF + 8 * D + FF) // tensor_size // dp
    if tensor_size == 2 and piece % LANES == 0 and dp % GROUPS == 0:
        mesh = Mesh(
            mesh.devices.reshape(GROUPS, dp // GROUPS, tensor_size), ("group", "slot", "tensor")
        )
        data = ("group", "slot")
        body = local_fast
    else:
        data = "dp"
        body = local_general
    every = ("group", "slot", "tensor") if body is local_fast else ("dp", "tensor")
    in_specs = (
        P(every, None),
        P(every, None),
        P(data),
        P(data),
        P("tensor", data),
        P("tensor", data, None, None),
        P("tensor", data, None, None),
        P("tensor", data),
    )
    out_specs = (
        P(every, None),
        P(every, None),
        P("tensor", data, None, None),
        P("tensor", data, None, None),
        P("tensor", data, None, None),
        P("tensor", data, None, None),
        P("tensor", data),
        P("tensor", data),
        P("tensor", data),
    )
    return jax.shard_map(body, mesh=mesh, in_specs=in_specs, out_specs=out_specs, check_vma=False)
```

```python
import functools

import jax
import jax.numpy as jnp
import numpy as np
from jax import lax
from jax.experimental import pallas as pl
from jax.experimental.pallas import tpu as pltpu
from jax.sharding import Mesh
from jax.sharding import PartitionSpec as P

D = 1024
HEADS = 16
HD = 64
FF = 4096
SEQ_LEN = 1024
GROUPS = 4
STEP = 10


NORM_EPS = 1e-05
MASKED = -1000000000.0
BETA_ONE = 0.9
BETA_TWO = 0.999
ADAM_EPS = 1e-08
INNER_RATE = 0.02
DECAY = 0.01
OUTER_MU = 0.9
OUTER_RATE = 0.7
ROOT_HALF = 0.7071067811865476
INV_ROOT_TWO_PI = 0.3989422804014327


def from_partner(block, axis, stride):
    count = lax.axis_size(axis)
    route = []
    for low in range(count):
        high = low | 1 << stride
        if high != low and high < count:
            route += [(low, high), (high, low)]
    return lax.ppermute(block, axis, route)


def boundaries(tensor_size):
    local_width = D // tensor_size
    hidden = FF // tensor_size
    lengths = [
        3 * D * local_width,
        local_width * D,
        D * hidden,
        hidden * D,
        local_width,
        local_width,
        hidden,
        6 * local_width,
    ]
    points = [0]
    for amount in lengths:
        points.append(points[-1] + amount)
    return points


def layer_norm(values, norm_gain, norm_shift):
    average = jnp.mean(values, axis=-1, keepdims=True)
    centred = values - average
    variance = jnp.mean(centred * centred, axis=-1, keepdims=True)
    inv_dev = lax.rsqrt(variance + NORM_EPS)
    normed = centred * inv_dev
    return (normed * norm_gain + norm_shift, normed, inv_dev)


def norm_back(grad_normed, normed, inv_dev):
    first_part = jnp.mean(grad_normed, axis=-1, keepdims=True)
    second_part = jnp.mean(grad_normed * normed, axis=-1, keepdims=True)
    return inv_dev * (grad_normed - first_part - normed * second_part)


def gelu_slope(inner):
    return (
        0.5 * (1.0 + jax.scipy.special.erf(inner * ROOT_HALF))
        + inner * jnp.exp(-0.5 * inner * inner) * INV_ROOT_TWO_PI
    )


def row_contract(left_side, right_side):
    return lax.dot_general(
        left_side, right_side, (((0,), (0,)), ((), ())), preferred_element_type=jnp.float32
    )


def col_contract(left_side, right_side):
    return lax.dot_general(
        left_side, right_side, (((1,), (1,)), ((), ())), preferred_element_type=jnp.float32
    )


def halve_rounds(values, bit_list, first_axis, top_bit, dp_index, site_call):
    for bit_number in bit_list:
        axis_number = first_axis + top_bit - bit_number
        my_bit = dp_index >> bit_number & 1
        kept = lax.dynamic_index_in_dim(values, my_bit, axis_number, keepdims=True)
        outgoing = lax.dynamic_index_in_dim(values, 1 - my_bit, axis_number, keepdims=True)
        values = kept + site_call(outgoing, bit_number)
    return values


def local_general(
    tokens,
    cotangent,
    segment_ids,
    padding,
    shared_weights,
    first_moment,
    second_moment,
    outer_momentum,
):
    tensor_size = lax.axis_size("tensor")
    local_width = D // tensor_size
    hidden = FF // tensor_size
    local_heads = HEADS // tensor_size
    seq_rows = segment_ids.shape[0]
    seq_count = seq_rows // SEQ_LEN
    block_rows = min(512, SEQ_LEN)
    per_seq = SEQ_LEN // block_rows
    block_total = seq_count * per_seq
    score_scale = HD ** (-0.5)
    bf16 = jnp.bfloat16
    f32 = jnp.float32
    masters = lax.all_gather(shared_weights, "dp", axis=1, tiled=True)[0]
    points = boundaries(tensor_size)
    segments = [masters[points[number] : points[number + 1]] for number in range(8)]
    proj_weight = segments[0].reshape(3, D, local_width).astype(bf16)
    out_weight = segments[1].reshape(local_width, D).astype(bf16)
    in_weight = segments[2].reshape(D, hidden).astype(bf16)
    down_weight = segments[3].reshape(hidden, D).astype(bf16)
    query_bias = segments[4]
    value_bias = segments[5]
    inner_bias = segments[6]
    vectors = lax.all_gather(segments[7].reshape(6, local_width), "tensor", axis=1, tiled=True)
    inputs_all = lax.all_gather(tokens, "tensor", axis=0, tiled=True)
    projected = jnp.einsum("td,kde->kte", inputs_all, proj_weight, preferred_element_type=f32)
    query = (projected[0] + query_bias).astype(bf16)
    keys = projected[1].astype(bf16)
    values = (projected[2] + value_bias).astype(bf16)
    query_four = query.reshape(seq_count, SEQ_LEN, local_heads, HD)
    keys_four = keys.reshape(seq_count, SEQ_LEN, local_heads, HD)
    values_four = values.reshape(seq_count, SEQ_LEN, local_heads, HD)
    seg_two = segment_ids.reshape(seq_count, SEQ_LEN)
    live_two = padding.reshape(seq_count, SEQ_LEN)
    key_pos = jnp.arange(SEQ_LEN, dtype=jnp.int32)

    def block_scores(block_index):
        sequence = block_index // per_seq
        offset = block_index % per_seq * block_rows
        query_rows = lax.dynamic_index_in_dim(query_four, sequence, 0, keepdims=False)
        query_block = lax.dynamic_slice_in_dim(query_rows, offset, block_rows, 0)
        key_rows = lax.dynamic_index_in_dim(keys_four, sequence, 0, keepdims=False)
        seg_row = lax.dynamic_index_in_dim(seg_two, sequence, 0, keepdims=False)
        live_row = lax.dynamic_index_in_dim(live_two, sequence, 0, keepdims=False)
        seg_block = lax.dynamic_slice_in_dim(seg_row, offset, block_rows, 0)
        query_pos = offset + jnp.arange(block_rows, dtype=jnp.int32)
        allowed = (seg_block[:, None] == seg_row[None, :]) & (
            (live_row[None, :] == 1) | (query_pos[:, None] == key_pos[None, :])
        )
        raw_scores = (
            jnp.einsum("qhd,khd->hqk", query_block, key_rows, preferred_element_type=f32)
            * score_scale
        )
        return (
            jnp.where(allowed[None], raw_scores, MASKED),
            query_block,
            key_rows,
            sequence,
            offset,
        )

    def forward_block(block_index):
        scores, query_block, key_rows, sequence, offset = block_scores(block_index)
        value_rows = lax.dynamic_index_in_dim(values_four, sequence, 0, keepdims=False)
        highest = jnp.max(scores, axis=-1, keepdims=True)
        exponent = jnp.exp(scores - highest)
        summed = jnp.sum(exponent, axis=-1, keepdims=True)
        probabilities = (exponent / summed).astype(bf16)
        context = jnp.einsum("hqk,khd->qhd", probabilities, value_rows, preferred_element_type=f32)
        return (context, (highest + jnp.log(summed))[..., 0])

    context_blocks, log_totals = lax.map(forward_block, jnp.arange(block_total, dtype=jnp.int32))
    context_low = context_blocks.reshape(seq_rows, local_width).astype(bf16)
    attn_sum = lax.psum_scatter(
        jnp.dot(context_low, out_weight, preferred_element_type=f32).astype(jnp.bfloat16),
        "tensor",
        scatter_dimension=0,
        tiled=True,
    ).astype(jnp.float32)
    tokens_f = tokens.astype(f32)
    middle, normed_one, inv_one = layer_norm(
        tokens_f + (attn_sum + vectors[4]), vectors[0], vectors[1]
    )
    middle_all = lax.all_gather(middle.astype(bf16), "tensor", axis=0, tiled=True)
    inner = jnp.dot(middle_all, in_weight, preferred_element_type=f32) + inner_bias
    activated = jax.nn.gelu(inner, approximate=False).astype(bf16)
    ffn_sum = lax.psum_scatter(
        jnp.dot(activated, down_weight, preferred_element_type=f32).astype(jnp.bfloat16),
        "tensor",
        scatter_dimension=0,
        tiled=True,
    ).astype(jnp.float32)
    result, normed_two, inv_two = layer_norm(
        middle + (ffn_sum + vectors[5]), vectors[2], vectors[3]
    )
    block_out = result.astype(bf16)
    grad_out = cotangent.astype(f32)
    grad_gain_two = jnp.sum(grad_out * normed_two, axis=0)
    grad_shift_two = jnp.sum(grad_out, axis=0)
    grad_two = norm_back(grad_out * vectors[2], normed_two, inv_two)
    grad_down_bias = jnp.sum(grad_two, axis=0)
    back_all = lax.all_gather(grad_two.astype(bf16), "tensor", axis=0, tiled=True)
    grad_down_weight = row_contract(activated, back_all)
    grad_act = col_contract(back_all, down_weight)
    grad_inner = (grad_act * gelu_slope(inner)).astype(bf16)
    grad_inner_bias = jnp.sum(grad_inner.astype(f32), axis=0)
    grad_in_weight = row_contract(middle_all, grad_inner)
    grad_middle = grad_two + lax.psum_scatter(
        col_contract(grad_inner, in_weight).astype(jnp.bfloat16),
        "tensor",
        scatter_dimension=0,
        tiled=True,
    ).astype(jnp.float32)
    grad_gain_one = jnp.sum(grad_middle * normed_one, axis=0)
    grad_shift_one = jnp.sum(grad_middle, axis=0)
    grad_one = norm_back(grad_middle * vectors[0], normed_one, inv_one)
    grad_out_bias = jnp.sum(grad_one, axis=0)
    attn_back_all = lax.all_gather(grad_one.astype(bf16), "tensor", axis=0, tiled=True)
    grad_out_weight = row_contract(context_low, attn_back_all)
    grad_context = col_contract(attn_back_all, out_weight).astype(bf16)
    grad_context_four = grad_context.reshape(seq_count, SEQ_LEN, local_heads, HD)

    def backward_block(carry, block_index):
        grad_keys, grad_values = carry
        scores, query_block, key_rows, sequence, offset = block_scores(block_index)
        value_rows = lax.dynamic_index_in_dim(values_four, sequence, 0, keepdims=False)
        log_total = lax.dynamic_index_in_dim(log_totals, block_index, 0, keepdims=False)
        probabilities = jnp.exp(scores - log_total[..., None])
        prob_low = probabilities.astype(bf16)
        grad_rows = lax.dynamic_index_in_dim(grad_context_four, sequence, 0, keepdims=False)
        grad_block = lax.dynamic_slice_in_dim(grad_rows, offset, block_rows, 0)
        grad_probs = jnp.einsum("qhd,khd->hqk", grad_block, value_rows, preferred_element_type=f32)
        grad_scores = probabilities * (
            grad_probs - jnp.sum(grad_probs * probabilities, axis=-1, keepdims=True)
        )
        scores_low = grad_scores.astype(bf16)
        grad_query = (
            jnp.einsum("hqk,khd->qhd", scores_low, key_rows, preferred_element_type=f32)
            * score_scale
        )
        key_term = (
            jnp.einsum("hqk,qhd->khd", scores_low, query_block, preferred_element_type=f32)
            * score_scale
        )
        value_term = jnp.einsum("hqk,qhd->khd", prob_low, grad_block, preferred_element_type=f32)
        grad_keys = lax.dynamic_update_index_in_dim(
            grad_keys,
            lax.dynamic_index_in_dim(grad_keys, sequence, 0, keepdims=False) + key_term,
            sequence,
            0,
        )
        grad_values = lax.dynamic_update_index_in_dim(
            grad_values,
            lax.dynamic_index_in_dim(grad_values, sequence, 0, keepdims=False) + value_term,
            sequence,
            0,
        )
        return ((grad_keys, grad_values), grad_query)

    empty = jnp.zeros((seq_count, SEQ_LEN, local_heads, HD), f32)
    (grad_keys, grad_values), grad_queries = lax.scan(
        backward_block, (empty, empty), jnp.arange(block_total, dtype=jnp.int32)
    )
    grad_proj = jnp.stack(
        [
            grad_queries.reshape(seq_rows, local_width),
            grad_keys.reshape(seq_rows, local_width),
            grad_values.reshape(seq_rows, local_width),
        ]
    ).astype(bf16)
    grad_proj_weight = jnp.einsum("td,kte->kde", inputs_all, grad_proj, preferred_element_type=f32)
    grad_query_bias = jnp.sum(grad_proj[0].astype(f32), axis=0)
    grad_value_bias = jnp.sum(grad_proj[2].astype(f32), axis=0)
    input_part = jnp.einsum("kte,kde->td", grad_proj, proj_weight, preferred_element_type=f32)
    vector_part = jnp.stack(
        [
            grad_gain_one,
            grad_shift_one,
            grad_gain_two,
            grad_shift_two,
            grad_out_bias,
            grad_down_bias,
        ]
    )
    input_share, vector_grad = (
        lax.psum_scatter(
            input_part.astype(jnp.bfloat16), "tensor", scatter_dimension=0, tiled=True
        ).astype(jnp.float32),
        lax.psum_scatter(
            vector_part.astype(jnp.bfloat16), "tensor", scatter_dimension=1, tiled=True
        ).astype(jnp.float32),
    )
    input_grad = (grad_one + input_share).astype(bf16)
    flat_grad = jnp.concatenate(
        [
            grad_proj_weight.reshape(-1),
            grad_out_weight.reshape(-1),
            grad_in_weight.reshape(-1),
            grad_down_weight.reshape(-1),
            grad_query_bias,
            grad_value_bias,
            grad_inner_bias,
            vector_grad.reshape(-1),
        ]
    )
    dp_size = lax.axis_size("dp")
    per_group = dp_size // GROUPS
    inner_bits = per_group.bit_length() - 1
    all_bits = dp_size.bit_length() - 1
    dp_index = lax.axis_index("dp")
    slot_index = dp_index % per_group
    piece_len = shared_weights.shape[1]
    grid_view = flat_grad.reshape(GROUPS, per_group, piece_len)
    inner_list = list(range(inner_bits))
    outer_list = list(range(inner_bits, all_bits))
    inner_list = inner_list[::-1]
    outer_list = outer_list[::-1]
    summed_grid = grid_view
    for bit_number in inner_list:
        summed_grid = summed_grid + from_partner(
            summed_grid.astype(jnp.bfloat16), "dp", bit_number
        ).astype(summed_grid.dtype)
    grad_block = lax.dynamic_index_in_dim(summed_grid, slot_index, 1, keepdims=False)
    weights_block = lax.dynamic_index_in_dim(
        masters.reshape(GROUPS, per_group, piece_len), slot_index, 1, keepdims=False
    )
    matrix_count = (4 * D * D + 2 * D * FF) // tensor_size
    flat_index = (
        jnp.arange(GROUPS, dtype=jnp.int32)[:, None] * per_group + slot_index
    ) * piece_len + jnp.arange(piece_len, dtype=jnp.int32)[None, :]
    decay_mask = (flat_index < matrix_count).astype(f32)
    first_new = BETA_ONE * first_moment[0, 0] + (1 - BETA_ONE) * grad_block
    second_new = BETA_TWO * second_moment[0, 0] + (1 - BETA_TWO) * grad_block * grad_block
    first_hat = first_new / (1 - BETA_ONE**STEP)
    second_hat = second_new / (1 - BETA_TWO**STEP)
    group_weights = weights_block - INNER_RATE * (
        first_hat / (jnp.sqrt(second_hat) + ADAM_EPS) + DECAY * decay_mask * weights_block
    )
    difference = weights_block - group_weights

    def outer_swap(outgoing, bit_number):
        return from_partner(outgoing.astype(jnp.bfloat16), "dp", bit_number).astype(outgoing.dtype)

    outer_bits = all_bits - inner_bits
    diff_view = difference.reshape((2,) * outer_bits + (piece_len,))
    diff_sum = halve_rounds(diff_view, outer_list, 0, all_bits - 1, dp_index, outer_swap).reshape(
        piece_len
    )
    mean_diff = diff_sum / GROUPS
    new_momentum = OUTER_MU * outer_momentum[0] + mean_diff
    new_weights = shared_weights[0] - OUTER_RATE * (mean_diff + OUTER_MU * new_momentum)
    return (
        block_out,
        input_grad,
        grad_block[None, None],
        first_new[None, None],
        second_new[None, None],
        group_weights[None, None],
        mean_diff[None],
        new_momentum[None],
        new_weights[None],
    )


LANES = 128
NT = (((1,), (1,)), ((), ()))
NN = (((1,), (0,)), ((), ()))
TN = (((0,), (0,)), ((), ()))
VMEM_BYTES = 61 << 20
f32 = jnp.float32
bf16 = jnp.bfloat16


def dot(left, right, dims):
    return lax.dot_general(left, right, dims, preferred_element_type=f32)


def params(**more):
    return pltpu.CompilerParams(vmem_limit_bytes=VMEM_BYTES, **more)


def round_up(number, step):
    return -(-number // step) * step


def matrix_table(tensor_size):
    local_width = D // tensor_size
    hidden = FF // tensor_size
    table = []
    offset = 0
    for rows, columns in ((3 * D, local_width), (local_width, D), (D, hidden), (hidden, D)):
        blocks = columns // LANES
        table.append((offset, rows, blocks))
        offset += rows * blocks
    return table, offset


def chunk_plan(table, first, end, tail_at, tail_rows):
    segments = []
    base = None
    for number, (offset, rows, blocks) in enumerate(table):
        low = max(first, offset)
        high = min(end, offset + rows * blocks)
        if low >= high:
            continue
        row_low = (low - offset) // blocks // 16 * 16
        row_high = min(rows, round_up(-(-(high - offset) // blocks), 16))
        if base is None:
            base = offset + row_low * blocks
        segments.append((number, row_low, row_high, blocks, offset + row_low * blocks - base))
    size = max(at + (high - low) * blocks for _, low, high, blocks, at in segments)
    if end > tail_at:
        size = max(size, tail_at + tail_rows - base)
    return segments, base, size


def row_parts(rows, count):
    size = rows // count // 16 * 16
    starts = [size * i for i in range(count)] + [rows]
    return [(low, high - low) for low, high in zip(starts[:-1], starts[1:])]


def in_steps(start, rows, step, body):
    @pl.loop(0, rows // step)
    def _(i):
        body(pl.multiple_of(start + i * step, 16), step)

    if rows % step:
        body(start + rows // step * step, rows % step)


def update_kernel(
    slot_ref, g_hbm, w_hbm, m_hbm, v_hbm, d_hbm, own_hbm, mom_hbm, dh1_hbm, dx_hbm,
    go, mo, vo, wo, mean_out, mom_out, new_out, input_out,
    g_s, w_s, m_s, v_s, m_new, v_new, w_new, sems, dh1_s, dx_s, input_s, input_sems,
    *, piece_rows, tail_rows, parts
):
    slot = slot_ref[0]
    units = [(b, part) for b in range(GROUPS) for part in parts] + [(None, part) for part in parts]

    def loads(u):
        b, (at, rows) = units[u]
        k = u % 3
        r = pl.ds(at, rows)
        wide = pl.ds(at, round_up(rows, 16))
        there, padded = pl.ds(0, rows), pl.ds(0, round_up(rows, 16))
        if b is None:
            pairs = (
                (d_hbm.at[wide], g_s.at[k, padded]),
                (own_hbm.at[r, 0, :], m_s.at[k, there]),
                (mom_hbm.at[r, 0, :], v_s.at[k, there]),
            )
        else:
            pairs = (
                (g_hbm.at[b, wide], g_s.at[k, padded]),
                (m_hbm.at[r, b, :], m_s.at[k, there]),
                (v_hbm.at[r, b, :], v_s.at[k, there]),
                (w_hbm.at[b, wide], w_s.at[k, padded]),
            )
        return [pltpu.make_async_copy(src, dst, sems.at[n, k]) for n, (src, dst) in enumerate(pairs)]

    def stores(u):
        b, (at, rows) = units[u]
        k = u % 3
        r = pl.ds(at, rows)
        there = pl.ds(0, rows)
        if b is None:
            pairs = (
                (m_new.at[k, there], mean_out.at[r, 0, :]),
                (v_new.at[k, there], mom_out.at[r, 0, :]),
                (w_new.at[k, there], new_out.at[r, 0, :]),
            )
        else:
            pairs = (
                (m_new.at[k, there], mo.at[r, b, :]),
                (v_new.at[k, there], vo.at[r, b, :]),
                (w_new.at[k, there], wo.at[r, b, :]),
                (g_s.at[k, there], go.at[r, b, :]),
            )
        return [pltpu.make_async_copy(src, dst, sems.at[4 + n, k]) for n, (src, dst) in enumerate(pairs)]

    input_loads = [
        pltpu.make_async_copy(dh1_hbm, dh1_s, input_sems.at[0]),
        pltpu.make_async_copy(dx_hbm, dx_s, input_sems.at[1]),
    ]
    input_store = pltpu.make_async_copy(input_s, input_out, input_sems.at[2])
    half = dh1_s.shape[0]

    def input_gradient():
        for copy in input_loads:
            copy.wait()

        @pl.loop(0, half // 32)
        def _(i):
            r = pl.ds(pl.multiple_of(i * 32, 32), 32)
            far = pl.ds(pl.multiple_of(half + i * 32, 32), 32)
            input_s[r, :] = (dh1_s[r, :] + dx_s[r, :].astype(f32) + dx_s[far, :].astype(f32)).astype(bf16)

        input_store.start()

    for copy in loads(0):
        copy.start()
    for u, (b, (at, rows)) in enumerate(units):
        if u == 1:
            for copy in input_loads:
                copy.start()
        if u == 4:
            input_gradient()
        k = u % 3
        if u > 1:
            for copy in stores(u - 2):
                copy.wait()
        if u + 1 < len(units):
            for copy in loads(u + 1):
                copy.start()
        for copy in loads(u):
            copy.wait()

        def inner(start, count, b=b, at=at, k=k):
            r = pl.ds(start, count)
            g = g_s[k, r, :]
            if b is None:
                average = g / GROUPS
                momentum = OUTER_MU * v_s[k, r, :] + average
                m_new[k, r, :] = average
                v_new[k, r, :] = momentum
                w_new[k, r, :] = m_s[k, r, :] - OUTER_RATE * (average + OUTER_MU * momentum)
                return
            w = w_s[k, r, :].astype(f32)
            first = BETA_ONE * m_s[k, r, :] + (1 - BETA_ONE) * g
            second = BETA_TWO * v_s[k, r, :] + (1 - BETA_TWO) * g * g
            root = jnp.sqrt(second * (1 / (1 - BETA_TWO**STEP))) + ADAM_EPS
            decay = INNER_RATE * DECAY
            if b == GROUPS - 1:
                here = lax.broadcasted_iota(jnp.int32, (count, LANES), 0) + (at + start)
                decay = jnp.where((slot < 3) | (here < piece_rows - tail_rows), decay, 0.0)
            m_new[k, r, :] = first
            v_new[k, r, :] = second
            w_new[k, r, :] = w - ((INNER_RATE / (1 - BETA_ONE**STEP)) * first / root + decay * w)

        in_steps(0, round_up(rows, 16), 128, inner)
        for copy in stores(u):
            copy.start()
    for u in (len(units) - 2, len(units) - 1):
        for copy in stores(u):
            copy.wait()
    input_store.wait()


def update(slot, grads, pieces, first, second, d_sum, own_rows, momentum_rows, dh1, dx, tail_rows):
    piece_rows = first.shape[0]
    hbm = pl.BlockSpec(memory_space=pl.ANY)
    parts = row_parts(piece_rows, 1)
    most = round_up(max(rows for _, rows in parts), 16)
    wide = pltpu.VMEM((3, most, LANES), f32)
    state = jax.ShapeDtypeStruct(first.shape, f32)
    piece = jax.ShapeDtypeStruct(own_rows.shape, f32)
    return pl.pallas_call(
        functools.partial(update_kernel, piece_rows=piece_rows, tail_rows=tail_rows, parts=parts),
        in_specs=[pl.BlockSpec(memory_space=pltpu.SMEM)] + [hbm] * 9,
        out_specs=[hbm] * 8,
        out_shape=[state] * 4 + [piece] * 3 + [jax.ShapeDtypeStruct(dh1.shape, bf16)],
        scratch_shapes=[wide, pltpu.VMEM((3, most, LANES), bf16)]
        + [wide] * 5
        + [
            pltpu.SemaphoreType.DMA((8, 3)),
            pltpu.VMEM(dh1.shape, f32),
            pltpu.VMEM(dx.shape, bf16),
            pltpu.VMEM(dh1.shape, bf16),
            pltpu.SemaphoreType.DMA((3,)),
        ],
        cost_estimate=pl.CostEstimate(
            flops=120 * piece_rows * LANES,
            bytes_accessed=120 * piece_rows * LANES,
            transcendentals=8 * piece_rows * LANES,
        ),
        compiler_params=params(),
        name="update",
    )(slot, grads, pieces, first, second, d_sum, own_rows, momentum_rows, dh1, dx)


def document_rows(seg_ref, live_ref, me):
    half = seg_ref.shape[1] // 2

    def own_first(row):
        left, right = row[:, :half], row[:, half:]
        return jnp.concatenate(
            [jnp.where(me == 0, left, right), jnp.where(me == 0, right, left)], axis=1
        )

    seg = own_first(seg_ref[...])
    return seg.astype(f32), jnp.where(own_first(live_ref[...]) == 1, seg, -1).astype(f32)


def as_column(row):
    return jnp.broadcast_to(row, (LANES, row.shape[1])).T


def attend_block(q, k, v_ones, code, seg_col, offset):
    rows_q, n = q.shape[0], k.shape[0]
    low = lax.broadcasted_iota(jnp.int32, (1, LANES), 1) < HD
    zero = jnp.zeros((), bf16)
    q = q * jnp.asarray(HD**-0.5, bf16)
    rows = lax.broadcasted_iota(jnp.int32, (rows_q, n), 0) + offset
    cols = lax.broadcasted_iota(jnp.int32, (rows_q, n), 1)
    allowed = (seg_col == code) | (rows == cols)
    outs = []
    tops = []
    for h in range(2):
        qh = jnp.where(low, q, zero) if h == 0 else jnp.where(low, zero, q)
        s = jnp.where(allowed, dot(qh, k, NT), MASKED)
        top = jnp.max(s, axis=1, keepdims=True)
        p = jnp.exp(s - top).astype(bf16)
        outs.append(dot(p, v_ones[h], NN))
        tops.append(top)
    num = jnp.where(low, outs[0], outs[1])
    den = pltpu.roll(jnp.where(low, outs[1], outs[0]), HD, 1)
    lse = (jnp.where(low, tops[0], tops[1]) + jnp.log(den)).T
    return (num / den).astype(bf16), lse[0:1], lse[HD : HD + 1]


def widen(src, low, high, flat, to):
    step = 128
    full = (high - low) // step

    @pl.loop(0, full)
    def _(i):
        rows = src[pl.ds(pl.multiple_of(low + i * step, 16), step), :]
        flat[pl.ds(to + i * step, step), :] = rows.astype(f32)

    rest = (high - low) % step
    if rest:
        flat[pl.ds(to + full * step, rest), :] = src[low + full * step : high, :].astype(f32)


def bring_rows(buf, flat, margin, offset, count, piece_rows):
    for p, low, high, at in piece_spans(offset, count, piece_rows, buf.shape[1]):
        widen(buf.at[p], low, high, flat, margin + at)


def emit_matrix(flat, out, margin, rows, blocks, first=0):
    chunk = 64

    @pl.loop(0, rows // chunk)
    def _(c):
        at = pl.ds(pl.multiple_of(first + c * chunk, chunk), chunk)
        for j in range(blocks):
            from_rows = pl.ds(margin + c * (chunk * blocks) + j, chunk, stride=blocks)
            out[at, j * LANES : (j + 1) * LANES] = flat[from_rows, :].astype(bf16)


def piece_spans(offset, count, piece_rows, padded):
    spans = []
    for p in range(offset // piece_rows, -(-(offset + count) // piece_rows)):
        low = max(offset - p * piece_rows, 0) // 16 * 16
        high = min(round_up(min(offset + count - p * piece_rows, piece_rows), 16), padded)
        spans.append((p, low, high, p * piece_rows + low - offset))
    return spans


def start_kernel(
    own_hbm, tokens_hbm, seg_ref, live_ref,
    proj_out, outw_out, inw_out, down_out, outw2_out, ctx2_out, pieces_out, x_out,
    q_out, k_out, v_out, ctx_out, vec_ref, c1_ref, lse_ref,
    rows32, buf, xbuf, flat, proj_s, outw_s, inw_s, down_s, outw2_s, obuf, ctx2_s, vec_s,
    zdown, zup, zrecv, ysend, yrecv, csend, crecv, xsem, local_sems, ctx_sems, wo_sems, q_ref, k_ref, v_ref, ctx_ref, seg_s,
    *, piece_rows, tail_rows, table, cuts, rows_q
):
    z = lax.axis_index("group")
    slot = lax.axis_index("slot")
    me = lax.axis_index("tensor")
    depth = GROUPS
    padded = buf.shape[1]
    half = tokens_hbm.shape[0]
    n = 2 * half
    mesh_id = pl.DeviceIdType.MESH

    load = pltpu.make_async_copy(own_hbm.at[:, 0, :], rows32, local_sems.at[0])
    load.start()
    x_load = pltpu.make_async_copy(tokens_hbm, xbuf.at[pl.ds(0, half)], local_sems.at[1])
    x_load.start()

    barrier = pltpu.get_barrier_semaphore()
    for where in ({"slot": slot ^ 1}, {"slot": slot ^ 2}, {"tensor": 1 - me}):
        pl.semaphore_signal(barrier, inc=1, device_id=where, device_id_type=mesh_id)

    @pl.when(z > 0)
    def _():
        pl.semaphore_signal(barrier, inc=1, device_id={"group": z - 1}, device_id_type=mesh_id)

    @pl.when(z < depth - 1)
    def _():
        pl.semaphore_signal(barrier, inc=1, device_id={"group": z + 1}, device_id_type=mesh_id)

    pl.semaphore_wait(barrier, 3 + jnp.where(z > 0, 1, 0) + jnp.where(z < depth - 1, 1, 0))

    load.wait()
    own = z * 4 + slot
    step = 128
    full = piece_rows // step

    @pl.loop(0, full)
    def _(i):
        r = pl.ds(pl.multiple_of(i * step, step), step)
        buf[own, r, :] = rows32[r, :].astype(bf16)

    tail = rows32[piece_rows - tail_rows :, :]
    left = tail - tail.astype(bf16).astype(f32)
    zeros = jnp.zeros((padded - piece_rows - tail_rows, LANES), f32)
    buf[own, full * step :, :] = jnp.concatenate([rows32[full * step :, :], left, zeros], axis=0).astype(bf16)

    def copy_of(piece, h, send, recv, where):
        part = buf.at[piece, pl.ds(*cuts[h])]
        return pltpu.make_async_remote_copy(
            src_ref=part, dst_ref=part, send_sem=send, recv_sem=recv, device_id=where, device_id_type=mesh_id
        )

    def down(b, h):
        return copy_of(b * 4 + slot, h, zdown.at[b, h], zrecv.at[b, h], {"group": z + 1})

    def up(b, h):
        return copy_of(b * 4 + slot, h, zup.at[b, h], zrecv.at[b, h], {"group": z - 1})

    def side(b, h):
        return copy_of(b * 4 + slot, h, ysend.at[b, h], yrecv.at[b, h], {"slot": slot ^ 2})

    def side_in(b, h):
        return copy_of(b * 4 + (slot ^ 2), h, ysend.at[b, h], yrecv.at[b, h], {"slot": slot ^ 2})

    def twin(b, h, k):
        return copy_of(
            b * 4 + (slot ^ (2 * k)), h, csend.at[2 * b + k, h], crecv.at[2 * b + k, h], {"slot": slot ^ 1}
        )

    def twin_in(b, h, k):
        return copy_of(
            b * 4 + (slot ^ 1 ^ (2 * k)), h, csend.at[2 * b + k, h], crecv.at[2 * b + k, h], {"slot": slot ^ 1}
        )

    parts = range(len(cuts))
    tail_part = len(cuts) - 1
    order = [tail_part] + list(range(tail_part))
    last = depth - 1
    ranked = (
        z,
        jnp.where(z == 0, 1, 0),
        jnp.where(z == 0, 2, jnp.where(z == 1, 3, 1)),
        jnp.where((z == 0) | (z == 2), 3, 2),
    )
    middle = (z == 1) | (z == 2)
    edge = jnp.logical_not(middle)

    def pass_on(b, h, aside=True):
        up(b, h).wait_recv()

        @pl.when((b < z) & (z < last))
        def _():
            down(b, h).start()

        @pl.when((b > z) & (z > 0))
        def _():
            up(b, h).start()

        if aside:
            side(b, h).start()
        twin(b, h, 0).start()

    def serve_z(b, h, when=None, aside=True):
        if h == tail_part:
            when = (b != last) if when is None else when & (b != last)
        if when is None:
            pass_on(b, h, aside)
        else:
            pl.when(when)(functools.partial(pass_on, b, h, aside))

    def serve_y(rank, h):
        b = ranked[rank]

        def go():
            side_in(b, h).wait_recv()
            twin(b, h, 1).start()

        if h == tail_part:
            pl.when(b != last)(go)
        else:
            go()

    for number, h in enumerate(order):
        pl.when(z > 0)(lambda h=h: up(z, h).start())
        at_once = (z == 0) | ((z == 1) & (number < 2)) | ((z == 2) & (number < 3))
        pl.when(at_once)(lambda h=h: down(z, h).start())
        side(z, h).start()
        twin(z, h, 0).start()

    x_load.wait()
    x_copy = pltpu.make_async_remote_copy(
        src_ref=xbuf.at[pl.ds(0, half)],
        dst_ref=xbuf.at[pl.ds(half, half)],
        send_sem=xsem.at[0],
        recv_sem=xsem.at[1],
        device_id={"tensor": 1 - me},
        device_id_type=mesh_id,
    )
    x_copy.start()

    pl.when(z == last - 1)(functools.partial(pass_on, last, tail_part))
    for h in order:
        serve_z(ranked[3], h, middle, False)
        serve_z(ranked[1], h)
    pl.when(z < last - 1)(functools.partial(pass_on, last, tail_part))

    def side_later(h):
        aside = middle & (ranked[3] != last) if h == tail_part else middle
        pl.when(aside)(lambda: side(ranked[3], h).start())

    for number, h in enumerate(order):
        later = ((z == 1) & (number >= 2)) | ((z == 2) & (number >= 3))
        pl.when(later)(lambda h=h: down(z, h).start())
        if number < 2:
            side_later(h)
    for h in order:
        serve_z(ranked[2], h, middle)
    for h in order[2:]:
        side_later(h)
    for h in order:
        serve_z(ranked[2], h, z == 0)
    for h in order[:3]:
        serve_z(ranked[3], h, z == last)
    side_in(last, tail_part).wait_recv()
    twin(last, tail_part, 1).start()
    for rank in range(2):
        for h in order:
            serve_y(rank, h)
    for k in range(2):
        twin_in(last, tail_part, k).wait_recv()
        for rank in range(2):
            b = ranked[rank]
            for h in parts:
                if h == tail_part:
                    pl.when(b != last)(lambda b=b, h=h, k=k: twin_in(b, h, k).wait_recv())
                else:
                    twin_in(b, h, k).wait_recv()

    at = (piece_rows - tail_rows) // 16 * 16
    shift = piece_rows - tail_rows - at
    ends = buf[4 * depth - 1, at:, :].astype(f32)
    vectors = ends[shift : shift + tail_rows] + ends[shift + tail_rows : shift + 2 * tail_rows]
    vec_s[0] = vectors

    def to_partner(src, dst, send, recv):
        return pltpu.make_async_remote_copy(
            src_ref=src, dst_ref=dst, send_sem=send, recv_sem=recv,
            device_id={"tensor": 1 - me}, device_id_type=mesh_id,
        )

    vec_copy = to_partner(vec_s.at[0], vec_s.at[1], xsem.at[2], xsem.at[3])
    vec_copy.start()
    (wo_offset, wo_rows, wo_blocks) = table[1]
    spans = piece_spans(wo_offset, wo_rows * wo_blocks, piece_rows, padded)
    total = sum(high - low for _, low, high, _ in spans)
    halves = (round_up(total // 2, 16), total)
    wo_parts = ([], [])
    at = 0
    for p, low, high, _ in spans:
        split = min(max(low + halves[0] - at, low), high)
        if split > low:
            wo_parts[0].append((p, low, split - low, at))
        if high > split:
            wo_parts[1].append((p, split, high - split, at + split - low))
        at += high - low
    in_core = slot % 2

    def wo_copies(c):
        return [
            to_partner(
                buf.at[p, pl.ds(low, count)], obuf.at[pl.ds(to, count)], wo_sems.at[0, j], wo_sems.at[1, j]
            )
            for j, (p, low, count, to) in enumerate(wo_parts[c])
        ]

    def wo_twin(c):
        first, end = (0, halves[0]) if c == 0 else halves
        part = obuf.at[pl.ds(first, end - first)]
        return pltpu.make_async_remote_copy(
            src_ref=part, dst_ref=part, send_sem=wo_sems.at[0, 3], recv_sem=wo_sems.at[1, 3],
            device_id={"slot": slot ^ 1}, device_id_type=mesh_id,
        )

    def by_core(action):
        for c in range(2):
            pl.when(in_core == c)(functools.partial(action, c))

    def wo_send(c):
        for copy in wo_copies(c):
            copy.start()

    def wo_pass(c):
        for copy in wo_copies(c):
            copy.wait_recv()
        wo_twin(c).start()

    def wo_done(c):
        wo_twin(1 - c).wait_recv()

    def wo_sent(c):
        for copy in wo_copies(c):
            copy.wait_send()
        wo_twin(c).wait_send()

    pl.when(z < 2)(lambda: by_core(wo_send))
    margin = 16
    (offset, rows, blocks) = table[0]
    bring_rows(buf, flat, margin, offset, rows * blocks, piece_rows)
    emit_matrix(flat, proj_s, margin, rows, blocks)
    out_copies = [pltpu.make_async_copy(proj_s, proj_out, local_sems.at[2])]
    out_copies[0].start()
    x_copy.wait()
    out_copies.append(pltpu.make_async_copy(xbuf, x_out, local_sems.at[3]))
    out_copies[1].start()
    query_bias = jnp.concatenate([vectors[j : j + 1] for j in range(blocks)], axis=1)
    value_bias = jnp.concatenate([vectors[blocks + j : blocks + j + 1] for j in range(blocks)], axis=1)
    depth_in = rows // 3
    for m, (ref, bias) in enumerate(((q_ref, query_bias), (k_ref, None), (v_ref, value_bias))):

        @pl.loop(0, n // 256)
        def _(i, m=m, ref=ref, bias=bias):
            r = pl.ds(pl.multiple_of(i * 256, 256), 256)
            acc = dot(xbuf[r, :], proj_s[m * depth_in : (m + 1) * depth_in, :], NN)
            if bias is not None:
                acc = acc + bias
            ref[r, :] = acc.astype(bf16)

    for number, (ref, out) in enumerate(((q_ref, q_out), (k_ref, k_out), (v_ref, v_out))):
        out_copies.append(pltpu.make_async_copy(ref, out, local_sems.at[13 + number]))
        out_copies[-1].start()
    third = jnp.where(z == 0, ranked[3], ranked[2])
    todo = [functools.partial(serve_z, third, h, edge) for h in order]
    todo += [functools.partial(serve_z, ranked[3], h, z == last) for h in order[3:]]
    todo += [functools.partial(serve_y, 2, h) for h in order]

    def landed(rank):
        b = ranked[rank]
        for h in parts:
            for k in range(2):
                if h == tail_part:
                    pl.when(b != last)(lambda b=b, h=h, k=k: twin_in(b, h, k).wait_recv())
                else:
                    twin_in(b, h, k).wait_recv()

    def ctx_copies(pair):
        columns = pl.ds(pair * LANES, LANES)
        return [
            to_partner(
                ctx_ref.at[pl.ds(half - first, half), columns],
                ctx2_s.at[pl.ds(first, half), columns],
                ctx_sems.at[0, 2 * pair + first // half],
                ctx_sems.at[1, 2 * pair + first // half],
            )
            for first in (0, half)
        ]

    low = lax.broadcasted_iota(jnp.int32, (1, LANES), 1) < HD
    one = jnp.ones((), bf16)
    seg, code = document_rows(seg_ref, live_ref, me)
    seg_s[...] = as_column(seg)
    for pair in range(blocks):
        c = slice(pair * LANES, (pair + 1) * LANES)
        k = k_ref[:, c]
        v = v_ref[:, c]
        v_ones = (jnp.where(low, v, one), jnp.where(low, one, v))
        for i in range(n // rows_q):
            r = slice(i * rows_q, (i + 1) * rows_q)
            ctx, lse_0, lse_1 = attend_block(q_ref[r, c], k, v_ones, code, seg_s[r, 0:1], i * rows_q)
            ctx_ref[r, c] = ctx
            lse_ref[pair, 0:1, r] = lse_0
            lse_ref[pair, 1:2, r] = lse_1
            if todo:
                todo.pop(0)()
        for copy in ctx_copies(pair):
            copy.start()
        if pair == 2:
            for act in todo:
                act()
            todo = []
            landed(2)
            pl.when(z >= 2)(lambda: by_core(wo_send))
    out_copies.append(pltpu.make_async_copy(ctx_ref, ctx_out, local_sems.at[16]))
    out_copies[-1].start()
    scratches = (None, outw_s, inw_s, down_s)
    mat_copies = [
        None,
        pltpu.make_async_copy(outw_s, outw_out, local_sems.at[4]),
        pltpu.make_async_copy(inw_s, inw_out, local_sems.at[5]),
        pltpu.make_async_copy(down_s, down_out, local_sems.at[6]),
    ]

    def matrix(m, first=0, end=None):
        (offset, rows, blocks) = table[m]
        count = (rows if end is None else end) - first
        bring_rows(buf, flat, margin, offset + first * blocks, count * blocks, piece_rows)
        emit_matrix(flat, scratches[m], margin, count, blocks, first)

    chunk_rows = 4 * piece_rows
    in_cut = (2 * chunk_rows - table[2][0]) // table[2][2] // 64 * 64
    down_cut = round_up(-(-(3 * chunk_rows - table[3][0]) // table[3][2]), 64)
    matrix(1)
    matrix(2, 0, in_cut)
    pl.when(ranked[3] == last)(lambda: matrix(2, in_cut))
    pl.when(ranked[3] != last)(lambda: matrix(3, down_cut))
    mat_copies[1].start()
    for h in order:
        serve_y(3, h)
    pl.when(z < 2)(lambda: by_core(wo_pass))
    landed(3)

    @pl.when(ranked[3] == last)
    def _():
        mat_copies[2].start()
        matrix(3, 0, down_cut)
        matrix(3, down_cut)
        mat_copies[3].start()

    @pl.when(ranked[3] != last)
    def _():
        matrix(3, 0, down_cut)
        mat_copies[3].start()
        matrix(2, in_cut)
        mat_copies[2].start()

    pl.when(z >= 2)(lambda: by_core(wo_pass))
    by_core(wo_done)
    at = 0
    for p, low, high, to in spans:
        widen(obuf, at, at + high - low, flat, margin + to)
        at += high - low
    emit_matrix(flat, outw2_s, margin, wo_rows, wo_blocks)
    out_copies.append(pltpu.make_async_copy(outw2_s, outw2_out, local_sems.at[11]))
    out_copies[-1].start()

    vec_copy.wait()
    hidden_rows = table[2][2]
    for j in range(hidden_rows):
        c1_ref[0:1, j * LANES : (j + 1) * LANES] = vec_s[0, 2 * blocks + j : 2 * blocks + j + 1, :]
    for row in range(6):
        for j in range(blocks):
            from_row = 2 * blocks + hidden_rows + row * blocks + j
            mine, theirs = vec_s[0, from_row : from_row + 1, :], vec_s[1, from_row : from_row + 1, :]
            left, right = jnp.where(me == 0, mine, theirs), jnp.where(me == 0, theirs, mine)
            vec_ref[row : row + 1, j * LANES : (j + 1) * LANES] = left
            vec_ref[row : row + 1, (blocks + j) * LANES : (blocks + j + 1) * LANES] = right

    for pair in range(blocks):
        for copy in ctx_copies(pair):
            copy.wait()
    out_copies.append(pltpu.make_async_copy(ctx2_s, ctx2_out, local_sems.at[12]))
    out_copies[-1].start()
    by_core(wo_sent)
    for b in range(depth):
        copy = pltpu.make_async_copy(buf.at[b * 4 + slot], pieces_out.at[b], local_sems.at[7 + b])
        copy.start()
        out_copies.append(copy)
    out_copies += mat_copies[1:]

    for b in range(depth):
        for h in parts:

            @pl.when((b <= z) & (z < depth - 1))
            def _(b=b, h=h):
                down(b, h).wait_send()

            @pl.when((b >= z) & (z > 0))
            def _(b=b, h=h):
                up(b, h).wait_send()

            side(b, h).wait_send()
            for k in range(2):
                twin(b, h, k).wait_send()
    for copy in out_copies:
        copy.wait()


def start(own_rows, tokens, seg_row, live_row, table, tail_rows, padded, cuts, rows_q=256):
    piece_rows = own_rows.shape[0]
    half, width = tokens.shape
    n = 2 * half
    pairs = table[0][2]
    local_width = pairs * LANES
    hbm = pl.BlockSpec(memory_space=pl.ANY)
    whole = pl.BlockSpec(memory_space=pltpu.VMEM)
    mats = [jax.ShapeDtypeStruct((rows, blocks * LANES), bf16) for _, rows, blocks in table]
    acts = [jax.ShapeDtypeStruct((n, local_width), bf16)] * 4
    most = max(rows * blocks for _, rows, blocks in table)
    parts = len(cuts)
    dma = pltpu.SemaphoreType.DMA
    return pl.pallas_call(
        functools.partial(
            start_kernel, piece_rows=piece_rows, tail_rows=tail_rows, table=table, cuts=cuts, rows_q=rows_q
        ),
        in_specs=[hbm, hbm, whole, whole],
        out_specs=[hbm] * 12 + [whole] * 3,
        out_shape=mats
        + [
            mats[1],
            jax.ShapeDtypeStruct((n, local_width), bf16),
            jax.ShapeDtypeStruct((GROUPS, padded, LANES), bf16),
            jax.ShapeDtypeStruct((n, width), bf16),
        ]
        + acts
        + [
            jax.ShapeDtypeStruct((6, width), f32),
            jax.ShapeDtypeStruct((1, table[2][2] * LANES), f32),
            jax.ShapeDtypeStruct((pairs, 2, n), f32)],
        scratch_shapes=[
            pltpu.VMEM((piece_rows, LANES), f32),
            pltpu.VMEM((4 * GROUPS, padded, LANES), bf16),
            pltpu.VMEM((n, width), bf16),
            pltpu.VMEM((most + 48, LANES), f32),
        ]
        + [pltpu.VMEM(m.shape, bf16) for m in mats]
        + [
            pltpu.VMEM(mats[1].shape, bf16),
            pltpu.VMEM((round_up(table[1][1] * table[1][2] + 64, 16), LANES), bf16),
            pltpu.VMEM((n, local_width), bf16),
            pltpu.VMEM((2, tail_rows, LANES), f32),
            dma((GROUPS, parts)),
            dma((GROUPS, parts)),
            dma((GROUPS, parts)),
            dma((GROUPS, parts)),
            dma((GROUPS, parts)),
            dma((2 * GROUPS, parts)),
            dma((2 * GROUPS, parts)),
            dma((4,)),
            dma((17,)),
            dma((2, 2 * pairs)),
            dma((2, 4)),
        ]
        + [pltpu.VMEM(a.shape, bf16) for a in acts]
        + [pltpu.VMEM((n, LANES), f32)],
        cost_estimate=pl.CostEstimate(
            flops=6 * n * width * local_width, bytes_accessed=60 << 20, transcendentals=8 * n * n
        ),
        compiler_params=params(collective_id=1, has_side_effects=True),
        name="start",
    )(own_rows, tokens, seg_row, live_row)


ERF = (0.254829592, -0.284496736, 1.421413741, -1.453152027, 1.061405429)
ERF_P = 0.3275911


def gelu_pair(u):
    bell = jnp.exp(-0.5 * u * u)
    t = 1.0 / (1.0 + (ERF_P * ROOT_HALF) * jnp.abs(u))
    poly = ERF[4]
    for number in ERF[3::-1]:
        poly = poly * t + number
    tail = (0.5 * poly * t) * bell
    phi = jnp.where(u >= 0, 1.0 - tail, tail)
    return u * phi, phi + u * bell * INV_ROOT_TWO_PI


def fold(values):
    return values.reshape(values.shape[0] // 8, 8, values.shape[1]).sum(axis=0)


def middle_kernel(
    outw_hbm, outw2_hbm, ctx_hbm, ctx2_hbm, x_hbm, inw_hbm, down_hbm, cot_hbm, vec_ref, c1_ref,
    block_hbm, dh1_hbm, dctx_hbm, d_outw_hbm, d_outw2_hbm, d_inw_hbm, d_down_hbm, tail_out,
    outw_ref, outw2_ref, ctx_ref, ctx2_ref, x_ref, inw_ref, down_ref, cot_ref,
    block_out, dh1_out, dctx_out, d_outw, d_outw2, d_inw, d_down,
    x1, norm1, inv1, x1_all, act, slope, dh2_all, dh1_low, dctx_send, part, dh2, box_send, box_recv, sums, c1_sum, vec_box, send_sems, recv_sems, vec_sems,
    load_sems, store_sems, in_sems,
    *, chunk
):
    me = lax.axis_index("tensor")
    loads = [
        pltpu.make_async_copy(src, dst, load_sems.at[number])
        for number, (src, dst) in enumerate(
            (
                (outw_hbm, outw_ref),
                (outw2_hbm, outw2_ref),
                (ctx_hbm, ctx_ref),
                (ctx2_hbm, ctx2_ref),
                (x_hbm, x_ref),
                (inw_hbm, inw_ref),
                (down_hbm, down_ref),
                (cot_hbm, cot_ref),
            )
        )
    ]
    for copy in loads:
        copy.start()
    block_store, dh1_store, dctx_store, outw_store, outw2_store, down_store = stores = [
        pltpu.make_async_copy(src, dst, store_sems.at[number])
        for number, (src, dst) in enumerate(
            (
                (block_out, block_hbm),
                (dh1_out, dh1_hbm),
                (dctx_out, dctx_hbm),
                (d_outw, d_outw_hbm),
                (d_outw2, d_outw2_hbm),
                (d_down, d_down_hbm),
            )
        )
    ]
    half, width = cot_ref.shape
    count = half // chunk
    mesh_id = pl.DeviceIdType.MESH
    other = {"tensor": 1 - me}
    barrier = pltpu.get_barrier_semaphore()
    pl.semaphore_signal(barrier, inc=1, device_id=other, device_id_type=mesh_id)
    pl.semaphore_wait(barrier, 1)

    def rows_of(i):
        return pl.ds(pl.multiple_of(i * chunk, chunk), chunk)

    def far_rows(i):
        return pl.ds(pl.multiple_of(half + i * chunk, chunk), chunk)

    def summed(stage, i):
        return pltpu.make_async_remote_copy(
            src_ref=box_send.at[stage, rows_of(i)],
            dst_ref=box_recv.at[stage, rows_of(i)],
            send_sem=send_sems.at[stage, i],
            recv_sem=recv_sems.at[stage, i],
            device_id=other,
            device_id_type=mesh_id,
        )

    def gathered(i):
        return pltpu.make_async_remote_copy(
            src_ref=dh2_all.at[rows_of(i)],
            dst_ref=dh2_all.at[far_rows(i)],
            send_sem=send_sems.at[2, i],
            recv_sem=recv_sems.at[2, i],
            device_id=other,
            device_id_type=mesh_id,
        )

    def handed(i):
        return pltpu.make_async_remote_copy(
            src_ref=dctx_send.at[rows_of(i)],
            dst_ref=dctx_out.at[far_rows(i)],
            send_sem=send_sems.at[3, i],
            recv_sem=recv_sems.at[3, i],
            device_id=other,
            device_id_type=mesh_id,
        )

    gain_1, shift_1 = vec_ref[0:1, :], vec_ref[1:2, :]
    gain_2, shift_2 = vec_ref[2:3, :], vec_ref[3:4, :]
    bias_o, bias_2 = vec_ref[4:5, :], vec_ref[5:6, :]
    sums[...] = jnp.zeros_like(sums)
    c1_sum[...] = jnp.zeros_like(c1_sum)

    def normed(h):
        centred = h - jnp.mean(h, axis=-1, keepdims=True)
        inv = lax.rsqrt(jnp.mean(centred * centred, axis=-1, keepdims=True) + NORM_EPS)
        return centred * inv, inv

    def normed_back(dn, n, inv):
        return inv * (
            dn - jnp.mean(dn, axis=-1, keepdims=True) - n * jnp.mean(dn * n, axis=-1, keepdims=True)
        )

    def forward(r):
        u = dot(x1_all[r, :], inw_ref[...], NN) + c1_ref[...]
        a, s = gelu_pair(u)
        act[r, :] = a.astype(bf16)
        slope[r, :] = s.astype(bf16)
        return dot(act[r, :], down_ref[...], NN)

    def backward(r):
        da = dot(dh2_all[r, :], down_ref[...], NT)
        du = da * slope[r, :].astype(f32)
        low = du.astype(bf16)
        slope[r, :] = low
        c1_sum[...] += fold(low.astype(f32))
        return dot(low, inw_ref[...], NT)

    def first_norm(r):
        branch = dot(ctx_ref[r, :], outw_ref[...], NN) + dot(ctx2_ref[r, :], outw2_ref[...], NN)
        n, inv = normed(x_ref[r, :].astype(f32) + (branch + bias_o))
        middle = n * gain_1 + shift_1
        x1_all[r, :] = middle.astype(bf16)
        return n, inv, middle

    for copy in loads[:5]:
        copy.wait()

    @pl.loop(0, count)
    def _(i):
        first_norm(far_rows(i))

    for copy in loads[5:7]:
        copy.wait()

    @pl.loop(0, count)
    def _(i):
        box_send[0, rows_of(i), :] = forward(far_rows(i)).astype(bf16)
        summed(0, i).start()

    @pl.loop(0, count)
    def _(i):
        r = rows_of(i)
        n, inv, middle = first_norm(r)
        norm1[r, :] = n
        inv1[r, :] = jnp.broadcast_to(inv, (chunk, LANES))
        x1[r, :] = middle
        part[r, :] = forward(r)

    loads[7].wait()

    @pl.loop(0, count)
    def _(i):
        r = rows_of(i)
        summed(0, i).wait_recv()
        h = x1[r, :] + (part[r, :] + box_recv[0, r, :].astype(f32) + bias_2)
        n, inv = normed(h)
        block_out[r, :] = (n * gain_2 + shift_2).astype(bf16)
        dy = cot_ref[r, :].astype(f32)
        dh = normed_back(dy * gain_2, n, inv)
        sums[2] += fold(dy * n)
        sums[3] += fold(dy)
        sums[5] += fold(dh)
        dh2[r, :] = dh
        dh2_all[r, :] = dh.astype(bf16)
        gathered(i).start()
        part[r, :] = backward(r)

    block_store.start()

    @pl.loop(0, count)
    def _(i):
        gathered(i).wait_recv()
        box_send[1, rows_of(i), :] = backward(far_rows(i)).astype(bf16)
        summed(1, i).start()

    hidden = act.shape[1]
    block = hidden // 8

    def down_grad(j):
        c = pl.ds(pl.multiple_of(j * block, block), block)
        d_down[c, :] = dot(act[:, c].T, dh2_all[...], NN).astype(bf16)

    def in_grad(j):
        c = pl.ds(pl.multiple_of(j * block, block), block)
        d_inw[:, c] = dot(x1_all[...].T, slope[:, c], NN).astype(bf16)
        in_store(j).start()

    def in_store(j):
        c = pl.ds(pl.multiple_of(j * block, block), block)
        return pltpu.make_async_copy(d_inw.at[:, c], d_inw_hbm.at[:, c], in_sems.at[j])

    per_chunk = 8 // count

    @pl.loop(0, count)
    def _(i):
        for j in range(per_chunk):
            down_grad(i * per_chunk + j)
        r = rows_of(i)
        summed(1, i).wait_recv()
        dx = dh2[r, :] + part[r, :] + box_recv[1, r, :].astype(f32)
        n = norm1[r, :]
        dh = normed_back(dx * gain_1, n, inv1[r, 0:1])
        sums[0] += fold(dx * n)
        sums[1] += fold(dx)
        sums[4] += fold(dh)
        dh1_out[r, :] = dh
        dh1_low[r, :] = dh.astype(bf16)
        dctx_send[r, :] = dot(dh1_low[r, :], outw2_ref[...], NT).astype(bf16)
        handed(i).start()
        dctx_out[r, :] = dot(dh1_low[r, :], outw_ref[...], NT).astype(bf16)

    dh1_store.start()
    down_store.start()
    for row in range(6):
        total = jnp.sum(sums[row], axis=0, keepdims=True)
        low, high = total[:, : width // 2], total[:, width // 2 :]
        mine, theirs = jnp.where(me == 0, low, high), jnp.where(me == 0, high, low)
        spread = width // 2 // LANES
        for j in range(spread):
            at = row * spread + j
            vec_box[0, at : at + 1, :] = mine[:, j * LANES : (j + 1) * LANES]
            vec_box[1, at : at + 1, :] = theirs[:, j * LANES : (j + 1) * LANES]
    vec_copy = pltpu.make_async_remote_copy(
        src_ref=vec_box.at[1],
        dst_ref=vec_box.at[2],
        send_sem=vec_sems.at[0],
        recv_sem=vec_sems.at[1],
        device_id=other,
        device_id_type=mesh_id,
    )
    vec_copy.start()

    @pl.loop(0, 8)
    def _(j):
        in_grad(j)

    d_outw2[...] = dot(ctx2_ref[0:half, :].T, dh1_low[...], NN).astype(bf16)
    outw2_store.start()
    d_outw[...] = dot(ctx_ref[0:half, :].T, dh1_low[...], NN).astype(bf16)
    outw_store.start()

    @pl.loop(0, count)
    def _(i):
        handed(i).wait_recv()

    dctx_store.start()

    blocks = ctx_ref.shape[1] // LANES
    tail_out[0 : 2 * blocks, :] = jnp.zeros((2 * blocks, LANES), f32)
    c1_total = jnp.sum(c1_sum[...], axis=0, keepdims=True)
    for j in range(hidden // LANES):
        tail_out[2 * blocks + j : 2 * blocks + j + 1, :] = c1_total[:, j * LANES : (j + 1) * LANES]
    vec_copy.wait()
    tail_out[2 * blocks + hidden // LANES :, :] = vec_box[0] + vec_box[2]

    @pl.loop(0, count)
    def _(i):
        for stage in range(2):
            summed(stage, i).wait_send()
        gathered(i).wait_send()
        handed(i).wait_send()

    @pl.loop(0, 8)
    def _(j):
        in_store(j).wait()

    for copy in stores:
        copy.wait()


def middle(context, context_2, x_all, cotangent, vectors, inner_bias, out_w, out_w2, in_w, down_w, chunk=128):
    half, width = cotangent.shape
    n = 2 * half
    hidden = in_w.shape[1]
    local_width = context.shape[1]
    whole = pl.BlockSpec(memory_space=pltpu.VMEM)
    hbm = pl.BlockSpec(memory_space=pl.ANY)
    operands = (out_w, out_w2, context, context_2, x_all, in_w, down_w, cotangent)
    wide = pltpu.VMEM((half, width), f32)
    every = pltpu.VMEM((n, width), bf16)
    box = pltpu.VMEM((2, half, width), bf16)
    count = half // chunk
    return pl.pallas_call(
        functools.partial(middle_kernel, chunk=chunk),
        in_specs=[hbm] * 8 + [whole] * 2,
        out_specs=[hbm] * 7 + [whole],
        out_shape=[
            jax.ShapeDtypeStruct((half, width), bf16),
            jax.ShapeDtypeStruct((half, width), f32),
            jax.ShapeDtypeStruct((n, local_width), bf16),
            jax.ShapeDtypeStruct(out_w.shape, bf16),
            jax.ShapeDtypeStruct(out_w.shape, bf16),
            jax.ShapeDtypeStruct(in_w.shape, bf16),
            jax.ShapeDtypeStruct(down_w.shape, bf16),
            jax.ShapeDtypeStruct(((2 * local_width + hidden + 3 * width) // LANES, LANES), f32),
        ],
        scratch_shapes=[pltpu.VMEM(operand.shape, operand.dtype) for operand in operands]
        + [
            pltpu.VMEM((half, width), bf16),
            wide,
            pltpu.VMEM((n, local_width), bf16),
            pltpu.VMEM(out_w.shape, bf16),
            pltpu.VMEM(out_w.shape, bf16),
            pltpu.VMEM(in_w.shape, bf16),
            pltpu.VMEM(down_w.shape, bf16),
            wide,
            wide,
            pltpu.VMEM((half, LANES), f32),
            every,
            pltpu.VMEM((n, hidden), bf16),
            pltpu.VMEM((n, hidden), bf16),
            every,
            pltpu.VMEM((half, width), bf16),
            pltpu.VMEM((half, local_width), bf16),
            wide,
            wide,
            box,
            box,
            pltpu.VMEM((6, 8, width), f32),
            pltpu.VMEM((8, hidden), f32),
            pltpu.VMEM((3, 3 * width // LANES, LANES), f32),
            pltpu.SemaphoreType.DMA((4, count)),
            pltpu.SemaphoreType.DMA((4, count)),
            pltpu.SemaphoreType.DMA((2,)),
            pltpu.SemaphoreType.DMA((8,)),
            pltpu.SemaphoreType.DMA((6,)),
            pltpu.SemaphoreType.DMA((8,)),
        ],
        cost_estimate=pl.CostEstimate(
            flops=14 * n * width * hidden, bytes_accessed=40 << 20, transcendentals=2 * n * hidden
        ),
        compiler_params=params(collective_id=2, has_side_effects=True),
        name="middle",
    )(*operands, vectors, inner_bias)


def attend_back(q_ref, k_ref, v_ref, ctx_ref, dctx_ref, code, seg_ref, lse_ref, dq_ref, dk_ref, dv_ref, pair, rows_q, after_step):
    n = q_ref.shape[0]
    c = slice(pair * LANES, (pair + 1) * LANES)
    low = lax.broadcasted_iota(jnp.int32, (1, LANES), 1) < HD
    zero = jnp.zeros((), bf16)
    k = k_ref[:, c]
    v = v_ref[:, c]
    k_t = k.T
    pick = (
        lax.broadcasted_iota(jnp.int32, (8, LANES), 1) // HD
        == lax.broadcasted_iota(jnp.int32, (8, LANES), 0)
    ).astype(f32)
    dks = [jnp.zeros((n, LANES), f32)] * 2
    dvs = [jnp.zeros((n, LANES), f32)] * 2
    scale = jnp.asarray(HD**-0.5, bf16)
    for i in range(n // rows_q):
        r = slice(i * rows_q, (i + 1) * rows_q)
        q = q_ref[r, c] * scale
        do = dctx_ref[r, c]
        prod = do.astype(f32) * ctx_ref[r, c].astype(f32)
        delta = lax.dot_general(
            pick, prod, NT, precision=lax.Precision.HIGHEST, preferred_element_type=f32
        )
        keys = lax.broadcasted_iota(jnp.int32, (n, rows_q), 0)
        qs = lax.broadcasted_iota(jnp.int32, (n, rows_q), 1) + i * rows_q
        allowed = (code == seg_ref[:, r]) | (keys == qs)
        dqs = []
        for h in range(2):
            qh = jnp.where(low, q, zero) if h == 0 else jnp.where(low, zero, q)
            doh = jnp.where(low, do, zero) if h == 0 else jnp.where(low, zero, do)
            s = jnp.where(allowed, dot(k, qh, NT), MASKED)
            p = jnp.exp(s - lse_ref[pair, h : h + 1, r])
            dp = dot(v, doh, NT)
            ds = (p * (dp - delta[h : h + 1])).astype(bf16)
            dvs[h] = dvs[h] + dot(p.astype(bf16), do, NN)
            dks[h] = dks[h] + dot(ds, q, NN)
            dqs.append(dot(k_t[h * HD : (h + 1) * HD], ds, NN))
        dq_ref[r, c] = (jnp.concatenate(dqs, axis=0).T * (HD**-0.5)).astype(bf16)
        after_step(i)
    dk_ref[:, c] = jnp.where(low, dks[0], dks[1]).astype(bf16)
    dv_ref[:, c] = jnp.where(low, dvs[0], dvs[1]).astype(bf16)


def lay_flat(ref, low, high, blocks, flat, at):
    chunk = 16 if (high - low) % 64 else 64

    @pl.loop(0, (high - low) // chunk)
    def _(c):
        rows = pl.ds(pl.multiple_of(low + c * chunk, 16), chunk)
        for j in range(blocks):
            to_rows = pl.ds(at + c * (chunk * blocks) + j, chunk, stride=blocks)
            flat[to_rows, :] = ref[rows, j * LANES : (j + 1) * LANES].astype(f32)


def emit_pieces(flat, keep, send, slot, skip, piece_rows, ready):
    padded = send.shape[1]
    step = 128
    full = piece_rows // step
    rest = piece_rows - full * step
    for j in (3, 2, 1, 0):
        out = send if j % 2 else keep
        start = skip + (slot ^ j) * piece_rows

        @pl.loop(0, full)
        def _(i, out=out, j=j, start=start):
            rows = flat[pl.ds(start + i * step, step), :]
            out[j // 2, pl.ds(pl.multiple_of(i * step, step), step), :] = rows.astype(bf16)

        parts = [jnp.zeros((padded - piece_rows, LANES), f32)]
        if rest:
            parts = [flat[pl.ds(start + full * step, rest), :]] + parts
        out[j // 2, full * step : padded, :] = jnp.concatenate(parts, axis=0).astype(bf16)
        if j % 2:
            ready(j // 2)


def back_kernel(
    seg_ref, live_ref, lse_ref, outw_ref, tail_ref,
    q_hbm, k_hbm, v_hbm, ctx_hbm, dctx_hbm, x_hbm, inw_hbm, down_hbm, m_hbm, s_hbm, w_hbm, proj_hbm, outw2_hbm,
    g_out, d_out, dx_out,
    dq_ref, dk_ref, dv_ref,
    flat, down_s, inw_s, keep, send, near, far, tails, zin, g_stage, m_in, v_in, w_in,
    near_send, near_recv, far_send, far_recv, tail_send, tail_recv, z_send, z_recv, load_sems, out_sems,
    x_sems, x_free, q_ref, k_ref, v_ref, ctx_ref, dctx_ref, x_ref, act_sems, seg_s, wo_in,
    *, plans, piece_rows, cuts, rows_q
):
    me = lax.axis_index("tensor")
    z = lax.axis_index("group")
    slot = lax.axis_index("slot")
    last = GROUPS - 1
    mesh_id = pl.DeviceIdType.MESH
    core = {"slot": slot ^ 1}
    side = {"slot": slot ^ 2}
    tail_rows = tail_ref.shape[0]
    padded = send.shape[1]
    stage_loads, rest_loads = [], []
    for number, low, high, _, _ in plans[2][0]:
        src, dst = ((inw_hbm, inw_s), (down_hbm, down_s))[number - 2]
        rows = pl.ds(low, high - low)
        stage_loads.append(pltpu.make_async_copy(src.at[rows], dst.at[rows], load_sems.at[number - 2]))
        for side_number, (first, end) in enumerate(((0, low), (high, src.shape[0]))):
            if end > first:
                rows = pl.ds(first, end - first)
                rest_loads.append(
                    pltpu.make_async_copy(
                        src.at[rows], dst.at[rows], load_sems.at[5 + 2 * (number - 2) + side_number]
                    )
                )
    act_loads = [
        pltpu.make_async_copy(src, dst, act_sems.at[number])
        for number, (src, dst) in enumerate(
            (
                (q_hbm, q_ref),
                (k_hbm, k_ref),
                (v_hbm, v_ref),
                (ctx_hbm, ctx_ref),
                (dctx_hbm, dctx_ref),
                (x_hbm, x_ref),
            )
        )
    ]
    for copy in stage_loads + rest_loads:
        copy.start()
    barrier = pltpu.get_barrier_semaphore()
    for where in (core, side, {"tensor": 1 - me}):
        pl.semaphore_signal(barrier, inc=1, device_id=where, device_id_type=mesh_id)

    @pl.when(z > 0)
    def _():
        pl.semaphore_signal(barrier, inc=1, device_id={"group": z - 1}, device_id_type=mesh_id)

    @pl.when(z < last)
    def _():
        pl.semaphore_signal(barrier, inc=1, device_id={"group": z + 1}, device_id_type=mesh_id)

    pl.semaphore_wait(barrier, 3 + jnp.where(z > 0, 1, 0) + jnp.where(z < last, 1, 0))

    def to_core(b, j):
        return pltpu.make_async_remote_copy(
            src_ref=send.at[j],
            dst_ref=near.at[b, j],
            send_sem=near_send.at[b, j],
            recv_sem=near_recv.at[b, j],
            device_id=core,
            device_id_type=mesh_id,
        )

    def to_side(b, h):
        rows = pl.ds(*cuts[h])
        return pltpu.make_async_remote_copy(
            src_ref=keep.at[b, 1, rows],
            dst_ref=far.at[b, rows],
            send_sem=far_send.at[b, h],
            recv_sem=far_recv.at[b, h],
            device_id=side,
            device_id_type=mesh_id,
        )

    def tail_copy(k, where):
        return pltpu.make_async_remote_copy(
            src_ref=tails.at[2 * k],
            dst_ref=tails.at[2 * k + 1],
            send_sem=tail_send.at[k],
            recv_sem=tail_recv.at[k],
            device_id=where,
            device_id_type=mesh_id,
        )

    def along(b, h, landing, where):
        return pltpu.make_async_remote_copy(
            src_ref=keep.at[b, 0, pl.ds(*cuts[h])],
            dst_ref=zin.at[landing, pl.ds(*cuts[h])],
            send_sem=z_send.at[b, h],
            recv_sem=z_recv.at[landing, h],
            device_id=where,
            device_id_type=mesh_id,
        )

    def upward(b, h):
        return along(b, h, b, {"group": z + 1})

    def downward(b, h):
        return along(b, h, jnp.where(z - 1 == b, GROUPS, b), {"group": z - 1})

    def pass_aside(b, first=0, end=None):
        if first == 0:
            to_core(b, 1).wait_recv()
        for h in range(first, len(cuts) if end is None else end):

            def add(at, count):
                r = pl.ds(at, count)
                keep[b, 1, r, :] = (keep[b, 1, r, :].astype(f32) + near[b, 1, r, :].astype(f32)).astype(bf16)

            in_steps(*cuts[h], 128, add)
            to_side(b, h).start()

    def sent(b):
        for j in (1, 0):
            to_core(b, j).wait_send()

    def loads(b):
        rows = pl.ds(0, piece_rows)
        return (
            pltpu.make_async_copy(m_hbm.at[rows, b, :], m_in.at[rows], load_sems.at[2]),
            pltpu.make_async_copy(s_hbm.at[rows, b, :], v_in.at[rows], load_sems.at[3]),
            pltpu.make_async_copy(w_hbm.at[b, pl.ds(0, padded)], w_in, load_sems.at[4]),
        )

    def store(b, h):
        rows = pl.ds(*cuts[h])
        return pltpu.make_async_copy(g_stage.at[rows], g_out.at[b, rows], out_sems.at[b, h])

    turn = (2, 1, 3, 0)

    def differ(b, h):
        k = turn.index(b)
        start, count = cuts[h]
        if h == 0:
            to_core(b, 0).wait_recv()
            for copy in loads(b):
                copy.wait()
        to_side(b, h).wait_recv()
        if b == last and h == len(cuts) - 1:
            at = piece_rows - tail_rows
            low = at // 16 * 16
            extra = jnp.where(slot == last, tails[2] + tails[3], 0.0)
            around = [extra]
            if at > low:
                around = [jnp.zeros((at - low, LANES), f32)] + around
            if padded > piece_rows:
                around = around + [jnp.zeros((padded - piece_rows, LANES), f32)]
            ends = slice(low, padded)
            far[b, ends, :] = (far[b, ends, :].astype(f32) + jnp.concatenate(around, axis=0)).astype(bf16)
        if k:
            store(turn[k - 1], h).wait()

        def step(at, rows):
            r = pl.ds(at, rows)
            g = keep[b, 0, r, :].astype(f32) + near[b, 0, r, :].astype(f32) + far[b, r, :].astype(f32)
            g_stage[r, :] = g
            first = BETA_ONE * m_in[r, :] + (1 - BETA_ONE) * g
            second = BETA_TWO * v_in[r, :] + (1 - BETA_TWO) * g * g
            root = jnp.sqrt(second * (1 / (1 - BETA_TWO**STEP))) + ADAM_EPS
            decay = INNER_RATE * DECAY
            if b == last:
                here = lax.broadcasted_iota(jnp.int32, (rows, LANES), 0) + at
                decay = jnp.where((slot < last) | (here < piece_rows - tail_rows), decay, 0.0)
            d = (INNER_RATE / (1 - BETA_ONE**STEP)) * first / root + decay * w_in[r, :].astype(f32)
            keep[b, 0, r, :] = d.astype(bf16)

        in_steps(start, count, 128, step)
        store(b, h).start()
        if b > 0:
            pl.when(z == 0)(lambda: upward(b, h).start())
        if b < last:
            pl.when(z == last)(lambda: downward(b, h).start())
        if h == len(cuts) - 1 and k + 1 < GROUPS:
            for copy in loads(turn[k + 1]):
                copy.start()

    def hop(b, at, h):
        def go():
            along(b, h, b, {"group": z}).wait_recv()

            def add(at, count):
                r = pl.ds(at, count)
                keep[b, 0, r, :] = (keep[b, 0, r, :].astype(f32) + zin[b, r, :].astype(f32)).astype(bf16)

            in_steps(*cuts[h], 128, add)
            (upward if at < b else downward)(b, h).start()

        pl.when(z == at)(go)

    blank = slice(piece_rows, padded)
    m_in[blank, :] = jnp.zeros((padded - piece_rows, LANES), f32)
    v_in[blank, :] = jnp.zeros((padded - piece_rows, LANES), f32)
    for copy in loads(turn[0]):
        copy.start()

    wo_copy = pltpu.make_async_remote_copy(
        src_ref=outw2_hbm,
        dst_ref=wo_in,
        send_sem=x_sems.at[6],
        recv_sem=x_sems.at[7],
        device_id={"tensor": 1 - me},
        device_id_type=mesh_id,
    )
    wo_copy.start()
    for copy in stage_loads:
        copy.wait()
    refs = {1: wo_in, 2: inw_s, 3: down_s}

    def lay_chunk(b):
        segments, skip, has_tail = plans[b]
        for number, low, high, blocks, at in segments:
            if number:
                lay_flat(refs[number], low, high, blocks, flat, at)
        if has_tail:
            at = skip + 4 * piece_rows - tail_rows
            flat[pl.ds(at, tail_rows), :] = jnp.zeros((tail_rows, LANES), f32)

    def emit_chunk(b):
        emit_pieces(flat, keep.at[b], send, slot, plans[b][1], piece_rows, lambda j: to_core(b, j).start())

    def output_chunk():
        wo_copy.wait()

        @pl.loop(0, wo_in.shape[0] // 16)
        def _(i):
            r = pl.ds(pl.multiple_of(i * 16, 16), 16)
            wo_in[r, :] = (wo_in[r, :].astype(f32) + outw_ref[r, :].astype(f32)).astype(bf16)

        lay_chunk(1)
        sent(3)
        emit_chunk(1)

    lay_chunk(2)
    emit_chunk(2)
    pass_aside(2)
    for copy in rest_loads:
        copy.wait()
    for copy in act_loads:
        copy.start()
    lay_chunk(3)
    sent(2)
    emit_chunk(3)

    half = q_ref.shape[0] // 2
    local_width = q_ref.shape[1]
    depth_in = x_ref.shape[1]
    proj_loads = [
        pltpu.make_async_copy(
            proj_hbm.at[pl.ds(m * depth_in, depth_in)],
            inw_s.at[:, pl.ds(m * local_width, local_width)],
            x_sems.at[2 + m],
        )
        for m in range(3)
    ]

    def make_free():
        pl.semaphore_signal(x_free, inc=1, device_id={"tensor": 1 - me}, device_id_type=mesh_id)
        for copy in proj_loads:
            copy.start()

    parts = range(len(cuts))
    act = functools.partial
    fourth = len(cuts) // 4

    def differ_some(b, part):
        for h in range(part * fourth, (part + 1) * fourth):
            differ(b, h)

    def hop_some(b, at, part):
        for h in range(part * fourth, (part + 1) * fourth):
            hop(b, at, h)

    events = {
        0: [act(differ_some, 2, 0)],
        2: [act(differ_some, 2, 1)],
        4: [act(differ_some, 2, 2), act(pass_aside, 3, 0, fourth)],
        5: [act(hop_some, 2, 1, 0)],
        6: [output_chunk, make_free],
        7: [act(pass_aside, 1), act(differ_some, 2, 3)],
        8: [act(pass_aside, 3, fourth), act(hop_some, 2, 1, 1)],
        9: [act(hop_some, 2, 1, 2)],
        10: [act(differ_some, 1, 0)],
        11: [act(hop_some, 2, 1, 3)],
        12: [act(differ_some, 1, 1)],
        13: [act(differ_some, 1, 2)],
        14: [act(hop_some, 1, 2, 0)],
        15: [act(differ_some, 1, 3)],
    }
    blocks = q_ref.shape[1] // LANES
    seg, code = document_rows(seg_ref, live_ref, me)
    seg_s[...] = seg
    code = as_column(code)[:, 0:1]
    per_pair = q_ref.shape[0] // rows_q

    def after_step(number):
        for act in events.get(number, ()):
            act()

    for copy in act_loads:
        copy.wait()
    for pair in range(blocks):
        attend_back(
            q_ref, k_ref, v_ref, ctx_ref, dctx_ref, code, seg_s, lse_ref, dq_ref, dk_ref, dv_ref, pair, rows_q,
            lambda i, pair=pair: after_step(pair * per_pair + i),
        )

    tails[0] = tail_ref[...]
    for m, ref in enumerate((dq_ref, dv_ref)):
        total = jnp.sum(ref[...].astype(f32), axis=0, keepdims=True)
        for j in range(blocks):
            row = m * blocks + j
            tails[0, row : row + 1, :] = total[:, j * LANES : (j + 1) * LANES]
    tail_copy(0, core).start()

    chunk = 256
    segments, skip, _ = plans[0]
    for m, ref in enumerate((dq_ref, dk_ref, dv_ref)):

        @pl.loop(0, depth_in // chunk)
        def _(c, m=m, ref=ref):
            columns = pl.ds(pl.multiple_of(c * chunk, chunk), chunk)
            acc = dot(x_ref[:, columns].T, ref[...], NN)
            for j in range(blocks):
                to_rows = pl.ds((m * depth_in + c * chunk) * blocks + j, chunk, stride=blocks)
                flat[to_rows, :] = acc[:, j * LANES : (j + 1) * LANES]

        if m == 0:
            tail_copy(0, core).wait()
            tails[2] = tails[0] + tails[1]
            tail_copy(1, side).start()
            hop_some(1, 2, 1)
        if m == 1:
            hop_some(1, 2, 2)

    for number, low, high, wide, at in segments:
        if number:
            lay_flat(refs[number], low, high, wide, flat, at)
    sent(1)
    emit_chunk(0)
    pass_aside(0)
    hop_some(1, 2, 3)
    tail_copy(1, side).wait()
    for h in parts:
        differ(3, h)

    for copy in proj_loads:
        copy.wait()

    def through(row):
        r = pl.ds(row, 256)
        acc = dot(dq_ref[r, :], inw_s[:, 0:local_width], NT)
        acc = acc + dot(dk_ref[r, :], inw_s[:, local_width : 2 * local_width], NT)
        return acc + dot(dv_ref[r, :], inw_s[:, 2 * local_width : 3 * local_width], NT)

    @pl.loop(0, half // 256)
    def _(i):
        down_s[pl.ds(pl.multiple_of(i * 256, 256), 256), :] = through(
            pl.multiple_of(half + i * 256, 256)
        ).astype(bf16)

    pl.semaphore_wait(x_free, 1)
    x_copy = pltpu.make_async_remote_copy(
        src_ref=down_s.at[pl.ds(0, half)],
        dst_ref=down_s.at[pl.ds(half, half)],
        send_sem=x_sems.at[0],
        recv_sem=x_sems.at[1],
        device_id={"tensor": 1 - me},
        device_id_type=mesh_id,
    )
    x_copy.start()
    differ(0, 0)

    @pl.loop(0, half // 256)
    def _(i):
        down_s[pl.ds(pl.multiple_of(2 * half + i * 256, 256), 256), :] = through(
            pl.multiple_of(i * 256, 256)
        ).astype(bf16)

    count = len(cuts)
    for t in range(1, count + 4):
        for act_on, lag in (
            (act(differ, 0), 0),
            (act(hop, 3, 1), 1),
            (act(hop, 0, 2), 2),
            (act(hop, 3, 2), 3),
            (act(hop, 0, 1), 4),
        ):
            if 0 <= t - lag < count:
                act_on(t - lag)

    for h in parts:
        store(0, h).wait()
    for b in range(GROUPS):

        def finish(b=b):
            for h in parts:
                if b > 0:
                    along(b, h, b, {"group": z}).wait_recv()
                if b < last:
                    along(b, h, GROUPS, {"group": z}).wait_recv()

                def add(at, count):
                    r = pl.ds(at, count)
                    total = keep[b, 0, r, :].astype(f32)
                    if b > 0:
                        total = total + zin[b, r, :].astype(f32)
                    if b < last:
                        total = total + zin[GROUPS, r, :].astype(f32)
                    g_stage[r, :] = total

                in_steps(*cuts[h], 128, add)

        pl.when(z == b)(finish)
    x_copy.wait()
    dx_copy = pltpu.make_async_copy(down_s.at[pl.ds(half, 2 * half)], dx_out, x_sems.at[5])
    dx_copy.start()
    copy = pltpu.make_async_copy(g_stage, d_out, out_sems.at[GROUPS, 0])
    copy.start()
    for b in range(GROUPS):
        for h in parts:
            to_side(b, h).wait_send()

            @pl.when(z != b)
            def _(b=b, h=h):
                along(b, h, b, {"group": z}).wait_send()

    sent(0)
    copy.wait()
    dx_copy.wait()


def back(
    q, k, v, ctx, dctx, seg_row, live_row, lse, x_all, d_outw, d_outw2, tail, d_inw, d_down, first, second, pieces, proj_w,
    table, tail_at, piece_rows, rows_q=256
):
    per = 4
    padded = round_up(piece_rows, 16)
    tail_rows = tail.shape[0]
    plans = []
    most = 0
    for b in range(GROUPS):
        begin = b * per * piece_rows
        segments, base, size = chunk_plan(table, begin, begin + per * piece_rows, tail_at, tail_rows)
        plans.append((segments, begin - base, begin + per * piece_rows > tail_at))
        most = max(most, size)
    parts = 8
    marks = [padded * i // parts // 16 * 16 for i in range(parts)] + [padded]
    cuts = [(low, high - low) for low, high in zip(marks[:-1], marks[1:])]
    whole = pl.BlockSpec(memory_space=pltpu.VMEM)
    hbm = pl.BlockSpec(memory_space=pl.ANY)
    dma = pltpu.SemaphoreType.DMA
    n, local_width = q.shape
    grad = pltpu.VMEM((n, local_width), bf16)
    wide = pltpu.VMEM((padded, LANES), f32)
    return pl.pallas_call(
        functools.partial(back_kernel, plans=plans, piece_rows=piece_rows, cuts=cuts, rows_q=rows_q),
        in_specs=[whole] * 5 + [hbm] * 13,
        out_specs=[hbm] * 3,
        out_shape=[
            jax.ShapeDtypeStruct((GROUPS, padded, LANES), f32),
            jax.ShapeDtypeStruct((padded, LANES), f32),
            jax.ShapeDtypeStruct((n, x_all.shape[1]), bf16),
        ],
        scratch_shapes=[
            grad,
            grad,
            grad,
            pltpu.VMEM((round_up(most, 8) + 64, LANES), f32),
            pltpu.VMEM(d_down.shape, bf16),
            pltpu.VMEM(d_inw.shape, bf16),
            pltpu.VMEM((GROUPS, 2, padded, LANES), bf16),
            pltpu.VMEM((2, padded, LANES), bf16),
            pltpu.VMEM((GROUPS, 2, padded, LANES), bf16),
            pltpu.VMEM((GROUPS, padded, LANES), bf16),
            pltpu.VMEM((4, tail_rows, LANES), f32),
            pltpu.VMEM((GROUPS + 1, padded, LANES), bf16),
            wide,
            wide,
            wide,
            pltpu.VMEM((padded, LANES), bf16),
            dma((GROUPS, 2)),
            dma((GROUPS, 2)),
            dma((GROUPS, parts)),
            dma((GROUPS, parts)),
            dma((2,)),
            dma((2,)),
            dma((GROUPS, parts)),
            dma((GROUPS + 1, parts)),
            dma((9,)),
            dma((GROUPS + 1, parts)),
            dma((8,)),
            pltpu.SemaphoreType.REGULAR,
            grad,
            grad,
            grad,
            grad,
            grad,
            pltpu.VMEM(x_all.shape, bf16),
            dma((6,)),
            pltpu.VMEM((1, n), f32),
            pltpu.VMEM(d_outw.shape, bf16),
        ],
        cost_estimate=pl.CostEstimate(
            flops=30 * n * n * local_width, bytes_accessed=40 << 20, transcendentals=n * n * 8
        ),
        compiler_params=params(collective_id=4, has_side_effects=True),
        name="back",
    )(
        seg_row, live_row, lse, d_outw, tail, q, k, v, ctx, dctx, x_all, d_inw, d_down, first, second, pieces, proj_w, d_outw2
    )


def partner(block):
    return lax.ppermute(block, "tensor", [(0, 1), (1, 0)])


def both(own):
    return jnp.concatenate([own, partner(own)], axis=0)


def own_sum(partial):
    half = partial.shape[0] // 2
    return partial[:half].astype(f32) + partner(partial[half:].astype(bf16)).astype(f32)


def local_fast(
    tokens,
    cotangent,
    segment_ids,
    padding,
    shared_weights,
    first_moment,
    second_moment,
    outer_momentum,
):
    per = lax.axis_size("slot")
    piece_rows = shared_weights.shape[1] // LANES
    table, tail_at = matrix_table(2)
    tail_rows = GROUPS * per * piece_rows - tail_at
    padded = round_up(piece_rows + tail_rows, 16)

    own_rows = shared_weights.reshape(piece_rows, 1, LANES)
    seg_row, live_row = segment_ids[None], padding[None]
    end = padded - round_up(2 * tail_rows + 16, 16)
    marks = [end * i // 4 // 16 * 16 for i in range(4)] + [end, padded]
    cuts = [(low, high - low) for low, high in zip(marks[:-1], marks[1:])]
    (
        proj_w, out_w, in_w, down_w, out_w2, context_2, pieces, x_all,
        query, keys, values, context, vectors, inner_bias, lse
    ) = start(own_rows, tokens, seg_row, live_row, table, tail_rows, padded, cuts)
    (
        block_out, grad_one, grad_context, grad_out_w, grad_out_w2, grad_in_w, grad_down_w, tail_grad
    ) = middle(context, context_2, x_all, cotangent, vectors, inner_bias, out_w, out_w2, in_w, down_w)

    def blocked(state):
        return state.reshape(GROUPS, piece_rows, LANES).transpose(1, 0, 2)

    def unblocked(state):
        return state.transpose(1, 0, 2).reshape(1, 1, GROUPS, piece_rows * LANES)

    first = blocked(first_moment)
    second = blocked(second_moment)
    grads, d_sum, dx = back(
        query, keys, values, context, grad_context, seg_row, live_row, lse, x_all, grad_out_w, grad_out_w2,
        tail_grad, grad_in_w, grad_down_w, first, second, pieces, proj_w, table, tail_at, piece_rows
    )
    slot_word = lax.axis_index("slot").astype(jnp.int32).reshape(1)
    *states, mean_diff, new_momentum, new_weights, input_grad = update(
        slot_word, grads, pieces, first, second, d_sum, own_rows,
        outer_momentum.reshape(piece_rows, 1, LANES), grad_one, dx, tail_rows
    )
    rows_out = [state.reshape(1, piece_rows * LANES) for state in (mean_diff, new_momentum, new_weights)]
    return (block_out, input_grad, *[unblocked(state) for state in states], *rows_out)


def solution(mesh):
    dp = mesh.shape["dp"]
    tensor_size = mesh.shape["tensor"]
    piece = (4 * D * D + 2 * D * FF + 8 * D + FF) // tensor_size // dp
    if tensor_size == 2 and piece % LANES == 0 and dp % GROUPS == 0:
        mesh = Mesh(
            mesh.devices.reshape(GROUPS, dp // GROUPS, tensor_size), ("group", "slot", "tensor")
        )
        data = ("group", "slot")
        body = local_fast
    else:
        data = "dp"
        body = local_general
    every = ("group", "slot", "tensor") if body is local_fast else ("dp", "tensor")
    in_specs = (
        P(every, None),
        P(every, None),
        P(data),
        P(data),
        P("tensor", data),
        P("tensor", data, None, None),
        P("tensor", data, None, None),
        P("tensor", data),
    )
    out_specs = (
        P(every, None),
        P(every, None),
        P("tensor", data, None, None),
        P("tensor", data, None, None),
        P("tensor", data, None, None),
        P("tensor", data, None, None),
        P("tensor", data),
        P("tensor", data),
        P("tensor", data),
    )
    return jax.shard_map(body, mesh=mesh, in_specs=in_specs, out_specs=out_specs, check_vma=False)
```

```python
import functools

import jax
import jax.numpy as jnp
import numpy as np
from jax import lax
from jax.experimental import pallas as pl
from jax.experimental.pallas import tpu as pltpu
from jax.sharding import Mesh
from jax.sharding import PartitionSpec as P

D = 1024
HEADS = 16
HD = 64
FF = 4096
SEQ_LEN = 1024
GROUPS = 4
STEP = 10


NORM_EPS = 1e-05
MASKED = -1000000000.0
BETA_ONE = 0.9
BETA_TWO = 0.999
ADAM_EPS = 1e-08
INNER_RATE = 0.02
DECAY = 0.01
OUTER_MU = 0.9
OUTER_RATE = 0.7
ROOT_HALF = 0.7071067811865476
INV_ROOT_TWO_PI = 0.3989422804014327


def from_partner(block, axis, stride):
    count = lax.axis_size(axis)
    route = []
    for low in range(count):
        high = low | 1 << stride
        if high != low and high < count:
            route += [(low, high), (high, low)]
    return lax.ppermute(block, axis, route)


def boundaries(tensor_size):
    local_width = D // tensor_size
    hidden = FF // tensor_size
    lengths = [
        3 * D * local_width,
        local_width * D,
        D * hidden,
        hidden * D,
        local_width,
        local_width,
        hidden,
        6 * local_width,
    ]
    points = [0]
    for amount in lengths:
        points.append(points[-1] + amount)
    return points


def layer_norm(values, norm_gain, norm_shift):
    average = jnp.mean(values, axis=-1, keepdims=True)
    centred = values - average
    variance = jnp.mean(centred * centred, axis=-1, keepdims=True)
    inv_dev = lax.rsqrt(variance + NORM_EPS)
    normed = centred * inv_dev
    return (normed * norm_gain + norm_shift, normed, inv_dev)


def norm_back(grad_normed, normed, inv_dev):
    first_part = jnp.mean(grad_normed, axis=-1, keepdims=True)
    second_part = jnp.mean(grad_normed * normed, axis=-1, keepdims=True)
    return inv_dev * (grad_normed - first_part - normed * second_part)


def gelu_slope(inner):
    return (
        0.5 * (1.0 + jax.scipy.special.erf(inner * ROOT_HALF))
        + inner * jnp.exp(-0.5 * inner * inner) * INV_ROOT_TWO_PI
    )


def row_contract(left_side, right_side):
    return lax.dot_general(
        left_side, right_side, (((0,), (0,)), ((), ())), preferred_element_type=jnp.float32
    )


def col_contract(left_side, right_side):
    return lax.dot_general(
        left_side, right_side, (((1,), (1,)), ((), ())), preferred_element_type=jnp.float32
    )


def halve_rounds(values, bit_list, first_axis, top_bit, dp_index, site_call):
    for bit_number in bit_list:
        axis_number = first_axis + top_bit - bit_number
        my_bit = dp_index >> bit_number & 1
        kept = lax.dynamic_index_in_dim(values, my_bit, axis_number, keepdims=True)
        outgoing = lax.dynamic_index_in_dim(values, 1 - my_bit, axis_number, keepdims=True)
        values = kept + site_call(outgoing, bit_number)
    return values


def local_general(
    tokens,
    cotangent,
    segment_ids,
    padding,
    shared_weights,
    first_moment,
    second_moment,
    outer_momentum,
):
    tensor_size = lax.axis_size("tensor")
    local_width = D // tensor_size
    hidden = FF // tensor_size
    local_heads = HEADS // tensor_size
    seq_rows = segment_ids.shape[0]
    seq_count = seq_rows // SEQ_LEN
    block_rows = min(512, SEQ_LEN)
    per_seq = SEQ_LEN // block_rows
    block_total = seq_count * per_seq
    score_scale = HD ** (-0.5)
    bf16 = jnp.bfloat16
    f32 = jnp.float32
    masters = lax.all_gather(shared_weights, "dp", axis=1, tiled=True)[0]
    points = boundaries(tensor_size)
    segments = [masters[points[number] : points[number + 1]] for number in range(8)]
    proj_weight = segments[0].reshape(3, D, local_width).astype(bf16)
    out_weight = segments[1].reshape(local_width, D).astype(bf16)
    in_weight = segments[2].reshape(D, hidden).astype(bf16)
    down_weight = segments[3].reshape(hidden, D).astype(bf16)
    query_bias = segments[4]
    value_bias = segments[5]
    inner_bias = segments[6]
    vectors = lax.all_gather(segments[7].reshape(6, local_width), "tensor", axis=1, tiled=True)
    inputs_all = lax.all_gather(tokens, "tensor", axis=0, tiled=True)
    projected = jnp.einsum("td,kde->kte", inputs_all, proj_weight, preferred_element_type=f32)
    query = (projected[0] + query_bias).astype(bf16)
    keys = projected[1].astype(bf16)
    values = (projected[2] + value_bias).astype(bf16)
    query_four = query.reshape(seq_count, SEQ_LEN, local_heads, HD)
    keys_four = keys.reshape(seq_count, SEQ_LEN, local_heads, HD)
    values_four = values.reshape(seq_count, SEQ_LEN, local_heads, HD)
    seg_two = segment_ids.reshape(seq_count, SEQ_LEN)
    live_two = padding.reshape(seq_count, SEQ_LEN)
    key_pos = jnp.arange(SEQ_LEN, dtype=jnp.int32)

    def block_scores(block_index):
        sequence = block_index // per_seq
        offset = block_index % per_seq * block_rows
        query_rows = lax.dynamic_index_in_dim(query_four, sequence, 0, keepdims=False)
        query_block = lax.dynamic_slice_in_dim(query_rows, offset, block_rows, 0)
        key_rows = lax.dynamic_index_in_dim(keys_four, sequence, 0, keepdims=False)
        seg_row = lax.dynamic_index_in_dim(seg_two, sequence, 0, keepdims=False)
        live_row = lax.dynamic_index_in_dim(live_two, sequence, 0, keepdims=False)
        seg_block = lax.dynamic_slice_in_dim(seg_row, offset, block_rows, 0)
        query_pos = offset + jnp.arange(block_rows, dtype=jnp.int32)
        allowed = (seg_block[:, None] == seg_row[None, :]) & (
            (live_row[None, :] == 1) | (query_pos[:, None] == key_pos[None, :])
        )
        raw_scores = (
            jnp.einsum("qhd,khd->hqk", query_block, key_rows, preferred_element_type=f32)
            * score_scale
        )
        return (
            jnp.where(allowed[None], raw_scores, MASKED),
            query_block,
            key_rows,
            sequence,
            offset,
        )

    def forward_block(block_index):
        scores, query_block, key_rows, sequence, offset = block_scores(block_index)
        value_rows = lax.dynamic_index_in_dim(values_four, sequence, 0, keepdims=False)
        highest = jnp.max(scores, axis=-1, keepdims=True)
        exponent = jnp.exp(scores - highest)
        summed = jnp.sum(exponent, axis=-1, keepdims=True)
        probabilities = (exponent / summed).astype(bf16)
        context = jnp.einsum("hqk,khd->qhd", probabilities, value_rows, preferred_element_type=f32)
        return (context, (highest + jnp.log(summed))[..., 0])

    context_blocks, log_totals = lax.map(forward_block, jnp.arange(block_total, dtype=jnp.int32))
    context_low = context_blocks.reshape(seq_rows, local_width).astype(bf16)
    attn_sum = lax.psum_scatter(
        jnp.dot(context_low, out_weight, preferred_element_type=f32).astype(jnp.bfloat16),
        "tensor",
        scatter_dimension=0,
        tiled=True,
    ).astype(jnp.float32)
    tokens_f = tokens.astype(f32)
    middle, normed_one, inv_one = layer_norm(
        tokens_f + (attn_sum + vectors[4]), vectors[0], vectors[1]
    )
    middle_all = lax.all_gather(middle.astype(bf16), "tensor", axis=0, tiled=True)
    inner = jnp.dot(middle_all, in_weight, preferred_element_type=f32) + inner_bias
    activated = jax.nn.gelu(inner, approximate=False).astype(bf16)
    ffn_sum = lax.psum_scatter(
        jnp.dot(activated, down_weight, preferred_element_type=f32).astype(jnp.bfloat16),
        "tensor",
        scatter_dimension=0,
        tiled=True,
    ).astype(jnp.float32)
    result, normed_two, inv_two = layer_norm(
        middle + (ffn_sum + vectors[5]), vectors[2], vectors[3]
    )
    block_out = result.astype(bf16)
    grad_out = cotangent.astype(f32)
    grad_gain_two = jnp.sum(grad_out * normed_two, axis=0)
    grad_shift_two = jnp.sum(grad_out, axis=0)
    grad_two = norm_back(grad_out * vectors[2], normed_two, inv_two)
    grad_down_bias = jnp.sum(grad_two, axis=0)
    back_all = lax.all_gather(grad_two.astype(bf16), "tensor", axis=0, tiled=True)
    grad_down_weight = row_contract(activated, back_all)
    grad_act = col_contract(back_all, down_weight)
    grad_inner = (grad_act * gelu_slope(inner)).astype(bf16)
    grad_inner_bias = jnp.sum(grad_inner.astype(f32), axis=0)
    grad_in_weight = row_contract(middle_all, grad_inner)
    grad_middle = grad_two + lax.psum_scatter(
        col_contract(grad_inner, in_weight).astype(jnp.bfloat16),
        "tensor",
        scatter_dimension=0,
        tiled=True,
    ).astype(jnp.float32)
    grad_gain_one = jnp.sum(grad_middle * normed_one, axis=0)
    grad_shift_one = jnp.sum(grad_middle, axis=0)
    grad_one = norm_back(grad_middle * vectors[0], normed_one, inv_one)
    grad_out_bias = jnp.sum(grad_one, axis=0)
    attn_back_all = lax.all_gather(grad_one.astype(bf16), "tensor", axis=0, tiled=True)
    grad_out_weight = row_contract(context_low, attn_back_all)
    grad_context = col_contract(attn_back_all, out_weight).astype(bf16)
    grad_context_four = grad_context.reshape(seq_count, SEQ_LEN, local_heads, HD)

    def backward_block(carry, block_index):
        grad_keys, grad_values = carry
        scores, query_block, key_rows, sequence, offset = block_scores(block_index)
        value_rows = lax.dynamic_index_in_dim(values_four, sequence, 0, keepdims=False)
        log_total = lax.dynamic_index_in_dim(log_totals, block_index, 0, keepdims=False)
        probabilities = jnp.exp(scores - log_total[..., None])
        prob_low = probabilities.astype(bf16)
        grad_rows = lax.dynamic_index_in_dim(grad_context_four, sequence, 0, keepdims=False)
        grad_block = lax.dynamic_slice_in_dim(grad_rows, offset, block_rows, 0)
        grad_probs = jnp.einsum("qhd,khd->hqk", grad_block, value_rows, preferred_element_type=f32)
        grad_scores = probabilities * (
            grad_probs - jnp.sum(grad_probs * probabilities, axis=-1, keepdims=True)
        )
        scores_low = grad_scores.astype(bf16)
        grad_query = (
            jnp.einsum("hqk,khd->qhd", scores_low, key_rows, preferred_element_type=f32)
            * score_scale
        )
        key_term = (
            jnp.einsum("hqk,qhd->khd", scores_low, query_block, preferred_element_type=f32)
            * score_scale
        )
        value_term = jnp.einsum("hqk,qhd->khd", prob_low, grad_block, preferred_element_type=f32)
        grad_keys = lax.dynamic_update_index_in_dim(
            grad_keys,
            lax.dynamic_index_in_dim(grad_keys, sequence, 0, keepdims=False) + key_term,
            sequence,
            0,
        )
        grad_values = lax.dynamic_update_index_in_dim(
            grad_values,
            lax.dynamic_index_in_dim(grad_values, sequence, 0, keepdims=False) + value_term,
            sequence,
            0,
        )
        return ((grad_keys, grad_values), grad_query)

    empty = jnp.zeros((seq_count, SEQ_LEN, local_heads, HD), f32)
    (grad_keys, grad_values), grad_queries = lax.scan(
        backward_block, (empty, empty), jnp.arange(block_total, dtype=jnp.int32)
    )
    grad_proj = jnp.stack(
        [
            grad_queries.reshape(seq_rows, local_width),
            grad_keys.reshape(seq_rows, local_width),
            grad_values.reshape(seq_rows, local_width),
        ]
    ).astype(bf16)
    grad_proj_weight = jnp.einsum("td,kte->kde", inputs_all, grad_proj, preferred_element_type=f32)
    grad_query_bias = jnp.sum(grad_proj[0].astype(f32), axis=0)
    grad_value_bias = jnp.sum(grad_proj[2].astype(f32), axis=0)
    input_part = jnp.einsum("kte,kde->td", grad_proj, proj_weight, preferred_element_type=f32)
    vector_part = jnp.stack(
        [
            grad_gain_one,
            grad_shift_one,
            grad_gain_two,
            grad_shift_two,
            grad_out_bias,
            grad_down_bias,
        ]
    )
    input_share, vector_grad = (
        lax.psum_scatter(
            input_part.astype(jnp.bfloat16), "tensor", scatter_dimension=0, tiled=True
        ).astype(jnp.float32),
        lax.psum_scatter(
            vector_part.astype(jnp.bfloat16), "tensor", scatter_dimension=1, tiled=True
        ).astype(jnp.float32),
    )
    input_grad = (grad_one + input_share).astype(bf16)
    flat_grad = jnp.concatenate(
        [
            grad_proj_weight.reshape(-1),
            grad_out_weight.reshape(-1),
            grad_in_weight.reshape(-1),
            grad_down_weight.reshape(-1),
            grad_query_bias,
            grad_value_bias,
            grad_inner_bias,
            vector_grad.reshape(-1),
        ]
    )
    dp_size = lax.axis_size("dp")
    per_group = dp_size // GROUPS
    inner_bits = per_group.bit_length() - 1
    all_bits = dp_size.bit_length() - 1
    dp_index = lax.axis_index("dp")
    slot_index = dp_index % per_group
    piece_len = shared_weights.shape[1]
    grid_view = flat_grad.reshape(GROUPS, per_group, piece_len)
    inner_list = list(range(inner_bits))
    outer_list = list(range(inner_bits, all_bits))
    inner_list = inner_list[::-1]
    outer_list = outer_list[::-1]
    summed_grid = grid_view
    for bit_number in inner_list:
        summed_grid = summed_grid + from_partner(
            summed_grid.astype(jnp.bfloat16), "dp", bit_number
        ).astype(summed_grid.dtype)
    grad_block = lax.dynamic_index_in_dim(summed_grid, slot_index, 1, keepdims=False)
    weights_block = lax.dynamic_index_in_dim(
        masters.reshape(GROUPS, per_group, piece_len), slot_index, 1, keepdims=False
    )
    matrix_count = (4 * D * D + 2 * D * FF) // tensor_size
    flat_index = (
        jnp.arange(GROUPS, dtype=jnp.int32)[:, None] * per_group + slot_index
    ) * piece_len + jnp.arange(piece_len, dtype=jnp.int32)[None, :]
    decay_mask = (flat_index < matrix_count).astype(f32)
    first_new = BETA_ONE * first_moment[0, 0] + (1 - BETA_ONE) * grad_block
    second_new = BETA_TWO * second_moment[0, 0] + (1 - BETA_TWO) * grad_block * grad_block
    first_hat = first_new / (1 - BETA_ONE**STEP)
    second_hat = second_new / (1 - BETA_TWO**STEP)
    group_weights = weights_block - INNER_RATE * (
        first_hat / (jnp.sqrt(second_hat) + ADAM_EPS) + DECAY * decay_mask * weights_block
    )
    difference = weights_block - group_weights

    def outer_swap(outgoing, bit_number):
        return from_partner(outgoing.astype(jnp.bfloat16), "dp", bit_number).astype(outgoing.dtype)

    outer_bits = all_bits - inner_bits
    diff_view = difference.reshape((2,) * outer_bits + (piece_len,))
    diff_sum = halve_rounds(diff_view, outer_list, 0, all_bits - 1, dp_index, outer_swap).reshape(
        piece_len
    )
    mean_diff = diff_sum / GROUPS
    new_momentum = OUTER_MU * outer_momentum[0] + mean_diff
    new_weights = shared_weights[0] - OUTER_RATE * (mean_diff + OUTER_MU * new_momentum)
    return (
        block_out,
        input_grad,
        grad_block[None, None],
        first_new[None, None],
        second_new[None, None],
        group_weights[None, None],
        mean_diff[None],
        new_momentum[None],
        new_weights[None],
    )


LANES = 128
NT = (((1,), (1,)), ((), ()))
NN = (((1,), (0,)), ((), ()))
TN = (((0,), (0,)), ((), ()))
VMEM_BYTES = 61 << 20
f32 = jnp.float32
bf16 = jnp.bfloat16


def dot(left, right, dims):
    return lax.dot_general(left, right, dims, preferred_element_type=f32)


def params(**more):
    return pltpu.CompilerParams(vmem_limit_bytes=VMEM_BYTES, **more)


def round_up(number, step):
    return -(-number // step) * step


def matrix_table(tensor_size):
    local_width = D // tensor_size
    hidden = FF // tensor_size
    table = []
    offset = 0
    for rows, columns in ((3 * D, local_width), (local_width, D), (D, hidden), (hidden, D)):
        blocks = columns // LANES
        table.append((offset, rows, blocks))
        offset += rows * blocks
    return table, offset


def chunk_plan(table, first, end, tail_at, tail_rows):
    segments = []
    base = None
    for number, (offset, rows, blocks) in enumerate(table):
        low = max(first, offset)
        high = min(end, offset + rows * blocks)
        if low >= high:
            continue
        row_low = (low - offset) // blocks // 16 * 16
        row_high = min(rows, round_up(-(-(high - offset) // blocks), 16))
        if base is None:
            base = offset + row_low * blocks
        segments.append((number, row_low, row_high, blocks, offset + row_low * blocks - base))
    size = max(at + (high - low) * blocks for _, low, high, blocks, at in segments)
    if end > tail_at:
        size = max(size, tail_at + tail_rows - base)
    return segments, base, size


def row_parts(rows, count):
    size = rows // count // 16 * 16
    starts = [size * i for i in range(count)] + [rows]
    return [(low, high - low) for low, high in zip(starts[:-1], starts[1:])]


def in_steps(start, rows, step, body):
    @pl.loop(0, rows // step)
    def _(i):
        body(pl.multiple_of(start + i * step, 16), step)

    if rows % step:
        body(start + rows // step * step, rows % step)


def update_kernel(
    slot_ref, g_hbm, w_hbm, m_hbm, v_hbm, d_hbm, own_hbm, mom_hbm, dh1_hbm, dx_hbm,
    go, mo, vo, wo, mean_out, mom_out, new_out, input_out,
    g_s, w_s, m_s, v_s, m_new, v_new, w_new, sems, dh1_s, dx_s, input_s, input_sems,
    *, piece_rows, tail_rows, parts
):
    slot = slot_ref[0]
    units = [(b, part) for b in range(GROUPS) for part in parts] + [(None, part) for part in parts]

    def loads(u):
        b, (at, rows) = units[u]
        k = u % 3
        r = pl.ds(at, rows)
        wide = pl.ds(at, round_up(rows, 16))
        there, padded = pl.ds(0, rows), pl.ds(0, round_up(rows, 16))
        if b is None:
            pairs = (
                (d_hbm.at[wide], g_s.at[k, padded]),
                (own_hbm.at[r, 0, :], m_s.at[k, there]),
                (mom_hbm.at[r, 0, :], v_s.at[k, there]),
            )
        else:
            pairs = (
                (g_hbm.at[b, wide], g_s.at[k, padded]),
                (m_hbm.at[r, b, :], m_s.at[k, there]),
                (v_hbm.at[r, b, :], v_s.at[k, there]),
                (w_hbm.at[b, wide], w_s.at[k, padded]),
            )
        return [pltpu.make_async_copy(src, dst, sems.at[n, k]) for n, (src, dst) in enumerate(pairs)]

    def stores(u):
        b, (at, rows) = units[u]
        k = u % 3
        r = pl.ds(at, rows)
        there = pl.ds(0, rows)
        if b is None:
            pairs = (
                (m_new.at[k, there], mean_out.at[r, 0, :]),
                (v_new.at[k, there], mom_out.at[r, 0, :]),
                (w_new.at[k, there], new_out.at[r, 0, :]),
            )
        else:
            pairs = (
                (m_new.at[k, there], mo.at[r, b, :]),
                (v_new.at[k, there], vo.at[r, b, :]),
                (w_new.at[k, there], wo.at[r, b, :]),
                (g_s.at[k, there], go.at[r, b, :]),
            )
        return [pltpu.make_async_copy(src, dst, sems.at[4 + n, k]) for n, (src, dst) in enumerate(pairs)]

    input_loads = [
        pltpu.make_async_copy(dh1_hbm, dh1_s, input_sems.at[0]),
        pltpu.make_async_copy(dx_hbm, dx_s, input_sems.at[1]),
    ]
    input_store = pltpu.make_async_copy(input_s, input_out, input_sems.at[2])
    half = dh1_s.shape[0]

    def input_gradient():
        for copy in input_loads:
            copy.wait()

        @pl.loop(0, half // 32)
        def _(i):
            r = pl.ds(pl.multiple_of(i * 32, 32), 32)
            far = pl.ds(pl.multiple_of(half + i * 32, 32), 32)
            input_s[r, :] = (dh1_s[r, :] + dx_s[r, :].astype(f32) + dx_s[far, :].astype(f32)).astype(bf16)

        input_store.start()

    for copy in loads(0):
        copy.start()
    for u, (b, (at, rows)) in enumerate(units):
        if u == 1:
            for copy in input_loads:
                copy.start()
        if u == 4:
            input_gradient()
        k = u % 3
        if u > 1:
            for copy in stores(u - 2):
                copy.wait()
        if u + 1 < len(units):
            for copy in loads(u + 1):
                copy.start()
        for copy in loads(u):
            copy.wait()

        def inner(start, count, b=b, at=at, k=k):
            r = pl.ds(start, count)
            g = g_s[k, r, :]
            if b is None:
                average = g / GROUPS
                momentum = OUTER_MU * v_s[k, r, :] + average
                m_new[k, r, :] = average
                v_new[k, r, :] = momentum
                w_new[k, r, :] = m_s[k, r, :] - OUTER_RATE * (average + OUTER_MU * momentum)
                return
            w = w_s[k, r, :].astype(f32)
            first = BETA_ONE * m_s[k, r, :] + (1 - BETA_ONE) * g
            second = BETA_TWO * v_s[k, r, :] + (1 - BETA_TWO) * g * g
            root = jnp.sqrt(second * (1 / (1 - BETA_TWO**STEP))) + ADAM_EPS
            decay = INNER_RATE * DECAY
            if b == GROUPS - 1:
                here = lax.broadcasted_iota(jnp.int32, (count, LANES), 0) + (at + start)
                decay = jnp.where((slot < 3) | (here < piece_rows - tail_rows), decay, 0.0)
            m_new[k, r, :] = first
            v_new[k, r, :] = second
            w_new[k, r, :] = w - ((INNER_RATE / (1 - BETA_ONE**STEP)) * first / root + decay * w)

        in_steps(0, round_up(rows, 16), 128, inner)
        for copy in stores(u):
            copy.start()
    for u in (len(units) - 2, len(units) - 1):
        for copy in stores(u):
            copy.wait()
    input_store.wait()


def update(slot, grads, pieces, first, second, d_sum, own_rows, momentum_rows, dh1, dx, tail_rows):
    piece_rows = first.shape[0]
    hbm = pl.BlockSpec(memory_space=pl.ANY)
    parts = row_parts(piece_rows, 1)
    most = round_up(max(rows for _, rows in parts), 16)
    wide = pltpu.VMEM((3, most, LANES), f32)
    state = jax.ShapeDtypeStruct(first.shape, f32)
    piece = jax.ShapeDtypeStruct(own_rows.shape, f32)
    return pl.pallas_call(
        functools.partial(update_kernel, piece_rows=piece_rows, tail_rows=tail_rows, parts=parts),
        in_specs=[pl.BlockSpec(memory_space=pltpu.SMEM)] + [hbm] * 9,
        out_specs=[hbm] * 8,
        out_shape=[state] * 4 + [piece] * 3 + [jax.ShapeDtypeStruct(dh1.shape, bf16)],
        scratch_shapes=[wide, pltpu.VMEM((3, most, LANES), bf16)]
        + [wide] * 5
        + [
            pltpu.SemaphoreType.DMA((8, 3)),
            pltpu.VMEM(dh1.shape, f32),
            pltpu.VMEM(dx.shape, bf16),
            pltpu.VMEM(dh1.shape, bf16),
            pltpu.SemaphoreType.DMA((3,)),
        ],
        cost_estimate=pl.CostEstimate(
            flops=120 * piece_rows * LANES,
            bytes_accessed=120 * piece_rows * LANES,
            transcendentals=8 * piece_rows * LANES,
        ),
        compiler_params=params(),
        name="update",
    )(slot, grads, pieces, first, second, d_sum, own_rows, momentum_rows, dh1, dx)


def document_rows(seg_ref, live_ref, me):
    half = seg_ref.shape[1] // 2

    def own_first(row):
        left, right = row[:, :half], row[:, half:]
        return jnp.concatenate(
            [jnp.where(me == 0, left, right), jnp.where(me == 0, right, left)], axis=1
        )

    seg = own_first(seg_ref[...])
    return seg.astype(f32), jnp.where(own_first(live_ref[...]) == 1, seg, -1).astype(f32)


def as_column(row):
    return jnp.broadcast_to(row, (LANES, row.shape[1])).T


def attend_block(q, k, v_ones, code, seg_col, offset):
    rows_q, n = q.shape[0], k.shape[0]
    low = lax.broadcasted_iota(jnp.int32, (1, LANES), 1) < HD
    zero = jnp.zeros((), bf16)
    q = q * jnp.asarray(HD**-0.5, bf16)
    rows = lax.broadcasted_iota(jnp.int32, (rows_q, n), 0) + offset
    cols = lax.broadcasted_iota(jnp.int32, (rows_q, n), 1)
    allowed = (seg_col == code) | (rows == cols)
    outs = []
    tops = []
    for h in range(2):
        qh = jnp.where(low, q, zero) if h == 0 else jnp.where(low, zero, q)
        s = jnp.where(allowed, dot(qh, k, NT), MASKED)
        top = jnp.max(s, axis=1, keepdims=True)
        p = jnp.exp(s - top).astype(bf16)
        outs.append(dot(p, v_ones[h], NN))
        tops.append(top)
    num = jnp.where(low, outs[0], outs[1])
    den = pltpu.roll(jnp.where(low, outs[1], outs[0]), HD, 1)
    lse = (jnp.where(low, tops[0], tops[1]) + jnp.log(den)).T
    return (num / den).astype(bf16), lse[0:1], lse[HD : HD + 1]


def widen(src, low, high, flat, to):
    step = 128
    full = (high - low) // step

    @pl.loop(0, full)
    def _(i):
        rows = src[pl.ds(pl.multiple_of(low + i * step, 16), step), :]
        flat[pl.ds(to + i * step, step), :] = rows.astype(f32)

    rest = (high - low) % step
    if rest:
        flat[pl.ds(to + full * step, rest), :] = src[low + full * step : high, :].astype(f32)


def bring_rows(buf, flat, margin, offset, count, piece_rows):
    for p, low, high, at in piece_spans(offset, count, piece_rows, buf.shape[1]):
        widen(buf.at[p], low, high, flat, margin + at)


def emit_matrix(flat, out, margin, rows, blocks, first=0):
    chunk = 64

    @pl.loop(0, rows // chunk)
    def _(c):
        at = pl.ds(pl.multiple_of(first + c * chunk, chunk), chunk)
        for j in range(blocks):
            from_rows = pl.ds(margin + c * (chunk * blocks) + j, chunk, stride=blocks)
            out[at, j * LANES : (j + 1) * LANES] = flat[from_rows, :].astype(bf16)


def piece_spans(offset, count, piece_rows, padded):
    spans = []
    for p in range(offset // piece_rows, -(-(offset + count) // piece_rows)):
        low = max(offset - p * piece_rows, 0) // 16 * 16
        high = min(round_up(min(offset + count - p * piece_rows, piece_rows), 16), padded)
        spans.append((p, low, high, p * piece_rows + low - offset))
    return spans


def start_kernel(
    own_hbm, tokens_hbm, seg_ref, live_ref,
    proj_out, outw_out, inw_out, down_out, outw2_out, ctx2_out, pieces_out, x_out,
    q_out, k_out, v_out, ctx_out, vec_ref, c1_ref, lse_ref,
    rows32, buf, xbuf, flat, proj_s, outw_s, inw_s, down_s, outw2_s, obuf, ctx2_s, vec_s,
    zdown, zup, zrecv, ysend, yrecv, csend, crecv, xsem, local_sems, ctx_sems, wo_sems, q_ref, k_ref, v_ref, ctx_ref, seg_s,
    *, piece_rows, tail_rows, table, cuts, rows_q
):
    z = lax.axis_index("group")
    slot = lax.axis_index("slot")
    me = lax.axis_index("tensor")
    depth = GROUPS
    padded = buf.shape[1]
    half = tokens_hbm.shape[0]
    n = 2 * half
    mesh_id = pl.DeviceIdType.MESH

    load = pltpu.make_async_copy(own_hbm.at[:, 0, :], rows32, local_sems.at[0])
    load.start()
    x_load = pltpu.make_async_copy(tokens_hbm, xbuf.at[pl.ds(0, half)], local_sems.at[1])
    x_load.start()

    barrier = pltpu.get_barrier_semaphore()
    for where in ({"slot": slot ^ 1}, {"slot": slot ^ 2}, {"tensor": 1 - me}):
        pl.semaphore_signal(barrier, inc=1, device_id=where, device_id_type=mesh_id)

    @pl.when(z > 0)
    def _():
        pl.semaphore_signal(barrier, inc=1, device_id={"group": z - 1}, device_id_type=mesh_id)

    @pl.when(z < depth - 1)
    def _():
        pl.semaphore_signal(barrier, inc=1, device_id={"group": z + 1}, device_id_type=mesh_id)

    pl.semaphore_wait(barrier, 3 + jnp.where(z > 0, 1, 0) + jnp.where(z < depth - 1, 1, 0))

    load.wait()
    own = z * 4 + slot
    step = 128
    full = piece_rows // step

    @pl.loop(0, full)
    def _(i):
        r = pl.ds(pl.multiple_of(i * step, step), step)
        buf[own, r, :] = rows32[r, :].astype(bf16)

    tail = rows32[piece_rows - tail_rows :, :]
    left = tail - tail.astype(bf16).astype(f32)
    zeros = jnp.zeros((padded - piece_rows - tail_rows, LANES), f32)
    buf[own, full * step :, :] = jnp.concatenate([rows32[full * step :, :], left, zeros], axis=0).astype(bf16)

    def copy_of(piece, h, send, recv, where):
        part = buf.at[piece, pl.ds(*cuts[h])]
        return pltpu.make_async_remote_copy(
            src_ref=part, dst_ref=part, send_sem=send, recv_sem=recv, device_id=where, device_id_type=mesh_id
        )

    def down(b, h):
        return copy_of(b * 4 + slot, h, zdown.at[b, h], zrecv.at[b, h], {"group": z + 1})

    def up(b, h):
        return copy_of(b * 4 + slot, h, zup.at[b, h], zrecv.at[b, h], {"group": z - 1})

    def side(b, h):
        return copy_of(b * 4 + slot, h, ysend.at[b, h], yrecv.at[b, h], {"slot": slot ^ 2})

    def side_in(b, h):
        return copy_of(b * 4 + (slot ^ 2), h, ysend.at[b, h], yrecv.at[b, h], {"slot": slot ^ 2})

    def twin(b, h, k):
        return copy_of(
            b * 4 + (slot ^ (2 * k)), h, csend.at[2 * b + k, h], crecv.at[2 * b + k, h], {"slot": slot ^ 1}
        )

    def twin_in(b, h, k):
        return copy_of(
            b * 4 + (slot ^ 1 ^ (2 * k)), h, csend.at[2 * b + k, h], crecv.at[2 * b + k, h], {"slot": slot ^ 1}
        )

    parts = range(len(cuts))
    tail_part = len(cuts) - 1
    order = [tail_part] + list(range(tail_part))
    last = depth - 1
    ranked = (
        z,
        jnp.where(z == 0, 1, 0),
        jnp.where(z == 0, 2, jnp.where(z == 1, 3, 1)),
        jnp.where((z == 0) | (z == 2), 3, 2),
    )
    middle = (z == 1) | (z == 2)
    edge = jnp.logical_not(middle)

    def pass_on(b, h, aside=True):
        up(b, h).wait_recv()

        @pl.when((b < z) & (z < last))
        def _():
            down(b, h).start()

        @pl.when((b > z) & (z > 0))
        def _():
            up(b, h).start()

        if aside:
            side(b, h).start()
        twin(b, h, 0).start()

    def serve_z(b, h, when=None, aside=True):
        if h == tail_part:
            when = (b != last) if when is None else when & (b != last)
        if when is None:
            pass_on(b, h, aside)
        else:
            pl.when(when)(functools.partial(pass_on, b, h, aside))

    def serve_y(rank, h):
        b = ranked[rank]

        def go():
            side_in(b, h).wait_recv()
            twin(b, h, 1).start()

        if h == tail_part:
            pl.when(b != last)(go)
        else:
            go()

    for number, h in enumerate(order):
        pl.when(z > 0)(lambda h=h: up(z, h).start())
        at_once = (z == 0) | ((z == 1) & (number < 2)) | ((z == 2) & (number < 3))
        pl.when(at_once)(lambda h=h: down(z, h).start())
        side(z, h).start()
        twin(z, h, 0).start()

    x_load.wait()
    x_copy = pltpu.make_async_remote_copy(
        src_ref=xbuf.at[pl.ds(0, half)],
        dst_ref=xbuf.at[pl.ds(half, half)],
        send_sem=xsem.at[0],
        recv_sem=xsem.at[1],
        device_id={"tensor": 1 - me},
        device_id_type=mesh_id,
    )
    x_copy.start()

    pl.when(z == last - 1)(functools.partial(pass_on, last, tail_part))
    for h in order:
        serve_z(ranked[3], h, middle, False)
        serve_z(ranked[1], h)
    pl.when(z < last - 1)(functools.partial(pass_on, last, tail_part))

    def side_later(h):
        aside = middle & (ranked[3] != last) if h == tail_part else middle
        pl.when(aside)(lambda: side(ranked[3], h).start())

    for number, h in enumerate(order):
        later = ((z == 1) & (number >= 2)) | ((z == 2) & (number >= 3))
        pl.when(later)(lambda h=h: down(z, h).start())
        if number < 2:
            side_later(h)
    for h in order:
        serve_z(ranked[2], h, middle)
    for h in order[2:]:
        side_later(h)
    for h in order:
        serve_z(ranked[2], h, z == 0)
    for h in order[:3]:
        serve_z(ranked[3], h, z == last)
    side_in(last, tail_part).wait_recv()
    twin(last, tail_part, 1).start()
    for rank in range(2):
        for h in order:
            serve_y(rank, h)
    for k in range(2):
        twin_in(last, tail_part, k).wait_recv()
        for rank in range(2):
            b = ranked[rank]
            for h in parts:
                if h == tail_part:
                    pl.when(b != last)(lambda b=b, h=h, k=k: twin_in(b, h, k).wait_recv())
                else:
                    twin_in(b, h, k).wait_recv()

    at = (piece_rows - tail_rows) // 16 * 16
    shift = piece_rows - tail_rows - at
    ends = buf[4 * depth - 1, at:, :].astype(f32)
    vectors = ends[shift : shift + tail_rows] + ends[shift + tail_rows : shift + 2 * tail_rows]
    vec_s[0] = vectors

    def to_partner(src, dst, send, recv):
        return pltpu.make_async_remote_copy(
            src_ref=src, dst_ref=dst, send_sem=send, recv_sem=recv,
            device_id={"tensor": 1 - me}, device_id_type=mesh_id,
        )

    vec_copy = to_partner(vec_s.at[0], vec_s.at[1], xsem.at[2], xsem.at[3])
    vec_copy.start()
    (wo_offset, wo_rows, wo_blocks) = table[1]
    spans = piece_spans(wo_offset, wo_rows * wo_blocks, piece_rows, padded)
    total = sum(high - low for _, low, high, _ in spans)
    halves = (round_up(total // 2, 16), total)
    wo_parts = ([], [])
    at = 0
    for p, low, high, _ in spans:
        split = min(max(low + halves[0] - at, low), high)
        if split > low:
            wo_parts[0].append((p, low, split - low, at))
        if high > split:
            wo_parts[1].append((p, split, high - split, at + split - low))
        at += high - low
    in_core = slot % 2

    def wo_copies(c):
        return [
            to_partner(
                buf.at[p, pl.ds(low, count)], obuf.at[pl.ds(to, count)], wo_sems.at[0, j], wo_sems.at[1, j]
            )
            for j, (p, low, count, to) in enumerate(wo_parts[c])
        ]

    def wo_twin(c):
        first, end = (0, halves[0]) if c == 0 else halves
        part = obuf.at[pl.ds(first, end - first)]
        return pltpu.make_async_remote_copy(
            src_ref=part, dst_ref=part, send_sem=wo_sems.at[0, 3], recv_sem=wo_sems.at[1, 3],
            device_id={"slot": slot ^ 1}, device_id_type=mesh_id,
        )

    def by_core(action):
        for c in range(2):
            pl.when(in_core == c)(functools.partial(action, c))

    def wo_send(c):
        for copy in wo_copies(c):
            copy.start()

    def wo_pass(c):
        for copy in wo_copies(c):
            copy.wait_recv()
        wo_twin(c).start()

    def wo_done(c):
        wo_twin(1 - c).wait_recv()

    def wo_sent(c):
        for copy in wo_copies(c):
            copy.wait_send()
        wo_twin(c).wait_send()

    pl.when(z < 2)(lambda: by_core(wo_send))
    margin = 16
    (offset, rows, blocks) = table[0]
    bring_rows(buf, flat, margin, offset, rows * blocks, piece_rows)
    emit_matrix(flat, proj_s, margin, rows, blocks)
    out_copies = [pltpu.make_async_copy(proj_s, proj_out, local_sems.at[2])]
    out_copies[0].start()
    x_copy.wait()
    out_copies.append(pltpu.make_async_copy(xbuf, x_out, local_sems.at[3]))
    out_copies[1].start()
    query_bias = jnp.concatenate([vectors[j : j + 1] for j in range(blocks)], axis=1)
    value_bias = jnp.concatenate([vectors[blocks + j : blocks + j + 1] for j in range(blocks)], axis=1)
    depth_in = rows // 3
    for m, (ref, bias) in enumerate(((q_ref, query_bias), (k_ref, None), (v_ref, value_bias))):

        @pl.loop(0, n // 256)
        def _(i, m=m, ref=ref, bias=bias):
            r = pl.ds(pl.multiple_of(i * 256, 256), 256)
            acc = dot(xbuf[r, :], proj_s[m * depth_in : (m + 1) * depth_in, :], NN)
            if bias is not None:
                acc = acc + bias
            ref[r, :] = acc.astype(bf16)

    for number, (ref, out) in enumerate(((q_ref, q_out), (k_ref, k_out), (v_ref, v_out))):
        out_copies.append(pltpu.make_async_copy(ref, out, local_sems.at[13 + number]))
        out_copies[-1].start()
    third = jnp.where(z == 0, ranked[3], ranked[2])
    todo = [functools.partial(serve_z, third, h, edge) for h in order]
    todo += [functools.partial(serve_z, ranked[3], h, z == last) for h in order[3:]]
    todo += [functools.partial(serve_y, 2, h) for h in order]

    def landed(rank):
        b = ranked[rank]
        for h in parts:
            for k in range(2):
                if h == tail_part:
                    pl.when(b != last)(lambda b=b, h=h, k=k: twin_in(b, h, k).wait_recv())
                else:
                    twin_in(b, h, k).wait_recv()

    def ctx_copies(pair):
        columns = pl.ds(pair * LANES, LANES)
        return [
            to_partner(
                ctx_ref.at[pl.ds(half - first, half), columns],
                ctx2_s.at[pl.ds(first, half), columns],
                ctx_sems.at[0, 2 * pair + first // half],
                ctx_sems.at[1, 2 * pair + first // half],
            )
            for first in (0, half)
        ]

    low = lax.broadcasted_iota(jnp.int32, (1, LANES), 1) < HD
    one = jnp.ones((), bf16)
    seg, code = document_rows(seg_ref, live_ref, me)
    seg_s[...] = as_column(seg)
    for pair in range(blocks):
        c = slice(pair * LANES, (pair + 1) * LANES)
        k = k_ref[:, c]
        v = v_ref[:, c]
        v_ones = (jnp.where(low, v, one), jnp.where(low, one, v))
        for i in range(n // rows_q):
            r = slice(i * rows_q, (i + 1) * rows_q)
            ctx, lse_0, lse_1 = attend_block(q_ref[r, c], k, v_ones, code, seg_s[r, 0:1], i * rows_q)
            ctx_ref[r, c] = ctx
            lse_ref[pair, 0:1, r] = lse_0
            lse_ref[pair, 1:2, r] = lse_1
            if todo:
                todo.pop(0)()
        for copy in ctx_copies(pair):
            copy.start()
        if pair == 2:
            for act in todo:
                act()
            todo = []
            landed(2)
            pl.when(z >= 2)(lambda: by_core(wo_send))
    out_copies.append(pltpu.make_async_copy(ctx_ref, ctx_out, local_sems.at[16]))
    out_copies[-1].start()
    scratches = (None, outw_s, inw_s, down_s)
    mat_copies = [
        None,
        pltpu.make_async_copy(outw_s, outw_out, local_sems.at[4]),
        pltpu.make_async_copy(inw_s, inw_out, local_sems.at[5]),
        pltpu.make_async_copy(down_s, down_out, local_sems.at[6]),
    ]

    def matrix(m, first=0, end=None):
        (offset, rows, blocks) = table[m]
        count = (rows if end is None else end) - first
        bring_rows(buf, flat, margin, offset + first * blocks, count * blocks, piece_rows)
        emit_matrix(flat, scratches[m], margin, count, blocks, first)

    chunk_rows = 4 * piece_rows
    in_cut = (2 * chunk_rows - table[2][0]) // table[2][2] // 64 * 64
    down_cut = round_up(-(-(3 * chunk_rows - table[3][0]) // table[3][2]), 64)
    matrix(1)
    matrix(2, 0, in_cut)
    pl.when(ranked[3] == last)(lambda: matrix(2, in_cut))
    pl.when(ranked[3] != last)(lambda: matrix(3, down_cut))
    mat_copies[1].start()
    for h in order:
        serve_y(3, h)
    pl.when(z < 2)(lambda: by_core(wo_pass))
    landed(3)

    @pl.when(ranked[3] == last)
    def _():
        mat_copies[2].start()
        matrix(3, 0, down_cut)
        matrix(3, down_cut)
        mat_copies[3].start()

    @pl.when(ranked[3] != last)
    def _():
        matrix(3, 0, down_cut)
        mat_copies[3].start()
        matrix(2, in_cut)
        mat_copies[2].start()

    pl.when(z >= 2)(lambda: by_core(wo_pass))
    by_core(wo_done)
    at = 0
    for p, low, high, to in spans:
        widen(obuf, at, at + high - low, flat, margin + to)
        at += high - low
    emit_matrix(flat, outw2_s, margin, wo_rows, wo_blocks)
    out_copies.append(pltpu.make_async_copy(outw2_s, outw2_out, local_sems.at[11]))
    out_copies[-1].start()

    vec_copy.wait()
    hidden_rows = table[2][2]
    for j in range(hidden_rows):
        c1_ref[0:1, j * LANES : (j + 1) * LANES] = vec_s[0, 2 * blocks + j : 2 * blocks + j + 1, :]
    for row in range(6):
        for j in range(blocks):
            from_row = 2 * blocks + hidden_rows + row * blocks + j
            mine, theirs = vec_s[0, from_row : from_row + 1, :], vec_s[1, from_row : from_row + 1, :]
            left, right = jnp.where(me == 0, mine, theirs), jnp.where(me == 0, theirs, mine)
            vec_ref[row : row + 1, j * LANES : (j + 1) * LANES] = left
            vec_ref[row : row + 1, (blocks + j) * LANES : (blocks + j + 1) * LANES] = right

    for pair in range(blocks):
        for copy in ctx_copies(pair):
            copy.wait()
    out_copies.append(pltpu.make_async_copy(ctx2_s, ctx2_out, local_sems.at[12]))
    out_copies[-1].start()
    by_core(wo_sent)
    for b in range(depth):
        copy = pltpu.make_async_copy(buf.at[b * 4 + slot], pieces_out.at[b], local_sems.at[7 + b])
        copy.start()
        out_copies.append(copy)
    out_copies += mat_copies[1:]

    for b in range(depth):
        for h in parts:

            @pl.when((b <= z) & (z < depth - 1))
            def _(b=b, h=h):
                down(b, h).wait_send()

            @pl.when((b >= z) & (z > 0))
            def _(b=b, h=h):
                up(b, h).wait_send()

            side(b, h).wait_send()
            for k in range(2):
                twin(b, h, k).wait_send()
    for copy in out_copies:
        copy.wait()


def start(own_rows, tokens, seg_row, live_row, table, tail_rows, padded, cuts, rows_q=256):
    piece_rows = own_rows.shape[0]
    half, width = tokens.shape
    n = 2 * half
    pairs = table[0][2]
    local_width = pairs * LANES
    hbm = pl.BlockSpec(memory_space=pl.ANY)
    whole = pl.BlockSpec(memory_space=pltpu.VMEM)
    mats = [jax.ShapeDtypeStruct((rows, blocks * LANES), bf16) for _, rows, blocks in table]
    acts = [jax.ShapeDtypeStruct((n, local_width), bf16)] * 4
    most = max(rows * blocks for _, rows, blocks in table)
    parts = len(cuts)
    dma = pltpu.SemaphoreType.DMA
    return pl.pallas_call(
        functools.partial(
            start_kernel, piece_rows=piece_rows, tail_rows=tail_rows, table=table, cuts=cuts, rows_q=rows_q
        ),
        in_specs=[hbm, hbm, whole, whole],
        out_specs=[hbm] * 12 + [whole] * 3,
        out_shape=mats
        + [
            mats[1],
            jax.ShapeDtypeStruct((n, local_width), bf16),
            jax.ShapeDtypeStruct((GROUPS, padded, LANES), bf16),
            jax.ShapeDtypeStruct((n, width), bf16),
        ]
        + acts
        + [
            jax.ShapeDtypeStruct((6, width), f32),
            jax.ShapeDtypeStruct((1, table[2][2] * LANES), f32),
            jax.ShapeDtypeStruct((pairs, 2, n), f32)],
        scratch_shapes=[
            pltpu.VMEM((piece_rows, LANES), f32),
            pltpu.VMEM((4 * GROUPS, padded, LANES), bf16),
            pltpu.VMEM((n, width), bf16),
            pltpu.VMEM((most + 48, LANES), f32),
        ]
        + [pltpu.VMEM(m.shape, bf16) for m in mats]
        + [
            pltpu.VMEM(mats[1].shape, bf16),
            pltpu.VMEM((round_up(table[1][1] * table[1][2] + 64, 16), LANES), bf16),
            pltpu.VMEM((n, local_width), bf16),
            pltpu.VMEM((2, tail_rows, LANES), f32),
            dma((GROUPS, parts)),
            dma((GROUPS, parts)),
            dma((GROUPS, parts)),
            dma((GROUPS, parts)),
            dma((GROUPS, parts)),
            dma((2 * GROUPS, parts)),
            dma((2 * GROUPS, parts)),
            dma((4,)),
            dma((17,)),
            dma((2, 2 * pairs)),
            dma((2, 4)),
        ]
        + [pltpu.VMEM(a.shape, bf16) for a in acts]
        + [pltpu.VMEM((n, LANES), f32)],
        cost_estimate=pl.CostEstimate(
            flops=6 * n * width * local_width, bytes_accessed=60 << 20, transcendentals=8 * n * n
        ),
        compiler_params=params(collective_id=1, has_side_effects=True),
        name="start",
    )(own_rows, tokens, seg_row, live_row)


ERF = (0.254829592, -0.284496736, 1.421413741, -1.453152027, 1.061405429)
ERF_P = 0.3275911


def gelu_pair(u):
    bell = jnp.exp(-0.5 * u * u)
    t = 1.0 / (1.0 + (ERF_P * ROOT_HALF) * jnp.abs(u))
    poly = ERF[4]
    for number in ERF[3::-1]:
        poly = poly * t + number
    tail = (0.5 * poly * t) * bell
    phi = jnp.where(u >= 0, 1.0 - tail, tail)
    return u * phi, phi + u * bell * INV_ROOT_TWO_PI


def fold(values):
    return values.reshape(values.shape[0] // 8, 8, values.shape[1]).sum(axis=0)


def middle_kernel(
    outw_hbm, outw2_hbm, ctx_hbm, ctx2_hbm, x_hbm, inw_hbm, down_hbm, cot_hbm, vec_ref, c1_ref,
    block_hbm, dh1_hbm, dctx_hbm, d_outw_hbm, d_outw2_hbm, d_inw_hbm, d_down_hbm, tail_out,
    outw_ref, outw2_ref, ctx_ref, ctx2_ref, x_ref, inw_ref, down_ref, cot_ref,
    block_out, dh1_out, dctx_out, d_outw, d_outw2, d_inw, d_down,
    x1, norm1, inv1, x1_all, act, slope, dh2_all, dh1_low, dctx_send, part, dh2, box_send, box_recv, sums, c1_sum, vec_box, send_sems, recv_sems, vec_sems,
    load_sems, store_sems, in_sems,
    *, chunk
):
    me = lax.axis_index("tensor")
    near_rows, other_rows = pl.ds(0, cot_ref.shape[0]), pl.ds(cot_ref.shape[0], cot_ref.shape[0])
    loads = [
        pltpu.make_async_copy(src, dst, load_sems.at[number])
        for number, (src, dst) in enumerate(
            (
                (outw_hbm, outw_ref),
                (outw2_hbm, outw2_ref),
                (ctx_hbm.at[other_rows], ctx_ref.at[other_rows]),
                (ctx2_hbm.at[other_rows], ctx2_ref.at[other_rows]),
                (x_hbm.at[other_rows], x_ref.at[other_rows]),
                (inw_hbm, inw_ref),
                (down_hbm, down_ref),
                (ctx_hbm.at[near_rows], ctx_ref.at[near_rows]),
                (ctx2_hbm.at[near_rows], ctx2_ref.at[near_rows]),
                (x_hbm.at[near_rows], x_ref.at[near_rows]),
                (cot_hbm, cot_ref),
            )
        )
    ]
    for copy in loads:
        copy.start()
    block_store, dh1_store, dctx_store, outw_store, outw2_store, down_store = stores = [
        pltpu.make_async_copy(src, dst, store_sems.at[number])
        for number, (src, dst) in enumerate(
            (
                (block_out, block_hbm),
                (dh1_out, dh1_hbm),
                (dctx_out, dctx_hbm),
                (d_outw, d_outw_hbm),
                (d_outw2, d_outw2_hbm),
                (d_down, d_down_hbm),
            )
        )
    ]
    half, width = cot_ref.shape
    count = half // chunk
    mesh_id = pl.DeviceIdType.MESH
    other = {"tensor": 1 - me}
    barrier = pltpu.get_barrier_semaphore()
    pl.semaphore_signal(barrier, inc=1, device_id=other, device_id_type=mesh_id)
    pl.semaphore_wait(barrier, 1)

    def rows_of(i):
        return pl.ds(pl.multiple_of(i * chunk, chunk), chunk)

    def far_rows(i):
        return pl.ds(pl.multiple_of(half + i * chunk, chunk), chunk)

    def summed(stage, i):
        return pltpu.make_async_remote_copy(
            src_ref=box_send.at[stage, rows_of(i)],
            dst_ref=box_recv.at[stage, rows_of(i)],
            send_sem=send_sems.at[stage, i],
            recv_sem=recv_sems.at[stage, i],
            device_id=other,
            device_id_type=mesh_id,
        )

    def gathered(i):
        return pltpu.make_async_remote_copy(
            src_ref=dh2_all.at[rows_of(i)],
            dst_ref=dh2_all.at[far_rows(i)],
            send_sem=send_sems.at[2, i],
            recv_sem=recv_sems.at[2, i],
            device_id=other,
            device_id_type=mesh_id,
        )

    def handed(i):
        return pltpu.make_async_remote_copy(
            src_ref=dctx_send.at[rows_of(i)],
            dst_ref=dctx_out.at[far_rows(i)],
            send_sem=send_sems.at[3, i],
            recv_sem=recv_sems.at[3, i],
            device_id=other,
            device_id_type=mesh_id,
        )

    gain_1, shift_1 = vec_ref[0:1, :], vec_ref[1:2, :]
    gain_2, shift_2 = vec_ref[2:3, :], vec_ref[3:4, :]
    bias_o, bias_2 = vec_ref[4:5, :], vec_ref[5:6, :]
    sums[...] = jnp.zeros_like(sums)
    c1_sum[...] = jnp.zeros_like(c1_sum)

    def normed(h):
        centred = h - jnp.mean(h, axis=-1, keepdims=True)
        inv = lax.rsqrt(jnp.mean(centred * centred, axis=-1, keepdims=True) + NORM_EPS)
        return centred * inv, inv

    def normed_back(dn, n, inv):
        return inv * (
            dn - jnp.mean(dn, axis=-1, keepdims=True) - n * jnp.mean(dn * n, axis=-1, keepdims=True)
        )

    def forward(r):
        u = dot(x1_all[r, :], inw_ref[...], NN) + c1_ref[...]
        a, s = gelu_pair(u)
        act[r, :] = a.astype(bf16)
        slope[r, :] = s.astype(bf16)
        return dot(act[r, :], down_ref[...], NN)

    def backward(r):
        da = dot(dh2_all[r, :], down_ref[...], NT)
        du = da * slope[r, :].astype(f32)
        low = du.astype(bf16)
        slope[r, :] = low
        c1_sum[...] += fold(low.astype(f32))
        return dot(low, inw_ref[...], NT)

    def first_norm(r):
        branch = dot(ctx_ref[r, :], outw_ref[...], NN) + dot(ctx2_ref[r, :], outw2_ref[...], NN)
        n, inv = normed(x_ref[r, :].astype(f32) + (branch + bias_o))
        middle = n * gain_1 + shift_1
        x1_all[r, :] = middle.astype(bf16)
        return n, inv, middle

    for copy in loads[:5]:
        copy.wait()
    first_norm(far_rows(0))
    for copy in loads[5:7]:
        copy.wait()

    @pl.loop(0, count)
    def _(i):
        @pl.when(i > 0)
        def _():
            first_norm(far_rows(i))

        box_send[0, rows_of(i), :] = forward(far_rows(i)).astype(bf16)
        summed(0, i).start()

    for copy in loads[7:10]:
        copy.wait()

    @pl.loop(0, count)
    def _(i):
        r = rows_of(i)
        n, inv, middle = first_norm(r)
        norm1[r, :] = n
        inv1[r, :] = jnp.broadcast_to(inv, (chunk, LANES))
        x1[r, :] = middle
        part[r, :] = forward(r)

    loads[10].wait()

    @pl.loop(0, count)
    def _(i):
        r = rows_of(i)
        summed(0, i).wait_recv()
        h = x1[r, :] + (part[r, :] + box_recv[0, r, :].astype(f32) + bias_2)
        n, inv = normed(h)
        block_out[r, :] = (n * gain_2 + shift_2).astype(bf16)
        dy = cot_ref[r, :].astype(f32)
        dh = normed_back(dy * gain_2, n, inv)
        sums[2] += fold(dy * n)
        sums[3] += fold(dy)
        sums[5] += fold(dh)
        dh2[r, :] = dh
        dh2_all[r, :] = dh.astype(bf16)
        gathered(i).start()
        part[r, :] = backward(r)

    block_store.start()

    @pl.loop(0, count)
    def _(i):
        gathered(i).wait_recv()
        box_send[1, rows_of(i), :] = backward(far_rows(i)).astype(bf16)
        summed(1, i).start()

    hidden = act.shape[1]
    block = hidden // 8

    def down_grad(j):
        c = pl.ds(pl.multiple_of(j * block, block), block)
        d_down[c, :] = dot(act[:, c].T, dh2_all[...], NN).astype(bf16)

    def in_grad(j):
        c = pl.ds(pl.multiple_of(j * block, block), block)
        d_inw[:, c] = dot(x1_all[...].T, slope[:, c], NN).astype(bf16)
        in_store(j).start()

    def in_store(j):
        c = pl.ds(pl.multiple_of(j * block, block), block)
        return pltpu.make_async_copy(d_inw.at[:, c], d_inw_hbm.at[:, c], in_sems.at[j])

    per_chunk = 8 // count

    @pl.loop(0, count)
    def _(i):
        for j in range(per_chunk):
            down_grad(i * per_chunk + j)
        r = rows_of(i)
        summed(1, i).wait_recv()
        dx = dh2[r, :] + part[r, :] + box_recv[1, r, :].astype(f32)
        n = norm1[r, :]
        dh = normed_back(dx * gain_1, n, inv1[r, 0:1])
        sums[0] += fold(dx * n)
        sums[1] += fold(dx)
        sums[4] += fold(dh)
        dh1_out[r, :] = dh
        dh1_low[r, :] = dh.astype(bf16)
        dctx_send[r, :] = dot(dh1_low[r, :], outw2_ref[...], NT).astype(bf16)
        handed(i).start()
        dctx_out[r, :] = dot(dh1_low[r, :], outw_ref[...], NT).astype(bf16)

    dh1_store.start()
    down_store.start()
    for row in range(6):
        total = jnp.sum(sums[row], axis=0, keepdims=True)
        low, high = total[:, : width // 2], total[:, width // 2 :]
        mine, theirs = jnp.where(me == 0, low, high), jnp.where(me == 0, high, low)
        spread = width // 2 // LANES
        for j in range(spread):
            at = row * spread + j
            vec_box[0, at : at + 1, :] = mine[:, j * LANES : (j + 1) * LANES]
            vec_box[1, at : at + 1, :] = theirs[:, j * LANES : (j + 1) * LANES]
    vec_copy = pltpu.make_async_remote_copy(
        src_ref=vec_box.at[1],
        dst_ref=vec_box.at[2],
        send_sem=vec_sems.at[0],
        recv_sem=vec_sems.at[1],
        device_id=other,
        device_id_type=mesh_id,
    )
    vec_copy.start()

    @pl.loop(0, 8)
    def _(j):
        in_grad(j)

    d_outw2[...] = dot(ctx2_ref[0:half, :].T, dh1_low[...], NN).astype(bf16)
    outw2_store.start()
    d_outw[...] = dot(ctx_ref[0:half, :].T, dh1_low[...], NN).astype(bf16)
    outw_store.start()

    @pl.loop(0, count)
    def _(i):
        handed(i).wait_recv()

    dctx_store.start()

    blocks = ctx_ref.shape[1] // LANES
    tail_out[0 : 2 * blocks, :] = jnp.zeros((2 * blocks, LANES), f32)
    c1_total = jnp.sum(c1_sum[...], axis=0, keepdims=True)
    for j in range(hidden // LANES):
        tail_out[2 * blocks + j : 2 * blocks + j + 1, :] = c1_total[:, j * LANES : (j + 1) * LANES]
    vec_copy.wait()
    tail_out[2 * blocks + hidden // LANES :, :] = vec_box[0] + vec_box[2]

    @pl.loop(0, count)
    def _(i):
        for stage in range(2):
            summed(stage, i).wait_send()
        gathered(i).wait_send()
        handed(i).wait_send()

    @pl.loop(0, 8)
    def _(j):
        in_store(j).wait()

    for copy in stores:
        copy.wait()


def middle(context, context_2, x_all, cotangent, vectors, inner_bias, out_w, out_w2, in_w, down_w, chunk=128):
    half, width = cotangent.shape
    n = 2 * half
    hidden = in_w.shape[1]
    local_width = context.shape[1]
    whole = pl.BlockSpec(memory_space=pltpu.VMEM)
    hbm = pl.BlockSpec(memory_space=pl.ANY)
    operands = (out_w, out_w2, context, context_2, x_all, in_w, down_w, cotangent)
    wide = pltpu.VMEM((half, width), f32)
    every = pltpu.VMEM((n, width), bf16)
    box = pltpu.VMEM((2, half, width), bf16)
    count = half // chunk
    return pl.pallas_call(
        functools.partial(middle_kernel, chunk=chunk),
        in_specs=[hbm] * 8 + [whole] * 2,
        out_specs=[hbm] * 7 + [whole],
        out_shape=[
            jax.ShapeDtypeStruct((half, width), bf16),
            jax.ShapeDtypeStruct((half, width), f32),
            jax.ShapeDtypeStruct((n, local_width), bf16),
            jax.ShapeDtypeStruct(out_w.shape, bf16),
            jax.ShapeDtypeStruct(out_w.shape, bf16),
            jax.ShapeDtypeStruct(in_w.shape, bf16),
            jax.ShapeDtypeStruct(down_w.shape, bf16),
            jax.ShapeDtypeStruct(((2 * local_width + hidden + 3 * width) // LANES, LANES), f32),
        ],
        scratch_shapes=[pltpu.VMEM(operand.shape, operand.dtype) for operand in operands]
        + [
            pltpu.VMEM((half, width), bf16),
            wide,
            pltpu.VMEM((n, local_width), bf16),
            pltpu.VMEM(out_w.shape, bf16),
            pltpu.VMEM(out_w.shape, bf16),
            pltpu.VMEM(in_w.shape, bf16),
            pltpu.VMEM(down_w.shape, bf16),
            wide,
            wide,
            pltpu.VMEM((half, LANES), f32),
            every,
            pltpu.VMEM((n, hidden), bf16),
            pltpu.VMEM((n, hidden), bf16),
            every,
            pltpu.VMEM((half, width), bf16),
            pltpu.VMEM((half, local_width), bf16),
            wide,
            wide,
            box,
            box,
            pltpu.VMEM((6, 8, width), f32),
            pltpu.VMEM((8, hidden), f32),
            pltpu.VMEM((3, 3 * width // LANES, LANES), f32),
            pltpu.SemaphoreType.DMA((4, count)),
            pltpu.SemaphoreType.DMA((4, count)),
            pltpu.SemaphoreType.DMA((2,)),
            pltpu.SemaphoreType.DMA((11,)),
            pltpu.SemaphoreType.DMA((6,)),
            pltpu.SemaphoreType.DMA((8,)),
        ],
        cost_estimate=pl.CostEstimate(
            flops=14 * n * width * hidden, bytes_accessed=40 << 20, transcendentals=2 * n * hidden
        ),
        compiler_params=params(collective_id=2, has_side_effects=True),
        name="middle",
    )(*operands, vectors, inner_bias)


def attend_back(q_ref, k_ref, v_ref, ctx_ref, dctx_ref, code, seg_ref, lse_ref, dq_ref, dk_ref, dv_ref, pair, rows_q, after_step):
    n = q_ref.shape[0]
    c = slice(pair * LANES, (pair + 1) * LANES)
    low = lax.broadcasted_iota(jnp.int32, (1, LANES), 1) < HD
    zero = jnp.zeros((), bf16)
    k = k_ref[:, c]
    v = v_ref[:, c]
    k_t = k.T
    pick = (
        lax.broadcasted_iota(jnp.int32, (8, LANES), 1) // HD
        == lax.broadcasted_iota(jnp.int32, (8, LANES), 0)
    ).astype(f32)
    dks = [jnp.zeros((n, LANES), f32)] * 2
    dvs = [jnp.zeros((n, LANES), f32)] * 2
    scale = jnp.asarray(HD**-0.5, bf16)
    for i in range(n // rows_q):
        r = slice(i * rows_q, (i + 1) * rows_q)
        q = q_ref[r, c] * scale
        do = dctx_ref[r, c]
        prod = do.astype(f32) * ctx_ref[r, c].astype(f32)
        delta = lax.dot_general(
            pick, prod, NT, precision=lax.Precision.HIGHEST, preferred_element_type=f32
        )
        keys = lax.broadcasted_iota(jnp.int32, (n, rows_q), 0)
        qs = lax.broadcasted_iota(jnp.int32, (n, rows_q), 1) + i * rows_q
        allowed = (code == seg_ref[:, r]) | (keys == qs)
        dqs = []
        for h in range(2):
            qh = jnp.where(low, q, zero) if h == 0 else jnp.where(low, zero, q)
            doh = jnp.where(low, do, zero) if h == 0 else jnp.where(low, zero, do)
            s = jnp.where(allowed, dot(k, qh, NT), MASKED)
            p = jnp.exp(s - lse_ref[pair, h : h + 1, r])
            dp = dot(v, doh, NT)
            ds = (p * (dp - delta[h : h + 1])).astype(bf16)
            dvs[h] = dvs[h] + dot(p.astype(bf16), do, NN)
            dks[h] = dks[h] + dot(ds, q, NN)
            dqs.append(dot(k_t[h * HD : (h + 1) * HD], ds, NN))
        dq_ref[r, c] = (jnp.concatenate(dqs, axis=0).T * (HD**-0.5)).astype(bf16)
        after_step(i)
    dk_ref[:, c] = jnp.where(low, dks[0], dks[1]).astype(bf16)
    dv_ref[:, c] = jnp.where(low, dvs[0], dvs[1]).astype(bf16)


def lay_flat(ref, low, high, blocks, flat, at):
    chunk = 16 if (high - low) % 64 else 64

    @pl.loop(0, (high - low) // chunk)
    def _(c):
        rows = pl.ds(pl.multiple_of(low + c * chunk, 16), chunk)
        for j in range(blocks):
            to_rows = pl.ds(at + c * (chunk * blocks) + j, chunk, stride=blocks)
            flat[to_rows, :] = ref[rows, j * LANES : (j + 1) * LANES].astype(f32)


def emit_pieces(flat, keep, send, slot, skip, piece_rows, ready):
    padded = send.shape[1]
    step = 128
    full = piece_rows // step
    rest = piece_rows - full * step
    for j in (3, 2, 1, 0):
        out = send if j % 2 else keep
        start = skip + (slot ^ j) * piece_rows

        @pl.loop(0, full)
        def _(i, out=out, j=j, start=start):
            rows = flat[pl.ds(start + i * step, step), :]
            out[j // 2, pl.ds(pl.multiple_of(i * step, step), step), :] = rows.astype(bf16)

        parts = [jnp.zeros((padded - piece_rows, LANES), f32)]
        if rest:
            parts = [flat[pl.ds(start + full * step, rest), :]] + parts
        out[j // 2, full * step : padded, :] = jnp.concatenate(parts, axis=0).astype(bf16)
        if j % 2:
            ready(j // 2)


def back_kernel(
    seg_ref, live_ref, lse_ref, outw_ref, tail_ref,
    q_hbm, k_hbm, v_hbm, ctx_hbm, dctx_hbm, x_hbm, inw_hbm, down_hbm, m_hbm, s_hbm, w_hbm, proj_hbm, outw2_hbm,
    g_out, d_out, dx_out,
    dq_ref, dk_ref, dv_ref,
    flat, down_s, inw_s, keep, send, near, far, tails, zin, g_stage, m_in, v_in, w_in,
    near_send, near_recv, far_send, far_recv, tail_send, tail_recv, z_send, z_recv, load_sems, out_sems,
    x_sems, x_free, q_ref, k_ref, v_ref, ctx_ref, dctx_ref, x_ref, act_sems, seg_s, wo_in,
    *, plans, piece_rows, cuts, rows_q
):
    me = lax.axis_index("tensor")
    z = lax.axis_index("group")
    slot = lax.axis_index("slot")
    last = GROUPS - 1
    mesh_id = pl.DeviceIdType.MESH
    core = {"slot": slot ^ 1}
    side = {"slot": slot ^ 2}
    tail_rows = tail_ref.shape[0]
    padded = send.shape[1]
    stage_loads, rest_loads = [], []
    for number, low, high, _, _ in plans[2][0]:
        src, dst = ((inw_hbm, inw_s), (down_hbm, down_s))[number - 2]
        rows = pl.ds(low, high - low)
        stage_loads.append(pltpu.make_async_copy(src.at[rows], dst.at[rows], load_sems.at[number - 2]))
        for side_number, (first, end) in enumerate(((0, low), (high, src.shape[0]))):
            if end > first:
                rows = pl.ds(first, end - first)
                rest_loads.append(
                    pltpu.make_async_copy(
                        src.at[rows], dst.at[rows], load_sems.at[5 + 2 * (number - 2) + side_number]
                    )
                )
    act_loads = [
        pltpu.make_async_copy(src, dst, act_sems.at[number])
        for number, (src, dst) in enumerate(
            (
                (q_hbm, q_ref),
                (k_hbm, k_ref),
                (v_hbm, v_ref),
                (ctx_hbm, ctx_ref),
                (dctx_hbm, dctx_ref),
                (x_hbm, x_ref),
            )
        )
    ]
    for copy in stage_loads + rest_loads:
        copy.start()
    barrier = pltpu.get_barrier_semaphore()
    for where in (core, side, {"tensor": 1 - me}):
        pl.semaphore_signal(barrier, inc=1, device_id=where, device_id_type=mesh_id)

    @pl.when(z > 0)
    def _():
        pl.semaphore_signal(barrier, inc=1, device_id={"group": z - 1}, device_id_type=mesh_id)

    @pl.when(z < last)
    def _():
        pl.semaphore_signal(barrier, inc=1, device_id={"group": z + 1}, device_id_type=mesh_id)

    pl.semaphore_wait(barrier, 3 + jnp.where(z > 0, 1, 0) + jnp.where(z < last, 1, 0))

    def to_core(b, j):
        return pltpu.make_async_remote_copy(
            src_ref=send.at[j],
            dst_ref=near.at[b, j],
            send_sem=near_send.at[b, j],
            recv_sem=near_recv.at[b, j],
            device_id=core,
            device_id_type=mesh_id,
        )

    def to_side(b, h):
        rows = pl.ds(*cuts[h])
        return pltpu.make_async_remote_copy(
            src_ref=keep.at[b, 1, rows],
            dst_ref=far.at[b, rows],
            send_sem=far_send.at[b, h],
            recv_sem=far_recv.at[b, h],
            device_id=side,
            device_id_type=mesh_id,
        )

    def tail_copy(k, where):
        return pltpu.make_async_remote_copy(
            src_ref=tails.at[2 * k],
            dst_ref=tails.at[2 * k + 1],
            send_sem=tail_send.at[k],
            recv_sem=tail_recv.at[k],
            device_id=where,
            device_id_type=mesh_id,
        )

    def along(b, h, landing, where):
        return pltpu.make_async_remote_copy(
            src_ref=keep.at[b, 0, pl.ds(*cuts[h])],
            dst_ref=zin.at[landing, pl.ds(*cuts[h])],
            send_sem=z_send.at[b, h],
            recv_sem=z_recv.at[landing, h],
            device_id=where,
            device_id_type=mesh_id,
        )

    def upward(b, h):
        return along(b, h, b, {"group": z + 1})

    def downward(b, h):
        return along(b, h, jnp.where(z - 1 == b, GROUPS, b), {"group": z - 1})

    def pass_aside(b, first=0, end=None):
        if first == 0:
            to_core(b, 1).wait_recv()
        for h in range(first, len(cuts) if end is None else end):

            def add(at, count):
                r = pl.ds(at, count)
                keep[b, 1, r, :] = (keep[b, 1, r, :].astype(f32) + near[b, 1, r, :].astype(f32)).astype(bf16)

            in_steps(*cuts[h], 128, add)
            to_side(b, h).start()

    def sent(b):
        for j in (1, 0):
            to_core(b, j).wait_send()

    def loads(b):
        rows = pl.ds(0, piece_rows)
        return (
            pltpu.make_async_copy(m_hbm.at[rows, b, :], m_in.at[rows], load_sems.at[2]),
            pltpu.make_async_copy(s_hbm.at[rows, b, :], v_in.at[rows], load_sems.at[3]),
            pltpu.make_async_copy(w_hbm.at[b, pl.ds(0, padded)], w_in, load_sems.at[4]),
        )

    def store(b, h):
        rows = pl.ds(*cuts[h])
        return pltpu.make_async_copy(g_stage.at[rows], g_out.at[b, rows], out_sems.at[b, h])

    turn = (2, 1, 3, 0)

    def differ(b, h):
        k = turn.index(b)
        start, count = cuts[h]
        if h == 0:
            to_core(b, 0).wait_recv()
            for copy in loads(b):
                copy.wait()
        to_side(b, h).wait_recv()
        if b == last and h == len(cuts) - 1:
            at = piece_rows - tail_rows
            low = at // 16 * 16
            extra = jnp.where(slot == last, tails[2] + tails[3], 0.0)
            around = [extra]
            if at > low:
                around = [jnp.zeros((at - low, LANES), f32)] + around
            if padded > piece_rows:
                around = around + [jnp.zeros((padded - piece_rows, LANES), f32)]
            ends = slice(low, padded)
            far[b, ends, :] = (far[b, ends, :].astype(f32) + jnp.concatenate(around, axis=0)).astype(bf16)
        if k:
            store(turn[k - 1], h).wait()

        def step(at, rows):
            r = pl.ds(at, rows)
            g = keep[b, 0, r, :].astype(f32) + near[b, 0, r, :].astype(f32) + far[b, r, :].astype(f32)
            g_stage[r, :] = g
            first = BETA_ONE * m_in[r, :] + (1 - BETA_ONE) * g
            second = BETA_TWO * v_in[r, :] + (1 - BETA_TWO) * g * g
            root = jnp.sqrt(second * (1 / (1 - BETA_TWO**STEP))) + ADAM_EPS
            decay = INNER_RATE * DECAY
            if b == last:
                here = lax.broadcasted_iota(jnp.int32, (rows, LANES), 0) + at
                decay = jnp.where((slot < last) | (here < piece_rows - tail_rows), decay, 0.0)
            d = (INNER_RATE / (1 - BETA_ONE**STEP)) * first / root + decay * w_in[r, :].astype(f32)
            keep[b, 0, r, :] = d.astype(bf16)

        in_steps(start, count, 128, step)
        store(b, h).start()
        if b > 0:
            pl.when(z == 0)(lambda: upward(b, h).start())
        if b < last:
            pl.when(z == last)(lambda: downward(b, h).start())
        if h == len(cuts) - 1 and k + 1 < GROUPS:
            for copy in loads(turn[k + 1]):
                copy.start()

    def hop(b, at, h):
        def go():
            along(b, h, b, {"group": z}).wait_recv()

            def add(at, count):
                r = pl.ds(at, count)
                keep[b, 0, r, :] = (keep[b, 0, r, :].astype(f32) + zin[b, r, :].astype(f32)).astype(bf16)

            in_steps(*cuts[h], 128, add)
            (upward if at < b else downward)(b, h).start()

        pl.when(z == at)(go)

    blank = slice(piece_rows, padded)
    m_in[blank, :] = jnp.zeros((padded - piece_rows, LANES), f32)
    v_in[blank, :] = jnp.zeros((padded - piece_rows, LANES), f32)
    for copy in loads(turn[0]):
        copy.start()

    wo_copy = pltpu.make_async_remote_copy(
        src_ref=outw2_hbm,
        dst_ref=wo_in,
        send_sem=x_sems.at[6],
        recv_sem=x_sems.at[7],
        device_id={"tensor": 1 - me},
        device_id_type=mesh_id,
    )
    wo_copy.start()
    for copy in stage_loads:
        copy.wait()
    refs = {1: wo_in, 2: inw_s, 3: down_s}

    def lay_chunk(b):
        segments, skip, has_tail = plans[b]
        for number, low, high, blocks, at in segments:
            if number:
                lay_flat(refs[number], low, high, blocks, flat, at)
        if has_tail:
            at = skip + 4 * piece_rows - tail_rows
            flat[pl.ds(at, tail_rows), :] = jnp.zeros((tail_rows, LANES), f32)

    def emit_chunk(b):
        emit_pieces(flat, keep.at[b], send, slot, plans[b][1], piece_rows, lambda j: to_core(b, j).start())

    def output_chunk():
        wo_copy.wait()

        @pl.loop(0, wo_in.shape[0] // 16)
        def _(i):
            r = pl.ds(pl.multiple_of(i * 16, 16), 16)
            wo_in[r, :] = (wo_in[r, :].astype(f32) + outw_ref[r, :].astype(f32)).astype(bf16)

        lay_chunk(1)
        sent(3)
        emit_chunk(1)

    lay_chunk(2)
    emit_chunk(2)
    pass_aside(2)
    for copy in rest_loads:
        copy.wait()
    for copy in act_loads:
        copy.start()
    lay_chunk(3)
    sent(2)
    emit_chunk(3)

    half = q_ref.shape[0] // 2
    local_width = q_ref.shape[1]
    depth_in = x_ref.shape[1]
    proj_loads = [
        pltpu.make_async_copy(
            proj_hbm.at[pl.ds(m * depth_in, depth_in)],
            inw_s.at[:, pl.ds(m * local_width, local_width)],
            x_sems.at[2 + m],
        )
        for m in range(3)
    ]

    def make_free():
        pl.semaphore_signal(x_free, inc=1, device_id={"tensor": 1 - me}, device_id_type=mesh_id)
        for copy in proj_loads:
            copy.start()

    parts = range(len(cuts))
    act = functools.partial
    fourth = len(cuts) // 4

    def differ_some(b, part):
        for h in range(part * fourth, (part + 1) * fourth):
            differ(b, h)

    def hop_some(b, at, part):
        for h in range(part * fourth, (part + 1) * fourth):
            hop(b, at, h)

    events = {
        0: [act(differ_some, 2, 0)],
        2: [act(differ_some, 2, 1)],
        4: [act(differ_some, 2, 2), act(pass_aside, 3, 0, fourth)],
        5: [act(hop_some, 2, 1, 0)],
        6: [output_chunk, make_free],
        7: [act(pass_aside, 1), act(differ_some, 2, 3)],
        8: [act(pass_aside, 3, fourth), act(hop_some, 2, 1, 1)],
        9: [act(hop_some, 2, 1, 2)],
        10: [act(differ_some, 1, 0)],
        11: [act(hop_some, 2, 1, 3)],
        12: [act(differ_some, 1, 1)],
        13: [act(differ_some, 1, 2)],
        14: [act(hop_some, 1, 2, 0)],
        15: [act(differ_some, 1, 3)],
    }
    blocks = q_ref.shape[1] // LANES
    seg, code = document_rows(seg_ref, live_ref, me)
    seg_s[...] = seg
    code = as_column(code)[:, 0:1]
    per_pair = q_ref.shape[0] // rows_q

    def after_step(number):
        for act in events.get(number, ()):
            act()

    for copy in act_loads:
        copy.wait()
    for pair in range(blocks):
        attend_back(
            q_ref, k_ref, v_ref, ctx_ref, dctx_ref, code, seg_s, lse_ref, dq_ref, dk_ref, dv_ref, pair, rows_q,
            lambda i, pair=pair: after_step(pair * per_pair + i),
        )

    tails[0] = tail_ref[...]
    for m, ref in enumerate((dq_ref, dv_ref)):
        total = jnp.sum(ref[...].astype(f32), axis=0, keepdims=True)
        for j in range(blocks):
            row = m * blocks + j
            tails[0, row : row + 1, :] = total[:, j * LANES : (j + 1) * LANES]
    tail_copy(0, core).start()

    chunk = 256
    segments, skip, _ = plans[0]
    for m, ref in enumerate((dq_ref, dk_ref, dv_ref)):

        @pl.loop(0, depth_in // chunk)
        def _(c, m=m, ref=ref):
            columns = pl.ds(pl.multiple_of(c * chunk, chunk), chunk)
            acc = dot(x_ref[:, columns].T, ref[...], NN)
            for j in range(blocks):
                to_rows = pl.ds((m * depth_in + c * chunk) * blocks + j, chunk, stride=blocks)
                flat[to_rows, :] = acc[:, j * LANES : (j + 1) * LANES]

        if m == 0:
            tail_copy(0, core).wait()
            tails[2] = tails[0] + tails[1]
            tail_copy(1, side).start()
            hop_some(1, 2, 1)
        if m == 1:
            hop_some(1, 2, 2)

    for number, low, high, wide, at in segments:
        if number:
            lay_flat(refs[number], low, high, wide, flat, at)
    sent(1)
    emit_chunk(0)
    pass_aside(0)
    hop_some(1, 2, 3)
    tail_copy(1, side).wait()
    for h in parts:
        differ(3, h)

    for copy in proj_loads:
        copy.wait()

    def through(row):
        r = pl.ds(row, 256)
        acc = dot(dq_ref[r, :], inw_s[:, 0:local_width], NT)
        acc = acc + dot(dk_ref[r, :], inw_s[:, local_width : 2 * local_width], NT)
        return acc + dot(dv_ref[r, :], inw_s[:, 2 * local_width : 3 * local_width], NT)

    @pl.loop(0, half // 256)
    def _(i):
        down_s[pl.ds(pl.multiple_of(i * 256, 256), 256), :] = through(
            pl.multiple_of(half + i * 256, 256)
        ).astype(bf16)

    pl.semaphore_wait(x_free, 1)
    x_copy = pltpu.make_async_remote_copy(
        src_ref=down_s.at[pl.ds(0, half)],
        dst_ref=down_s.at[pl.ds(half, half)],
        send_sem=x_sems.at[0],
        recv_sem=x_sems.at[1],
        device_id={"tensor": 1 - me},
        device_id_type=mesh_id,
    )
    x_copy.start()
    differ(0, 0)

    @pl.loop(0, half // 256)
    def _(i):
        down_s[pl.ds(pl.multiple_of(2 * half + i * 256, 256), 256), :] = through(
            pl.multiple_of(i * 256, 256)
        ).astype(bf16)

    count = len(cuts)
    for t in range(1, count + 4):
        for act_on, lag in (
            (act(differ, 0), 0),
            (act(hop, 3, 1), 1),
            (act(hop, 3, 2), 2),
            (act(hop, 0, 2), 2),
            (act(hop, 0, 1), 4),
        ):
            if 0 <= t - lag < count:
                act_on(t - lag)

    for h in parts:
        store(0, h).wait()
    for b in range(GROUPS):

        def finish(b=b):
            for h in parts:
                if b > 0:
                    along(b, h, b, {"group": z}).wait_recv()
                if b < last:
                    along(b, h, GROUPS, {"group": z}).wait_recv()

                def add(at, count):
                    r = pl.ds(at, count)
                    total = keep[b, 0, r, :].astype(f32)
                    if b > 0:
                        total = total + zin[b, r, :].astype(f32)
                    if b < last:
                        total = total + zin[GROUPS, r, :].astype(f32)
                    g_stage[r, :] = total

                in_steps(*cuts[h], 128, add)

        pl.when(z == b)(finish)
    x_copy.wait()
    dx_copy = pltpu.make_async_copy(down_s.at[pl.ds(half, 2 * half)], dx_out, x_sems.at[5])
    dx_copy.start()
    copy = pltpu.make_async_copy(g_stage, d_out, out_sems.at[GROUPS, 0])
    copy.start()
    for b in range(GROUPS):
        for h in parts:
            to_side(b, h).wait_send()

            @pl.when(z != b)
            def _(b=b, h=h):
                along(b, h, b, {"group": z}).wait_send()

    sent(0)
    copy.wait()
    dx_copy.wait()


def back(
    q, k, v, ctx, dctx, seg_row, live_row, lse, x_all, d_outw, d_outw2, tail, d_inw, d_down, first, second, pieces, proj_w,
    table, tail_at, piece_rows, rows_q=256
):
    per = 4
    padded = round_up(piece_rows, 16)
    tail_rows = tail.shape[0]
    plans = []
    most = 0
    for b in range(GROUPS):
        begin = b * per * piece_rows
        segments, base, size = chunk_plan(table, begin, begin + per * piece_rows, tail_at, tail_rows)
        plans.append((segments, begin - base, begin + per * piece_rows > tail_at))
        most = max(most, size)
    parts = 8
    marks = [padded * i // parts // 16 * 16 for i in range(parts)] + [padded]
    cuts = [(low, high - low) for low, high in zip(marks[:-1], marks[1:])]
    whole = pl.BlockSpec(memory_space=pltpu.VMEM)
    hbm = pl.BlockSpec(memory_space=pl.ANY)
    dma = pltpu.SemaphoreType.DMA
    n, local_width = q.shape
    grad = pltpu.VMEM((n, local_width), bf16)
    wide = pltpu.VMEM((padded, LANES), f32)
    return pl.pallas_call(
        functools.partial(back_kernel, plans=plans, piece_rows=piece_rows, cuts=cuts, rows_q=rows_q),
        in_specs=[whole] * 5 + [hbm] * 13,
        out_specs=[hbm] * 3,
        out_shape=[
            jax.ShapeDtypeStruct((GROUPS, padded, LANES), f32),
            jax.ShapeDtypeStruct((padded, LANES), f32),
            jax.ShapeDtypeStruct((n, x_all.shape[1]), bf16),
        ],
        scratch_shapes=[
            grad,
            grad,
            grad,
            pltpu.VMEM((round_up(most, 8) + 64, LANES), f32),
            pltpu.VMEM(d_down.shape, bf16),
            pltpu.VMEM(d_inw.shape, bf16),
            pltpu.VMEM((GROUPS, 2, padded, LANES), bf16),
            pltpu.VMEM((2, padded, LANES), bf16),
            pltpu.VMEM((GROUPS, 2, padded, LANES), bf16),
            pltpu.VMEM((GROUPS, padded, LANES), bf16),
            pltpu.VMEM((4, tail_rows, LANES), f32),
            pltpu.VMEM((GROUPS + 1, padded, LANES), bf16),
            wide,
            wide,
            wide,
            pltpu.VMEM((padded, LANES), bf16),
            dma((GROUPS, 2)),
            dma((GROUPS, 2)),
            dma((GROUPS, parts)),
            dma((GROUPS, parts)),
            dma((2,)),
            dma((2,)),
            dma((GROUPS, parts)),
            dma((GROUPS + 1, parts)),
            dma((9,)),
            dma((GROUPS + 1, parts)),
            dma((8,)),
            pltpu.SemaphoreType.REGULAR,
            grad,
            grad,
            grad,
            grad,
            grad,
            pltpu.VMEM(x_all.shape, bf16),
            dma((6,)),
            pltpu.VMEM((1, n), f32),
            pltpu.VMEM(d_outw.shape, bf16),
        ],
        cost_estimate=pl.CostEstimate(
            flops=30 * n * n * local_width, bytes_accessed=40 << 20, transcendentals=n * n * 8
        ),
        compiler_params=params(collective_id=4, has_side_effects=True),
        name="back",
    )(
        seg_row, live_row, lse, d_outw, tail, q, k, v, ctx, dctx, x_all, d_inw, d_down, first, second, pieces, proj_w, d_outw2
    )


def partner(block):
    return lax.ppermute(block, "tensor", [(0, 1), (1, 0)])


def both(own):
    return jnp.concatenate([own, partner(own)], axis=0)


def own_sum(partial):
    half = partial.shape[0] // 2
    return partial[:half].astype(f32) + partner(partial[half:].astype(bf16)).astype(f32)


def local_fast(
    tokens,
    cotangent,
    segment_ids,
    padding,
    shared_weights,
    first_moment,
    second_moment,
    outer_momentum,
):
    per = lax.axis_size("slot")
    piece_rows = shared_weights.shape[1] // LANES
    table, tail_at = matrix_table(2)
    tail_rows = GROUPS * per * piece_rows - tail_at
    padded = round_up(piece_rows + tail_rows, 16)

    own_rows = shared_weights.reshape(piece_rows, 1, LANES)
    seg_row, live_row = segment_ids[None], padding[None]
    end = padded - round_up(2 * tail_rows + 16, 16)
    marks = [end * i // 4 // 16 * 16 for i in range(4)] + [end, padded]
    cuts = [(low, high - low) for low, high in zip(marks[:-1], marks[1:])]
    (
        proj_w, out_w, in_w, down_w, out_w2, context_2, pieces, x_all,
        query, keys, values, context, vectors, inner_bias, lse
    ) = start(own_rows, tokens, seg_row, live_row, table, tail_rows, padded, cuts)
    (
        block_out, grad_one, grad_context, grad_out_w, grad_out_w2, grad_in_w, grad_down_w, tail_grad
    ) = middle(context, context_2, x_all, cotangent, vectors, inner_bias, out_w, out_w2, in_w, down_w)

    def blocked(state):
        return state.reshape(GROUPS, piece_rows, LANES).transpose(1, 0, 2)

    def unblocked(state):
        return state.transpose(1, 0, 2).reshape(1, 1, GROUPS, piece_rows * LANES)

    first = blocked(first_moment)
    second = blocked(second_moment)
    grads, d_sum, dx = back(
        query, keys, values, context, grad_context, seg_row, live_row, lse, x_all, grad_out_w, grad_out_w2,
        tail_grad, grad_in_w, grad_down_w, first, second, pieces, proj_w, table, tail_at, piece_rows
    )
    slot_word = lax.axis_index("slot").astype(jnp.int32).reshape(1)
    *states, mean_diff, new_momentum, new_weights, input_grad = update(
        slot_word, grads, pieces, first, second, d_sum, own_rows,
        outer_momentum.reshape(piece_rows, 1, LANES), grad_one, dx, tail_rows
    )
    rows_out = [state.reshape(1, piece_rows * LANES) for state in (mean_diff, new_momentum, new_weights)]
    return (block_out, input_grad, *[unblocked(state) for state in states], *rows_out)


def solution(mesh):
    dp = mesh.shape["dp"]
    tensor_size = mesh.shape["tensor"]
    piece = (4 * D * D + 2 * D * FF + 8 * D + FF) // tensor_size // dp
    if tensor_size == 2 and piece % LANES == 0 and dp % GROUPS == 0:
        mesh = Mesh(
            mesh.devices.reshape(GROUPS, dp // GROUPS, tensor_size), ("group", "slot", "tensor")
        )
        data = ("group", "slot")
        body = local_fast
    else:
        data = "dp"
        body = local_general
    every = ("group", "slot", "tensor") if body is local_fast else ("dp", "tensor")
    in_specs = (
        P(every, None),
        P(every, None),
        P(data),
        P(data),
        P("tensor", data),
        P("tensor", data, None, None),
        P("tensor", data, None, None),
        P("tensor", data),
    )
    out_specs = (
        P(every, None),
        P(every, None),
        P("tensor", data, None, None),
        P("tensor", data, None, None),
        P("tensor", data, None, None),
        P("tensor", data, None, None),
        P("tensor", data),
        P("tensor", data),
        P("tensor", data),
    )
    return jax.shard_map(body, mesh=mesh, in_specs=in_specs, out_specs=out_specs, check_vma=False)
```
